32 devices in a mesh: mod: 2 (over core), dp: 8 (over z, y), tensor: 2 (over x).
Axes of the slice: x: 2, y: 2, z: 4, core: 2. Of those that a mesh axis runs over, the one named last changes fastest.
Arguments:
- tokens: bfloat16 [5120, 4096], P('dp', 'tensor'), may hold values from -400 to 400
- modality: int32 [5120], P('dp'), may hold values from 0 to 1, as said below
- norm_gains: float32 [2, 4096], P('mod'), may hold values from 0.5 to 2
- qkv_weight: bfloat16 [2, 4096, 3, 2048], P('mod', 'dp', None, 'tensor'), may hold values from -3 to 3
- out_weight: bfloat16 [2, 2048, 4096], P('mod', 'dp', 'tensor'), may hold values from -0.125 to 0.125
Outputs:
- mixed: bfloat16 [5120, 4096], P('dp', 'tensor')
The draws below stay inside these ranges and needn't reach their ends.
Inputs may be any that keep to these rules, and one draw needn't show every extreme that they name: Each sequence's positions fall into aligned spans of 32 positions of one modality each. Each sequence holds at most 480 tokens of either modality; in every draw some sequence holds exactly 480 image tokens and another exactly 480 text tokens.
All inputs are finite; a program needn't handle non-finite values.
Results may differ from the reference program's by a relative error of at most 0.015.
Values may be sent and summed in bfloat16 or wider, within the bound.
No kernel may reach another device: no remote copies, remote signals or barrier semaphores. Data moves between devices by JAX's collectives and lax.ppermute only.
A program may use at most 128 MiB of HBM per device.

```python
import math
import jax
import jax.numpy as jnp
from jax import lax

D = 4096
HEADS = 16
HDIM = 128
HD = 2048
LEN = 640
SPAN = 32
CAP = 480
SEQS = 8
TOKENS = 5120


def draw_modality(key, part):
    keys = jax.random.split(key, 4)
    span_count = LEN // SPAN
    most_spans = CAP // SPAN
    least_spans = span_count - most_spans
    counts = jax.random.randint(keys[0], (SEQS,), least_spans, most_spans + 1)
    first_seq = jax.random.randint(keys[1], (), 0, SEQS)
    second_seq = (first_seq + jax.random.randint(keys[2], (), 1, SEQS)) % SEQS
    seq_index = jnp.arange(SEQS)
    counts = jnp.where(seq_index == first_seq, most_spans, jnp.where(seq_index == second_seq, least_spans, counts))
    span_ranks = jax.vmap(lambda sub_key: jax.random.permutation(sub_key, span_count))(jax.random.split(keys[3], SEQS))
    image_span = (span_ranks < counts[:, None]).astype(jnp.int32)
    return jnp.repeat(image_span, SPAN, axis=1).reshape(SEQS * LEN).astype(jnp.int32)


def draw_tokens(key, part):
    keys = jax.random.split(key, 3)
    noise_base = jax.random.truncated_normal(keys[0], -4.0, 4.0, (TOKENS, D), jnp.float32)
    row_scale = jnp.exp(jax.random.uniform(keys[1], (TOKENS, 1), jnp.float32, 0.0, math.log(10.0)))
    col_scale = jnp.exp(jax.random.uniform(keys[2], (1, D), jnp.float32, 0.0, math.log(10.0)))
    values = noise_base * row_scale * col_scale / 4.0
    return values.astype(jnp.bfloat16)


def draw_qkv_weight(key, part):
    keys = jax.random.split(key, 1)
    base_rows = jax.random.truncated_normal(keys[0], -4.0, 4.0, (2, D, 3, HEADS, HDIM), jnp.float32) / math.sqrt(D)
    blocks = base_rows
    return blocks.reshape(2, D, 3, HD).astype(jnp.bfloat16)


def levels(own_key, shape, shards, smallest, high):
    def one(dim, shards_of):
        steps = jax.random.uniform(jax.random.fold_in(jax.random.fold_in(own_key, 6), dim), (shards_of,), jnp.float32, smallest / len(shards), high / len(shards))
        return jnp.repeat(jnp.exp(steps), shape[dim] // shards_of).reshape((-1,) + (1,) * (len(shape) - dim - 1))

    gain = one(*shards[0])
    for cut in shards[1:]:
        gain = gain * one(*cut)
    return gain


def bell_draw(own_key, shape, spread, reach, cuts=(), kind=jnp.bfloat16):
    loudness = levels(own_key, shape, cuts, -0.22, 0.18) if cuts else 1.0
    drawn = jax.random.normal(own_key, shape, jnp.float32) * spread * loudness
    return jnp.minimum(jnp.maximum(drawn, -reach), reach).astype(kind)


def setup_inputs(seed: int = 0) -> dict:
    streams_of = jax.random.split(jax.random.key(seed), 6)
    return {
        "tokens": draw_tokens(jax.random.fold_in(streams_of[5], 71), 0),
        "modality": draw_modality(jax.random.fold_in(streams_of[5], 71), 0),
        "norm_gains": jnp.clip(jnp.exp(math.log(2.0) - 1.3862944 * jax.random.uniform(streams_of[2], (2, D), jnp.float32) ** levels(streams_of[2], (2, D), ((0, 2),), -0.2, 0.2)), 0.5, 2.0),
        "qkv_weight": draw_qkv_weight(jax.random.fold_in(streams_of[5], 71), 0),
        "out_weight": bell_draw(streams_of[4], (2, HD, D), HD ** -0.5, 0.125, ((0, 2), (1, 8), (2, 2))),
    }


def reference(tokens, modality, norm_gains, qkv_weight, out_weight):
    seq_tokens_all = tokens.reshape(SEQS, LEN, D)
    seq_modes_all = modality.reshape(SEQS, LEN)
    text_qkv = qkv_weight[0].reshape(D, 3 * HD)
    image_qkv = qkv_weight[1].reshape(D, 3 * HD)
    scale = HDIM ** (-0.5)

    def per_sequence(inputs):
        seq_tokens, seq_modes = inputs
        wide_rows = seq_tokens.astype(jnp.float32)
        inverse = lax.rsqrt(lax.optimization_barrier(jnp.mean(wide_rows * wide_rows, axis=-1, keepdims=True)) + 1e-05)
        gain_rows = norm_gains[seq_modes]
        normed = (wide_rows * inverse * gain_rows).astype(jnp.bfloat16)
        is_image = (seq_modes == 1)[:, None]
        projected = jnp.where(is_image, jnp.dot(normed, image_qkv, preferred_element_type=jnp.float32), jnp.dot(normed, text_qkv, preferred_element_type=jnp.float32))
        projected = projected.astype(jnp.bfloat16).reshape(LEN, 3, HEADS, HDIM)
        queries = projected[:, 0].astype(jnp.float32)
        keys_all = projected[:, 1].astype(jnp.float32)
        values = projected[:, 2].astype(jnp.float32)
        scores = jnp.einsum('phd,rhd->hpr', queries, keys_all) * scale
        position = jnp.arange(LEN, dtype=jnp.int32)
        causal = position[None, :] <= position[:, None]
        scores = jnp.where(causal[None], scores, -jnp.inf)
        probs = jax.nn.softmax(scores, axis=-1).astype(jnp.bfloat16)
        attended = jnp.einsum('hpr,rhd->phd', probs.astype(jnp.float32), values)
        attended = attended.astype(jnp.bfloat16).reshape(LEN, HD)
        result = jnp.where(is_image, jnp.dot(attended, out_weight[1], preferred_element_type=jnp.float32), jnp.dot(attended, out_weight[0], preferred_element_type=jnp.float32))
        return result.astype(jnp.bfloat16)
    mixed = lax.map(per_sequence, (seq_tokens_all, seq_modes_all))
    return mixed.reshape(TOKENS, D)
```

```python
import jax
import jax.numpy as jnp
from jax import lax
from jax.sharding import PartitionSpec as P

HDIM = 128
AXES = ("mod", "dp", "tensor")


def make_move(mesh):
    mods, rings, shards = mesh.shape["mod"], mesh.shape["dp"] // 2, mesh.shape["tensor"]

    def flat(m, z, y, x):
        return (m * rings * 2 + z * 2 + y) * shards + x

    def move(array, where):
        pairs = [
            (flat(m, z, y, x), flat(*where(m, z, y, x)))
            for m in range(mods)
            for z in range(rings)
            for y in range(2)
            for x in range(shards)
        ]
        return lax.ppermute(array, AXES, pairs)

    return move


def solution(mesh):
    rings, shards = mesh.shape["dp"] // 2, mesh.shape["tensor"]
    move = make_move(mesh)

    def to_core(array):
        return move(array, lambda m, z, y, x: (1 - m, z, y, x))

    def to_pair(array):
        return move(array, lambda m, z, y, x: (m, z, 1 - y, x))

    def around(array, step):
        return move(array, lambda m, z, y, x: (m, (z + step) % rings, y, x))

    def over_tensor(array):
        own = lax.axis_index("tensor")
        held = jnp.zeros((shards,) + array.shape, array.dtype)
        held = lax.dynamic_update_index_in_dim(held, array, own, 0)
        for step in range(1, shards):
            got = move(array, lambda m, z, y, x: (m, z, y, (x + step) % shards))
            held = lax.dynamic_update_index_in_dim(held, got, (own - step) % shards, 0)
        return held

    def ring(block, ahead, back):
        found = []
        for count, step in ((ahead, 1), (back, -1)):
            held = block
            for hop in range(1, count + 1):
                held = around(held, step)
                found.append((-step * hop, held))
        return found

    def on_device(tokens, modality, norm_gains, qkv_weight, out_weight):
        core = lax.axis_index("mod")
        place = lax.axis_index("dp")
        z, y = place // 2, place % 2
        length, features = tokens.shape
        kept = qkv_weight.shape[1]
        width = qkv_weight.shape[3] // 2
        heads = width // HDIM
        scale = HDIM ** (-0.5)

        def half(which):
            parts = [
                lax.dynamic_slice_in_dim(qkv_weight[0, :, j, :], which * width, width, 1)
                for j in range(3)
            ]
            return jnp.concatenate(parts, axis=1)

        own_block = half(y)
        pair_block = to_pair(half(1 - y))
        mid, rest = rings // 2, rings - 1 - rings // 2
        blocks = [(2 * z + y, own_block), (2 * z + 1 - y, pair_block)]
        blocks += [(2 * ((z + k) % rings) + y, b) for k, b in ring(own_block, mid, rest)]
        blocks += [(2 * ((z + k) % rings) + 1 - y, b) for k, b in ring(pair_block, rest, mid)]

        some = length // 2
        rows = lax.dynamic_slice_in_dim(tokens, core * some, some, 0)
        other_rows = to_pair(rows)
        fetched = jnp.stack([over_tensor(rows), over_tensor(other_rows)])
        swapped = to_core(fetched)
        first = jnp.where(core == 0, fetched, swapped)
        second = jnp.where(core == 0, swapped, fetched)
        full = jnp.stack([first, second], axis=2)
        full = full.reshape(2, shards, length, features)
        wide = full.astype(jnp.float32)
        inverse = lax.rsqrt(
            jnp.sum(wide * wide, axis=(1, 3), keepdims=True) / (shards * features) + 1e-05
        )
        gains = norm_gains[0].reshape(1, shards, 1, features)
        normed = (wide * inverse * gains).astype(jnp.bfloat16)
        normed = normed.reshape(2, shards, length, features // kept, kept)
        normed = normed.transpose(1, 3, 0, 2, 4).reshape(2 * rings, 2 * length, kept)

        total = jnp.zeros((2 * length, 3 * width), jnp.float32)
        for index, block in blocks:
            columns = lax.dynamic_index_in_dim(normed, index, 0, keepdims=False)
            total = total + jnp.dot(columns, block, preferred_element_type=jnp.float32)
        projected = total.astype(jnp.bfloat16).reshape(2, length, 3 * width)

        which = core ^ y
        own = lax.dynamic_index_in_dim(projected, which, 0, keepdims=False)
        got = to_core(lax.dynamic_index_in_dim(projected, 1 - which, 0, keepdims=False))
        kinds = jnp.stack([modality, to_pair(modality)])
        kind = lax.dynamic_index_in_dim(kinds, which, 0, keepdims=False)
        qkv = jnp.where((kind == core)[:, None], own, got).reshape(length, 3, heads, HDIM)
        position = jnp.arange(length, dtype=jnp.int32)
        allowed = position[None, :] <= position[:, None]
        scores = (
            jnp.einsum("qhd,khd->hqk", qkv[:, 0], qkv[:, 1], preferred_element_type=jnp.float32)
            * scale
        )
        scores = jnp.where(allowed[None], scores, -jnp.inf)
        probs = jax.nn.softmax(scores, axis=-1).astype(jnp.bfloat16)
        attended = jnp.einsum(
            "hqk,khd->qhd", probs, qkv[:, 2], preferred_element_type=jnp.float32
        )
        attended = attended.astype(jnp.bfloat16).reshape(length, width)

        attended = move(
            attended, lambda m, z, y, x: (m, z, y, x) if m == y else (1 - m, z, 1 - y, x)
        )
        attended = over_tensor(attended)
        swapped = to_core(attended)
        first = jnp.where(core == 0, attended, swapped)
        second = jnp.where(core == 0, swapped, attended)
        all_heads = jnp.stack([first, second], axis=1)
        all_heads = all_heads.transpose(2, 0, 1, 3).reshape(length, shards * 2 * width)

        held = out_weight.shape[1]
        own_out = out_weight[0]
        pair_out = to_pair(own_out)
        outs = [(2 * z + y, own_out), (2 * z + 1 - y, pair_out)]
        outs += [(2 * ((z + k) % rings) + y, b) for k, b in ring(own_out, mid, rest)]
        outs += [(2 * ((z + k) % rings) + 1 - y, b) for k, b in ring(pair_out, rest, mid)]
        result = jnp.zeros((length, out_weight.shape[2]), jnp.float32)
        for index, block in outs:
            columns = lax.dynamic_slice_in_dim(all_heads, index * held, held, 1)
            result = result + jnp.dot(columns, block, preferred_element_type=jnp.float32)
        result = result.astype(jnp.bfloat16)
        return jnp.where((modality == core)[:, None], result, to_core(result))

    return jax.shard_map(
        on_device,
        mesh=mesh,
        in_specs=(
            P("dp", "tensor"),
            P("dp"),
            P("mod", None),
            P("mod", "dp", None, "tensor"),
            P("mod", "dp", "tensor"),
        ),
        out_specs=P("dp", "tensor"),
        check_vma=False,
    )
```

```python
import jax
import jax.numpy as jnp
from jax import lax
from jax.experimental import pallas as pl
from jax.experimental.pallas import tpu as pltpu
from jax.sharding import PartitionSpec as P

HDIM = 128
AXES = ("mod", "dp", "tensor")
VMEM = 50 * 1024 * 1024
F32, BF16, I32 = jnp.float32, jnp.bfloat16, jnp.int32


def make_move(mesh):
    mods, rings, shards = mesh.shape["mod"], mesh.shape["dp"] // 2, mesh.shape["tensor"]

    def flat(m, z, y, x):
        return (m * rings * 2 + z * 2 + y) * shards + x

    def move(array, where):
        pairs = [
            (flat(m, z, y, x), flat(*where(m, z, y, x)))
            for m in range(mods)
            for z in range(rings)
            for y in range(2)
            for x in range(shards)
        ]
        return lax.ppermute(array, AXES, pairs)

    return move


def after(array, *earlier):
    return lax.optimization_barrier((array,) + earlier)[0]


def call(kernel, grid, in_specs, out_specs, out_shape, prefetch, args, flops, aliases=None, moved=0):
    outs = jax.tree.leaves(out_shape)
    moved = moved or sum(a.size * a.dtype.itemsize for a in list(args) + outs)
    return pl.pallas_call(
        kernel,
        grid_spec=pltpu.PrefetchScalarGridSpec(
            num_scalar_prefetch=1, grid=grid, in_specs=in_specs, out_specs=out_specs
        ),
        out_shape=out_shape,
        input_output_aliases=aliases or {},
        cost_estimate=pl.CostEstimate(flops=flops, bytes_accessed=moved, transcendentals=0),
        compiler_params=pltpu.CompilerParams(vmem_limit_bytes=VMEM),
    )(prefetch, *args)


def halves(weight, y):
    kinds, depth, width = weight.shape
    half, tile = width // 2, min(depth, 128)

    def kernel(y_ref, in_ref, own_ref, other_ref):
        low, high = in_ref[:, :, :half], in_ref[:, :, half:]
        first = y_ref[0] == 0
        own_ref[...] = jnp.where(first, low, high)
        other_ref[...] = jnp.where(first, high, low)

    out = jax.ShapeDtypeStruct((kinds, depth, half), weight.dtype)
    spec = pl.BlockSpec((kinds, tile, half), lambda i, y: (0, i, 0))
    return call(
        kernel,
        (depth // tile,),
        [pl.BlockSpec((kinds, tile, width), lambda i, y: (0, i, 0))],
        [spec, spec],
        [out, out],
        y.reshape(1),
        [weight],
        0,
    )


def normalize(places, held, gains, mine, theirs, shape, start, kept):
    slots, blocks, length, _ = shape
    shards = len(mine)
    count, features = mine[0].shape
    tile = 80 if count % 80 == 0 else count
    steps, half = count // tile, length // 2
    per = features // kept

    def kernel(p_ref, *refs):
        refs = refs[1:] if held is not None else refs
        gain_ref, out_ref = refs[0], refs[-1]
        core, own = p_ref[0], p_ref[1]

        def write(group):
            wide = [ref[...].astype(F32) for ref in group]
            total = sum(jnp.sum(w * w, axis=-1, keepdims=True) for w in wide)
            inverse = lax.rsqrt(total / (shards * features) + 1e-05)
            for step, w in enumerate(wide):
                shard = lax.rem(own - step + shards, shards)
                for i in range(per):
                    block = shard * per + i
                    part = w[:, i * kept : (i + 1) * kept] * inverse * gain_ref[block]
                    out_ref[0, block] = part.astype(BF16)

        @pl.when(pl.program_id(0) == core)
        def _():
            write(refs[1 : 1 + shards])

        @pl.when(pl.program_id(0) != core)
        def _():
            write(refs[1 + shards : 1 + 2 * shards])

    own_spec = pl.BlockSpec(
        (tile, features), lambda h, i, p: (jnp.where(h == p[0], i, jnp.where(h == 0, 0, steps - 1)), 0)
    )
    other_spec = pl.BlockSpec(
        (tile, features), lambda h, i, p: (jnp.where(h != p[0], i, jnp.where(h == 0, 0, steps - 1)), 0)
    )
    in_specs = [pl.BlockSpec((blocks, 1, kept), lambda h, i, p: (0, 0, 0))]
    in_specs += [own_spec] * shards + [other_spec] * shards
    args = [gains] + list(mine) + list(theirs)
    if held is not None:
        in_specs = [pl.BlockSpec(memory_space=pl.ANY)] + in_specs
        args = [held] + args
    out_spec = pl.BlockSpec(
        (1, blocks, tile, kept), lambda h, i, p: (p[2], 0, (h * half + start) // tile + i, 0)
    )
    return call(
        kernel,
        (2, steps),
        in_specs,
        out_spec,
        jax.ShapeDtypeStruct(shape, BF16),
        places,
        args,
        0,
        {1: 0} if held is not None else None,
        moved=8 * count * features * shards,
    )


def project(places, normed, blocks, total, final, fresh):
    slots, _, length, kept = normed.shape
    kinds, _, width = blocks[0].shape
    tile = min(width, 256)
    per = width // tile
    count = len(blocks)

    def kernel(p_ref, *refs):
        out_ref = refs[-1]
        summed = None if fresh else refs[2 * count][0]
        for i in range(count):
            part = jnp.dot(refs[i][0, 0], refs[count + i][0], preferred_element_type=F32)
            summed = part if summed is None else summed + part
        if final:
            out_ref[...] = summed.astype(BF16)
        else:
            out_ref[0] = summed

    def columns(i):
        return pl.BlockSpec((1, 1, length, kept), lambda n, p: (p[0], p[1 + i], 0, 0))

    total_spec = pl.BlockSpec((1, length, tile), lambda n, p: (p[0], 0, n))
    in_specs = [columns(i) for i in range(count)]
    in_specs += [pl.BlockSpec((1, kept, tile), lambda n, p: (n // per, 0, n % per))] * count
    args = [normed] * count + list(blocks)
    if total is not None:
        in_specs.append(pl.BlockSpec(memory_space=pl.ANY) if fresh else total_spec)
        args.append(total)
    aliases = None
    if final:
        out_spec = pl.BlockSpec((length, tile), lambda n, p: (0, n))
        out_shape = jax.ShapeDtypeStruct((length, kinds * width), BF16)
    else:
        out_spec, out_shape = total_spec, jax.ShapeDtypeStruct((slots, length, kinds * width), F32)
        if total is not None:
            aliases = {1 + 2 * count: 0}
    return call(
        kernel,
        (kinds * per,),
        in_specs,
        out_spec,
        out_shape,
        places,
        args,
        2 * count * length * kept * kinds * width,
        aliases,
        moved=2 * count * kept * (length + kinds * width) + 4 * length * kinds * width,
    )


def attend(own, got, mine):
    length, width = own.shape[0], own.shape[1] // 3
    heads = width // HDIM
    scale = HDIM ** (-0.5)
    tile = 128 if length % 128 == 0 else length

    def kernel(_, mine_ref, qo, ko, vo, qg, kg, vg, out_ref):
        keep = mine_ref[...] != 0

        def pick(a, b):
            return jnp.where(keep, a[...].astype(F32), b[...].astype(F32)).astype(BF16)

        query, key, value = pick(qo, qg), pick(ko, kg), pick(vo, vg)
        for i in range(length // tile):
            low, high = i * tile, (i + 1) * tile
            scores = lax.dot_general(
                query[low:high], key[:high], (((1,), (1,)), ((), ())), preferred_element_type=F32
            )
            rows = low + lax.broadcasted_iota(I32, (tile, high), 0)
            cols = lax.broadcasted_iota(I32, (tile, high), 1)
            scores = jnp.where(cols <= rows, scores * scale, -jnp.inf)
            top = jnp.max(scores, axis=-1, keepdims=True)
            raised = jnp.exp(scores - top)
            probs = (raised / jnp.sum(raised, axis=-1, keepdims=True)).astype(BF16)
            out = jnp.dot(probs, value[:high], preferred_element_type=F32)
            out_ref[low:high, :] = out.astype(BF16)

    def part(j):
        return pl.BlockSpec((length, HDIM), lambda h, p: (0, j * heads + h))

    return call(
        kernel,
        (heads,),
        [pl.BlockSpec((length, 1), lambda h, p: (0, 0))] + [part(0), part(1), part(2)] * 2,
        pl.BlockSpec((length, HDIM), lambda h, p: (0, h)),
        jax.ShapeDtypeStruct((length, width), BF16),
        jnp.zeros((1,), I32),
        [mine, own, own, own, got, got, got],
        4 * length * length * width,
    )


def combine(places, pieces, blocks, total, final):
    _, length, width = pieces.shape
    held, features = blocks[0][0].shape
    tile = min(features, 512)
    count = len(blocks)

    def kernel(p_ref, *refs):
        out_ref = refs[-1]
        summed = None if total is None else refs[3 * count][...]
        first = p_ref[0] == 0
        for i in range(count):
            low, high = refs[i][0, :, :held], refs[i][0, :, held:]
            near, far = jnp.where(first, low, high), jnp.where(first, high, low)
            part = jnp.dot(near, refs[count + 2 * i][...], preferred_element_type=F32)
            part += jnp.dot(far, refs[count + 2 * i + 1][...], preferred_element_type=F32)
            summed = part if summed is None else summed + part
        out_ref[...] = summed.astype(out_ref.dtype)

    def piece(i):
        return pl.BlockSpec((1, length, width), lambda n, p: (p[1 + i], 0, 0))

    total_spec = pl.BlockSpec((length, tile), lambda n, p: (0, n))
    in_specs = [piece(i) for i in range(count)]
    in_specs += [pl.BlockSpec((held, tile), lambda n, p: (0, n))] * (2 * count)
    args = [pieces] * count + [b for pair in blocks for b in pair]
    if total is not None:
        in_specs.append(total_spec)
        args.append(total)
    return call(
        kernel,
        (features // tile,),
        in_specs,
        total_spec,
        jax.ShapeDtypeStruct((length, features), BF16 if final else F32),
        places,
        args,
        2 * count * length * width * features,
        moved=2 * count * width * (length + features) + 4 * length * features,
    )


def solution(mesh):
    rings, shards = mesh.shape["dp"] // 2, mesh.shape["tensor"]
    move = make_move(mesh)

    def to_core(array):
        return move(array, lambda m, z, y, x: (1 - m, z, y, x))

    def to_pair(array):
        return move(array, lambda m, z, y, x: (m, z, 1 - y, x))

    def around(array, step):
        return move(array, lambda m, z, y, x: (m, (z + step) % rings, y, x))

    def over_tensor(array):
        return [array] + [
            move(array, lambda m, z, y, x: (m, z, y, (x + step) % shards))
            for step in range(1, shards)
        ]

    def ring(own, pair, begin):
        mid, rest = rings // 2, rings - 1 - rings // 2
        found, last = {}, []
        for step, counts in ((1, (mid, rest)), (-1, (rest, mid))):
            held, before = [own, pair], begin
            for hop in range(1, mid + 1):
                for kind in range(2):
                    if hop <= counts[kind]:
                        held[kind] = around(after(held[kind], *before), step)
                        before = (held[kind],)
                        found[kind, (-step * hop) % rings] = held[kind]
            last += list(before)
        return found, tuple(last)

    def on_device(tokens, modality, norm_gains, qkv_weight, out_weight):
        core = lax.axis_index("mod").astype(I32)
        place = lax.axis_index("dp").astype(I32)
        own = lax.axis_index("tensor").astype(I32)
        z, y = place // 2, place % 2
        length, features = tokens.shape
        kept = qkv_weight.shape[1]
        width = qkv_weight.shape[3] // 2
        half, quarter = length // 2, length // 4
        which = core ^ y

        own_block, away_block = halves(qkv_weight[0].transpose(1, 0, 2), y)
        pair_block = to_pair(away_block)
        found, ring_end = ring(own_block, pair_block, ())

        rows = lax.dynamic_slice_in_dim(tokens, core * half, half, 0)
        rest_rows = lax.dynamic_slice_in_dim(tokens, (1 - core) * half, half, 0)
        fetched = over_tensor(rows)
        swapped = [rest_rows] + [to_core(a) for a in fetched[1:]]
        gains = norm_gains[0].reshape(2 * rings, 1, kept)
        shape = (2, 2 * rings, length, kept)
        normed = normalize(
            jnp.stack([core, own, which]), None, gains, fetched, swapped, shape, 0, kept
        )
        before = pair_block
        behind = fetched[-1]
        for start in (0, quarter):
            part = to_pair(after(lax.slice_in_dim(rows, start, start + quarter, axis=0), before))
            before = part
            part = over_tensor(after(part, behind))
            behind = part[-1]
            normed = normalize(
                jnp.stack([core, own, 1 - which]),
                normed,
                gains,
                part,
                [to_core(a) for a in part],
                shape,
                start,
                kept,
            )
        y_end = before

        def index(kind, distance):
            return 2 * ((z + distance) % rings) + (y if kind == 0 else 1 - y)

        tags = {(0, 0): own_block, (1, 0): pair_block, **found}
        far = [t for t in ((0, rings // 2), (1, rings // 2)) if t in found]
        early = [t for t in tags if t not in far and (t[1] == 0 or (t[0] == 0 and t[1] in (1, rings - 1)))]
        middle = [t for t in tags if t not in early and t not in far]

        def add(slot, group, total, final=False, fresh=False):
            places = jnp.stack([slot] + [index(*t) for t in group]).astype(I32)
            return project(places, normed, [tags[t] for t in group], total, final, fresh)

        total = add(which, early, None, fresh=True)
        if middle:
            total = add(which, middle, total)
        total = add(1 - which, early + middle, total, fresh=True)
        zero = jnp.zeros((), I32)
        theirs = add(zero + 1, far, total, final=True)
        got = to_core(theirs)
        ours = add(zero, far, total, final=True)

        kinds = jnp.stack([modality, to_pair(modality)])
        kind = lax.dynamic_index_in_dim(kinds, which, 0, keepdims=False)
        attended = attend(ours, got, (kind == core).astype(I32)[:, None])

        attended = move(
            attended, lambda m, z, y, x: (m, z, y, x) if m == y else (1 - m, z, 1 - y, x)
        )
        held = over_tensor(attended)
        pieces = jnp.concatenate([jnp.stack(held), jnp.stack([to_core(a) for a in held])])

        own_out = after(out_weight[0], y_end)
        pair_out = to_pair(own_out)
        found, _ = ring(own_out, pair_out, ring_end)
        tags_out = {(0, 0): own_out, (1, 0): pair_out, **found}
        far_out = [rings // 2]
        near_out = [k for k in range(rings) if k not in far_out]

        def gather(group, total, final):
            found_at = []
            for distance in group:
                piece = (z + distance) % rings
                shard, part = piece // 2, piece % 2
                found_at.append(
                    jnp.where(part == core, 0, shards) + (own - shard + shards) % shards
                )
            places = jnp.stack([y] + found_at).astype(I32)
            blocks = [(tags_out[0, k], tags_out[1, k]) for k in group]
            return combine(places, pieces, blocks, total, final)

        result = gather(far_out, gather(near_out, None, False), True)
        return jnp.where((modality == core)[:, None], result, to_core(result))

    return jax.shard_map(
        on_device,
        mesh=mesh,
        in_specs=(
            P("dp", "tensor"),
            P("dp"),
            P("mod", None),
            P("mod", "dp", None, "tensor"),
            P("mod", "dp", "tensor"),
        ),
        out_specs=P("dp", "tensor"),
        check_vma=False,
    )
```

```python
import jax
import jax.numpy as jnp
from jax import lax
from jax.experimental import pallas as pl
from jax.experimental.pallas import tpu as pltpu
from jax.sharding import PartitionSpec as P

HDIM = 128
AXES = ("mod", "dp", "tensor")
VMEM = 50 * 1024 * 1024
F32, BF16, I32 = jnp.float32, jnp.bfloat16, jnp.int32


def after(array, *earlier):
    return lax.optimization_barrier((array,) + earlier)[0]


def call(kernel, grid, in_specs, out_specs, out_shape, prefetch, args, flops, aliases=None, moved=0):
    outs = jax.tree.leaves(out_shape)
    moved = moved or sum(a.size * a.dtype.itemsize for a in list(args) + outs)
    return pl.pallas_call(
        kernel,
        grid_spec=pltpu.PrefetchScalarGridSpec(
            num_scalar_prefetch=1, grid=grid, in_specs=in_specs, out_specs=out_specs
        ),
        out_shape=out_shape,
        input_output_aliases=aliases or {},
        cost_estimate=pl.CostEstimate(flops=flops, bytes_accessed=moved, transcendentals=0),
        compiler_params=pltpu.CompilerParams(vmem_limit_bytes=VMEM),
    )(prefetch, *args)


def halves(weight, outer, chunks):
    kinds, depth, width = weight.shape
    half, rows = width // 2, depth // chunks

    def kernel(o_ref, in_ref, low_ref, high_ref, mine_ref, away_ref):
        low, high = in_ref[:, :, :half], in_ref[:, :, half:]
        first = o_ref[0] == 1
        low_ref[...] = low
        high_ref[...] = high
        mine_ref[...] = jnp.where(first, low, high)
        away_ref[...] = jnp.where(first, high, low)

    tile = min(rows, 64)
    out = jax.ShapeDtypeStruct((kinds, rows, half), weight.dtype)
    spec = pl.BlockSpec((kinds, tile, half), lambda i, o: (0, i, 0))
    found = []
    for chunk in range(chunks):
        first = chunk * (rows // tile)
        found.append(
            call(
                kernel,
                (rows // tile,),
                [pl.BlockSpec((kinds, tile, width), lambda i, o, first=first: (0, first + i, 0))],
                [spec] * 4,
                [out] * 4,
                outer.reshape(1).astype(I32),
                [weight],
                0,
                moved=6 * kinds * rows * width,
            )
        )
    return found


def normalize(places, held, gains, mine, theirs, shape, start, kept):
    slots, blocks, length, _ = shape
    shards = len(mine)
    count, features = mine[0].shape
    tile = 80 if count % 80 == 0 else count
    steps, half = count // tile, length // 2
    per = features // kept

    def kernel(p_ref, *refs):
        refs = refs[1:] if held is not None else refs
        gain_ref, out_ref = refs[0], refs[-1]
        core, own = p_ref[0], p_ref[1]

        def write(group):
            wide = [ref[...].astype(F32) for ref in group]
            total = sum(jnp.sum(w * w, axis=-1, keepdims=True) for w in wide)
            inverse = lax.rsqrt(total / (shards * features) + 1e-05)
            for step, w in enumerate(wide):
                shard = lax.rem(own - step + shards, shards)
                for i in range(per):
                    block = shard * per + i
                    part = w[:, i * kept : (i + 1) * kept] * inverse * gain_ref[block]
                    out_ref[0, block] = part.astype(BF16)

        @pl.when(pl.program_id(0) == core)
        def _():
            write(refs[1 : 1 + shards])

        @pl.when(pl.program_id(0) != core)
        def _():
            write(refs[1 + shards : 1 + 2 * shards])

    own_spec = pl.BlockSpec(
        (tile, features), lambda h, i, p: (jnp.where(h == p[0], i, jnp.where(h == 0, 0, steps - 1)), 0)
    )
    other_spec = pl.BlockSpec(
        (tile, features), lambda h, i, p: (jnp.where(h != p[0], i, jnp.where(h == 0, 0, steps - 1)), 0)
    )
    in_specs = [pl.BlockSpec((blocks, 1, kept), lambda h, i, p: (0, 0, 0))]
    in_specs += [own_spec] * shards + [other_spec] * shards
    args = [gains] + list(mine) + list(theirs)
    if held is not None:
        in_specs = [pl.BlockSpec(memory_space=pl.ANY)] + in_specs
        args = [held] + args
    out_spec = pl.BlockSpec(
        (1, blocks, tile, kept), lambda h, i, p: (p[2], 0, (h * half + start) // tile + i, 0)
    )
    return call(
        kernel,
        (2, steps),
        in_specs,
        out_spec,
        jax.ShapeDtypeStruct(shape, BF16),
        places,
        args,
        0,
        {1: 0} if held is not None else None,
        moved=8 * count * features * shards,
    )


def project(places, normed, blocks, total, final, fresh):
    slots, _, length, kept = normed.shape
    kinds, _, width = blocks[0].shape
    tile = min(width, 256)
    per = width // tile
    count = len(blocks)

    def kernel(p_ref, *refs):
        out_ref = refs[-1]
        summed = None if fresh else refs[2 * count][0]
        for i in range(count):
            part = jnp.dot(refs[i][0, 0], refs[count + i][0], preferred_element_type=F32)
            summed = part if summed is None else summed + part
        if final:
            out_ref[...] = summed.astype(BF16)
        else:
            out_ref[0] = summed

    def columns(i):
        return pl.BlockSpec((1, 1, length, kept), lambda n, p: (p[0], p[1 + i], 0, 0))

    total_spec = pl.BlockSpec((1, length, tile), lambda n, p: (p[0], 0, n))
    in_specs = [columns(i) for i in range(count)]
    in_specs += [pl.BlockSpec((1, kept, tile), lambda n, p: (n // per, 0, n % per))] * count
    args = [normed] * count + list(blocks)
    if total is not None:
        in_specs.append(pl.BlockSpec(memory_space=pl.ANY) if fresh else total_spec)
        args.append(total)
    aliases = None
    if final:
        out_spec = pl.BlockSpec((length, tile), lambda n, p: (0, n))
        out_shape = jax.ShapeDtypeStruct((length, kinds * width), BF16)
    else:
        out_spec, out_shape = total_spec, jax.ShapeDtypeStruct((slots, length, kinds * width), F32)
        if total is not None:
            aliases = {1 + 2 * count: 0}
    return call(
        kernel,
        (kinds * per,),
        in_specs,
        out_spec,
        out_shape,
        places,
        args,
        2 * count * length * kept * kinds * width,
        aliases,
        moved=2 * count * kept * (length + kinds * width) + 4 * length * kinds * width,
    )


def attend(own, got, mine):
    length, width = own.shape[0], own.shape[1] // 3
    heads = width // HDIM
    scale = HDIM ** (-0.5)
    tile = 128 if length % 128 == 0 else length

    def kernel(_, mine_ref, qo, ko, vo, qg, kg, vg, out_ref):
        keep = mine_ref[...] != 0

        def pick(a, b):
            return jnp.where(keep, a[...].astype(F32), b[...].astype(F32)).astype(BF16)

        query, key, value = pick(qo, qg), pick(ko, kg), pick(vo, vg)
        for i in range(length // tile):
            low, high = i * tile, (i + 1) * tile
            scores = lax.dot_general(
                query[low:high], key[:high], (((1,), (1,)), ((), ())), preferred_element_type=F32
            )
            rows = low + lax.broadcasted_iota(I32, (tile, high), 0)
            cols = lax.broadcasted_iota(I32, (tile, high), 1)
            scores = jnp.where(cols <= rows, scores * scale, -jnp.inf)
            top = jnp.max(scores, axis=-1, keepdims=True)
            raised = jnp.exp(scores - top)
            probs = (raised / jnp.sum(raised, axis=-1, keepdims=True)).astype(BF16)
            out = jnp.dot(probs, value[:high], preferred_element_type=F32)
            out_ref[low:high, :] = out.astype(BF16)

    def part(j):
        return pl.BlockSpec((length, HDIM), lambda h, p: (0, j * heads + h))

    return call(
        kernel,
        (heads,),
        [pl.BlockSpec((length, 1), lambda h, p: (0, 0))] + [part(0), part(1), part(2)] * 2,
        pl.BlockSpec((length, HDIM), lambda h, p: (0, h)),
        jax.ShapeDtypeStruct((length, width), BF16),
        jnp.zeros((1,), I32),
        [mine, own, own, own, got, got, got],
        4 * length * length * width,
    )


def combine(places, pieces, blocks, total, final):
    _, _, length, width = pieces.shape
    _, held, features = blocks[0].shape
    tile = min(features, 256)
    count = len(blocks)
    cut = held % 128 == 0

    def kernel(p_ref, *refs):
        out_ref = refs[-1]
        summed = None if total is None else refs[2 * count][...]
        for i in range(count):
            if cut:
                columns = refs[i][0, 0]
            else:
                whole = refs[i][0, 0]
                columns = jnp.where(p_ref[2 + 2 * i] == 0, whole[:, :held], whole[:, held:])
            part = jnp.dot(columns, refs[count + i][0], preferred_element_type=F32)
            summed = part if summed is None else summed + part
        out_ref[...] = summed.astype(out_ref.dtype)

    def piece(i):
        if cut:
            return pl.BlockSpec(
                (1, 1, length, held), lambda n, p: (p[0], p[1 + 2 * i], 0, p[2 + 2 * i])
            )
        return pl.BlockSpec((1, 1, length, width), lambda n, p: (p[0], p[1 + 2 * i], 0, 0))

    total_spec = pl.BlockSpec((length, tile), lambda n, p: (0, n))
    in_specs = [piece(i) for i in range(count)]
    in_specs += [pl.BlockSpec((1, held, tile), lambda n, p: (0, 0, n))] * count
    args = [pieces] * count + list(blocks)
    if total is not None:
        in_specs.append(total_spec)
        args.append(total)
    return call(
        kernel,
        (features // tile,),
        in_specs,
        total_spec,
        jax.ShapeDtypeStruct((length, features), BF16 if final else F32),
        places,
        args,
        2 * count * length * held * features,
        moved=2 * count * held * (length + features) + 4 * length * features,
    )


def assemble(places, mine, near, near_other, far, far_other):
    length, width = near.shape
    tile = 80 if length % 160 == 0 else length // 2
    steps = length // 2 // tile

    def kernel(p_ref, mine_ref, a_ref, b_ref, c_ref, d_ref, out_ref):
        keep = mine_ref[...] != 0
        own = jnp.where(keep, a_ref[...].astype(F32), b_ref[...].astype(F32)).astype(BF16)
        held = (pl.program_id(0) // steps) == p_ref[0]
        other = jnp.where(held, c_ref[...], d_ref[...])
        first = p_ref[1] == 0
        out_ref[:, :width] = jnp.where(first, own, other)
        out_ref[:, width:] = jnp.where(first, other, own)

    rows = pl.BlockSpec((tile, width), lambda i, p: (i, 0))
    part = pl.BlockSpec((tile, width), lambda i, p: (i % steps, 0))
    return call(
        kernel,
        (2 * steps,),
        [pl.BlockSpec((tile, 1), lambda i, p: (i, 0)), rows, rows, part, part],
        pl.BlockSpec((tile, 2 * width), lambda i, p: (i, 0)),
        jax.ShapeDtypeStruct((length, 2 * width), BF16),
        places,
        [mine, near, near_other, far, far_other],
        0,
    )


def solution(mesh):
    places, shards = mesh.shape["dp"], mesh.shape["tensor"]
    mods = mesh.shape["mod"]
    lined = places == 8

    def move(array, where):
        pairs = []
        for m in range(mods):
            for d in range(places):
                for x in range(shards):
                    to = where(m, d, x)
                    if to is not None:
                        target = (to[0] * places + to[1]) * shards + to[2]
                        pairs.append(((m * places + d) * shards + x, target))
        return lax.ppermute(array, AXES, pairs)

    def to_core(array):
        return move(array, lambda m, d, x: (1 - m, d, x))

    def over_tensor(array):
        return [array] + [
            move(array, lambda m, d, x: (m, d, (x + step) % shards)) for step in range(1, shards)
        ]

    def edge(m, d, x):
        return m, d ^ 2, x

    def outward(m, d, x):
        return (m, d ^ 2, x) if d // 2 in (1, 2) else None

    def across(m, d, x):
        return (m, (3 - d // 2) * 2 + d % 2, x) if d // 2 in (1, 2) else None

    def across_or_stay(m, d, x):
        return across(m, d, x) or (m, d, x)

    def pair(m, d, x):
        return m, d ^ 1, x

    class Links:
        def __init__(self, depth):
            self.depth, self.sent = depth, {}

        def send(self, link, array, where):
            sent = self.sent.setdefault(link, [])
            if len(sent) >= self.depth:
                array = after(array, sent[-self.depth])
            sent.append(move(array, where))
            return sent[-1]

    def gather(links, chunks, place, outer, between):
        steps = range(len(chunks))
        z, y = place // 2, place % 2
        if not lined:
            column = (z ^ (z // 2)) & 1
            group = [(place, c, chunks[c][2]) for c in steps]
            for step in range(1, places):
                to = ((place + step) % places) // 2
                same = ((to ^ (to // 2)) & 1) == column
                for c in steps:
                    sent = jnp.where(same, chunks[c][2], chunks[c][3])
                    got = move(sent, lambda m, d, x: (m, (d + step) % places, x))
                    group.append(((place - step) % places, c, got))
            between()
            return [[], group[:-2], group[-2:]]
        send = links.send
        far_inner = jnp.where(z < 2, 2, 1)
        far_outer = 3 - 3 * (z // 2)
        first, second, third, fourth = [], [], [], []
        e1, e2, m1, m2 = [], [], [], []
        for c in steps:
            low, high, mine, away = chunks[c]
            e1.append(send("edge", away, edge))
            m1.append(send("middle", low, across_or_stay))
            first += [(place, c, mine), (place ^ 1, c, send("pair", mine, pair))]
        for c in steps:
            e2.append(send("edge", m1[c], edge))
            m2.append(send("middle", chunks[c][1], across))
            second += [(place ^ 2, c, e1[c]), (place ^ 3, c, send("pair", e1[c], pair))]
        between()
        for c in steps:
            block = jnp.where(outer, e2[c], m2[c])
            index = far_inner * 2
            third += [(index + y, c, block), (index + 1 - y, c, send("pair", block, pair))]
        for c in steps:
            m3 = send("middle", e2[c], across)
            m4 = send("middle", e1[c], across)
            block = jnp.where(outer, send("edge", m3, outward), m4)
            index = far_outer * 2
            fourth += [(index + y, c, block), (index + 1 - y, c, send("pair", block, pair))]
        return [first + second, third, fourth]

    def on_device(tokens, modality, norm_gains, qkv_weight, out_weight):
        core = lax.axis_index("mod").astype(I32)
        place = lax.axis_index("dp").astype(I32)
        own = lax.axis_index("tensor").astype(I32)
        z = place // 2
        column = (z ^ (z // 2)) & 1
        outer = column == 0
        length, features = tokens.shape
        chunks = 2 if lined else 1
        kept = qkv_weight.shape[1] // chunks
        half = length // 2
        which = core ^ (z & 1)
        links = Links(1)

        rows = lax.dynamic_slice_in_dim(tokens, core * half, half, 0)
        rest_rows = lax.dynamic_slice_in_dim(tokens, (1 - core) * half, half, 0)
        fetched = over_tensor(rows)
        other_modality = move(modality, edge)
        passed = []

        def pass_rows():
            passed.append(links.send("edge", after(rows, other_modality, fetched[-1]), edge))

        weights = halves(qkv_weight[0].transpose(1, 0, 2), outer, chunks)
        early, middle, last = gather(links, weights, place, outer, pass_rows)

        gains = norm_gains[0].reshape(places * chunks, 1, kept)
        shape = (2, places * chunks, length, kept)
        swapped = [rest_rows] + [to_core(a) for a in fetched[1:]]
        normed = normalize(
            jnp.stack([core, own, which]), None, gains, fetched, swapped, shape, 0, kept
        )
        part = over_tensor(passed[0])
        normed = normalize(
            jnp.stack([core, own, 1 - which]),
            normed,
            gains,
            part,
            [to_core(a) for a in part],
            shape,
            0,
            kept,
        )

        def add(slot, group, total, final=False, fresh=False):
            found = jnp.stack([slot] + [i * chunks + c for i, c, _ in group]).astype(I32)
            return project(found, normed, [b for _, _, b in group], total, final, fresh)

        total = None
        if early:
            total = add(which, early, None, fresh=True)
            total = add(which, middle, total)
        else:
            total = add(which, middle, None, fresh=True)
        total = add(1 - which, early + middle, total, fresh=True)
        zero = jnp.zeros((), I32)
        theirs = add(zero + 1, last, total, final=True)
        got = to_core(theirs)
        ours = add(zero, last, total, final=True)

        own_rows = (modality == core).astype(I32)[:, None]
        other_rows = (other_modality == core).astype(I32)[:, None]
        attended = attend(ours, got, jnp.where(which == 0, own_rows, other_rows))

        held = over_tensor(attended)
        held += over_tensor(move(attended, edge))
        pieces = jnp.stack([jnp.stack(held), jnp.stack([to_core(a) for a in held])])

        blocks = halves(out_weight, outer, 1)
        early, middle, last = gather(links, blocks, place, outer, lambda: None)

        def gathered(slot, group, total, final):
            found = [slot]
            for index, _, _ in group:
                piece = index // 2
                shard, part = piece // 2, piece % 2
                found.append(jnp.where(part == column, 0, shards) + (own - shard + shards) % shards)
                found.append(index % 2)
            found = jnp.stack(found).astype(I32)
            return combine(found, pieces, [b for _, _, b in group], total, final)

        sums = [gathered(slot, early + middle, None, False) for slot in (1 - which, which)]
        away = gathered(1 - which, last, sums[0], True)
        near = gathered(which, last, sums[1], True)

        kept_away = lax.dynamic_slice_in_dim(away, core * half, half, 0)
        sent_away = to_core(lax.dynamic_slice_in_dim(away, (1 - core) * half, half, 0))
        keep = lax.dynamic_slice_in_dim(other_rows, core * half, half, 0)
        far = move(jnp.where(keep != 0, kept_away, sent_away), edge)
        return assemble(
            jnp.stack([core, column]), own_rows, near, to_core(near), far, to_core(far)
        )

    return jax.shard_map(
        on_device,
        mesh=mesh,
        in_specs=(
            P("dp", "tensor"),
            P("dp"),
            P("mod", None),
            P("mod", "dp", None, "tensor"),
            P("mod", "dp", "tensor"),
        ),
        out_specs=P("dp", "tensor"),
        check_vma=False,
    )
```

```python
import jax
import jax.numpy as jnp
from jax import lax
from jax.experimental import pallas as pl
from jax.experimental.pallas import tpu as pltpu
from jax.sharding import PartitionSpec as P

HDIM = 128
AXES = ("mod", "dp", "tensor")
VMEM = 64 * 1024 * 1024
F32, BF16, I32 = jnp.float32, jnp.bfloat16, jnp.int32


def after(array, *earlier):
    return lax.optimization_barrier((array,) + earlier)[0]


def call(kernel, grid, in_specs, out_specs, out_shape, prefetch, args, flops, aliases=None, moved=0):
    outs = jax.tree.leaves(out_shape)
    moved = moved or sum(a.size * a.dtype.itemsize for a in list(args) + outs)
    return pl.pallas_call(
        kernel,
        grid_spec=pltpu.PrefetchScalarGridSpec(
            num_scalar_prefetch=1, grid=grid, in_specs=in_specs, out_specs=out_specs
        ),
        out_shape=out_shape,
        input_output_aliases=aliases or {},
        cost_estimate=pl.CostEstimate(flops=flops, bytes_accessed=moved, transcendentals=0),
        compiler_params=pltpu.CompilerParams(vmem_limit_bytes=VMEM),
    )(prefetch, *args)


def halves(weight, outer, chunk, chunks, *earlier):
    kinds, depth, width = weight.shape
    part = width // 2 // chunks
    tile = min(depth, 128)

    def kernel(o_ref, first_ref, last_ref, low_ref, high_ref, mine_ref, away_ref):
        low, high = first_ref[...], last_ref[...]
        first = o_ref[0] == 1
        low_ref[...] = low
        high_ref[...] = high
        mine_ref[...] = jnp.where(first, low, high)
        away_ref[...] = jnp.where(first, high, low)

    out = jax.ShapeDtypeStruct((kinds, depth, part), weight.dtype)
    spec = pl.BlockSpec((kinds, tile, part), lambda i, o: (0, i, 0))
    return call(
        kernel,
        (depth // tile,),
        [
            pl.BlockSpec((kinds, tile, part), lambda i, o: (0, i, chunk)),
            pl.BlockSpec((kinds, tile, part), lambda i, o: (0, i, chunks + chunk)),
        ],
        [spec] * 4,
        [out] * 4,
        after(outer, *earlier).reshape(1),
        [weight, weight],
        0,
        moved=6 * kinds * depth * part,
    )


def normalize(places, held, gains, mine, theirs, shape, start, kept):
    slots, blocks, length, _ = shape
    shards = len(mine)
    count, features = mine[0].shape
    tile = 80 if count % 80 == 0 else count
    steps, half = count // tile, length // 2
    per = features // kept

    def kernel(p_ref, *refs):
        refs = refs[1:] if held is not None else refs
        gain_ref, out_ref = refs[0], refs[-1]
        core, own = p_ref[0], p_ref[1]

        def write(group):
            wide = [ref[...].astype(F32) for ref in group]
            total = sum(jnp.sum(w * w, axis=-1, keepdims=True) for w in wide)
            inverse = lax.rsqrt(total / (shards * features) + 1e-05)
            for step, w in enumerate(wide):
                shard = lax.rem(own - step + shards, shards)
                for i in range(per):
                    block = shard * per + i
                    part = w[:, i * kept : (i + 1) * kept] * inverse * gain_ref[block]
                    out_ref[0, block] = part.astype(BF16)

        @pl.when(pl.program_id(0) == core)
        def _():
            write(refs[1 : 1 + shards])

        @pl.when(pl.program_id(0) != core)
        def _():
            write(refs[1 + shards : 1 + 2 * shards])

    own_spec = pl.BlockSpec(
        (tile, features), lambda h, i, p: (jnp.where(h == p[0], i, jnp.where(h == 0, 0, steps - 1)), 0)
    )
    other_spec = pl.BlockSpec(
        (tile, features), lambda h, i, p: (jnp.where(h != p[0], i, jnp.where(h == 0, 0, steps - 1)), 0)
    )
    in_specs = [pl.BlockSpec((blocks, 1, kept), lambda h, i, p: (0, 0, 0))]
    in_specs += [own_spec] * shards + [other_spec] * shards
    args = [gains] + list(mine) + list(theirs)
    if held is not None:
        in_specs = [pl.BlockSpec(memory_space=pl.ANY)] + in_specs
        args = [held] + args
    out_spec = pl.BlockSpec(
        (1, blocks, tile, kept), lambda h, i, p: (p[2], 0, (h * half + start) // tile + i, 0)
    )
    return call(
        kernel,
        (2, steps),
        in_specs,
        out_spec,
        jax.ShapeDtypeStruct(shape, BF16),
        places,
        args,
        0,
        {1: 0} if held is not None else None,
        moved=8 * count * features * shards,
    )


def project(places, normed, blocks, total, final, fresh):
    slots, _, length, kept = normed.shape
    kinds, _, width = blocks[0].shape
    tile = min(width, 256)
    per = width // tile
    count = len(blocks)

    def kernel(p_ref, *refs):
        out_ref = refs[-1]
        summed = None if fresh else refs[2 * count][0]
        for i in range(count):
            part = jnp.dot(refs[i][0, 0], refs[count + i][0], preferred_element_type=F32)
            summed = part if summed is None else summed + part
        if final:
            out_ref[...] = summed.astype(BF16)
        else:
            out_ref[0] = summed

    def columns(i):
        return pl.BlockSpec((1, 1, length, kept), lambda n, p: (p[0], p[1 + i], 0, 0))

    total_spec = pl.BlockSpec((1, length, tile), lambda n, p: (p[0], 0, n))
    in_specs = [columns(i) for i in range(count)]
    in_specs += [pl.BlockSpec((1, kept, tile), lambda n, p: (n // per, 0, n % per))] * count
    args = [normed] * count + list(blocks)
    if total is not None:
        in_specs.append(pl.BlockSpec(memory_space=pl.ANY) if fresh else total_spec)
        args.append(total)
    aliases = None
    if final:
        out_spec = pl.BlockSpec((length, tile), lambda n, p: (0, n))
        out_shape = jax.ShapeDtypeStruct((length, kinds * width), BF16)
    else:
        out_spec, out_shape = total_spec, jax.ShapeDtypeStruct((slots, length, kinds * width), F32)
        if total is not None:
            aliases = {1 + 2 * count: 0}
    return call(
        kernel,
        (kinds * per,),
        in_specs,
        out_spec,
        out_shape,
        places,
        args,
        0,
        aliases,
        moved=2 * count * kept * (length + kinds * width) + 4 * length * kinds * width,
    )


def attend(own, got, mine):
    length, width = own.shape[0], own.shape[1] // 3
    heads = width // HDIM
    scale = HDIM ** (-0.5)
    tile = 128 if length % 128 == 0 else length

    def kernel(_, mine_ref, own_ref, got_ref, out_ref):
        keep = mine_ref[...] != 0

        def pick(j):
            columns = slice(j * HDIM, (j + 1) * HDIM)
            return jnp.where(
                keep, own_ref[:, columns].astype(F32), got_ref[:, columns].astype(F32)
            ).astype(BF16)

        for h in range(heads):
            query, key, value = pick(h), pick(heads + h), pick(2 * heads + h)
            for i in range(length // tile):
                low, high = i * tile, (i + 1) * tile
                scores = lax.dot_general(
                    query[low:high], key[:high], (((1,), (1,)), ((), ())), preferred_element_type=F32
                )
                rows = low + lax.broadcasted_iota(I32, (tile, high), 0)
                cols = lax.broadcasted_iota(I32, (tile, high), 1)
                scores = jnp.where(cols <= rows, scores * scale, -jnp.inf)
                top = jnp.max(scores, axis=-1, keepdims=True)
                raised = jnp.exp(scores - top)
                share = 1.0 / jnp.sum(raised, axis=-1, keepdims=True)
                probs = (raised * share).astype(BF16)
                out = jnp.dot(probs, value[:high], preferred_element_type=F32)
                out_ref[low:high, h * HDIM : (h + 1) * HDIM] = out.astype(BF16)

    full = pl.BlockSpec((length, 3 * width), lambda i, p: (0, 0))
    return call(
        kernel,
        (1,),
        [pl.BlockSpec((length, 1), lambda i, p: (0, 0)), full, full],
        pl.BlockSpec((length, width), lambda i, p: (0, 0)),
        jax.ShapeDtypeStruct((length, width), BF16),
        jnp.zeros((1,), I32),
        [mine, own, got],
        0,
    )


def combine(places, groups, total, final, slots):
    _, _, length, held = groups[0][0].shape
    features = groups[0][2][0][0].shape[2]
    tile = min(features, 256)
    terms = [(pieces, parity, pair) for pieces, parity, pairs in groups for pair in pairs]
    count = len(terms)

    def kernel(p_ref, *refs):
        out_ref = refs[-1]
        summed = None if total is None else refs[3 * count][0]
        for i, (_, parity, _) in enumerate(terms):
            near, far = refs[count + 2 * i][0], refs[count + 2 * i + 1][0]
            block = jnp.where(p_ref[1] == parity, near, far)
            part = jnp.dot(refs[i][0, 0], block, preferred_element_type=F32)
            summed = part if summed is None else summed + part
        out_ref[0] = summed.astype(out_ref.dtype)

    def piece(i):
        return pl.BlockSpec((1, 1, length, held), lambda s, n, p: (p[0] + s, p[2 + i], 0, 0))

    block_spec = pl.BlockSpec((1, held, tile), lambda s, n, p: (0, 0, n))
    in_specs = [piece(i) for i in range(count)] + [block_spec] * (2 * count)
    args = [pieces for pieces, _, _ in terms] + [b for _, _, pair in terms for b in pair]
    if total is not None:
        in_specs.append(pl.BlockSpec((1, length, tile), lambda s, n, p: (p[0] + s, 0, n)))
        args.append(total)
    return call(
        kernel,
        (slots, features // tile),
        in_specs,
        pl.BlockSpec((1, length, tile), lambda s, n, p: (s, 0, n)),
        jax.ShapeDtypeStruct((slots, length, features), BF16 if final else F32),
        places,
        args,
        0,
    )


def assemble(places, mine, near, near_other, far, far_other):
    length, width = near.shape
    tile = 160 if length % 320 == 0 else length // 2
    steps = length // 2 // tile

    def kernel(p_ref, mine_ref, a_ref, b_ref, c_ref, d_ref, out_ref):
        keep = mine_ref[...] != 0
        own = jnp.where(keep, a_ref[...].astype(F32), b_ref[...].astype(F32)).astype(BF16)
        held = (pl.program_id(0) // steps) == p_ref[0]
        other = jnp.where(held, c_ref[...], d_ref[...])
        first = p_ref[1] == 0
        out_ref[:, :width] = jnp.where(first, own, other)
        out_ref[:, width:] = jnp.where(first, other, own)

    rows = pl.BlockSpec((tile, width), lambda i, p: (i, 0))
    part = pl.BlockSpec((tile, width), lambda i, p: (i % steps, 0))
    return call(
        kernel,
        (2 * steps,),
        [pl.BlockSpec((tile, 1), lambda i, p: (i, 0)), rows, rows, part, part],
        pl.BlockSpec((tile, 2 * width), lambda i, p: (i, 0)),
        jax.ShapeDtypeStruct((length, 2 * width), BF16),
        places,
        [mine, near, near_other, far, far_other],
        0,
    )


def from_partner(x, axis, bit):
    return lax.ppermute(x, axis, [(i, i ^ 1 << bit) for i in range(lax.axis_size(axis))])


def gathered_plan(tokens, modality, norm_gains, qkv_weight, out_weight):
    tower_id = lax.axis_index("mod")
    own_rows = modality == tower_id
    gathered = lax.all_gather(tokens, "tensor", axis=1, tiled=True)
    length = gathered.shape[0]
    local_width = qkv_weight.shape[3]
    local_heads = local_width // HDIM
    gain_row = norm_gains[0]
    scale = HDIM ** (-0.5)
    wide_rows = gathered.astype(jnp.float32)
    inverse = lax.rsqrt(jnp.mean(wide_rows * wide_rows, axis=-1, keepdims=True) + 1e-05)
    row_block = (wide_rows * inverse * gain_row).astype(jnp.bfloat16)
    weight_piece = lax.all_gather(qkv_weight, "dp", axis=1, tiled=True)
    count = weight_piece.shape[1]
    columns = row_block
    projected = (
        jnp.dot(
            columns,
            weight_piece[0].reshape(count, 3 * local_width),
            preferred_element_type=jnp.float32,
        )
        .astype(jnp.bfloat16)
        .reshape(length, 3, local_heads, HDIM)
    )
    queries = projected[:, 0]
    own_pair = projected[:, 1:]
    other_pair = from_partner(own_pair, "mod", 0)
    key_pairs = jnp.where(own_rows[:, None, None, None], own_pair, other_pair)
    key_pos = jnp.arange(length, dtype=jnp.int32)
    scores = (
        jnp.einsum("qhd,khd->hqk", queries, key_pairs[:, 0], preferred_element_type=jnp.float32)
        * scale
    )
    allowed = key_pos[None, :] <= key_pos[:, None]
    scores = jnp.where(allowed[None], scores, -jnp.inf)
    soft_weights = jax.nn.softmax(scores, axis=-1).astype(jnp.bfloat16)
    attended = jnp.einsum(
        "hqk,khd->qhd", soft_weights, key_pairs[:, 1], preferred_element_type=jnp.float32
    )
    attended = attended.astype(jnp.bfloat16).reshape(queries.shape[0], local_width)
    all_heads = lax.all_gather(attended, "tensor", axis=1, tiled=True)
    weight_piece = lax.all_gather(out_weight, "dp", axis=1, tiled=True)
    columns = all_heads
    projected_out = jnp.dot(columns, weight_piece[0], preferred_element_type=jnp.float32).astype(
        jnp.bfloat16
    )
    placed = jnp.where(own_rows[:, None], projected_out, jnp.zeros_like(projected_out))
    combined = lax.psum(placed.astype(jnp.float32).astype(jnp.bfloat16), "mod")
    return combined


def solution(mesh):
    places, shards = mesh.shape["dp"], mesh.shape["tensor"]
    mods = mesh.shape["mod"]

    def move(array, where, *earlier):
        pairs = []
        for m in range(mods):
            for d in range(places):
                for x in range(shards):
                    to = where(m, d, x)
                    if to is not None:
                        target = (to[0] * places + to[1]) * shards + to[2]
                        pairs.append(((m * places + d) * shards + x, target))
        return lax.ppermute(after(array, *earlier) if earlier else array, AXES, pairs)

    def to_core(array, *earlier):
        return move(array, lambda m, d, x: (1 - m, d, x), *earlier)

    def over_tensor(array, *earlier):
        return [array] + [
            move(array, lambda m, d, x: (m, d, (x + step) % shards), *earlier)
            for step in range(1, shards)
        ]

    def edge(m, d, x):
        return m, d ^ 2, x

    def outward(m, d, x):
        return (m, d ^ 2, x) if d // 2 in (1, 2) else None

    def across(m, d, x):
        return (m, (3 - d // 2) * 2 + d % 2, x) if d // 2 in (1, 2) else None

    def across_or_stay(m, d, x):
        return across(m, d, x) or (m, d, x)

    def pair(m, d, x):
        return m, d ^ 1, x

    def line_plan(tokens, modality, norm_gains, qkv_weight, out_weight):
        core = lax.axis_index("mod").astype(I32)
        place = lax.axis_index("dp").astype(I32)
        own = lax.axis_index("tensor").astype(I32)
        z, y = place // 2, place % 2
        column = (z ^ (z // 2)) & 1
        outer = 1 - column
        length, features = tokens.shape
        kept = qkv_weight.shape[1]
        half = length // 2
        which = core ^ (z & 1)
        at = [z, z ^ 1, jnp.where(z < 2, 2, 1), 3 - 3 * (z // 2)]

        def choose(edge_block, middle_block):
            return jnp.where(outer == 1, edge_block, middle_block)

        weight = qkv_weight[0].transpose(1, 0, 2)
        low_a, high_a, mine_a, away_a = halves(weight, outer, 0, 2)
        e1a = move(away_a, edge)
        m1a = move(low_a, across_or_stay)
        p1a = move(mine_a, pair)
        rows = lax.dynamic_slice_in_dim(tokens, core * half, half, 0)
        fetched = over_tensor(rows, mine_a)
        other_modality = move(modality, edge)
        low_b, high_b, mine_b, away_b = halves(weight, outer, 1, 2, mine_a)
        rest_rows = lax.dynamic_slice_in_dim(tokens, (1 - core) * half, half, 0)

        ready = (e1a, m1a, p1a, mine_b, other_modality)
        e2a = move(m1a, edge, *ready)
        m2a = move(high_a, across, *ready)
        p2a = move(e1a, pair, *ready)
        low_o, high_o, mine_o, away_o = halves(out_weight, outer, 0, 1, mine_b, e1a)
        swapped = [rest_rows] + [to_core(a) for a in fetched[1:]]

        ready = (e2a, m2a, p2a, mine_o, fetched[-1])
        m3a = move(e2a, across, *ready)
        passed = move(rows, edge, *ready)
        third_a = choose(e2a, m2a)
        p3a = move(third_a, pair, *ready)
        gains = norm_gains[0].reshape(places, 1, kept)
        shape = (2, places, length, kept)
        normed = normalize(
            jnp.stack([core, own, which]), None, gains, fetched, swapped, shape, 0, kept
        )

        ready = (m3a, p3a, normed)
        m4a = move(e1a, across, *ready)
        p1b = move(mine_b, pair, *ready)

        def add(slot, blocks, total, final=False, fresh=False):
            found = [slot]
            for k, _, _ in blocks:
                found += [2 * k + y, 2 * k + 1 - y]
            flat = [b for _, near, far in blocks for b in (near, far)]
            return project(jnp.stack(found).astype(I32), normed, flat, total, final, fresh)

        first_a = [(at[0], mine_a, p1a), (at[1], e1a, p2a), (at[2], third_a, p3a)]
        total_a = add(which, first_a, None, fresh=True)

        e3a = move(m3a, outward, passed)
        part = over_tensor(passed)
        m1b = move(low_b, across_or_stay, m4a, p1b, total_a)
        part_swapped = [to_core(a) for a in part]
        fourth_a = choose(e3a, m4a)
        p4a = move(fourth_a, pair, p1b)

        m2b = move(high_b, across, m1b)
        e2b = move(m1b, edge, e3a)
        normed = normalize(
            jnp.stack([core, own, 1 - which]), normed, gains, part, part_swapped, shape, 0, kept
        )

        ready = (m2b, e2b, p4a, normed)
        m3b = move(e2b, across, *ready)
        e1b = move(away_b, edge, *ready)
        third_b = choose(e2b, m2b)
        p3b = move(third_b, pair, *ready)
        total_a = add(1 - which, first_a, total_a, fresh=True)
        zero, one = jnp.zeros((), I32), jnp.ones((), I32)
        last_a = [(at[3], fourth_a, p4a)]
        theirs_a = add(one, last_a, total_a, final=True)
        got_a = to_core(theirs_a)
        ours_a = add(zero, last_a, total_a, final=True)
        own_rows = (modality == core).astype(I32)[:, None]
        other_rows = (other_modality == core).astype(I32)[:, None]
        mine_rows = jnp.where(which == 0, own_rows, other_rows)
        attended_a = attend(ours_a, got_a, mine_rows)

        ready = (m3b, e1b, p3b, attended_a)
        m4b = move(e1b, across, *ready)
        e3b = move(m3b, outward, *ready)
        p2b = move(e1b, pair, *ready)
        held_a = over_tensor(attended_a, *ready)
        first_b = [(at[0], mine_b, p1b), (at[1], e1b, p2b), (at[2], third_b, p3b)]
        some_b = [first_b[0], first_b[2]]
        total_b = add(which, some_b, None, fresh=True)
        total_b = add(1 - which, some_b, total_b, fresh=True)

        ready = (m4b, e3b, p2b, total_b)
        fourth_b = choose(e3b, m4b)
        p4b = move(fourth_b, pair, *ready)
        m1o = move(low_o, across_or_stay, *ready)
        e1o = move(away_o, edge, *ready)
        last_b = [(at[1], e1b, p2b), (at[3], fourth_b, p4b)]

        ready = (m1o, e1o)
        m2o = move(high_o, across, *ready)
        e2o = move(m1o, edge, *ready)
        p1o = move(mine_o, pair, p4b)
        p2o = move(e1o, pair, p1o)
        theirs_b = add(one, last_b, total_b, final=True)
        got_b = to_core(theirs_b)
        ours_b = add(zero, last_b, total_b, final=True)
        attended_b = attend(ours_b, got_b, mine_rows)

        held_a += over_tensor(move(attended_a, edge, e2o))
        m3o = move(e2o, across, m2o)
        m4o = move(e1o, across, m3o)
        e3o = move(m3o, outward)
        third_o, fourth_o = choose(e2o, m2o), choose(e3o, m4o)
        p3o = move(third_o, pair, p2o)
        p4o = move(fourth_o, pair, p3o)
        held_b = over_tensor(attended_b)
        held_b += over_tensor(move(attended_b, edge))

        pieces = [
            jnp.stack([jnp.stack(held), jnp.stack([to_core(a) for a in held])])
            for held in (held_a, held_b)
        ]
        blocks = [(mine_o, p1o), (e1o, p2o), (third_o, p3o), (fourth_o, p4o)]

        def piece_of(k):
            shard, part = k // 2, k % 2
            return jnp.where(part == column, 0, shards) + (own - shard + shards) % shards

        found = [piece_of(k) for k in at]
        near = [(pieces[0], 0, blocks[:3])]
        rest = [(pieces[0], 0, blocks[3:]), (pieces[1], 1, blocks)]
        total = combine(
            jnp.stack([zero, y] + found[:3]).astype(I32), near, None, False, 2
        )

        def finish(slot):
            order = jnp.stack([slot, y, found[3]] + found).astype(I32)
            return combine(order, rest, total, True, 1)[0]

        away = finish(1 - which)
        near = finish(which)
        kept_away = lax.dynamic_slice_in_dim(away, core * half, half, 0)
        sent_away = to_core(lax.dynamic_slice_in_dim(away, (1 - core) * half, half, 0))
        keep = lax.dynamic_slice_in_dim(other_rows, core * half, half, 0)
        far = move(jnp.where(keep != 0, kept_away, sent_away), edge)
        return assemble(
            jnp.stack([core, column]), own_rows, near, to_core(near), far, to_core(far)
        )

    return jax.shard_map(
        line_plan if places == 8 else gathered_plan,
        mesh=mesh,
        in_specs=(
            P("dp", "tensor"),
            P("dp"),
            P("mod", None),
            P("mod", "dp", None, "tensor"),
            P("mod", "dp", "tensor"),
        ),
        out_specs=P("dp", "tensor"),
        check_vma=False,
    )
```

```python
import jax
import jax.numpy as jnp
from jax import lax
from jax.experimental import pallas as pl
from jax.experimental.pallas import tpu as pltpu
from jax.sharding import PartitionSpec as P

HDIM = 128
AXES = ("mod", "dp", "tensor")
VMEM = 64 * 1024 * 1024
F32, BF16, I32 = jnp.float32, jnp.bfloat16, jnp.int32


def after(array, *earlier):
    return lax.optimization_barrier((array,) + earlier)[0]


def call(kernel, grid, in_specs, out_specs, out_shape, prefetch, args, flops, aliases=None, moved=0):
    outs = jax.tree.leaves(out_shape)
    moved = moved or sum(a.size * a.dtype.itemsize for a in list(args) + outs)
    return pl.pallas_call(
        kernel,
        grid_spec=pltpu.PrefetchScalarGridSpec(
            num_scalar_prefetch=1, grid=grid, in_specs=in_specs, out_specs=out_specs
        ),
        out_shape=out_shape,
        input_output_aliases=aliases or {},
        cost_estimate=pl.CostEstimate(flops=flops, bytes_accessed=moved, transcendentals=0),
        compiler_params=pltpu.CompilerParams(vmem_limit_bytes=VMEM),
    )(prefetch, *args)


def halves(weight, outer, chunk, chunks, *earlier):
    kinds, depth, width = weight.shape
    part = width // 2 // chunks
    tile = min(depth, 256)

    def kernel(o_ref, first_ref, last_ref, low_ref, high_ref, mine_ref, away_ref):
        low, high = first_ref[...], last_ref[...]
        first = o_ref[0] == 1
        low_ref[...] = low
        high_ref[...] = high
        mine_ref[...] = jnp.where(first, low, high)
        away_ref[...] = jnp.where(first, high, low)

    out = jax.ShapeDtypeStruct((kinds, depth, part), weight.dtype)
    spec = pl.BlockSpec((kinds, tile, part), lambda i, o: (0, i, 0))
    return call(
        kernel,
        (depth // tile,),
        [
            pl.BlockSpec((kinds, tile, part), lambda i, o: (0, i, chunk)),
            pl.BlockSpec((kinds, tile, part), lambda i, o: (0, i, chunks + chunk)),
        ],
        [spec] * 4,
        [out] * 4,
        after(outer, *earlier).reshape(1),
        [weight, weight],
        0,
        moved=6 * kinds * depth * part,
    )


def normalize(places, held, gains, mine, theirs, shape, start, kept):
    slots, blocks, length, _ = shape
    shards = len(mine)
    count, features = mine[0].shape
    tile = 160 if count % 160 == 0 else count
    steps, half = count // tile, length // 2
    per = features // kept

    def kernel(p_ref, *refs):
        refs = refs[1:] if held is not None else refs
        gain_ref, out_ref = refs[0], refs[-1]
        core, own = p_ref[0], p_ref[1]

        def write(group):
            wide = [ref[...].astype(F32) for ref in group]
            total = sum(jnp.sum(w * w, axis=-1, keepdims=True) for w in wide)
            inverse = lax.rsqrt(total / (shards * features) + 1e-05)
            for step, w in enumerate(wide):
                shard = lax.rem(own - step + shards, shards)
                for i in range(per):
                    block = shard * per + i
                    part = w[:, i * kept : (i + 1) * kept] * inverse * gain_ref[block]
                    out_ref[0, block] = part.astype(BF16)

        @pl.when(pl.program_id(0) == core)
        def _():
            write(refs[1 : 1 + shards])

        @pl.when(pl.program_id(0) != core)
        def _():
            write(refs[1 + shards : 1 + 2 * shards])

    own_spec = pl.BlockSpec(
        (tile, features), lambda h, i, p: (jnp.where(h == p[0], i, jnp.where(h == 0, 0, steps - 1)), 0)
    )
    other_spec = pl.BlockSpec(
        (tile, features), lambda h, i, p: (jnp.where(h != p[0], i, jnp.where(h == 0, 0, steps - 1)), 0)
    )
    in_specs = [pl.BlockSpec((blocks, 1, kept), lambda h, i, p: (0, 0, 0))]
    in_specs += [own_spec] * shards + [other_spec] * shards
    args = [gains] + list(mine) + list(theirs)
    if held is not None:
        in_specs = [pl.BlockSpec(memory_space=pl.ANY)] + in_specs
        args = [held] + args
    out_spec = pl.BlockSpec(
        (1, blocks, tile, kept), lambda h, i, p: (p[2], 0, (h * half + start) // tile + i, 0)
    )
    return call(
        kernel,
        (2, steps),
        in_specs,
        out_spec,
        jax.ShapeDtypeStruct(shape, BF16),
        places,
        args,
        0,
        {1: 0} if held is not None else None,
        moved=8 * count * features * shards,
    )


def project(places, normed, blocks, total, final, fresh):
    slots, _, length, kept = normed.shape
    kinds, _, width = blocks[0].shape
    tile = min(width, 256)
    per = width // tile
    count = len(blocks)

    def kernel(p_ref, *refs):
        out_ref = refs[-1]
        summed = None if fresh else refs[2 * count][0]
        for i in range(count):
            part = jnp.dot(refs[i][0, 0], refs[count + i][0], preferred_element_type=F32)
            summed = part if summed is None else summed + part
        if final:
            out_ref[...] = summed.astype(BF16)
        else:
            out_ref[0] = summed

    def columns(i):
        return pl.BlockSpec((1, 1, length, kept), lambda n, p: (p[0], p[1 + i], 0, 0))

    total_spec = pl.BlockSpec((1, length, tile), lambda n, p: (p[0], 0, n))
    in_specs = [columns(i) for i in range(count)]
    in_specs += [pl.BlockSpec((1, kept, tile), lambda n, p: (n // per, 0, n % per))] * count
    args = [normed] * count + list(blocks)
    if total is not None:
        in_specs.append(pl.BlockSpec(memory_space=pl.ANY) if fresh else total_spec)
        args.append(total)
    aliases = None
    if final:
        out_spec = pl.BlockSpec((length, tile), lambda n, p: (0, n))
        out_shape = jax.ShapeDtypeStruct((length, kinds * width), BF16)
    else:
        out_spec, out_shape = total_spec, jax.ShapeDtypeStruct((slots, length, kinds * width), F32)
        if total is not None:
            aliases = {1 + 2 * count: 0}
    return call(
        kernel,
        (kinds * per,),
        in_specs,
        out_spec,
        out_shape,
        places,
        args,
        0,
        aliases,
        moved=2 * count * kept * (length + kinds * width) + 4 * length * kinds * width,
    )


def attend(own, got, mine):
    length, width = own.shape[0], own.shape[1] // 3
    heads = width // HDIM
    scale = HDIM ** (-0.5)
    tile = 128 if length % 128 == 0 else length

    def kernel(_, mine_ref, own_ref, got_ref, out_ref):
        keep = mine_ref[...] != 0

        def pick(j):
            columns = slice(j * HDIM, (j + 1) * HDIM)
            return jnp.where(
                keep, own_ref[:, columns].astype(F32), got_ref[:, columns].astype(F32)
            ).astype(BF16)

        for h in range(heads):
            query, key, value = pick(h), pick(heads + h), pick(2 * heads + h)
            for i in range(length // tile):
                low, high = i * tile, (i + 1) * tile
                scores = lax.dot_general(
                    query[low:high], key[:high], (((1,), (1,)), ((), ())), preferred_element_type=F32
                )
                rows = low + lax.broadcasted_iota(I32, (tile, high), 0)
                cols = lax.broadcasted_iota(I32, (tile, high), 1)
                scores = jnp.where(cols <= rows, scores * scale, -jnp.inf)
                top = jnp.max(scores, axis=-1, keepdims=True)
                raised = jnp.exp(scores - top)
                share = 1.0 / jnp.sum(raised, axis=-1, keepdims=True)
                probs = (raised * share).astype(BF16)
                out = jnp.dot(probs, value[:high], preferred_element_type=F32)
                out_ref[low:high, h * HDIM : (h + 1) * HDIM] = out.astype(BF16)

    full = pl.BlockSpec((length, 3 * width), lambda i, p: (0, 0))
    return call(
        kernel,
        (1,),
        [pl.BlockSpec((length, 1), lambda i, p: (0, 0)), full, full],
        pl.BlockSpec((length, width), lambda i, p: (0, 0)),
        jax.ShapeDtypeStruct((length, width), BF16),
        jnp.zeros((1,), I32),
        [mine, own, got],
        0,
    )


def combine(places, groups, total, final, slots, offset=0):
    _, length, held = groups[0][0].shape
    features = groups[0][3][0][0].shape[2]
    tile = min(features, 256)
    terms = [group[:3] + (pair,) for group in groups for pair in group[3]]
    count = len(terms)

    def kernel(p_ref, *refs):
        out_ref = refs[-1]
        summed = None if total is None else refs[4 * count][0]
        slot = (p_ref[0] + pl.program_id(0)) % 2
        for i, (_, _, parity, _) in enumerate(terms):
            near, far = refs[2 * count + 2 * i][0], refs[2 * count + 2 * i + 1][0]
            block = jnp.where(p_ref[1] == parity, near, far)
            rows = jnp.where(slot == 0, refs[2 * i][0], refs[2 * i + 1][0])
            part = jnp.dot(rows, block, preferred_element_type=F32)
            summed = part if summed is None else summed + part
        out_ref[0] = summed.astype(out_ref.dtype)

    def piece(i):
        return pl.BlockSpec((1, length, held), lambda s, n, p: (p[2 + i], 0, 0))

    block_spec = pl.BlockSpec((1, held, tile), lambda s, n, p: (0, 0, n))
    in_specs = [piece(i) for i in range(count) for _ in range(2)] + [block_spec] * (2 * count)
    args = [pieces for term in terms for pieces in term[:2]]
    args += [b for term in terms for b in term[3]]
    if total is not None:
        in_specs.append(pl.BlockSpec((1, length, tile), lambda s, n, p: (offset + s, 0, n)))
        args.append(total)
    return call(
        kernel,
        (slots, features // tile),
        in_specs,
        pl.BlockSpec((1, length, tile), lambda s, n, p: (s, 0, n)),
        jax.ShapeDtypeStruct((slots, length, features), BF16 if final else F32),
        places,
        args,
        0,
    )


def assemble(places, mine, near, near_other, far, far_other):
    length, width = near.shape
    tile = 160 if length % 320 == 0 else length // 2
    steps = length // 2 // tile

    def kernel(p_ref, mine_ref, a_ref, b_ref, c_ref, d_ref, out_ref):
        keep = mine_ref[...] != 0
        own = jnp.where(keep, a_ref[...].astype(F32), b_ref[...].astype(F32)).astype(BF16)
        held = (pl.program_id(0) // steps) == p_ref[0]
        other = jnp.where(held, c_ref[...], d_ref[...])
        first = p_ref[1] == 0
        out_ref[:, :width] = jnp.where(first, own, other)
        out_ref[:, width:] = jnp.where(first, other, own)

    rows = pl.BlockSpec((tile, width), lambda i, p: (i, 0))
    part = pl.BlockSpec((tile, width), lambda i, p: (i % steps, 0))
    return call(
        kernel,
        (2 * steps,),
        [pl.BlockSpec((tile, 1), lambda i, p: (i, 0)), rows, rows, part, part],
        pl.BlockSpec((tile, 2 * width), lambda i, p: (i, 0)),
        jax.ShapeDtypeStruct((length, 2 * width), BF16),
        places,
        [mine, near, near_other, far, far_other],
        0,
    )


def from_partner(x, axis, bit):
    return lax.ppermute(x, axis, [(i, i ^ 1 << bit) for i in range(lax.axis_size(axis))])


def gathered_plan(tokens, modality, norm_gains, qkv_weight, out_weight):
    tower_id = lax.axis_index("mod")
    own_rows = modality == tower_id
    gathered = lax.all_gather(tokens, "tensor", axis=1, tiled=True)
    length = gathered.shape[0]
    local_width = qkv_weight.shape[3]
    local_heads = local_width // HDIM
    gain_row = norm_gains[0]
    scale = HDIM ** (-0.5)
    wide_rows = gathered.astype(jnp.float32)
    inverse = lax.rsqrt(jnp.mean(wide_rows * wide_rows, axis=-1, keepdims=True) + 1e-05)
    row_block = (wide_rows * inverse * gain_row).astype(jnp.bfloat16)
    weight_piece = lax.all_gather(qkv_weight, "dp", axis=1, tiled=True)
    count = weight_piece.shape[1]
    columns = row_block
    projected = (
        jnp.dot(
            columns,
            weight_piece[0].reshape(count, 3 * local_width),
            preferred_element_type=jnp.float32,
        )
        .astype(jnp.bfloat16)
        .reshape(length, 3, local_heads, HDIM)
    )
    queries = projected[:, 0]
    own_pair = projected[:, 1:]
    other_pair = from_partner(own_pair, "mod", 0)
    key_pairs = jnp.where(own_rows[:, None, None, None], own_pair, other_pair)
    key_pos = jnp.arange(length, dtype=jnp.int32)
    scores = (
        jnp.einsum("qhd,khd->hqk", queries, key_pairs[:, 0], preferred_element_type=jnp.float32)
        * scale
    )
    allowed = key_pos[None, :] <= key_pos[:, None]
    scores = jnp.where(allowed[None], scores, -jnp.inf)
    soft_weights = jax.nn.softmax(scores, axis=-1).astype(jnp.bfloat16)
    attended = jnp.einsum(
        "hqk,khd->qhd", soft_weights, key_pairs[:, 1], preferred_element_type=jnp.float32
    )
    attended = attended.astype(jnp.bfloat16).reshape(queries.shape[0], local_width)
    all_heads = lax.all_gather(attended, "tensor", axis=1, tiled=True)
    weight_piece = lax.all_gather(out_weight, "dp", axis=1, tiled=True)
    columns = all_heads
    projected_out = jnp.dot(columns, weight_piece[0], preferred_element_type=jnp.float32).astype(
        jnp.bfloat16
    )
    placed = jnp.where(own_rows[:, None], projected_out, jnp.zeros_like(projected_out))
    combined = lax.psum(placed.astype(jnp.float32).astype(jnp.bfloat16), "mod")
    return combined


def solution(mesh):
    places, shards = mesh.shape["dp"], mesh.shape["tensor"]
    mods = mesh.shape["mod"]

    def move(array, where, *earlier):
        pairs = []
        for m in range(mods):
            for d in range(places):
                for x in range(shards):
                    to = where(m, d, x)
                    if to is not None:
                        target = (to[0] * places + to[1]) * shards + to[2]
                        pairs.append(((m * places + d) * shards + x, target))
        return lax.ppermute(after(array, *earlier) if earlier else array, AXES, pairs)

    def to_core(array, *earlier):
        return move(array, lambda m, d, x: (1 - m, d, x), *earlier)

    def over_tensor(array, *earlier):
        return [array] + [
            move(array, lambda m, d, x: (m, d, (x + step) % shards), *earlier)
            for step in range(1, shards)
        ]

    def edge(m, d, x):
        return m, d ^ 2, x

    def outward(m, d, x):
        return (m, d ^ 2, x) if d // 2 in (1, 2) else None

    def across(m, d, x):
        return (m, (3 - d // 2) * 2 + d % 2, x) if d // 2 in (1, 2) else None

    def across_or_stay(m, d, x):
        return across(m, d, x) or (m, d, x)

    def pair(m, d, x):
        return m, d ^ 1, x

    def line_plan(tokens, modality, norm_gains, qkv_weight, out_weight):
        core = lax.axis_index("mod").astype(I32)
        place = lax.axis_index("dp").astype(I32)
        own = lax.axis_index("tensor").astype(I32)
        z, y = place // 2, place % 2
        column = (z ^ (z // 2)) & 1
        outer = 1 - column
        length, features = tokens.shape
        kept = qkv_weight.shape[1]
        half = length // 2
        which = core ^ (z & 1)
        at = [z, z ^ 1, jnp.where(z < 2, 2, 1), 3 - 3 * (z // 2)]

        def choose(edge_block, middle_block):
            return jnp.where(outer == 1, edge_block, middle_block)

        weight = qkv_weight[0].transpose(1, 0, 2)
        low_a, high_a, mine_a, away_a = halves(weight, outer, 0, 2)
        m1a = move(low_a, across_or_stay)
        e1a = move(away_a, edge)
        p1a = move(mine_a, pair)
        rows = lax.dynamic_slice_in_dim(tokens, core * half, half, 0)
        fetched = over_tensor(rows, mine_a)
        other_modality = move(modality, edge, mine_a)
        low_b, high_b, mine_b, away_b = halves(weight, outer, 1, 2, mine_a)
        rest_rows = lax.dynamic_slice_in_dim(tokens, (1 - core) * half, half, 0)
        top, bottom = rows[: half // 2], rows[half // 2 :]

        m2a = move(high_a, across, m1a)
        e2a = move(m1a, edge, e1a)
        p2a = move(e1a, pair, p1a, mine_b, rest_rows)
        low_o, high_o, mine_o, away_o = halves(out_weight, outer, 0, 1, mine_b, e1a)
        swapped = [rest_rows] + [to_core(a) for a in fetched[1:]]

        m3a = move(e2a, across, m2a)
        passed_top = move(top, edge, e2a, other_modality)
        third_a = choose(e2a, m2a)
        p3a = move(third_a, pair, p2a, mine_o)
        gains = norm_gains[0].reshape(places, 1, kept)
        shape = (2, places, length, kept)
        normed = normalize(
            jnp.stack([core, own, which]), None, gains, fetched, swapped, shape, 0, kept
        )

        m4a = move(e1a, across, m3a)
        passed_bottom = move(bottom, edge, passed_top)
        p1b = move(mine_b, pair, p3a, normed)
        part_top = over_tensor(passed_top, passed_top)

        def add(slot, blocks, total, final=False, fresh=False):
            found = [slot]
            for k, _, _ in blocks:
                found += [2 * k + y, 2 * k + 1 - y]
            flat = [b for _, near, far in blocks for b in (near, far)]
            return project(jnp.stack(found).astype(I32), normed, flat, total, final, fresh)

        first_a = [(at[0], mine_a, p1a), (at[1], e1a, p2a), (at[2], third_a, p3a)]
        total_a = add(which, first_a, None, fresh=True)

        m1b = move(low_b, across_or_stay, m4a)
        e3a = move(m3a, outward, passed_bottom)
        part_bottom = over_tensor(passed_bottom, passed_bottom)
        top_swapped = [to_core(a) for a in part_top]
        normed = normalize(
            jnp.stack([core, own, 1 - which]), normed, gains, part_top, top_swapped, shape, 0, kept
        )

        m2b = move(high_b, across, m1b)
        e2b = move(m1b, edge, e3a)
        fourth_a = choose(e3a, m4a)
        p4a = move(fourth_a, pair, p1b, total_a, normed)
        bottom_swapped = [to_core(a) for a in part_bottom]
        normed = normalize(
            jnp.stack([core, own, 1 - which]),
            normed,
            gains,
            part_bottom,
            bottom_swapped,
            shape,
            half // 2,
            kept,
        )
        total_a = add(1 - which, first_a, total_a, fresh=True)

        m3b = move(e2b, across, m2b)
        e1b = move(away_b, edge, e2b)
        third_b = choose(e2b, m2b)
        p3b = move(third_b, pair, p4a, total_a)
        zero, one = jnp.zeros((), I32), jnp.ones((), I32)
        last_a = [(at[3], fourth_a, p4a)]
        theirs_a = add(one, last_a, total_a, final=True)
        got_a = to_core(theirs_a)
        ours_a = add(zero, last_a, total_a, final=True)
        own_rows = (modality == core).astype(I32)[:, None]
        other_rows = (other_modality == core).astype(I32)[:, None]
        mine_rows = jnp.where(which == 0, own_rows, other_rows)

        m4b = move(e1b, across, m3b)
        e3b = move(m3b, outward, e1b)
        p2b = move(e1b, pair, p3b, ours_a)
        attended_a = attend(ours_a, got_a, mine_rows)
        first_b = [(at[0], mine_b, p1b), (at[2], third_b, p3b)]
        total_b = add(which, first_b, None, fresh=True)
        held_a = over_tensor(attended_a)

        m1o = move(low_o, across_or_stay, m4b)
        fourth_b = choose(e3b, m4b)
        p4b = move(fourth_b, pair, p2b, attended_a)
        e1o = move(away_o, edge, e3b)
        total_b = add(1 - which, first_b, total_b, fresh=True)
        held_a += over_tensor(move(attended_a, edge, e1o))

        m2o = move(high_o, across, m1o)
        e2o = move(m1o, edge, held_a[shards])
        p1o = move(mine_o, pair, p4b)
        last_b = [(at[1], e1b, p2b), (at[3], fourth_b, p4b)]
        theirs_b = add(one, last_b, total_b, final=True)
        got_b = to_core(theirs_b)
        ours_b = add(zero, last_b, total_b, final=True)
        stack_a = jnp.stack(held_a)
        pieces_a = (stack_a, to_core(stack_a))
        attended_b = attend(ours_b, got_b, mine_rows)

        p2o = move(e1o, pair, p1o)
        m3o = move(e2o, across, m2o)
        m4o = move(e1o, across, m3o)
        third_o = choose(e2o, m2o)
        p3o = move(third_o, pair, p2o)
        e3o = move(m3o, outward)
        fourth_o = choose(e3o, m4o)
        held_b = over_tensor(attended_b)
        held_b += over_tensor(move(attended_b, edge, e2o))
        blocks = [(mine_o, p1o), (e1o, p2o), (third_o, p3o)]

        def piece_of(k):
            shard, part = k // 2, k % 2
            return jnp.where(part == column, 0, shards) + (own - shard + shards) % shards

        found = [piece_of(k) for k in at]
        total = combine(
            jnp.stack([1 - which, y] + found[:3]).astype(I32), [pieces_a + (0, blocks)], None, False, 2
        )
        p4o = move(fourth_o, pair, p3o)
        last = [(fourth_o, p4o)]
        stack_b = jnp.stack(held_b)
        pieces_b = (stack_b, to_core(stack_b))
        rest = [pieces_a + (0, last), pieces_b + (1, blocks + last)]

        def finish(slot, offset):
            order = jnp.stack([slot, y, found[3]] + found).astype(I32)
            return combine(order, rest, total, True, 1, offset)[0]

        away = finish(1 - which, 0)
        kept_away = lax.dynamic_slice_in_dim(away, core * half, half, 0)
        sent_away = to_core(lax.dynamic_slice_in_dim(away, (1 - core) * half, half, 0))
        near = finish(which, 1)
        keep = lax.dynamic_slice_in_dim(other_rows, core * half, half, 0)
        far = move(jnp.where(keep != 0, kept_away, sent_away), edge)
        return assemble(
            jnp.stack([core, column]), own_rows, near, to_core(near), far, to_core(far)
        )

    return jax.shard_map(
        line_plan if places == 8 else gathered_plan,
        mesh=mesh,
        in_specs=(
            P("dp", "tensor"),
            P("dp"),
            P("mod", None),
            P("mod", "dp", None, "tensor"),
            P("mod", "dp", "tensor"),
        ),
        out_specs=P("dp", "tensor"),
        check_vma=False,
    )
```

```python
import jax
import jax.numpy as jnp
from jax import lax
from jax.experimental import pallas as pl
from jax.experimental.pallas import tpu as pltpu
from jax.sharding import PartitionSpec as P

HDIM = 128
AXES = ("mod", "dp", "tensor")
F32, BF16, I32 = jnp.float32, jnp.bfloat16, jnp.int32
VMEM, SMEM = pltpu.VMEM, pltpu.SMEM


def after(array, *earlier):
    return lax.optimization_barrier((array,) + earlier)[0]


def call(kernel, places, args, out_shape, aliases=None, scratch=8):
    return pl.pallas_call(
        kernel,
        in_specs=[pl.BlockSpec(memory_space=SMEM)] + [pl.BlockSpec(memory_space=VMEM)] * len(args),
        out_specs=jax.tree.map(lambda _: pl.BlockSpec(memory_space=VMEM), out_shape),
        out_shape=jax.tree.map(lambda shape: VMEM(shape.shape, shape.dtype), out_shape),
        input_output_aliases=aliases or {},
        compiler_params=pltpu.CompilerParams(vmem_limit_bytes=scratch * 2**20),
    )(places, *[pltpu.with_memory_space_constraint(a, VMEM) for a in args])


def shaped(shape, dtype=BF16):
    return jax.ShapeDtypeStruct(shape, dtype)


def scalars(*values):
    return jnp.stack([jnp.asarray(v, I32) for v in values])


def halves(weight, outer, chunk, chunks):
    kinds, depth, width = weight.shape
    half = width // 2
    part = half // chunks

    def kernel(p_ref, in_ref, low_ref, high_ref, mine_ref, away_ref):
        first = p_ref[0] == 1
        for kind in range(kinds):
            low = in_ref[kind, :, chunk * part : (chunk + 1) * part]
            high = in_ref[kind, :, half + chunk * part : half + (chunk + 1) * part]
            low_ref[kind] = low
            high_ref[kind] = high
            mine_ref[kind] = jnp.where(first, low, high)
            away_ref[kind] = jnp.where(first, high, low)

    return call(kernel, scalars(outer), [weight], [shaped((kinds, depth, part))] * 4)


def own_rows_of(tokens, core):
    length, features = tokens.shape
    half = length // 2

    def kernel(p_ref, in_ref, rows_ref, top_ref, bottom_ref):
        first = p_ref[0] == 0
        rows = jnp.where(first, in_ref[:half], in_ref[half:])
        rows_ref[...] = rows
        top_ref[...] = rows[: half // 2]
        bottom_ref[...] = rows[half // 2 :]

    part = shaped((half // 2, features))
    return call(kernel, scalars(core), [tokens], [shaped((half, features)), part, part])


def normalize(places, held, gains, whole, mine, theirs, shape, start, count, kept):
    _, _, length, _ = shape
    shards = len(mine) + (whole is not None)
    features = (whole if whole is not None else mine[0]).shape[1]
    tile = 32 if count % 32 == 0 else count
    half = length // 2
    per = features // kept
    args = ([] if held is None else [held]) + [gains] + ([] if whole is None else [whole])
    args += list(mine) + list(theirs)

    def kernel(p_ref, *refs):
        out_ref = refs[-1]
        refs = list(refs[0 if held is None else 1 : -1])
        gain_ref = refs.pop(0)
        whole_ref = None if whole is None else refs.pop(0)
        core, own, slot = p_ref[0], p_ref[1], p_ref[2]
        shard_of = [lax.rem(own - step + shards, shards) for step in range(shards)]

        def step(i, carry):
            for group, first in ((refs[: len(mine)], core), (refs[len(mine) :], 1 - core)):
                row = pl.multiple_of(first * half + start + i * tile, tile)
                at = pl.ds(pl.multiple_of(i * tile, tile), tile)
                found = [(ref, at) for ref in group]
                if whole_ref is not None:
                    found = [(whole_ref, pl.ds(row, tile))] + found
                total = jnp.zeros((tile, 1), F32)
                for ref, rows in found:
                    wide = ref[rows, :].astype(F32)
                    total = total + jnp.sum(wide * wide, axis=-1, keepdims=True)
                inverse = lax.rsqrt(total / (shards * features) + 1e-05)
                for shard, (ref, rows) in zip(shard_of, found):
                    for j in range(per):
                        block = shard * per + j
                        wide = ref[rows, j * kept : (j + 1) * kept].astype(F32)
                        out_ref[slot, block, pl.ds(row, tile), :] = (
                            wide * inverse * gain_ref[block]
                        ).astype(BF16)
            return carry

        lax.fori_loop(0, count // tile, step, 0)

    return call(kernel, places, args, shaped(shape), None if held is None else {1: 0})


def project(places, normed, blocks, total, final, fresh):
    slots, _, length, kept = normed.shape
    kinds, _, width = blocks[0].shape
    count = len(blocks)
    args = [normed] + list(blocks) + ([] if total is None else [total])

    def kernel(p_ref, *refs):
        normed_ref, out_ref = refs[0], refs[-1]
        slot = p_ref[0]
        for kind in range(kinds):
            columns = slice(kind * width, (kind + 1) * width)
            summed = None if fresh else refs[1 + count][slot, :, columns]
            for i in range(count):
                part = jnp.dot(
                    normed_ref[slot, p_ref[1 + i]], refs[1 + i][kind], preferred_element_type=F32
                )
                summed = part if summed is None else summed + part
            if final:
                out_ref[:, columns] = summed.astype(BF16)
            else:
                out_ref[slot, :, columns] = summed

    if final:
        return call(kernel, places, args, shaped((length, kinds * width)))
    aliases = None if total is None else {2 + count: 0}
    return call(kernel, places, args, shaped((slots, length, kinds * width), F32), aliases)


def attend(own, got, mine):
    length, width = own.shape[0], own.shape[1] // 3
    heads = width // HDIM
    scale = HDIM ** (-0.5)
    tile = 128 if length % 128 == 0 else length

    def kernel(_, mine_ref, own_ref, got_ref, out_ref):
        keep = mine_ref[...] != 0

        def pick(j):
            columns = slice(j * HDIM, (j + 1) * HDIM)
            return jnp.where(
                keep, own_ref[:, columns].astype(F32), got_ref[:, columns].astype(F32)
            ).astype(BF16)

        for h in range(heads):
            query, key, value = pick(h), pick(heads + h), pick(2 * heads + h)
            for i in range(length // tile):
                low, high = i * tile, (i + 1) * tile
                scores = lax.dot_general(
                    query[low:high], key[:high], (((1,), (1,)), ((), ())), preferred_element_type=F32
                )
                rows = low + lax.broadcasted_iota(I32, (tile, high), 0)
                cols = lax.broadcasted_iota(I32, (tile, high), 1)
                scores = jnp.where(cols <= rows, scores * scale, -jnp.inf)
                top = jnp.max(scores, axis=-1, keepdims=True)
                raised = jnp.exp(scores - top)
                share = 1.0 / jnp.sum(raised, axis=-1, keepdims=True)
                probs = (raised * share).astype(BF16)
                out = jnp.dot(probs, value[:high], preferred_element_type=F32)
                out_ref[low:high, h * HDIM : (h + 1) * HDIM] = out.astype(BF16)

    return call(kernel, scalars(0), [mine, own, got], shaped((length, width)))


def combine(places, groups, total, slots, offset=0, cut=False):
    _, length, held = groups[0][0].shape
    features = groups[0][3][0][0].shape[2]
    tile = min(features, 256)
    half = length // 2
    terms = [group[:3] + (pair,) for group in groups for pair in group[3]]
    count = len(terms)
    args = [pieces for term in terms for pieces in term[:2]]
    args += [b for term in terms for b in term[3]] + ([] if total is None else [total])

    def kernel(p_ref, *refs):
        outs = refs[-2:] if cut else refs[-1:]
        for s in range(slots):
            slot = (p_ref[0] + s) % 2
            rows = [
                jnp.where(slot == 0, refs[2 * i][p_ref[3 + i]], refs[2 * i + 1][p_ref[3 + i]])
                for i in range(count)
            ]
            for n in range(features // tile):
                columns = slice(n * tile, (n + 1) * tile)
                summed = None if total is None else refs[4 * count][offset + s, :, columns]
                for i, (_, _, parity, _) in enumerate(terms):
                    near = refs[2 * count + 2 * i][0, :, columns]
                    far = refs[2 * count + 2 * i + 1][0, :, columns]
                    block = jnp.where(p_ref[1] == parity, near, far)
                    part = jnp.dot(rows[i], block, preferred_element_type=F32)
                    summed = part if summed is None else summed + part
                if total is None:
                    outs[0][s, :, columns] = summed
                elif cut:
                    result = summed.astype(BF16)
                    first = p_ref[2] == 0
                    outs[0][:, columns] = jnp.where(first, result[:half], result[half:])
                    outs[1][:, columns] = jnp.where(first, result[half:], result[:half])
                else:
                    outs[0][:, columns] = summed.astype(BF16)

    if total is None:
        out_shape = shaped((slots, length, features), F32)
    elif cut:
        out_shape = [shaped((half, features))] * 2
    else:
        out_shape = shaped((length, features))
    return call(kernel, places, args, out_shape, scratch=12)


def assemble(places, mine, near, near_other, far, far_other):
    length, width = near.shape
    steps = 4
    tile = length // steps
    half = length // 2
    args = [mine, near, near_other, far, far_other]

    def kernel(p_ref, mine_ref, a_ref, b_ref, c_ref, d_ref, out_ref, held, sems):
        core, first = p_ref[0], p_ref[1] == 0
        copies = []
        for i in range(steps):
            rows = slice(i * tile, (i + 1) * tile)
            keep = mine_ref[rows] != 0
            own = jnp.where(keep, a_ref[rows].astype(F32), b_ref[rows].astype(F32)).astype(BF16)
            part = slice(i * tile % half, i * tile % half + tile)
            other = jnp.where(core == i * tile // half, c_ref[part], d_ref[part])
            held[i, :, :width] = jnp.where(first, own, other)
            held[i, :, width:] = jnp.where(first, other, own)
            copies.append(pltpu.make_async_copy(held.at[i], out_ref.at[rows], sems.at[i]))
            copies[-1].start()
        for copy in copies:
            copy.wait()

    return pl.pallas_call(
        kernel,
        in_specs=[pl.BlockSpec(memory_space=SMEM)] + [pl.BlockSpec(memory_space=VMEM)] * 5,
        out_specs=pl.BlockSpec(memory_space=pl.ANY),
        out_shape=shaped((length, 2 * width)),
        scratch_shapes=[VMEM((steps, tile, 2 * width), BF16), pltpu.SemaphoreType.DMA((steps,))],
        compiler_params=pltpu.CompilerParams(vmem_limit_bytes=12 * 2**20),
    )(places, *[pltpu.with_memory_space_constraint(a, VMEM) for a in args])


def from_partner(x, axis, bit):
    return lax.ppermute(x, axis, [(i, i ^ 1 << bit) for i in range(lax.axis_size(axis))])


def gathered_plan(tokens, modality, norm_gains, qkv_weight, out_weight):
    tower_id = lax.axis_index("mod")
    own_rows = modality == tower_id
    gathered = lax.all_gather(tokens, "tensor", axis=1, tiled=True)
    length = gathered.shape[0]
    local_width = qkv_weight.shape[3]
    local_heads = local_width // HDIM
    gain_row = norm_gains[0]
    scale = HDIM ** (-0.5)
    wide_rows = gathered.astype(jnp.float32)
    inverse = lax.rsqrt(jnp.mean(wide_rows * wide_rows, axis=-1, keepdims=True) + 1e-05)
    row_block = (wide_rows * inverse * gain_row).astype(jnp.bfloat16)
    weight_piece = lax.all_gather(qkv_weight, "dp", axis=1, tiled=True)
    count = weight_piece.shape[1]
    columns = row_block
    projected = (
        jnp.dot(
            columns,
            weight_piece[0].reshape(count, 3 * local_width),
            preferred_element_type=jnp.float32,
        )
        .astype(jnp.bfloat16)
        .reshape(length, 3, local_heads, HDIM)
    )
    queries = projected[:, 0]
    own_pair = projected[:, 1:]
    other_pair = from_partner(own_pair, "mod", 0)
    key_pairs = jnp.where(own_rows[:, None, None, None], own_pair, other_pair)
    key_pos = jnp.arange(length, dtype=jnp.int32)
    scores = (
        jnp.einsum("qhd,khd->hqk", queries, key_pairs[:, 0], preferred_element_type=jnp.float32)
        * scale
    )
    allowed = key_pos[None, :] <= key_pos[:, None]
    scores = jnp.where(allowed[None], scores, -jnp.inf)
    soft_weights = jax.nn.softmax(scores, axis=-1).astype(jnp.bfloat16)
    attended = jnp.einsum(
        "hqk,khd->qhd", soft_weights, key_pairs[:, 1], preferred_element_type=jnp.float32
    )
    attended = attended.astype(jnp.bfloat16).reshape(queries.shape[0], local_width)
    all_heads = lax.all_gather(attended, "tensor", axis=1, tiled=True)
    weight_piece = lax.all_gather(out_weight, "dp", axis=1, tiled=True)
    columns = all_heads
    projected_out = jnp.dot(columns, weight_piece[0], preferred_element_type=jnp.float32).astype(
        jnp.bfloat16
    )
    placed = jnp.where(own_rows[:, None], projected_out, jnp.zeros_like(projected_out))
    combined = lax.psum(placed.astype(jnp.float32).astype(jnp.bfloat16), "mod")
    return combined


def solution(mesh):
    places, shards = mesh.shape["dp"], mesh.shape["tensor"]
    mods = mesh.shape["mod"]

    def move(array, where, *earlier):
        pairs = []
        for m in range(mods):
            for d in range(places):
                for x in range(shards):
                    to = where(m, d, x)
                    if to is not None:
                        target = (to[0] * places + to[1]) * shards + to[2]
                        pairs.append(((m * places + d) * shards + x, target))
        return lax.ppermute(after(array, *earlier) if earlier else array, AXES, pairs)

    def to_core(array, *earlier):
        return move(array, lambda m, d, x: (1 - m, d, x), *earlier)

    def over_tensor(array, *earlier):
        return [array] + [
            move(array, lambda m, d, x: (m, d, (x + step) % shards), *earlier)
            for step in range(1, shards)
        ]

    def edge(m, d, x):
        return m, d ^ 2, x

    def outward(m, d, x):
        return (m, d ^ 2, x) if d // 2 in (1, 2) else None

    def across(m, d, x):
        return (m, (3 - d // 2) * 2 + d % 2, x) if d // 2 in (1, 2) else None

    def across_or_stay(m, d, x):
        return across(m, d, x) or (m, d, x)

    def pair(m, d, x):
        return m, d ^ 1, x

    def line_plan(tokens, modality, norm_gains, qkv_weight, out_weight):
        core = lax.axis_index("mod").astype(I32)
        place = lax.axis_index("dp").astype(I32)
        own = lax.axis_index("tensor").astype(I32)
        z, y = place // 2, place % 2
        column = (z ^ (z // 2)) & 1
        outer = 1 - column
        length, features = tokens.shape
        kept = qkv_weight.shape[1]
        half = length // 2
        which = core ^ (z & 1)
        at = [z, z ^ 1, jnp.where(z < 2, 2, 1), 3 - 3 * (z // 2)]

        def choose(edge_block, middle_block):
            return jnp.where(outer == 1, edge_block, middle_block)

        weight = qkv_weight[0].transpose(1, 0, 2)
        low_a, high_a, mine_a, away_a = halves(weight, outer, 0, 2)
        m1a = move(low_a, across_or_stay)
        e1a = move(away_a, edge)
        p1a = move(mine_a, pair)
        rows, top, bottom = own_rows_of(after(tokens, mine_a), core)
        fetched = over_tensor(rows)
        other_modality = move(modality, edge, mine_a)
        low_b, high_b, mine_b, away_b = halves(weight, outer, 1, 2)

        m2a = move(high_a, across, m1a)
        e2a = move(m1a, edge, e1a)
        p2a = move(e1a, pair, p1a, mine_b, rows)
        low_o, high_o, mine_o, away_o = halves(out_weight, after(outer, e1a), 0, 1)
        swapped = [to_core(a) for a in fetched[1:]]

        m3a = move(e2a, across, m2a)
        passed_top = move(top, edge, e2a, other_modality)
        third_a = choose(e2a, m2a)
        p3a = move(third_a, pair, p2a, mine_o)
        gains = norm_gains[0].reshape(places, 1, kept)
        shape = (2, places, length, kept)
        normed = normalize(
            scalars(core, own, which), None, gains, tokens, fetched[1:], swapped, shape, 0, half, kept
        )

        m4a = move(e1a, across, m3a)
        passed_bottom = move(bottom, edge, passed_top)
        p1b = move(mine_b, pair, p3a, normed)
        part_top = over_tensor(passed_top, passed_top)

        def add(slot, blocks, total, final=False, fresh=False):
            found = [slot]
            for k, _, _ in blocks:
                found += [2 * k + y, 2 * k + 1 - y]
            flat = [b for _, near, far in blocks for b in (near, far)]
            return project(scalars(*found), normed, flat, total, final, fresh)

        first_a = [(at[0], mine_a, p1a), (at[1], e1a, p2a), (at[2], third_a, p3a)]
        total_a = add(which, first_a, None, fresh=True)

        m1b = move(low_b, across_or_stay, m4a)
        e3a = move(m3a, outward, passed_bottom)
        part_bottom = over_tensor(passed_bottom, passed_bottom)
        top_swapped = [to_core(a) for a in part_top]
        normed = normalize(
            scalars(core, own, 1 - which),
            normed,
            gains,
            None,
            part_top,
            top_swapped,
            shape,
            0,
            half // 2,
            kept,
        )

        m2b = move(high_b, across, m1b)
        e2b = move(m1b, edge, e3a)
        fourth_a = choose(e3a, m4a)
        p4a = move(fourth_a, pair, p1b, total_a, normed)
        bottom_swapped = [to_core(a) for a in part_bottom]
        normed = normalize(
            scalars(core, own, 1 - which),
            normed,
            gains,
            None,
            part_bottom,
            bottom_swapped,
            shape,
            half // 2,
            half // 2,
            kept,
        )
        total_a = add(1 - which, first_a, total_a, fresh=True)

        m3b = move(e2b, across, m2b)
        e1b = move(away_b, edge, e2b)
        third_b = choose(e2b, m2b)
        p3b = move(third_b, pair, p4a, total_a)
        zero, one = jnp.zeros((), I32), jnp.ones((), I32)
        last_a = [(at[3], fourth_a, p4a)]
        theirs_a = add(one, last_a, total_a, final=True)
        got_a = to_core(theirs_a)
        ours_a = add(zero, last_a, total_a, final=True)
        own_rows = (modality == core).astype(I32)[:, None]
        other_rows = (other_modality == core).astype(I32)[:, None]
        mine_rows = jnp.where(which == 0, own_rows, other_rows)

        m4b = move(e1b, across, m3b)
        e3b = move(m3b, outward, e1b)
        p2b = move(e1b, pair, p3b, ours_a)
        attended_a = attend(ours_a, got_a, mine_rows)
        first_b = [(at[0], mine_b, p1b), (at[2], third_b, p3b)]
        total_b = add(which, first_b, None, fresh=True)
        held_a = over_tensor(attended_a)

        m1o = move(low_o, across_or_stay, m4b)
        fourth_b = choose(e3b, m4b)
        p4b = move(fourth_b, pair, p2b, attended_a)
        e1o = move(away_o, edge, e3b)
        total_b = add(1 - which, first_b, total_b, fresh=True)
        held_a += over_tensor(move(attended_a, edge, e1o))

        m2o = move(high_o, across, m1o)
        e2o = move(m1o, edge, held_a[shards])
        p1o = move(mine_o, pair, p4b)
        last_b = [(at[1], e1b, p2b), (at[3], fourth_b, p4b)]
        theirs_b = add(one, last_b, total_b, final=True)
        got_b = to_core(theirs_b)
        ours_b = add(zero, last_b, total_b, final=True)
        stack_a = jnp.stack(held_a)
        pieces_a = (stack_a, to_core(stack_a))
        attended_b = attend(ours_b, got_b, mine_rows)

        p2o = move(e1o, pair, p1o)
        m3o = move(e2o, across, m2o)
        m4o = move(e1o, across, m3o)
        third_o = choose(e2o, m2o)
        p3o = move(third_o, pair, p2o)
        e3o = move(m3o, outward)
        fourth_o = choose(e3o, m4o)
        held_b = over_tensor(attended_b)
        held_b += over_tensor(move(attended_b, edge, e2o))
        blocks = [(mine_o, p1o), (e1o, p2o), (third_o, p3o)]

        def piece_of(k):
            shard, part = k // 2, k % 2
            return jnp.where(part == column, 0, shards) + (own - shard + shards) % shards

        found = [piece_of(k) for k in at]
        total = combine(
            scalars(1 - which, y, core, *found[:3]), [pieces_a + (0, blocks)], None, 2
        )
        p4o = move(fourth_o, pair, p3o)
        last = [(fourth_o, p4o)]
        stack_b = jnp.stack(held_b)
        pieces_b = (stack_b, to_core(stack_b))
        rest = [pieces_a + (0, last), pieces_b + (1, blocks + last)]

        def finish(slot, offset):
            order = scalars(slot, y, core, found[3], *found)
            return combine(order, rest, total, 1, offset, offset == 0)

        kept_away, sent_away = finish(1 - which, 0)
        sent_away = to_core(sent_away)
        near = finish(which, 1)
        keep = lax.dynamic_slice_in_dim(other_rows, core * half, half, 0)
        far = move(jnp.where(keep != 0, kept_away, sent_away), edge)
        return assemble(
            scalars(core, column), own_rows, near, to_core(near), far, to_core(far)
        )

    return jax.shard_map(
        line_plan if places == 8 else gathered_plan,
        mesh=mesh,
        in_specs=(
            P("dp", "tensor"),
            P("dp"),
            P("mod", None),
            P("mod", "dp", None, "tensor"),
            P("mod", "dp", "tensor"),
        ),
        out_specs=P("dp", "tensor"),
        check_vma=False,
    )
```

```python
import jax
import jax.numpy as jnp
from jax import lax
from jax.experimental import pallas as pl
from jax.experimental.pallas import tpu as pltpu
from jax.sharding import PartitionSpec as P

HDIM = 128
AXES = ("mod", "dp", "tensor")
F32, BF16, I32 = jnp.float32, jnp.bfloat16, jnp.int32
VMEM, SMEM = pltpu.VMEM, pltpu.SMEM


def after(array, *earlier):
    return lax.optimization_barrier((array,) + earlier)[0]


class Here:
    def __init__(self, ref):
        self.core, place, self.own = ref[0], ref[1], ref[2]
        self.z, self.y = place >> 1, place & 1
        self.column = (self.z ^ (self.z >> 1)) & 1
        self.outer = self.column == 0
        self.which = self.core ^ (self.z & 1)
        self.at = [self.z, self.z ^ 1, jnp.where(self.z < 2, 2, 1), 3 - 3 * (self.z >> 1)]

    def slot(self, name):
        return {"own": self.which, "partner": 1 - self.which}.get(name, name)


def call(kernel, here, args, out_shape, aliases=None, scratch=8):
    return pl.pallas_call(
        kernel,
        in_specs=[pl.BlockSpec(memory_space=SMEM)] + [pl.BlockSpec(memory_space=VMEM)] * len(args),
        out_specs=jax.tree.map(lambda _: pl.BlockSpec(memory_space=VMEM), out_shape),
        out_shape=jax.tree.map(lambda shape: VMEM(shape.shape, shape.dtype), out_shape),
        input_output_aliases=aliases or {},
        compiler_params=pltpu.CompilerParams(vmem_limit_bytes=scratch * 2**20),
    )(here, *[pltpu.with_memory_space_constraint(a, VMEM) for a in args])


def shaped(shape, dtype=BF16):
    return jax.ShapeDtypeStruct(shape, dtype)


def halves(here, weight, chunk, chunks):
    kinds, depth, width = weight.shape
    half = width // 2
    part = half // chunks

    def kernel(h_ref, in_ref, low_ref, high_ref, mine_ref, away_ref):
        outer = Here(h_ref).outer
        for kind in range(kinds):
            low = in_ref[kind, :, chunk * part : (chunk + 1) * part]
            high = in_ref[kind, :, half + chunk * part : half + (chunk + 1) * part]
            low_ref[kind] = low
            high_ref[kind] = high
            mine_ref[kind] = jnp.where(outer, low, high)
            away_ref[kind] = jnp.where(outer, high, low)

    return call(kernel, here, [weight], [shaped((kinds, depth, part))] * 4)


def own_rows_of(here, tokens):
    length, features = tokens.shape
    half = length // 2

    def kernel(h_ref, in_ref, rows_ref, top_ref, bottom_ref):
        rows = jnp.where(h_ref[0] == 0, in_ref[:half], in_ref[half:])
        rows_ref[...] = rows
        top_ref[...] = rows[: half // 2]
        bottom_ref[...] = rows[half // 2 :]

    part = shaped((half // 2, features))
    return call(kernel, here, [tokens], [shaped((half, features)), part, part])


def choose(here, from_edge, from_middle):
    def kernel(h_ref, a_ref, b_ref, out_ref):
        outer = Here(h_ref).outer

        @pl.when(outer)
        def _():
            out_ref[...] = a_ref[...]

        @pl.when(jnp.logical_not(outer))
        def _():
            out_ref[...] = b_ref[...]

    return call(kernel, here, [from_edge, from_middle], shaped(from_edge.shape))


def stack(here, arrays):
    def kernel(_, *refs):
        for i in range(len(arrays)):
            refs[-1][i] = refs[i][...]

    return call(kernel, here, arrays, shaped((len(arrays),) + arrays[0].shape))


def normalize(here, slot, held, gains, whole, mine, theirs, shape, start, count):
    _, _, length, kept = shape
    shards = len(mine) + (whole is not None)
    features = (whole if whole is not None else mine[0]).shape[1]
    tile = 32 if count % 32 == 0 else count
    half = length // 2
    per = features // kept
    args = ([] if held is None else [held]) + [gains] + ([] if whole is None else [whole])
    args += list(mine) + list(theirs)

    def kernel(h_ref, *refs):
        at_place = Here(h_ref)
        core, own, into = at_place.core, at_place.own, at_place.slot(slot)
        out_ref = refs[-1]
        refs = list(refs[0 if held is None else 1 : -1])
        gain_ref = refs.pop(0)
        whole_ref = None if whole is None else refs.pop(0)
        shard_of = [lax.rem(own - step + shards, shards) for step in range(shards)]

        def step(i, carry):
            for group, first in ((refs[: len(mine)], core), (refs[len(mine) :], 1 - core)):
                row = pl.multiple_of(first * half + start + i * tile, tile)
                at = pl.ds(pl.multiple_of(i * tile, tile), tile)
                found = [(ref, at) for ref in group]
                if whole_ref is not None:
                    found = [(whole_ref, pl.ds(row, tile))] + found
                total = jnp.zeros((tile, 1), F32)
                for ref, rows in found:
                    wide = ref[rows, :].astype(F32)
                    total = total + jnp.sum(wide * wide, axis=-1, keepdims=True)
                inverse = lax.rsqrt(total / (shards * features) + 1e-05)
                for shard, (ref, rows) in zip(shard_of, found):
                    for j in range(per):
                        block = shard * per + j
                        wide = ref[rows, j * kept : (j + 1) * kept].astype(F32)
                        out_ref[into, block, pl.ds(row, tile), :] = (
                            wide * inverse * gain_ref[block]
                        ).astype(BF16)
            return carry

        lax.fori_loop(0, count // tile, step, 0)

    return call(kernel, here, args, shaped(shape), None if held is None else {1: 0})


def project(here, slot, normed, blocks, total=None, final=False, fresh=False):
    slots, _, length, kept = normed.shape
    kinds, _, width = blocks[0][1].shape
    count = len(blocks)
    args = [normed] + [b for _, near, far in blocks for b in (near, far)]
    args += [] if total is None else [total]

    def kernel(h_ref, *refs):
        at_place = Here(h_ref)
        into = at_place.slot(slot)
        normed_ref, out_ref = refs[0], refs[-1]
        for kind in range(kinds):
            columns = slice(kind * width, (kind + 1) * width)
            summed = None if fresh else refs[1 + 2 * count][into, :, columns]
            for i, (arrival, _, _) in enumerate(blocks):
                for j, y in enumerate((at_place.y, 1 - at_place.y)):
                    part = jnp.dot(
                        normed_ref[into, at_place.at[arrival] * 2 + y],
                        refs[1 + 2 * i + j][kind],
                        preferred_element_type=F32,
                    )
                    summed = part if summed is None else summed + part
            if final:
                out_ref[:, columns] = summed.astype(BF16)
            else:
                out_ref[into, :, columns] = summed

    if final:
        return call(kernel, here, args, shaped((length, kinds * width)))
    aliases = None if total is None else {2 + 2 * count: 0}
    return call(kernel, here, args, shaped((slots, length, kinds * width), F32), aliases)


def attend(here, own_kind, other_kind, own, got):
    length, width = own.shape[0], own.shape[1] // 3
    heads = width // HDIM
    scale = HDIM ** (-0.5)
    tile = 128 if length % 128 == 0 else length

    def kernel(h_ref, own_kind_ref, other_kind_ref, own_ref, got_ref, out_ref):
        at_place = Here(h_ref)
        kind = jnp.where(at_place.which == 0, own_kind_ref[...], other_kind_ref[...])
        keep = kind == at_place.core

        def pick(j):
            columns = slice(j * HDIM, (j + 1) * HDIM)
            return jnp.where(
                keep, own_ref[:, columns].astype(F32), got_ref[:, columns].astype(F32)
            ).astype(BF16)

        for h in range(heads):
            query, key, value = pick(h), pick(heads + h), pick(2 * heads + h)
            for i in range(length // tile):
                low, high = i * tile, (i + 1) * tile
                scores = lax.dot_general(
                    query[low:high], key[:high], (((1,), (1,)), ((), ())), preferred_element_type=F32
                )
                rows = low + lax.broadcasted_iota(I32, (tile, high), 0)
                cols = lax.broadcasted_iota(I32, (tile, high), 1)
                scores = jnp.where(cols <= rows, scores * scale, -jnp.inf)
                top = jnp.max(scores, axis=-1, keepdims=True)
                raised = jnp.exp(scores - top)
                share = 1.0 / jnp.sum(raised, axis=-1, keepdims=True)
                probs = (raised * share).astype(BF16)
                out = jnp.dot(probs, value[:high], preferred_element_type=F32)
                out_ref[low:high, h * HDIM : (h + 1) * HDIM] = out.astype(BF16)

    return call(kernel, here, [own_kind, other_kind, own, got], shaped((length, width)))


def combine(here, slots, groups, total=None, offset=0, cut=False):
    held_pieces, length, held = groups[0][0].shape
    shards = held_pieces // 2
    features = groups[0][3][0][1].shape[2]
    tile = min(features, 256)
    half = length // 2
    terms = [group[:3] + (pair,) for group in groups for pair in group[3]]
    count = len(terms)
    args = [pieces for term in terms for pieces in term[:2]]
    args += [b for term in terms for b in term[3][1:]] + ([] if total is None else [total])

    def kernel(h_ref, *refs):
        at_place = Here(h_ref)
        outs = refs[-2:] if cut else refs[-1:]
        found = []
        for z in at_place.at:
            shard = lax.rem(at_place.own - (z >> 1) + shards, shards)
            found.append(jnp.where((z & 1) == at_place.column, 0, shards) + shard)
        for s, name in enumerate(slots):
            first_slot = at_place.slot(name) == 0
            rows = [
                jnp.where(
                    first_slot, refs[2 * i][found[arrival]], refs[2 * i + 1][found[arrival]]
                )
                for i, (_, _, _, (arrival, _, _)) in enumerate(terms)
            ]
            for n in range(features // tile):
                columns = slice(n * tile, (n + 1) * tile)
                summed = None if total is None else refs[4 * count][offset + s, :, columns]
                for i, (_, _, parity, _) in enumerate(terms):
                    near = refs[2 * count + 2 * i][0, :, columns]
                    far = refs[2 * count + 2 * i + 1][0, :, columns]
                    block = jnp.where(at_place.y == parity, near, far)
                    part = jnp.dot(rows[i], block, preferred_element_type=F32)
                    summed = part if summed is None else summed + part
                if total is None:
                    outs[0][s, :, columns] = summed
                elif cut:
                    result = summed.astype(BF16)
                    first = at_place.core == 0
                    outs[0][:, columns] = jnp.where(first, result[:half], result[half:])
                    outs[1][:, columns] = jnp.where(first, result[half:], result[:half])
                else:
                    outs[0][:, columns] = summed.astype(BF16)

    if total is None:
        out_shape = shaped((len(slots), length, features), F32)
    elif cut:
        out_shape = [shaped((half, features))] * 2
    else:
        out_shape = shaped((length, features))
    return call(kernel, here, args, out_shape)


def join(here, kind, kept, got):
    half = kept.shape[0]

    def kernel(h_ref, kind_ref, a_ref, b_ref, out_ref):
        core = h_ref[0]
        rows = jnp.where(core == 0, kind_ref[:half], kind_ref[half:])
        out_ref[...] = jnp.where(
            rows == core, a_ref[...].astype(F32), b_ref[...].astype(F32)
        ).astype(BF16)

    return call(kernel, here, [kind, kept, got], shaped(kept.shape))


def assemble(here, kind, near, near_other, far, far_other):
    length, width = near.shape
    steps = 4
    tile = length // steps
    half = length // 2
    args = [kind, near, near_other, far, far_other]

    def kernel(h_ref, kind_ref, a_ref, b_ref, c_ref, d_ref, out_ref, held, sems):
        at_place = Here(h_ref)
        core, first = at_place.core, at_place.column == 0
        copies = []
        for i in range(steps):
            rows = slice(i * tile, (i + 1) * tile)
            keep = kind_ref[rows] == core
            own = jnp.where(keep, a_ref[rows].astype(F32), b_ref[rows].astype(F32)).astype(BF16)
            part = slice(i * tile % half, i * tile % half + tile)
            other = jnp.where(core == i * tile // half, c_ref[part], d_ref[part])
            held[i, :, :width] = jnp.where(first, own, other)
            held[i, :, width:] = jnp.where(first, other, own)
            copies.append(pltpu.make_async_copy(held.at[i], out_ref.at[rows], sems.at[i]))
            copies[-1].start()
        for copy in copies:
            copy.wait()

    return pl.pallas_call(
        kernel,
        in_specs=[pl.BlockSpec(memory_space=SMEM)] + [pl.BlockSpec(memory_space=VMEM)] * 5,
        out_specs=pl.BlockSpec(memory_space=pl.ANY),
        out_shape=shaped((length, 2 * width)),
        scratch_shapes=[VMEM((steps, tile, 2 * width), BF16), pltpu.SemaphoreType.DMA((steps,))],
        compiler_params=pltpu.CompilerParams(vmem_limit_bytes=8 * 2**20),
    )(here, *[pltpu.with_memory_space_constraint(a, VMEM) for a in args])


def from_partner(x, axis, bit):
    return lax.ppermute(x, axis, [(i, i ^ 1 << bit) for i in range(lax.axis_size(axis))])


def gathered_plan(tokens, modality, norm_gains, qkv_weight, out_weight):
    tower_id = lax.axis_index("mod")
    own_rows = modality == tower_id
    gathered = lax.all_gather(tokens, "tensor", axis=1, tiled=True)
    length = gathered.shape[0]
    local_width = qkv_weight.shape[3]
    local_heads = local_width // HDIM
    gain_row = norm_gains[0]
    scale = HDIM ** (-0.5)
    wide_rows = gathered.astype(jnp.float32)
    inverse = lax.rsqrt(jnp.mean(wide_rows * wide_rows, axis=-1, keepdims=True) + 1e-05)
    row_block = (wide_rows * inverse * gain_row).astype(jnp.bfloat16)
    weight_piece = lax.all_gather(qkv_weight, "dp", axis=1, tiled=True)
    count = weight_piece.shape[1]
    columns = row_block
    projected = (
        jnp.dot(
            columns,
            weight_piece[0].reshape(count, 3 * local_width),
            preferred_element_type=jnp.float32,
        )
        .astype(jnp.bfloat16)
        .reshape(length, 3, local_heads, HDIM)
    )
    queries = projected[:, 0]
    own_pair = projected[:, 1:]
    other_pair = from_partner(own_pair, "mod", 0)
    key_pairs = jnp.where(own_rows[:, None, None, None], own_pair, other_pair)
    key_pos = jnp.arange(length, dtype=jnp.int32)
    scores = (
        jnp.einsum("qhd,khd->hqk", queries, key_pairs[:, 0], preferred_element_type=jnp.float32)
        * scale
    )
    allowed = key_pos[None, :] <= key_pos[:, None]
    scores = jnp.where(allowed[None], scores, -jnp.inf)
    soft_weights = jax.nn.softmax(scores, axis=-1).astype(jnp.bfloat16)
    attended = jnp.einsum(
        "hqk,khd->qhd", soft_weights, key_pairs[:, 1], preferred_element_type=jnp.float32
    )
    attended = attended.astype(jnp.bfloat16).reshape(queries.shape[0], local_width)
    all_heads = lax.all_gather(attended, "tensor", axis=1, tiled=True)
    weight_piece = lax.all_gather(out_weight, "dp", axis=1, tiled=True)
    columns = all_heads
    projected_out = jnp.dot(columns, weight_piece[0], preferred_element_type=jnp.float32).astype(
        jnp.bfloat16
    )
    placed = jnp.where(own_rows[:, None], projected_out, jnp.zeros_like(projected_out))
    combined = lax.psum(placed.astype(jnp.float32).astype(jnp.bfloat16), "mod")
    return combined


def solution(mesh):
    places, shards = mesh.shape["dp"], mesh.shape["tensor"]
    mods = mesh.shape["mod"]

    def move(array, where, *earlier):
        pairs = []
        for m in range(mods):
            for d in range(places):
                for x in range(shards):
                    to = where(m, d, x)
                    if to is not None:
                        target = (to[0] * places + to[1]) * shards + to[2]
                        pairs.append(((m * places + d) * shards + x, target))
        return lax.ppermute(after(array, *earlier) if earlier else array, AXES, pairs)

    def to_core(array, *earlier):
        return move(array, lambda m, d, x: (1 - m, d, x), *earlier)

    def over_tensor(array, *earlier):
        return [array] + [
            move(array, lambda m, d, x: (m, d, (x + step) % shards), *earlier)
            for step in range(1, shards)
        ]

    def edge(m, d, x):
        return m, d ^ 2, x

    def outward(m, d, x):
        return (m, d ^ 2, x) if d // 2 in (1, 2) else None

    def across(m, d, x):
        return (m, (3 - d // 2) * 2 + d % 2, x) if d // 2 in (1, 2) else None

    def across_or_stay(m, d, x):
        return across(m, d, x) or (m, d, x)

    def pair(m, d, x):
        return m, d ^ 1, x

    def line_plan(tokens, modality, norm_gains, qkv_weight, out_weight):
        here = jnp.stack([lax.axis_index(name).astype(I32) for name in AXES])
        length = tokens.shape[0]
        kept = qkv_weight.shape[1]
        half = length // 2
        gains = norm_gains[0].reshape(places, 1, kept)
        own_kind = modality[:, None]

        weight = after(qkv_weight[0].transpose(1, 0, 2), here, gains, own_kind)
        low_a, high_a, mine_a, away_a = halves(here, weight, 0, 2)
        m1a = move(low_a, across_or_stay)
        e1a = move(away_a, edge)
        rows, top, bottom = own_rows_of(here, after(tokens, mine_a))
        p1a = move(mine_a, pair, rows)
        fetched = over_tensor(rows)
        other_kind = move(own_kind, edge, rows)
        low_b, high_b, mine_b, away_b = halves(here, after(weight, rows), 1, 2)
        low_o, high_o, mine_o, away_o = halves(here, after(out_weight, mine_b), 0, 1)

        m2a = move(high_a, across, m1a, mine_o)
        e2a = move(m1a, edge, e1a, p1a)
        p2a = move(e1a, pair, p1a)
        swapped = [to_core(a) for a in fetched[1:]]

        m3a = move(e2a, across, m2a)
        passed_top = move(top, edge, e2a, other_kind)
        third_a = choose(here, e2a, m2a)
        p3a = move(third_a, pair, p2a)
        shape = (2, places, length, kept)
        normed = normalize(here, "own", None, gains, tokens, fetched[1:], swapped, shape, 0, half)

        m4a = move(e1a, across, m3a)
        passed_bottom = move(bottom, edge, passed_top)
        p1b = move(mine_b, pair, p3a, normed)
        part_top = over_tensor(passed_top)
        first_a = [(0, mine_a, p1a), (1, e1a, p2a), (2, third_a, p3a)]
        total_a = project(here, "own", normed, first_a, fresh=True)

        m1b = move(low_b, across_or_stay, m4a)
        e3a = move(m3a, outward, passed_bottom)
        p1o = move(mine_o, pair, p1b, total_a)
        part_bottom = over_tensor(passed_bottom)
        top_swapped = [to_core(a) for a in part_top]
        normed = normalize(
            here, "partner", normed, gains, None, part_top, top_swapped, shape, 0, half // 2
        )

        m2b = move(high_b, across, m1b)
        e2b = move(m1b, edge, e3a)
        fourth_a = choose(here, e3a, m4a)
        p4a = move(fourth_a, pair, p1o, normed)
        bottom_swapped = [to_core(a) for a in part_bottom]
        normed = normalize(
            here, "partner", normed, gains, None, part_bottom, bottom_swapped, shape, half // 2, half // 2
        )
        total_a = project(here, "partner", normed, first_a, total_a, fresh=True)

        m3b = move(e2b, across, m2b)
        e1b = move(away_b, edge, e2b)
        third_b = choose(here, e2b, m2b)
        p3b = move(third_b, pair, p4a, total_a)
        last_a = [(3, fourth_a, p4a)]
        theirs_a = project(here, 1, normed, last_a, total_a, final=True)
        got_a = to_core(theirs_a)
        ours_a = project(here, 0, normed, last_a, total_a, final=True)

        m4b = move(e1b, across, m3b)
        e3b = move(m3b, outward, e1b)
        p2b = move(e1b, pair, p3b, ours_a)
        attended_a = attend(here, own_kind, other_kind, ours_a, got_a)
        first_b = [(0, mine_b, p1b), (2, third_b, p3b)]
        total_b = project(here, "own", normed, first_b, fresh=True)
        total_b = project(here, "partner", normed, first_b, total_b, fresh=True)
        held_a = over_tensor(attended_a)

        m1o = move(low_o, across_or_stay, m4b)
        fourth_b = choose(here, e3b, m4b)
        p4b = move(fourth_b, pair, p2b, attended_a, total_b)
        e1o = move(away_o, edge, e3b)
        second_b = [(1, e1b, p2b)]
        total_b = project(here, "own", normed, second_b, total_b)
        total_b = project(here, "partner", normed, second_b, total_b)

        m2o = move(high_o, across, m1o)
        e2o = move(m1o, edge, e1o)
        last_b = [(3, fourth_b, p4b)]
        theirs_b = project(here, 1, normed, last_b, total_b, final=True)
        got_b = to_core(theirs_b)
        ours_b = project(here, 0, normed, last_b, total_b, final=True)
        attended_b = attend(here, own_kind, other_kind, ours_b, got_b)

        p2o = move(e1o, pair, p4b)
        m3o = move(e2o, across, m2o)
        m4o = move(e1o, across, m3o)
        third_o = choose(here, e2o, m2o)
        p3o = move(third_o, pair, p2o)
        passed_a = move(attended_a, edge, e2o)
        held_a += over_tensor(passed_a)
        e3o = move(m3o, outward, passed_a)
        pieces_a = stack(here, held_a)
        pieces_a = (pieces_a, to_core(pieces_a))
        fourth_o = choose(here, e3o, m4o)
        held_b = over_tensor(attended_b)
        held_b += over_tensor(move(attended_b, edge, passed_a))
        blocks = [(0, mine_o, p1o), (1, e1o, p2o), (2, third_o, p3o)]

        total = combine(here, ("partner", "own"), [pieces_a + (0, blocks)])
        p4o = move(fourth_o, pair, p3o)
        last = [(3, fourth_o, p4o)]
        pieces_b = stack(here, held_b)
        pieces_b = (pieces_b, to_core(pieces_b))
        rest = [pieces_a + (0, last), pieces_b + (1, blocks + last)]

        kept_away, sent_away = combine(here, ("partner",), rest, total, 0, True)
        sent_away = to_core(sent_away)
        near = combine(here, ("own",), rest, total, 1)
        far = move(join(here, other_kind, kept_away, sent_away), edge)
        return assemble(here, own_kind, near, to_core(near), far, to_core(far))

    return jax.shard_map(
        line_plan if places == 8 else gathered_plan,
        mesh=mesh,
        in_specs=(
            P("dp", "tensor"),
            P("dp"),
            P("mod", None),
            P("mod", "dp", None, "tensor"),
            P("mod", "dp", "tensor"),
        ),
        out_specs=P("dp", "tensor"),
        check_vma=False,
    )
```

```python
import jax
import jax.numpy as jnp
from jax import lax
from jax.experimental import pallas as pl
from jax.experimental.pallas import tpu as pltpu
from jax.sharding import PartitionSpec as P

HDIM = 128
AXES = ("mod", "dp", "tensor")
F32, BF16, I32 = jnp.float32, jnp.bfloat16, jnp.int32
VMEM, SMEM = pltpu.VMEM, pltpu.SMEM


def after(array, *earlier):
    return lax.optimization_barrier((array,) + earlier)[0]


class Here:
    def __init__(self, ref):
        self.core, place, self.own = ref[0], ref[1], ref[2]
        self.z, self.y = place >> 1, place & 1
        self.column = (self.z ^ (self.z >> 1)) & 1
        self.outer = self.column == 0
        self.which = self.core ^ (self.z & 1)
        self.at = [self.z, self.z ^ 1, jnp.where(self.z < 2, 2, 1), 3 - 3 * (self.z >> 1)]

    def slot(self, name):
        return {"own": self.which, "partner": 1 - self.which}.get(name, name)


def call(kernel, here, args, out_shape, aliases=None, scratch=8):
    return pl.pallas_call(
        kernel,
        in_specs=[pl.BlockSpec(memory_space=SMEM)] + [pl.BlockSpec(memory_space=VMEM)] * len(args),
        out_specs=jax.tree.map(lambda _: pl.BlockSpec(memory_space=VMEM), out_shape),
        out_shape=jax.tree.map(lambda shape: VMEM(shape.shape, shape.dtype), out_shape),
        input_output_aliases=aliases or {},
        compiler_params=pltpu.CompilerParams(vmem_limit_bytes=scratch * 2**20),
    )(here, *[pltpu.with_memory_space_constraint(a, VMEM) for a in args])


def shaped(shape, dtype=BF16):
    return jax.ShapeDtypeStruct(shape, dtype)


def halves(here, weight, chunk, chunks):
    kinds, depth, width = weight.shape
    half = width // 2
    part = half // chunks

    def kernel(h_ref, in_ref, low_ref, high_ref, mine_ref, away_ref):
        outer = Here(h_ref).outer
        for kind in range(kinds):
            low = in_ref[kind, :, chunk * part : (chunk + 1) * part]
            high = in_ref[kind, :, half + chunk * part : half + (chunk + 1) * part]
            low_ref[kind] = low
            high_ref[kind] = high
            mine_ref[kind] = jnp.where(outer, low, high)
            away_ref[kind] = jnp.where(outer, high, low)

    return call(kernel, here, [weight], [shaped((kinds, depth, part))] * 4)


def own_rows_of(here, tokens):
    length, features = tokens.shape
    half = length // 2

    def kernel(h_ref, in_ref, rows_ref, top_ref, bottom_ref):
        rows = jnp.where(h_ref[0] == 0, in_ref[:half], in_ref[half:])
        rows_ref[...] = rows
        top_ref[...] = rows[: half // 2]
        bottom_ref[...] = rows[half // 2 :]

    part = shaped((half // 2, features))
    return call(kernel, here, [tokens], [shaped((half, features)), part, part])


def choose(here, from_edge, from_middle):
    def kernel(h_ref, a_ref, b_ref, out_ref):
        outer = Here(h_ref).outer

        @pl.when(outer)
        def _():
            out_ref[...] = a_ref[...]

        @pl.when(jnp.logical_not(outer))
        def _():
            out_ref[...] = b_ref[...]

    return call(kernel, here, [from_edge, from_middle], shaped(from_edge.shape))


def stack(here, arrays):
    def kernel(_, *refs):
        for i in range(len(arrays)):
            refs[-1][i] = refs[i][...]

    return call(kernel, here, arrays, shaped((len(arrays),) + arrays[0].shape))


def normalize(here, slot, held, gains, whole, mine, theirs, shape, start, count):
    _, _, length, kept = shape
    shards = len(mine) + (whole is not None)
    features = (whole if whole is not None else mine[0]).shape[1]
    tile = 32 if count % 32 == 0 else count
    half = length // 2
    per = features // kept
    args = ([] if held is None else [held]) + [gains] + ([] if whole is None else [whole])
    args += list(mine) + list(theirs)

    def kernel(h_ref, *refs):
        at_place = Here(h_ref)
        core, own, into = at_place.core, at_place.own, at_place.slot(slot)
        out_ref = refs[-1]
        refs = list(refs[0 if held is None else 1 : -1])
        gain_ref = refs.pop(0)
        whole_ref = None if whole is None else refs.pop(0)
        shard_of = [lax.rem(own - step + shards, shards) for step in range(shards)]

        def step(i, carry):
            for group, first in ((refs[: len(mine)], core), (refs[len(mine) :], 1 - core)):
                row = pl.multiple_of(first * half + start + i * tile, tile)
                at = pl.ds(pl.multiple_of(i * tile, tile), tile)
                found = [(ref, at) for ref in group]
                if whole_ref is not None:
                    found = [(whole_ref, pl.ds(row, tile))] + found
                total = jnp.zeros((tile, 1), F32)
                for ref, rows in found:
                    wide = ref[rows, :].astype(F32)
                    total = total + jnp.sum(wide * wide, axis=-1, keepdims=True)
                inverse = lax.rsqrt(total / (shards * features) + 1e-05)
                for shard, (ref, rows) in zip(shard_of, found):
                    for j in range(per):
                        block = shard * per + j
                        wide = ref[rows, j * kept : (j + 1) * kept].astype(F32)
                        out_ref[into, block, pl.ds(row, tile), :] = (
                            wide * inverse * gain_ref[block]
                        ).astype(BF16)
            return carry

        lax.fori_loop(0, count // tile, step, 0)

    return call(kernel, here, args, shaped(shape), None if held is None else {1: 0})


def project(here, slot, normed, blocks, total=None, final=False, fresh=False):
    slots, _, length, kept = normed.shape
    kinds, _, width = blocks[0][1].shape
    count = len(blocks)
    args = [normed] + [b for _, near, far in blocks for b in (near, far)]
    args += [] if total is None else [total]

    def kernel(h_ref, *refs):
        at_place = Here(h_ref)
        into = at_place.slot(slot)
        normed_ref, out_ref = refs[0], refs[-1]
        for kind in range(kinds):
            columns = slice(kind * width, (kind + 1) * width)
            summed = None if fresh else refs[1 + 2 * count][into, :, columns]
            for i, (arrival, _, _) in enumerate(blocks):
                for j, y in enumerate((at_place.y, 1 - at_place.y)):
                    part = jnp.dot(
                        normed_ref[into, at_place.at[arrival] * 2 + y],
                        refs[1 + 2 * i + j][kind],
                        preferred_element_type=F32,
                    )
                    summed = part if summed is None else summed + part
            if final:
                out_ref[:, columns] = summed.astype(BF16)
            else:
                out_ref[into, :, columns] = summed

    if final:
        return call(kernel, here, args, shaped((length, kinds * width)))
    aliases = None if total is None else {2 + 2 * count: 0}
    return call(kernel, here, args, shaped((slots, length, kinds * width), F32), aliases)


def attend(here, own_kind, other_kind, own, got):
    length, width = own.shape[0], own.shape[1] // 3
    heads = width // HDIM
    scale = HDIM ** (-0.5)
    tile = 128 if length % 128 == 0 else length

    def kernel(h_ref, own_kind_ref, other_kind_ref, own_ref, got_ref, out_ref):
        at_place = Here(h_ref)
        kind = jnp.where(at_place.which == 0, own_kind_ref[...], other_kind_ref[...])
        keep = kind == at_place.core

        def pick(j):
            columns = slice(j * HDIM, (j + 1) * HDIM)
            return jnp.where(
                keep, own_ref[:, columns].astype(F32), got_ref[:, columns].astype(F32)
            ).astype(BF16)

        for h in range(heads):
            query, key, value = pick(h), pick(heads + h), pick(2 * heads + h)
            for i in range(length // tile):
                low, high = i * tile, (i + 1) * tile
                scores = lax.dot_general(
                    query[low:high], key[:high], (((1,), (1,)), ((), ())), preferred_element_type=F32
                )
                rows = low + lax.broadcasted_iota(I32, (tile, high), 0)
                cols = lax.broadcasted_iota(I32, (tile, high), 1)
                scores = jnp.where(cols <= rows, scores * scale, -jnp.inf)
                top = jnp.max(scores, axis=-1, keepdims=True)
                raised = jnp.exp(scores - top)
                share = 1.0 / jnp.sum(raised, axis=-1, keepdims=True)
                probs = (raised * share).astype(BF16)
                out = jnp.dot(probs, value[:high], preferred_element_type=F32)
                out_ref[low:high, h * HDIM : (h + 1) * HDIM] = out.astype(BF16)

    return call(kernel, here, [own_kind, other_kind, own, got], shaped((length, width)))


def combine(here, slots, groups, total=None, offset=0, cut=False):
    held_pieces, length, held = groups[0][0].shape
    shards = held_pieces // 2
    features = groups[0][3][0][1].shape[2]
    tile = min(features, 256)
    half = length // 2
    terms = [group[:3] + (pair,) for group in groups for pair in group[3]]
    count = len(terms)
    args = [pieces for term in terms for pieces in term[:2]]
    args += [b for term in terms for b in term[3][1:]] + ([] if total is None else [total])

    def kernel(h_ref, *refs):
        at_place = Here(h_ref)
        outs = refs[-2:] if cut else refs[-1:]
        found = []
        for z in at_place.at:
            shard = lax.rem(at_place.own - (z >> 1) + shards, shards)
            found.append(jnp.where((z & 1) == at_place.column, 0, shards) + shard)
        for s, name in enumerate(slots):
            first_slot = at_place.slot(name) == 0
            rows = [
                jnp.where(
                    first_slot, refs[2 * i][found[arrival]], refs[2 * i + 1][found[arrival]]
                )
                for i, (_, _, _, (arrival, _, _)) in enumerate(terms)
            ]
            for n in range(features // tile):
                columns = slice(n * tile, (n + 1) * tile)
                summed = None if total is None else refs[4 * count][offset + s, :, columns]
                for i, (_, _, parity, _) in enumerate(terms):
                    near = refs[2 * count + 2 * i][0, :, columns]
                    far = refs[2 * count + 2 * i + 1][0, :, columns]
                    block = jnp.where(at_place.y == parity, near, far)
                    part = jnp.dot(rows[i], block, preferred_element_type=F32)
                    summed = part if summed is None else summed + part
                if total is None:
                    outs[0][s, :, columns] = summed
                elif cut:
                    result = summed.astype(BF16)
                    first = at_place.core == 0
                    outs[0][:, columns] = jnp.where(first, result[:half], result[half:])
                    outs[1][:, columns] = jnp.where(first, result[half:], result[:half])
                else:
                    outs[0][:, columns] = summed.astype(BF16)

    if total is None:
        out_shape = shaped((len(slots), length, features), F32)
    elif cut:
        out_shape = [shaped((half, features))] * 2
    else:
        out_shape = shaped((length, features))
    return call(kernel, here, args, out_shape)


def join(here, kind, kept, got):
    half = kept.shape[0]

    def kernel(h_ref, kind_ref, a_ref, b_ref, out_ref):
        core = h_ref[0]
        rows = jnp.where(core == 0, kind_ref[:half], kind_ref[half:])
        out_ref[...] = jnp.where(
            rows == core, a_ref[...].astype(F32), b_ref[...].astype(F32)
        ).astype(BF16)

    return call(kernel, here, [kind, kept, got], shaped(kept.shape))


def assemble(here, kind, near, near_other, far, far_other):
    length, width = near.shape
    steps = 4
    tile = length // steps
    half = length // 2
    args = [kind, near, near_other, far, far_other]

    def kernel(h_ref, kind_ref, a_ref, b_ref, c_ref, d_ref, out_ref, held, sems):
        at_place = Here(h_ref)
        core, first = at_place.core, at_place.column == 0
        copies = []
        for i in range(steps):
            rows = slice(i * tile, (i + 1) * tile)
            keep = kind_ref[rows] == core
            own = jnp.where(keep, a_ref[rows].astype(F32), b_ref[rows].astype(F32)).astype(BF16)
            part = slice(i * tile % half, i * tile % half + tile)
            other = jnp.where(core == i * tile // half, c_ref[part], d_ref[part])
            held[i, :, :width] = jnp.where(first, own, other)
            held[i, :, width:] = jnp.where(first, other, own)
            copies.append(pltpu.make_async_copy(held.at[i], out_ref.at[rows], sems.at[i]))
            copies[-1].start()
        for copy in copies:
            copy.wait()

    return pl.pallas_call(
        kernel,
        in_specs=[pl.BlockSpec(memory_space=SMEM)] + [pl.BlockSpec(memory_space=VMEM)] * 5,
        out_specs=pl.BlockSpec(memory_space=pl.ANY),
        out_shape=shaped((length, 2 * width)),
        scratch_shapes=[VMEM((steps, tile, 2 * width), BF16), pltpu.SemaphoreType.DMA((steps,))],
        compiler_params=pltpu.CompilerParams(vmem_limit_bytes=8 * 2**20),
    )(here, *[pltpu.with_memory_space_constraint(a, VMEM) for a in args])


def from_partner(x, axis, bit):
    return lax.ppermute(x, axis, [(i, i ^ 1 << bit) for i in range(lax.axis_size(axis))])


def gathered_plan(tokens, modality, norm_gains, qkv_weight, out_weight):
    tower_id = lax.axis_index("mod")
    own_rows = modality == tower_id
    gathered = lax.all_gather(tokens, "tensor", axis=1, tiled=True)
    length = gathered.shape[0]
    local_width = qkv_weight.shape[3]
    local_heads = local_width // HDIM
    gain_row = norm_gains[0]
    scale = HDIM ** (-0.5)
    wide_rows = gathered.astype(jnp.float32)
    inverse = lax.rsqrt(jnp.mean(wide_rows * wide_rows, axis=-1, keepdims=True) + 1e-05)
    row_block = (wide_rows * inverse * gain_row).astype(jnp.bfloat16)
    weight_piece = lax.all_gather(qkv_weight, "dp", axis=1, tiled=True)
    count = weight_piece.shape[1]
    columns = row_block
    projected = (
        jnp.dot(
            columns,
            weight_piece[0].reshape(count, 3 * local_width),
            preferred_element_type=jnp.float32,
        )
        .astype(jnp.bfloat16)
        .reshape(length, 3, local_heads, HDIM)
    )
    queries = projected[:, 0]
    own_pair = projected[:, 1:]
    other_pair = from_partner(own_pair, "mod", 0)
    key_pairs = jnp.where(own_rows[:, None, None, None], own_pair, other_pair)
    key_pos = jnp.arange(length, dtype=jnp.int32)
    scores = (
        jnp.einsum("qhd,khd->hqk", queries, key_pairs[:, 0], preferred_element_type=jnp.float32)
        * scale
    )
    allowed = key_pos[None, :] <= key_pos[:, None]
    scores = jnp.where(allowed[None], scores, -jnp.inf)
    soft_weights = jax.nn.softmax(scores, axis=-1).astype(jnp.bfloat16)
    attended = jnp.einsum(
        "hqk,khd->qhd", soft_weights, key_pairs[:, 1], preferred_element_type=jnp.float32
    )
    attended = attended.astype(jnp.bfloat16).reshape(queries.shape[0], local_width)
    all_heads = lax.all_gather(attended, "tensor", axis=1, tiled=True)
    weight_piece = lax.all_gather(out_weight, "dp", axis=1, tiled=True)
    columns = all_heads
    projected_out = jnp.dot(columns, weight_piece[0], preferred_element_type=jnp.float32).astype(
        jnp.bfloat16
    )
    placed = jnp.where(own_rows[:, None], projected_out, jnp.zeros_like(projected_out))
    combined = lax.psum(placed.astype(jnp.float32).astype(jnp.bfloat16), "mod")
    return combined


def solution(mesh):
    places, shards = mesh.shape["dp"], mesh.shape["tensor"]
    mods = mesh.shape["mod"]

    def move(array, where, *earlier):
        pairs = []
        for m in range(mods):
            for d in range(places):
                for x in range(shards):
                    to = where(m, d, x)
                    if to is not None:
                        target = (to[0] * places + to[1]) * shards + to[2]
                        pairs.append(((m * places + d) * shards + x, target))
        return lax.ppermute(after(array, *earlier) if earlier else array, AXES, pairs)

    def to_core(array, *earlier):
        return move(array, lambda m, d, x: (1 - m, d, x), *earlier)

    def over_tensor(array, *earlier):
        return [array] + [
            move(array, lambda m, d, x: (m, d, (x + step) % shards), *earlier)
            for step in range(1, shards)
        ]

    def edge(m, d, x):
        return m, d ^ 2, x

    def outward(m, d, x):
        return (m, d ^ 2, x) if d // 2 in (1, 2) else None

    def inward(m, d, x):
        return (m, d ^ 2, x) if d // 2 in (0, 3) else None

    def across(m, d, x):
        return (m, (3 - d // 2) * 2 + d % 2, x) if d // 2 in (1, 2) else None

    def across_or_stay(m, d, x):
        return across(m, d, x) or (m, d, x)

    def pair(m, d, x):
        return m, d ^ 1, x

    def line_plan(tokens, modality, norm_gains, qkv_weight, out_weight):
        here = jnp.stack([lax.axis_index(name).astype(I32) for name in AXES])
        length = tokens.shape[0]
        kept = qkv_weight.shape[1]
        half = length // 2
        gains = norm_gains[0].reshape(places, 1, kept)
        own_kind = modality[:, None]

        weight = after(qkv_weight[0].transpose(1, 0, 2), here, gains, own_kind)
        low_a, high_a, mine_a, away_a = halves(here, weight, 0, 2)
        m1a = move(low_a, across_or_stay)
        e1a = move(away_a, edge)
        p1a = move(mine_a, pair)
        other_kind = move(own_kind, edge)
        rows, top, bottom = own_rows_of(here, after(tokens, mine_a))
        fetched = over_tensor(rows)

        m2a = move(high_a, across, m1a)
        e2a = move(m1a, edge, e1a, p1a, other_kind)
        p2a = move(e1a, pair, p1a)
        low_b, high_b, mine_b, away_b = halves(here, after(weight, m1a), 1, 2)
        swapped = [to_core(a) for a in fetched[1:]]

        m3a = move(e2a, across, m2a, mine_b)
        passed_top = move(top, edge, e2a, m2a)
        third_a = choose(here, e2a, m2a)
        p3a = move(third_a, pair, p2a)
        shape = (2, places, length, kept)
        normed = normalize(
            here, "own", None, gains, after(tokens, m2a), fetched[1:], swapped, shape, 0, half
        )

        m4a = move(e1a, across, m3a)
        passed_bottom = move(bottom, edge, passed_top, m3a)
        p1b = move(mine_b, pair, p3a, normed)
        part_top = over_tensor(passed_top)
        first_a = [(0, mine_a, p1a), (1, e1a, p2a), (2, third_a, p3a)]
        total_a = project(here, "own", after(normed, m3a), first_a, fresh=True)
        low_o, high_o, mine_o, away_o = halves(here, after(out_weight, m3a), 0, 1)

        m1b = move(low_b, across_or_stay, m4a)
        e3a = move(m3a, outward, passed_bottom)
        i1o = move(low_o, inward, passed_bottom)
        p1o = move(mine_o, pair, p1b, total_a)
        part_bottom = over_tensor(passed_bottom)
        top_swapped = [to_core(a) for a in part_top]
        normed = normalize(
            here,
            "partner",
            normed,
            gains,
            None,
            [after(part_top[0], m4a)] + part_top[1:],
            top_swapped,
            shape,
            0,
            half // 2,
        )

        m2b = move(high_b, across, m1b)
        e2b = move(m1b, edge, e3a, i1o)
        fourth_a = choose(here, e3a, m4a)
        p4a = move(fourth_a, pair, p1o, normed)
        bottom_swapped = [to_core(a) for a in part_bottom]
        normed = normalize(
            here,
            "partner",
            normed,
            gains,
            None,
            [after(part_bottom[0], m1b)] + part_bottom[1:],
            bottom_swapped,
            shape,
            half // 2,
            half // 2,
        )
        total_a = project(here, "partner", normed, first_a, total_a, fresh=True)

        m3b = move(e2b, across, m2b)
        e1b = move(away_b, edge, e2b, m2b)
        third_b = choose(here, e2b, m2b)
        p3b = move(third_b, pair, p4a, total_a)
        last_a = [(3, fourth_a, p4a)]
        theirs_a = project(here, 1, after(normed, m2b), last_a, total_a, final=True)
        got_a = to_core(theirs_a)
        ours_a = project(here, 0, normed, last_a, total_a, final=True)

        m4b = move(e1b, across, m3b)
        e3b = move(m3b, outward, e1b)
        i2o = move(high_o, inward, e1b)
        p2b = move(e1b, pair, p3b, ours_a)
        attended_a = attend(here, own_kind, other_kind, after(ours_a, m3b), got_a)
        first_b = [(0, mine_b, p1b), (2, third_b, p3b)]
        late_normed = after(normed, m3b)
        total_b = project(here, "own", late_normed, first_b, fresh=True)
        total_b = project(here, "partner", late_normed, first_b, total_b, fresh=True)
        held_a = over_tensor(attended_a)

        m1o = move(low_o, across, m4b)
        m3o = move(i1o, across, m4b)
        fourth_b = choose(here, e3b, m4b)
        p4b = move(fourth_b, pair, p2b)
        o1o = move(low_o, outward, e3b, m4b)
        second_b = [(1, e1b, p2b)]
        late_normed = after(normed, m4b, attended_a)
        total_b = project(here, "own", late_normed, second_b, total_b)
        total_b = project(here, "partner", late_normed, second_b, total_b)
        passed_a = move(attended_a, edge, o1o)
        held_a += over_tensor(passed_a)

        second_o = choose(here, o1o, i2o)
        p2o = move(second_o, pair, p4b)
        last_b = [(3, fourth_b, p4b)]
        theirs_b = project(here, 1, normed, last_b, total_b, final=True)
        got_b = to_core(theirs_b)
        ours_b = project(here, 0, normed, last_b, total_b, final=True)
        m2o = move(high_o, across, m1o)
        m4o = move(i2o, across, m3o)
        o2o = move(m1o, outward, passed_a)
        o3o = move(m3o, outward, o2o)
        attended_b = attend(here, own_kind, other_kind, ours_b, got_b)
        passed_b = move(attended_b, edge, passed_a)
        held_b = over_tensor(attended_b)
        held_b += over_tensor(passed_b)

        third_o = choose(here, o2o, m2o)
        p3o = move(third_o, pair, p2o)
        pieces_a = stack(here, held_a)
        pieces_a = (pieces_a, to_core(pieces_a))
        fourth_o = choose(here, o3o, m4o)
        p4o = move(fourth_o, pair, p3o)
        blocks = [(0, mine_o, p1o), (1, second_o, p2o), (2, third_o, p3o)]
        total = combine(here, ("partner", "own"), [pieces_a + (0, blocks)])
        last = [(3, fourth_o, p4o)]
        pieces_b = stack(here, held_b)
        pieces_b = (pieces_b, to_core(pieces_b))
        rest = [pieces_a + (0, last), pieces_b + (1, blocks + last)]

        kept_away, sent_away = combine(here, ("partner",), rest, total, 0, True)
        sent_away = to_core(sent_away)
        near = combine(here, ("own",), rest, total, 1)
        far = move(join(here, other_kind, kept_away, sent_away), edge)
        return assemble(here, own_kind, near, to_core(near), far, to_core(far))

    return jax.shard_map(
        line_plan if places == 8 else gathered_plan,
        mesh=mesh,
        in_specs=(
            P("dp", "tensor"),
            P("dp"),
            P("mod", None),
            P("mod", "dp", None, "tensor"),
            P("mod", "dp", "tensor"),
        ),
        out_specs=P("dp", "tensor"),
        check_vma=False,
    )
```

```python
import jax
import jax.numpy as jnp
from jax import lax
from jax.experimental import pallas as pl
from jax.experimental.pallas import tpu as pltpu
from jax.sharding import PartitionSpec as P

HDIM = 128
AXES = ("mod", "dp", "tensor")
F32, BF16, I32 = jnp.float32, jnp.bfloat16, jnp.int32
VMEM, SMEM = pltpu.VMEM, pltpu.SMEM


def after(array, *earlier):
    return lax.optimization_barrier((array,) + earlier)[0]


class Here:
    def __init__(self, ref):
        self.core, place, self.own = ref[0], ref[1], ref[2]
        self.z, self.y = place >> 1, place & 1
        self.column = (self.z ^ (self.z >> 1)) & 1
        self.outer = self.column == 0
        self.which = self.core ^ (self.z & 1)
        self.at = [self.z, self.z ^ 1, jnp.where(self.z < 2, 2, 1), 3 - 3 * (self.z >> 1)]

    def slot(self, name):
        return {"own": self.which, "partner": 1 - self.which}.get(name, name)


def call(name, kernel, here, args, out_shape, aliases=None, scratch=8):
    return pl.pallas_call(
        kernel,
        in_specs=[pl.BlockSpec(memory_space=SMEM)] + [pl.BlockSpec(memory_space=VMEM)] * len(args),
        out_specs=jax.tree.map(lambda _: pl.BlockSpec(memory_space=VMEM), out_shape),
        out_shape=jax.tree.map(lambda shape: VMEM(shape.shape, shape.dtype), out_shape),
        input_output_aliases=aliases or {},
        compiler_params=pltpu.CompilerParams(vmem_limit_bytes=scratch * 2**20),
        name=name,
    )(here, *[pltpu.with_memory_space_constraint(a, VMEM) for a in args])


def shaped(shape, dtype=BF16):
    return jax.ShapeDtypeStruct(shape, dtype)


def by_row(kind):
    return jnp.broadcast_to(kind.astype(F32), (128, kind.shape[1])).T.astype(I32)


def halves(here, weight, chunk, chunks):
    kinds, depth, width = weight.shape
    half = width // 2
    part = half // chunks

    def kernel(h_ref, in_ref, low_ref, high_ref, mine_ref, away_ref):
        outer = Here(h_ref).outer
        for kind in range(kinds):
            low = in_ref[kind, :, chunk * part : (chunk + 1) * part]
            high = in_ref[kind, :, half + chunk * part : half + (chunk + 1) * part]
            low_ref[kind] = low
            high_ref[kind] = high
            mine_ref[kind] = jnp.where(outer, low, high)
            away_ref[kind] = jnp.where(outer, high, low)

    return call("halves", kernel, here, [weight], [shaped((kinds, depth, part))] * 4)


def own_rows_of(here, tokens):
    length, features = tokens.shape
    half = length // 2

    def kernel(h_ref, in_ref, rows_ref, top_ref, bottom_ref):
        rows = jnp.where(h_ref[0] == 0, in_ref[:half], in_ref[half:])
        rows_ref[...] = rows
        top_ref[...] = rows[: half // 2]
        bottom_ref[...] = rows[half // 2 :]

    part = shaped((half // 2, features))
    return call("own_rows_of", kernel, here, [tokens], [shaped((half, features)), part, part])


def choose(here, from_edge, from_middle):
    def kernel(h_ref, a_ref, b_ref, out_ref):
        outer = Here(h_ref).outer

        @pl.when(outer)
        def _():
            out_ref[...] = a_ref[...]

        @pl.when(jnp.logical_not(outer))
        def _():
            out_ref[...] = b_ref[...]

    return call("choose", kernel, here, [from_edge, from_middle], shaped(from_edge.shape))


def stack(here, arrays):
    def kernel(_, *refs):
        for i in range(len(arrays)):
            refs[-1][i] = refs[i][...]

    return call("stack", kernel, here, arrays, shaped((len(arrays),) + arrays[0].shape))


def pack(here, block, piece):
    _, depth, features = block.shape
    length, width = piece.shape
    cuts = features // width

    def kernel(_, block_ref, piece_ref, out_ref):
        for i in range(cuts):
            out_ref[i * depth : (i + 1) * depth] = block_ref[0, :, i * width : (i + 1) * width]
        out_ref[cuts * depth :] = piece_ref[...]

    return call("pack", kernel, here, [block, piece], shaped((cuts * depth + length, width)))


def unpack(here, packed, block, piece):
    _, depth, features = block.shape
    _, width = piece.shape
    cuts = features // width

    def kernel(_, in_ref, block_ref, piece_ref):
        for i in range(cuts):
            block_ref[0, :, i * width : (i + 1) * width] = in_ref[i * depth : (i + 1) * depth]
        piece_ref[...] = in_ref[cuts * depth :]

    return call("unpack", kernel, here, [packed], [shaped(block.shape), shaped(piece.shape)])


def normalize(here, slot, held, gains, whole, mine, theirs, shape, start, count):
    _, _, length, kept = shape
    shards = len(mine) + (whole is not None)
    features = (whole if whole is not None else mine[0]).shape[1]
    tile = 32 if count % 32 == 0 else count
    half = length // 2
    per = features // kept
    args = ([] if held is None else [held]) + [gains] + ([] if whole is None else [whole])
    args += list(mine) + list(theirs)

    def kernel(h_ref, *refs):
        at_place = Here(h_ref)
        core, own, into = at_place.core, at_place.own, at_place.slot(slot)
        out_ref = refs[-1]
        refs = list(refs[0 if held is None else 1 : -1])
        gain_ref = refs.pop(0)
        whole_ref = None if whole is None else refs.pop(0)
        shard_of = [lax.rem(own - step + shards, shards) for step in range(shards)]

        def step(i, carry):
            for group, first in ((refs[: len(mine)], core), (refs[len(mine) :], 1 - core)):
                row = pl.multiple_of(first * half + start + i * tile, tile)
                at = pl.ds(pl.multiple_of(i * tile, tile), tile)
                found = [(ref, at) for ref in group]
                if whole_ref is not None:
                    found = [(whole_ref, pl.ds(row, tile))] + found
                total = jnp.zeros((tile, 1), F32)
                for ref, rows in found:
                    wide = ref[rows, :].astype(F32)
                    total = total + jnp.sum(wide * wide, axis=-1, keepdims=True)
                inverse = lax.rsqrt(total / (shards * features) + 1e-05)
                for shard, (ref, rows) in zip(shard_of, found):
                    for j in range(per):
                        block = shard * per + j
                        wide = ref[rows, j * kept : (j + 1) * kept].astype(F32)
                        out_ref[into, block, pl.ds(row, tile), :] = (
                            wide * inverse * gain_ref[block]
                        ).astype(BF16)
            return carry

        lax.fori_loop(0, count // tile, step, 0)

    return call("normalize", kernel, here, args, shaped(shape), None if held is None else {1: 0})


def project(here, slot, normed, blocks, total=None, final=False, fresh=False):
    slots, _, length, kept = normed.shape
    kinds, _, width = blocks[0][1].shape
    count = len(blocks)
    args = [normed] + [b for _, near, far in blocks for b in (near, far)]
    args += [] if total is None else [total]

    def kernel(h_ref, *refs):
        at_place = Here(h_ref)
        into = at_place.slot(slot)
        normed_ref, out_ref = refs[0], refs[-1]
        for kind in range(kinds):
            columns = slice(kind * width, (kind + 1) * width)
            summed = None if fresh else refs[1 + 2 * count][into, :, columns]
            for i, (arrival, _, _) in enumerate(blocks):
                for j, y in enumerate((at_place.y, 1 - at_place.y)):
                    part = jnp.dot(
                        normed_ref[into, at_place.at[arrival] * 2 + y],
                        refs[1 + 2 * i + j][kind],
                        preferred_element_type=F32,
                    )
                    summed = part if summed is None else summed + part
            if final:
                out_ref[:, columns] = summed.astype(BF16)
            else:
                out_ref[into, :, columns] = summed

    if final:
        return call("project", kernel, here, args, shaped((length, kinds * width)))
    aliases = None if total is None else {2 + 2 * count: 0}
    return call("project", kernel, here, args, shaped((slots, length, kinds * width), F32), aliases)


def attend(here, own_kind, other_kind, own, got):
    length, width = own.shape[0], own.shape[1] // 3
    heads = width // HDIM
    scale = HDIM ** (-0.5)
    tile = 128 if length % 128 == 0 else length

    def kernel(h_ref, own_kind_ref, other_kind_ref, own_ref, got_ref, out_ref):
        at_place = Here(h_ref)
        kind = jnp.where(at_place.which == 0, own_kind_ref[...], other_kind_ref[...])
        keep = by_row(kind) == at_place.core

        def pick(j):
            columns = slice(j * HDIM, (j + 1) * HDIM)
            return jnp.where(
                keep, own_ref[:, columns].astype(F32), got_ref[:, columns].astype(F32)
            ).astype(BF16)

        for h in range(heads):
            query, key, value = pick(h), pick(heads + h), pick(2 * heads + h)
            for i in range(length // tile):
                low, high = i * tile, (i + 1) * tile
                scores = lax.dot_general(
                    query[low:high], key[:high], (((1,), (1,)), ((), ())), preferred_element_type=F32
                )
                rows = low + lax.broadcasted_iota(I32, (tile, high), 0)
                cols = lax.broadcasted_iota(I32, (tile, high), 1)
                scores = jnp.where(cols <= rows, scores * scale, -jnp.inf)
                top = jnp.max(scores, axis=-1, keepdims=True)
                raised = jnp.exp(scores - top)
                share = 1.0 / jnp.sum(raised, axis=-1, keepdims=True)
                probs = (raised * share).astype(BF16)
                out = jnp.dot(probs, value[:high], preferred_element_type=F32)
                out_ref[low:high, h * HDIM : (h + 1) * HDIM] = out.astype(BF16)

    return call("attend", kernel, here, [own_kind, other_kind, own, got], shaped((length, width)))


def combine(here, slots, groups, total=None, offset=0, cut=False):
    held_pieces, length, held = groups[0][0].shape
    shards = held_pieces // 2
    features = groups[0][3][0][1].shape[2]
    tile = min(features, 256)
    half = length // 2
    terms = [group[:3] + (pair,) for group in groups for pair in group[3]]
    count = len(terms)
    args = [pieces for term in terms for pieces in term[:2]]
    args += [b for term in terms for b in term[3][1:]] + ([] if total is None else [total])

    def kernel(h_ref, *refs):
        at_place = Here(h_ref)
        outs = refs[-2:] if cut else refs[-1:]
        found = []
        for z in at_place.at:
            shard = lax.rem(at_place.own - (z >> 1) + shards, shards)
            found.append(jnp.where((z & 1) == at_place.column, 0, shards) + shard)
        for s, name in enumerate(slots):
            first_slot = at_place.slot(name) == 0
            rows = [
                jnp.where(
                    first_slot, refs[2 * i][found[arrival]], refs[2 * i + 1][found[arrival]]
                )
                for i, (_, _, _, (arrival, _, _)) in enumerate(terms)
            ]
            for n in range(features // tile):
                columns = slice(n * tile, (n + 1) * tile)
                summed = None if total is None else refs[4 * count][offset + s, :, columns]
                for i, (_, _, parity, _) in enumerate(terms):
                    near = refs[2 * count + 2 * i][0, :, columns]
                    far = refs[2 * count + 2 * i + 1][0, :, columns]
                    block = jnp.where(at_place.y == parity, near, far)
                    part = jnp.dot(rows[i], block, preferred_element_type=F32)
                    summed = part if summed is None else summed + part
                if total is None:
                    outs[0][s, :, columns] = summed
                elif cut:
                    result = summed.astype(BF16)
                    first = at_place.core == 0
                    outs[0][:, columns] = jnp.where(first, result[:half], result[half:])
                    outs[1][:, columns] = jnp.where(first, result[half:], result[:half])
                else:
                    outs[0][:, columns] = summed.astype(BF16)

    if total is None:
        out_shape = shaped((len(slots), length, features), F32)
    elif cut:
        out_shape = [shaped((half, features))] * 2
    else:
        out_shape = shaped((length, features))
    return call("combine", kernel, here, args, out_shape)


def join(here, kind, kept, got):
    half = kept.shape[0]

    def kernel(h_ref, kind_ref, a_ref, b_ref, out_ref):
        core = h_ref[0]
        rows = by_row(kind_ref[...])[:, :1]
        rows = jnp.where(core == 0, rows[:half], rows[half:])
        out_ref[...] = jnp.where(
            rows == core, a_ref[...].astype(F32), b_ref[...].astype(F32)
        ).astype(BF16)

    return call("join", kernel, here, [kind, kept, got], shaped(kept.shape))


def assemble(here, kind, near, near_other, far, far_other):
    length, width = near.shape
    steps = 4
    tile = length // steps
    half = length // 2
    args = [kind, near, near_other, far, far_other]

    def kernel(h_ref, kind_ref, a_ref, b_ref, c_ref, d_ref, out_ref, held, sems):
        at_place = Here(h_ref)
        core, first = at_place.core, at_place.column == 0
        copies = []
        kind = by_row(kind_ref[...])[:, :1]
        for i in range(steps):
            rows = slice(i * tile, (i + 1) * tile)
            keep = kind[rows] == core
            own = jnp.where(keep, a_ref[rows].astype(F32), b_ref[rows].astype(F32)).astype(BF16)
            part = slice(i * tile % half, i * tile % half + tile)
            other = jnp.where(core == i * tile // half, c_ref[part], d_ref[part])
            held[i, :, :width] = jnp.where(first, own, other)
            held[i, :, width:] = jnp.where(first, other, own)
            copies.append(pltpu.make_async_copy(held.at[i], out_ref.at[rows], sems.at[i]))
            copies[-1].start()
        for copy in copies:
            copy.wait()

    return pl.pallas_call(
        kernel,
        in_specs=[pl.BlockSpec(memory_space=SMEM)] + [pl.BlockSpec(memory_space=VMEM)] * 5,
        out_specs=pl.BlockSpec(memory_space=pl.ANY),
        out_shape=shaped((length, 2 * width)),
        scratch_shapes=[VMEM((steps, tile, 2 * width), BF16), pltpu.SemaphoreType.DMA((steps,))],
        compiler_params=pltpu.CompilerParams(vmem_limit_bytes=8 * 2**20),
    )(here, *[pltpu.with_memory_space_constraint(a, VMEM) for a in args])


def from_partner(x, axis, bit):
    return lax.ppermute(x, axis, [(i, i ^ 1 << bit) for i in range(lax.axis_size(axis))])


def gathered_plan(tokens, modality, norm_gains, qkv_weight, out_weight):
    tower_id = lax.axis_index("mod")
    own_rows = modality == tower_id
    gathered = lax.all_gather(tokens, "tensor", axis=1, tiled=True)
    length = gathered.shape[0]
    local_width = qkv_weight.shape[3]
    local_heads = local_width // HDIM
    gain_row = norm_gains[0]
    scale = HDIM ** (-0.5)
    wide_rows = gathered.astype(jnp.float32)
    inverse = lax.rsqrt(jnp.mean(wide_rows * wide_rows, axis=-1, keepdims=True) + 1e-05)
    row_block = (wide_rows * inverse * gain_row).astype(jnp.bfloat16)
    weight_piece = lax.all_gather(qkv_weight, "dp", axis=1, tiled=True)
    count = weight_piece.shape[1]
    columns = row_block
    projected = (
        jnp.dot(
            columns,
            weight_piece[0].reshape(count, 3 * local_width),
            preferred_element_type=jnp.float32,
        )
        .astype(jnp.bfloat16)
        .reshape(length, 3, local_heads, HDIM)
    )
    queries = projected[:, 0]
    own_pair = projected[:, 1:]
    other_pair = from_partner(own_pair, "mod", 0)
    key_pairs = jnp.where(own_rows[:, None, None, None], own_pair, other_pair)
    key_pos = jnp.arange(length, dtype=jnp.int32)
    scores = (
        jnp.einsum("qhd,khd->hqk", queries, key_pairs[:, 0], preferred_element_type=jnp.float32)
        * scale
    )
    allowed = key_pos[None, :] <= key_pos[:, None]
    scores = jnp.where(allowed[None], scores, -jnp.inf)
    soft_weights = jax.nn.softmax(scores, axis=-1).astype(jnp.bfloat16)
    attended = jnp.einsum(
        "hqk,khd->qhd", soft_weights, key_pairs[:, 1], preferred_element_type=jnp.float32
    )
    attended = attended.astype(jnp.bfloat16).reshape(queries.shape[0], local_width)
    all_heads = lax.all_gather(attended, "tensor", axis=1, tiled=True)
    weight_piece = lax.all_gather(out_weight, "dp", axis=1, tiled=True)
    columns = all_heads
    projected_out = jnp.dot(columns, weight_piece[0], preferred_element_type=jnp.float32).astype(
        jnp.bfloat16
    )
    placed = jnp.where(own_rows[:, None], projected_out, jnp.zeros_like(projected_out))
    combined = lax.psum(placed.astype(jnp.float32).astype(jnp.bfloat16), "mod")
    return combined


def solution(mesh):
    places, shards = mesh.shape["dp"], mesh.shape["tensor"]
    mods = mesh.shape["mod"]

    def move(array, where, *earlier):
        pairs = []
        for m in range(mods):
            for d in range(places):
                for x in range(shards):
                    to = where(m, d, x)
                    if to is not None:
                        target = (to[0] * places + to[1]) * shards + to[2]
                        pairs.append(((m * places + d) * shards + x, target))
        return lax.ppermute(after(array, *earlier) if earlier else array, AXES, pairs)

    def to_core(array, *earlier):
        return move(array, lambda m, d, x: (1 - m, d, x), *earlier)

    def over_tensor(array, *earlier):
        return [array] + [
            move(array, lambda m, d, x: (m, d, (x + step) % shards), *earlier)
            for step in range(1, shards)
        ]

    def edge(m, d, x):
        return m, d ^ 2, x

    def outward(m, d, x):
        return (m, d ^ 2, x) if d // 2 in (1, 2) else None

    def inward(m, d, x):
        return (m, d ^ 2, x) if d // 2 in (0, 3) else None

    def across(m, d, x):
        return (m, (3 - d // 2) * 2 + d % 2, x) if d // 2 in (1, 2) else None

    def across_or_stay(m, d, x):
        return across(m, d, x) or (m, d, x)

    def pair(m, d, x):
        return m, d ^ 1, x

    def line_plan(tokens, modality, norm_gains, qkv_weight, out_weight):
        here = jnp.stack([lax.axis_index(name).astype(I32) for name in AXES])
        length = tokens.shape[0]
        kept = qkv_weight.shape[1]
        half = length // 2
        gains = norm_gains[0].reshape(places, 1, kept)
        own_kind = modality[None, :]

        weight = after(qkv_weight[0].transpose(1, 0, 2), here, gains, own_kind)
        low_a, high_a, mine_a, away_a = halves(here, weight, 0, 2)
        m1a = move(low_a, across_or_stay)
        e1a = move(away_a, edge)
        p1a = move(mine_a, pair)

        begun = (m1a,)
        m2a = move(high_a, across, e1a, p1a, *begun)
        e2a = move(m1a, edge, e1a, p1a)
        p2a = move(e1a, pair, p1a, *begun)
        rows, top, bottom = own_rows_of(here, after(tokens, *begun))
        fetched = over_tensor(rows)
        low_b, high_b, mine_b, away_b = halves(here, after(weight, *begun), 1, 2)

        begun = (m2a, mine_b)
        m3a = move(e2a, across, p2a, *begun)
        other_kind = move(own_kind, edge, e2a, p2a, *begun)
        passed_top = move(top, edge, e2a, p2a, *begun)
        third_a = choose(here, after(e2a, *begun), m2a)
        p3a = move(third_a, pair, p2a)

        begun = (m3a,)
        swapped = [to_core(a, *begun) for a in fetched[1:]]
        shape = (2, places, length, kept)
        normed = normalize(
            here, "own", None, gains, after(tokens, *begun), fetched[1:], swapped, shape, 0, half
        )
        m4a = move(e1a, across, passed_top, p3a, *begun)
        passed_bottom = move(bottom, edge, passed_top, p3a, *begun)
        p1b = move(mine_b, pair, p3a, *begun)
        part_top = over_tensor(after(passed_top, *begun))
        low_o, high_o, mine_o, away_o = halves(here, after(out_weight, *begun), 0, 1)

        begun = (m4a, normed, mine_o)
        m1b = move(low_b, across_or_stay, *begun)
        e3a = move(m3a, outward, passed_bottom, p1b, part_top[-1], *begun)
        i1o = move(low_o, inward, passed_bottom, p1b, part_top[-1], *begun)
        p1o = move(mine_o, pair, p1b, *begun)
        part_bottom = over_tensor(after(passed_bottom, *begun))
        top_swapped = [to_core(a, *begun) for a in part_top]
        first_a = [(0, mine_a, p1a), (1, e1a, p2a), (2, third_a, p3a)]
        total_a = project(here, "own", after(normed, *begun), first_a, fresh=True)
        normed = normalize(
            here, "partner", normed, gains, None, part_top, top_swapped, shape, 0, half // 2
        )

        begun = (m1b, normed, total_a)
        m2b = move(high_b, across, *begun)
        e2b = move(m1b, edge, e3a, i1o, p1o, part_bottom[-1], *begun)
        fourth_a = choose(here, after(e3a, *begun), m4a)
        p4a = move(fourth_a, pair, p1o)
        bottom_swapped = [to_core(a, *begun) for a in part_bottom]
        normed = normalize(
            here, "partner", normed, gains, None, part_bottom, bottom_swapped, shape, half // 2, half // 2
        )
        total_a = project(here, "partner", normed, first_a, total_a, fresh=True)

        begun = (m2b, total_a)
        m3b = move(e2b, across, *begun)
        e1b = move(away_b, edge, e2b, p4a, *begun)
        third_b = choose(here, after(e2b, *begun), m2b)
        p3b = move(third_b, pair, p4a)
        last_a = [(3, fourth_a, p4a)]
        late_normed = after(normed, *begun)
        theirs_a = project(here, 1, late_normed, last_a, total_a, final=True)
        got_a = to_core(theirs_a)
        ours_a = project(here, 0, late_normed, last_a, total_a, final=True)

        begun = (m3b, theirs_a, ours_a)
        m4b = move(e1b, across, *begun)
        e3b = move(m3b, outward, e1b, p3b, *begun)
        i2o = move(high_o, inward, e1b, p3b, *begun)
        p2b = move(e1b, pair, p3b, *begun)
        attended_a = attend(here, own_kind, other_kind, after(ours_a, *begun), got_a)
        first_b = [(0, mine_b, p1b), (2, third_b, p3b)]
        late_normed = after(normed, *begun)
        total_b = project(here, "own", late_normed, first_b, fresh=True)
        total_b = project(here, "partner", late_normed, first_b, total_b, fresh=True)

        begun = (m4b, attended_a, total_b)
        m1o = move(low_o, across, *begun)
        m2o = move(high_o, across, *begun)
        fourth_b = choose(here, after(e3b, *begun), m4b)
        p4b = move(fourth_b, pair, p2b)
        packed_a = move(pack(here, after(low_o, *begun), attended_a), edge, e3b, i2o, p2b)
        held_a = over_tensor(after(attended_a, *begun))
        second_b = [(1, e1b, p2b)]
        late_normed = after(normed, *begun)
        total_b = project(here, "own", late_normed, second_b, total_b)
        total_b = project(here, "partner", late_normed, second_b, total_b)

        last_b = [(3, fourth_b, p4b)]
        theirs_b = project(here, 1, normed, last_b, total_b, final=True)
        got_b = to_core(theirs_b)
        ours_b = project(here, 0, normed, last_b, total_b, final=True)
        o1o, passed_a = unpack(here, after(packed_a, theirs_b), low_o, attended_a)
        second_o = choose(here, o1o, i2o)
        p2o = move(second_o, pair, p4b)
        held_a += over_tensor(passed_a)

        begun = (m1o, m2o, ours_b, second_o)
        m3o = move(i1o, across, *begun)
        o2o = move(m1o, outward, *begun)
        attended_b = attend(here, own_kind, other_kind, after(ours_b, *begun), got_b)

        begun = (m3o, attended_b)
        m4o = move(i2o, across, *begun)
        packed_b = move(pack(here, m3o, attended_b), edge, o2o, p2o, held_a[-1], *begun)
        held_b = over_tensor(attended_b)
        third_o = choose(here, after(o2o, *begun), m2o)
        p3o = move(third_o, pair, p2o)
        pieces_a = stack(here, [after(held_a[0], *begun)] + held_a[1:])
        pieces_a = (pieces_a, to_core(pieces_a))

        begun = (m4o, pieces_a[0])
        o3o, passed_b = unpack(here, after(packed_b, p3o, held_b[-1], *begun), low_o, attended_b)
        held_b += over_tensor(passed_b)
        fourth_o = choose(here, o3o, m4o)
        p4o = move(fourth_o, pair, p3o)
        blocks = [(0, mine_o, p1o), (1, second_o, p2o), (2, third_o, p3o)]
        pieces_b = stack(here, held_b)
        pieces_b = (pieces_b, to_core(pieces_b))
        total = combine(
            here, ("partner", "own"), [pieces_a + (0, blocks), pieces_b + (1, blocks)]
        )
        last = [(3, fourth_o, p4o)]
        rest = [pieces_a + (0, last), pieces_b + (1, last)]

        kept_away, sent_away = combine(here, ("partner",), rest, total, 0, True)
        sent_away = to_core(sent_away)
        near = combine(here, ("own",), rest, total, 1)
        far = move(join(here, other_kind, kept_away, sent_away), edge)
        return assemble(here, own_kind, near, to_core(near), far, to_core(far))

    return jax.shard_map(
        line_plan if places == 8 else gathered_plan,
        mesh=mesh,
        in_specs=(
            P("dp", "tensor"),
            P("dp"),
            P("mod", None),
            P("mod", "dp", None, "tensor"),
            P("mod", "dp", "tensor"),
        ),
        out_specs=P("dp", "tensor"),
        check_vma=False,
    )
```

```python
import jax
import jax.numpy as jnp
from jax import lax
from jax.experimental import pallas as pl
from jax.experimental.pallas import tpu as pltpu
from jax.sharding import PartitionSpec as P

HDIM = 128
AXES = ("mod", "dp", "tensor")
F32, BF16, I32 = jnp.float32, jnp.bfloat16, jnp.int32
VMEM, SMEM = pltpu.VMEM, pltpu.SMEM


def after(array, *earlier):
    return lax.optimization_barrier((array,) + earlier)[0]


class Here:
    def __init__(self, ref):
        self.core, place, self.own = ref[0], ref[1], ref[2]
        self.z, self.y = place >> 1, place & 1
        self.column = (self.z ^ (self.z >> 1)) & 1
        self.outer = self.column == 0
        self.which = self.core ^ (self.z & 1)
        self.at = [self.z, self.z ^ 1, jnp.where(self.z < 2, 2, 1), 3 - 3 * (self.z >> 1)]

    def slot(self, name):
        return {"own": self.which, "partner": 1 - self.which}.get(name, name)


def call(name, kernel, here, args, out_shape, aliases=None, scratch=8):
    return pl.pallas_call(
        kernel,
        in_specs=[pl.BlockSpec(memory_space=SMEM)] + [pl.BlockSpec(memory_space=VMEM)] * len(args),
        out_specs=jax.tree.map(lambda _: pl.BlockSpec(memory_space=VMEM), out_shape),
        out_shape=jax.tree.map(lambda shape: VMEM(shape.shape, shape.dtype), out_shape),
        input_output_aliases=aliases or {},
        compiler_params=pltpu.CompilerParams(vmem_limit_bytes=scratch * 2**20),
        name=name,
    )(here, *[pltpu.with_memory_space_constraint(a, VMEM) for a in args])


def shaped(shape, dtype=BF16):
    return jax.ShapeDtypeStruct(shape, dtype)


def by_row(kind):
    return jnp.broadcast_to(kind.astype(F32), (128, kind.shape[1])).T.astype(I32)


def halves(here, weight, chunk, chunks):
    kinds, depth, width = weight.shape
    half = width // 2
    part = half // chunks

    def kernel(h_ref, in_ref, low_ref, high_ref, mine_ref, away_ref):
        outer = Here(h_ref).outer
        for kind in range(kinds):
            low = in_ref[kind, :, chunk * part : (chunk + 1) * part]
            high = in_ref[kind, :, half + chunk * part : half + (chunk + 1) * part]
            low_ref[kind] = low
            high_ref[kind] = high
            mine_ref[kind] = jnp.where(outer, low, high)
            away_ref[kind] = jnp.where(outer, high, low)

    return call("halves", kernel, here, [weight], [shaped((kinds, depth, part))] * 4)


def own_rows_of(here, tokens, kind):
    length, features = tokens.shape
    half = length // 2
    extra = 16

    def kernel(h_ref, in_ref, kind_ref, rows_ref, top_ref, bottom_ref):
        rows = jnp.where(h_ref[0] == 0, in_ref[:half], in_ref[half:])
        rows_ref[...] = rows
        top_ref[...] = rows[: half // 2]
        bottom_ref[: half // 2] = rows[half // 2 :]
        bottom_ref[half // 2 :, :length] = jnp.broadcast_to(
            kind_ref[...].astype(F32), (extra, length)
        ).astype(BF16)
        bottom_ref[half // 2 :, length:] = jnp.zeros((extra, features - length), BF16)

    outs = [shaped((rows, features)) for rows in (half, half // 2, half // 2 + extra)]
    return call("own_rows_of", kernel, here, [tokens, kind], outs)


def kinds_behind(here, part, length):
    def kernel(_, in_ref, out_ref):
        out_ref[...] = in_ref[length // 4 :, :length].astype(F32)[:1].astype(I32)

    return call("kinds_behind", kernel, here, [part], shaped((1, length), I32))


def choose(here, from_edge, from_middle):
    def kernel(h_ref, a_ref, b_ref, out_ref):
        outer = Here(h_ref).outer

        @pl.when(outer)
        def _():
            out_ref[...] = a_ref[...]

        @pl.when(jnp.logical_not(outer))
        def _():
            out_ref[...] = b_ref[...]

    return call("choose", kernel, here, [from_edge, from_middle], shaped(from_edge.shape))


def stack(here, arrays):
    def kernel(_, *refs):
        for i in range(len(arrays)):
            refs[-1][i] = refs[i][...]

    return call("stack", kernel, here, arrays, shaped((len(arrays),) + arrays[0].shape))


def pack(here, block, piece):
    _, depth, features = block.shape
    length, width = piece.shape
    cuts = features // width

    def kernel(_, block_ref, piece_ref, out_ref):
        for i in range(cuts):
            out_ref[i * depth : (i + 1) * depth] = block_ref[0, :, i * width : (i + 1) * width]
        out_ref[cuts * depth :] = piece_ref[...]

    return call("pack", kernel, here, [block, piece], shaped((cuts * depth + length, width)))


def unpack(here, packed, block, piece):
    _, depth, features = block.shape
    _, width = piece.shape
    cuts = features // width

    def kernel(_, in_ref, block_ref, piece_ref):
        for i in range(cuts):
            block_ref[0, :, i * width : (i + 1) * width] = in_ref[i * depth : (i + 1) * depth]
        piece_ref[...] = in_ref[cuts * depth :]

    return call("unpack", kernel, here, [packed], [shaped(block.shape), shaped(piece.shape)])


def normalize(here, slot, held, gains, whole, mine, theirs, shape, start, count):
    _, _, length, kept = shape
    shards = len(mine) + (whole is not None)
    features = (whole if whole is not None else mine[0]).shape[1]
    tile = 32 if count % 32 == 0 else count
    half = length // 2
    per = features // kept
    args = ([] if held is None else [held]) + [gains] + ([] if whole is None else [whole])
    args += list(mine) + list(theirs)

    def kernel(h_ref, *refs):
        at_place = Here(h_ref)
        core, own, into = at_place.core, at_place.own, at_place.slot(slot)
        out_ref = refs[-1]
        refs = list(refs[0 if held is None else 1 : -1])
        gain_ref = refs.pop(0)
        whole_ref = None if whole is None else refs.pop(0)
        shard_of = [lax.rem(own - step + shards, shards) for step in range(shards)]

        def step(i, carry):
            for group, first in ((refs[: len(mine)], core), (refs[len(mine) :], 1 - core)):
                row = pl.multiple_of(first * half + start + i * tile, tile)
                at = pl.ds(pl.multiple_of(i * tile, tile), tile)
                found = [(ref, at) for ref in group]
                if whole_ref is not None:
                    found = [(whole_ref, pl.ds(row, tile))] + found
                total = jnp.zeros((tile, 1), F32)
                for ref, rows in found:
                    wide = ref[rows, :].astype(F32)
                    total = total + jnp.sum(wide * wide, axis=-1, keepdims=True)
                inverse = lax.rsqrt(total / (shards * features) + 1e-05)
                for shard, (ref, rows) in zip(shard_of, found):
                    for j in range(per):
                        block = shard * per + j
                        wide = ref[rows, j * kept : (j + 1) * kept].astype(F32)
                        out_ref[into, block, pl.ds(row, tile), :] = (
                            wide * inverse * gain_ref[block]
                        ).astype(BF16)
            return carry

        lax.fori_loop(0, count // tile, step, 0)

    return call("normalize", kernel, here, args, shaped(shape), None if held is None else {1: 0})


def project(here, slot, normed, blocks, total=None, final=False, fresh=False):
    slots, _, length, kept = normed.shape
    kinds, _, width = blocks[0][1].shape
    count = len(blocks)
    args = [normed] + [b for _, near, far in blocks for b in (near, far)]
    args += [] if total is None else [total]

    def kernel(h_ref, *refs):
        at_place = Here(h_ref)
        into = at_place.slot(slot)
        normed_ref, out_ref = refs[0], refs[-1]
        for kind in range(kinds):
            columns = slice(kind * width, (kind + 1) * width)
            summed = None if fresh else refs[1 + 2 * count][into, :, columns]
            for i, (arrival, _, _) in enumerate(blocks):
                for j, y in enumerate((at_place.y, 1 - at_place.y)):
                    part = jnp.dot(
                        normed_ref[into, at_place.at[arrival] * 2 + y],
                        refs[1 + 2 * i + j][kind],
                        preferred_element_type=F32,
                    )
                    summed = part if summed is None else summed + part
            if final:
                out_ref[:, columns] = summed.astype(BF16)
            else:
                out_ref[into, :, columns] = summed

    if final:
        return call("project", kernel, here, args, shaped((length, kinds * width)))
    aliases = None if total is None else {2 + 2 * count: 0}
    return call("project", kernel, here, args, shaped((slots, length, kinds * width), F32), aliases)


def attend(here, own_kind, other_kind, own, got):
    length, width = own.shape[0], own.shape[1] // 3
    heads = width // HDIM
    scale = HDIM ** (-0.5)
    tile = 128 if length % 128 == 0 else length

    def kernel(h_ref, own_kind_ref, other_kind_ref, own_ref, got_ref, out_ref):
        at_place = Here(h_ref)
        kind = jnp.where(at_place.which == 0, own_kind_ref[...], other_kind_ref[...])
        keep = by_row(kind) == at_place.core

        def pick(j):
            columns = slice(j * HDIM, (j + 1) * HDIM)
            return jnp.where(
                keep, own_ref[:, columns].astype(F32), got_ref[:, columns].astype(F32)
            ).astype(BF16)

        for h in range(heads):
            query, key, value = pick(h), pick(heads + h), pick(2 * heads + h)
            for i in range(length // tile):
                low, high = i * tile, (i + 1) * tile
                scores = lax.dot_general(
                    query[low:high], key[:high], (((1,), (1,)), ((), ())), preferred_element_type=F32
                )
                rows = low + lax.broadcasted_iota(I32, (tile, high), 0)
                cols = lax.broadcasted_iota(I32, (tile, high), 1)
                scores = jnp.where(cols <= rows, scores * scale, -jnp.inf)
                top = jnp.max(scores, axis=-1, keepdims=True)
                raised = jnp.exp(scores - top)
                share = 1.0 / jnp.sum(raised, axis=-1, keepdims=True)
                probs = (raised * share).astype(BF16)
                out = jnp.dot(probs, value[:high], preferred_element_type=F32)
                out_ref[low:high, h * HDIM : (h + 1) * HDIM] = out.astype(BF16)

    return call("attend", kernel, here, [own_kind, other_kind, own, got], shaped((length, width)))


def combine(here, slots, groups, total=None, final=False, offset=0, cut=False):
    held_pieces, length, held = groups[0][0].shape
    shards = held_pieces // 2
    features = groups[0][3][0][1].shape[2]
    tile = min(features, 256)
    half = length // 2
    terms = [group[:3] + (pair,) for group in groups for pair in group[3]]
    count = len(terms)
    args = [pieces for term in terms for pieces in term[:2]]
    args += [b for term in terms for b in term[3][1:]] + ([] if total is None else [total])

    def kernel(h_ref, *refs):
        at_place = Here(h_ref)
        outs = refs[-2:] if cut else refs[-1:]
        found = []
        for z in at_place.at:
            shard = lax.rem(at_place.own - (z >> 1) + shards, shards)
            found.append(jnp.where((z & 1) == at_place.column, 0, shards) + shard)
        for s, name in enumerate(slots):
            first_slot = at_place.slot(name) == 0
            rows = [
                jnp.where(
                    first_slot, refs[2 * i][found[arrival]], refs[2 * i + 1][found[arrival]]
                )
                for i, (_, _, _, (arrival, _, _)) in enumerate(terms)
            ]
            for n in range(features // tile):
                columns = slice(n * tile, (n + 1) * tile)
                summed = None if total is None else refs[4 * count][offset + s, :, columns]
                for i, (_, _, parity, _) in enumerate(terms):
                    near = refs[2 * count + 2 * i][0, :, columns]
                    far = refs[2 * count + 2 * i + 1][0, :, columns]
                    block = jnp.where(at_place.y == parity, near, far)
                    part = jnp.dot(rows[i], block, preferred_element_type=F32)
                    summed = part if summed is None else summed + part
                if not final:
                    outs[0][s, :, columns] = summed
                elif cut:
                    result = summed.astype(BF16)
                    first = at_place.core == 0
                    outs[0][:, columns] = jnp.where(first, result[:half], result[half:])
                    outs[1][:, columns] = jnp.where(first, result[half:], result[:half])
                else:
                    outs[0][:, columns] = summed.astype(BF16)

    if not final:
        out_shape = shaped((len(slots), length, features), F32)
    elif cut:
        out_shape = [shaped((half, features))] * 2
    else:
        out_shape = shaped((length, features))
    return call("combine", kernel, here, args, out_shape)


def join(here, kind, kept, got):
    half = kept.shape[0]

    def kernel(h_ref, kind_ref, a_ref, b_ref, out_ref):
        core = h_ref[0]
        rows = by_row(kind_ref[...])[:, :1]
        rows = jnp.where(core == 0, rows[:half], rows[half:])
        out_ref[...] = jnp.where(
            rows == core, a_ref[...].astype(F32), b_ref[...].astype(F32)
        ).astype(BF16)

    return call("join", kernel, here, [kind, kept, got], shaped(kept.shape))


def assemble(here, kind, near, near_other, far, far_other):
    length, width = near.shape
    steps = 4
    tile = length // steps
    half = length // 2
    args = [kind, near, near_other, far, far_other]

    def kernel(h_ref, kind_ref, a_ref, b_ref, c_ref, d_ref, out_ref, held, sems):
        at_place = Here(h_ref)
        core, first = at_place.core, at_place.column == 0
        copies = []
        kind = by_row(kind_ref[...])[:, :1]
        for i in range(steps):
            rows = slice(i * tile, (i + 1) * tile)
            keep = kind[rows] == core
            own = jnp.where(keep, a_ref[rows].astype(F32), b_ref[rows].astype(F32)).astype(BF16)
            part = slice(i * tile % half, i * tile % half + tile)
            other = jnp.where(core == i * tile // half, c_ref[part], d_ref[part])
            held[i, :, :width] = jnp.where(first, own, other)
            held[i, :, width:] = jnp.where(first, other, own)
            copies.append(pltpu.make_async_copy(held.at[i], out_ref.at[rows], sems.at[i]))
            copies[-1].start()
        for copy in copies:
            copy.wait()

    return pl.pallas_call(
        kernel,
        in_specs=[pl.BlockSpec(memory_space=SMEM)] + [pl.BlockSpec(memory_space=VMEM)] * 5,
        out_specs=pl.BlockSpec(memory_space=pl.ANY),
        out_shape=shaped((length, 2 * width)),
        scratch_shapes=[VMEM((steps, tile, 2 * width), BF16), pltpu.SemaphoreType.DMA((steps,))],
        compiler_params=pltpu.CompilerParams(vmem_limit_bytes=8 * 2**20),
    )(here, *[pltpu.with_memory_space_constraint(a, VMEM) for a in args])


def from_partner(x, axis, bit):
    return lax.ppermute(x, axis, [(i, i ^ 1 << bit) for i in range(lax.axis_size(axis))])


def gathered_plan(tokens, modality, norm_gains, qkv_weight, out_weight):
    tower_id = lax.axis_index("mod")
    own_rows = modality == tower_id
    gathered = lax.all_gather(tokens, "tensor", axis=1, tiled=True)
    length = gathered.shape[0]
    local_width = qkv_weight.shape[3]
    local_heads = local_width // HDIM
    gain_row = norm_gains[0]
    scale = HDIM ** (-0.5)
    wide_rows = gathered.astype(jnp.float32)
    inverse = lax.rsqrt(jnp.mean(wide_rows * wide_rows, axis=-1, keepdims=True) + 1e-05)
    row_block = (wide_rows * inverse * gain_row).astype(jnp.bfloat16)
    weight_piece = lax.all_gather(qkv_weight, "dp", axis=1, tiled=True)
    count = weight_piece.shape[1]
    columns = row_block
    projected = (
        jnp.dot(
            columns,
            weight_piece[0].reshape(count, 3 * local_width),
            preferred_element_type=jnp.float32,
        )
        .astype(jnp.bfloat16)
        .reshape(length, 3, local_heads, HDIM)
    )
    queries = projected[:, 0]
    own_pair = projected[:, 1:]
    other_pair = from_partner(own_pair, "mod", 0)
    key_pairs = jnp.where(own_rows[:, None, None, None], own_pair, other_pair)
    key_pos = jnp.arange(length, dtype=jnp.int32)
    scores = (
        jnp.einsum("qhd,khd->hqk", queries, key_pairs[:, 0], preferred_element_type=jnp.float32)
        * scale
    )
    allowed = key_pos[None, :] <= key_pos[:, None]
    scores = jnp.where(allowed[None], scores, -jnp.inf)
    soft_weights = jax.nn.softmax(scores, axis=-1).astype(jnp.bfloat16)
    attended = jnp.einsum(
        "hqk,khd->qhd", soft_weights, key_pairs[:, 1], preferred_element_type=jnp.float32
    )
    attended = attended.astype(jnp.bfloat16).reshape(queries.shape[0], local_width)
    all_heads = lax.all_gather(attended, "tensor", axis=1, tiled=True)
    weight_piece = lax.all_gather(out_weight, "dp", axis=1, tiled=True)
    columns = all_heads
    projected_out = jnp.dot(columns, weight_piece[0], preferred_element_type=jnp.float32).astype(
        jnp.bfloat16
    )
    placed = jnp.where(own_rows[:, None], projected_out, jnp.zeros_like(projected_out))
    combined = lax.psum(placed.astype(jnp.float32).astype(jnp.bfloat16), "mod")
    return combined


def solution(mesh):
    places, shards = mesh.shape["dp"], mesh.shape["tensor"]
    mods = mesh.shape["mod"]

    def move(array, where, *earlier):
        pairs = []
        for m in range(mods):
            for d in range(places):
                for x in range(shards):
                    to = where(m, d, x)
                    if to is not None:
                        target = (to[0] * places + to[1]) * shards + to[2]
                        pairs.append(((m * places + d) * shards + x, target))
        return lax.ppermute(after(array, *earlier) if earlier else array, AXES, pairs)

    def to_core(array, *earlier):
        return move(array, lambda m, d, x: (1 - m, d, x), *earlier)

    def over_tensor(array, *earlier):
        return [array] + [
            move(array, lambda m, d, x: (m, d, (x + step) % shards), *earlier)
            for step in range(1, shards)
        ]

    def edge(m, d, x):
        return m, d ^ 2, x

    def outward(m, d, x):
        return (m, d ^ 2, x) if d // 2 in (1, 2) else None

    def inward(m, d, x):
        return (m, d ^ 2, x) if d // 2 in (0, 3) else None

    def across(m, d, x):
        return (m, (3 - d // 2) * 2 + d % 2, x) if d // 2 in (1, 2) else None

    def across_or_stay(m, d, x):
        return across(m, d, x) or (m, d, x)

    def pair(m, d, x):
        return m, d ^ 1, x

    def line_plan(tokens, modality, norm_gains, qkv_weight, out_weight):
        here = jnp.stack([lax.axis_index(name).astype(I32) for name in AXES])
        length = tokens.shape[0]
        kept = qkv_weight.shape[1]
        half = length // 2
        gains = norm_gains[0].reshape(places, 1, kept)
        own_kind = modality[None, :]

        weight = after(qkv_weight[0].transpose(1, 0, 2), here, gains, own_kind)
        low_a, high_a, mine_a, away_a = halves(here, weight, 0, 2)
        m1a = move(low_a, across_or_stay)
        e1a = move(away_a, edge)
        p1a = move(mine_a, pair)

        begun = (m1a,)
        m2a = move(high_a, across, e1a, p1a, *begun)
        e2a = move(m1a, edge, e1a, p1a)
        p2a = move(e1a, pair, p1a, *begun)
        rows, top, bottom = own_rows_of(here, after(tokens, *begun), own_kind)
        fetched = over_tensor(rows)
        low_b, high_b, mine_b, away_b = halves(here, after(weight, *begun), 1, 2)

        begun = (m2a, mine_b)
        m3a = move(e2a, across, p2a, *begun)
        passed_top = move(top, edge, e2a, p2a, *begun)
        third_a = choose(here, after(e2a, *begun), m2a)
        p3a = move(third_a, pair, p2a)

        begun = (m3a,)
        swapped = [to_core(a, *begun) for a in fetched[1:]]
        shape = (2, places, length, kept)
        normed = normalize(
            here, "own", None, gains, after(tokens, *begun), fetched[1:], swapped, shape, 0, half
        )
        m4a = move(e1a, across, passed_top, p3a, *begun)
        m1b = move(low_b, across_or_stay, passed_top, p3a, *begun)
        passed_bottom = move(bottom, edge, passed_top, p3a, *begun)
        p1b = move(mine_b, pair, p3a, *begun)
        part_top = over_tensor(after(passed_top, *begun))
        low_o, high_o, mine_o, away_o = halves(here, after(out_weight, *begun), 0, 1)

        begun = (passed_bottom, normed, mine_o)
        e3a = move(m3a, outward, part_top[-1], *begun)
        i1o = move(low_o, inward, part_top[-1], *begun)
        p1o = move(mine_o, pair, p1b, *begun)
        other_kind = kinds_behind(here, after(passed_bottom, *begun), length)
        part_bottom = over_tensor(after(passed_bottom, *begun))
        top_swapped = [to_core(a, *begun) for a in part_top]
        first_a = [(0, mine_a, p1a), (1, e1a, p2a), (2, third_a, p3a)]
        total_a = project(here, "own", after(normed, *begun), first_a, fresh=True)
        normed = normalize(
            here, "partner", normed, gains, None, part_top, top_swapped, shape, 0, half // 2
        )

        begun = (m4a, m1b, normed, total_a, other_kind)
        m2b = move(high_b, across, *begun)
        e2b = move(m1b, edge, e3a, i1o, p1o, part_bottom[-1], *begun)
        fourth_a = choose(here, after(e3a, *begun), m4a)
        p4a = move(fourth_a, pair, p1o)
        bottom_swapped = [to_core(a, *begun) for a in part_bottom]
        normed = normalize(
            here, "partner", normed, gains, None, part_bottom, bottom_swapped, shape, half // 2, half // 2
        )
        total_a = project(here, "partner", normed, first_a, total_a, fresh=True)

        begun = (m2b, total_a)
        m3b = move(e2b, across, *begun)
        e1b = move(away_b, edge, e2b, p4a, *begun)
        third_b = choose(here, after(e2b, *begun), m2b)
        p3b = move(third_b, pair, p4a)
        last_a = [(3, fourth_a, p4a)]
        late_normed = after(normed, *begun)
        theirs_a = project(here, 1, late_normed, last_a, total_a, final=True)
        got_a = to_core(theirs_a)
        ours_a = project(here, 0, late_normed, last_a, total_a, final=True)

        begun = (m3b, theirs_a, ours_a)
        m4b = move(e1b, across, *begun)
        e3b = move(m3b, outward, e1b, p3b, *begun)
        i2o = move(high_o, inward, e1b, p3b, *begun)
        p2b = move(e1b, pair, p3b, *begun)
        attended_a = attend(here, own_kind, other_kind, after(ours_a, *begun), got_a)
        first_b = [(0, mine_b, p1b), (2, third_b, p3b)]
        late_normed = after(normed, *begun)
        total_b = project(here, "own", late_normed, first_b, fresh=True)
        total_b = project(here, "partner", late_normed, first_b, total_b, fresh=True)

        begun = (m4b, attended_a, total_b)
        m1o = move(low_o, across, *begun)
        m2o = move(high_o, across, *begun)
        fourth_b = choose(here, after(e3b, *begun), m4b)
        p4b = move(fourth_b, pair, p2b)
        packed_a = move(pack(here, after(low_o, *begun), attended_a), edge, e3b, i2o, p2b)
        held_a = over_tensor(after(attended_a, *begun))
        second_b = [(1, e1b, p2b)]
        late_normed = after(normed, *begun)
        total_b = project(here, "own", late_normed, second_b, total_b)
        total_b = project(here, "partner", late_normed, second_b, total_b)

        last_b = [(3, fourth_b, p4b)]
        theirs_b = project(here, 1, normed, last_b, total_b, final=True)
        got_b = to_core(theirs_b)
        ours_b = project(here, 0, normed, last_b, total_b, final=True)
        o1o, passed_a = unpack(here, after(packed_a, theirs_b), low_o, attended_a)
        second_o = choose(here, o1o, i2o)
        p2o = move(second_o, pair, p4b)
        held_a += over_tensor(passed_a)

        begun = (m1o, m2o, ours_b, second_o)
        m3o = move(i1o, across, held_a[1], *begun)
        o2o = move(m1o, outward, *begun)
        attended_b = attend(here, own_kind, other_kind, after(ours_b, *begun), got_b)

        passed_b = move(attended_b, edge, o2o, p2o, held_a[-1])
        begun = (m3o, passed_b)
        m4o = move(i2o, across, *begun)
        o3o = move(m3o, outward, *begun)
        held_b = over_tensor(after(attended_b, *begun)) + over_tensor(after(passed_b, *begun))
        third_o = choose(here, after(o2o, *begun), m2o)
        p3o = move(third_o, pair, p2o)
        pieces_a = stack(here, [after(held_a[0], *begun)] + held_a[1:])
        pieces_a = (pieces_a, to_core(pieces_a))
        both = ("partner", "own")
        blocks = [(0, mine_o, p1o), (1, second_o, p2o), (2, third_o, p3o)]
        total = combine(here, both, [pieces_a + (0, blocks[:2])])

        begun = (o3o, m4o, p3o, total)
        fourth_o = choose(here, after(o3o, *begun), m4o)
        p4o = move(fourth_o, pair)
        pieces_b = stack(here, [after(held_b[0], fourth_o)] + held_b[1:])
        pieces_b = (pieces_b, to_core(pieces_b))
        total = combine(here, both, [pieces_b + (1, blocks)], total)
        last = [(3, fourth_o, p4o)]
        rest = [pieces_a + (0, blocks[2:] + last), pieces_b + (1, last)]

        kept_away, sent_away = combine(here, ("partner",), rest, total, True, 0, True)
        sent_away = to_core(sent_away)
        near = combine(here, ("own",), rest, total, True, 1)
        far = move(join(here, other_kind, kept_away, sent_away), edge)
        return assemble(here, own_kind, near, to_core(near), far, to_core(far))

    return jax.shard_map(
        line_plan if places == 8 else gathered_plan,
        mesh=mesh,
        in_specs=(
            P("dp", "tensor"),
            P("dp"),
            P("mod", None),
            P("mod", "dp", None, "tensor"),
            P("mod", "dp", "tensor"),
        ),
        out_specs=P("dp", "tensor"),
        check_vma=False,
    )
```

```python
import jax
import jax.numpy as jnp
from jax import lax
from jax.experimental import pallas as pl
from jax.experimental.pallas import tpu as pltpu
from jax.sharding import PartitionSpec as P

HDIM = 128
AXES = ("mod", "dp", "tensor")
F32, BF16, I32 = jnp.float32, jnp.bfloat16, jnp.int32
VMEM, SMEM = pltpu.VMEM, pltpu.SMEM


def after(array, *earlier):
    return lax.optimization_barrier((array,) + earlier)[0]


class Here:
    def __init__(self, ref):
        self.core, place, self.own = ref[0], ref[1], ref[2]
        self.z, self.y = place >> 1, place & 1
        self.column = (self.z ^ (self.z >> 1)) & 1
        self.outer = self.column == 0
        self.which = self.core ^ (self.z & 1)
        self.at = [self.z, self.z ^ 1, jnp.where(self.z < 2, 2, 1), 3 - 3 * (self.z >> 1)]

    def slot(self, name):
        return {"own": self.which, "partner": 1 - self.which}.get(name, name)


def call(name, kernel, here, args, out_shape, aliases=None, scratch=8):
    return pl.pallas_call(
        kernel,
        in_specs=[pl.BlockSpec(memory_space=SMEM)] + [pl.BlockSpec(memory_space=VMEM)] * len(args),
        out_specs=jax.tree.map(lambda _: pl.BlockSpec(memory_space=VMEM), out_shape),
        out_shape=jax.tree.map(lambda shape: VMEM(shape.shape, shape.dtype), out_shape),
        input_output_aliases=aliases or {},
        compiler_params=pltpu.CompilerParams(vmem_limit_bytes=scratch * 2**20),
        name=name,
    )(here, *[pltpu.with_memory_space_constraint(a, VMEM) for a in args])


def shaped(shape, dtype=BF16):
    return jax.ShapeDtypeStruct(shape, dtype)


def by_row(kind):
    return jnp.broadcast_to(kind.astype(F32), (128, kind.shape[1])).T.astype(I32)


def halves(here, weight, chunk, chunks):
    kinds, depth, width = weight.shape
    half = width // 2
    part = half // chunks

    def kernel(h_ref, in_ref, low_ref, high_ref, mine_ref, away_ref):
        outer = Here(h_ref).outer
        for kind in range(kinds):
            low = in_ref[kind, :, chunk * part : (chunk + 1) * part]
            high = in_ref[kind, :, half + chunk * part : half + (chunk + 1) * part]
            low_ref[kind] = low
            high_ref[kind] = high
            mine_ref[kind] = jnp.where(outer, low, high)
            away_ref[kind] = jnp.where(outer, high, low)

    return call("halves", kernel, here, [weight], [shaped((kinds, depth, part))] * 4)


def own_rows_of(here, tokens, kind):
    length, features = tokens.shape
    half = length // 2
    extra = 16

    def kernel(h_ref, in_ref, kind_ref, rows_ref, top_ref, bottom_ref):
        rows = jnp.where(h_ref[0] == 0, in_ref[:half], in_ref[half:])
        rows_ref[...] = rows
        top_ref[...] = rows[: half // 2]
        bottom_ref[: half // 2] = rows[half // 2 :]
        bottom_ref[half // 2 :, :length] = jnp.broadcast_to(
            kind_ref[...].astype(F32), (extra, length)
        ).astype(BF16)
        bottom_ref[half // 2 :, length:] = jnp.zeros((extra, features - length), BF16)

    outs = [shaped((rows, features)) for rows in (half, half // 2, half // 2 + extra)]
    return call("own_rows_of", kernel, here, [tokens, kind], outs)


def kinds_behind(here, part, length):
    def kernel(_, in_ref, out_ref):
        out_ref[...] = in_ref[length // 4 :, :length].astype(F32)[:1].astype(I32)

    return call("kinds_behind", kernel, here, [part], shaped((1, length), I32))


def split(here, block):
    kinds, depth, width = block.shape
    half = width // 2

    def kernel(_, in_ref, low_ref, high_ref):
        low_ref[...] = in_ref[:, :, :half]
        high_ref[...] = in_ref[:, :, half:]

    return call("split", kernel, here, [block], [shaped((kinds, depth, half))] * 2)


def choose(here, from_edge, from_middle):
    def kernel(h_ref, a_ref, b_ref, out_ref):
        outer = Here(h_ref).outer

        @pl.when(outer)
        def _():
            out_ref[...] = a_ref[...]

        @pl.when(jnp.logical_not(outer))
        def _():
            out_ref[...] = b_ref[...]

    return call("choose", kernel, here, [from_edge, from_middle], shaped(from_edge.shape))


def stack(here, arrays):
    def kernel(_, *refs):
        for i in range(len(arrays)):
            refs[-1][i] = refs[i][...]

    return call("stack", kernel, here, arrays, shaped((len(arrays),) + arrays[0].shape))


def normalize(here, slot, held, gains, whole, mine, theirs, shape, start, count):
    _, _, length, kept = shape
    shards = len(mine) + (whole is not None)
    features = (whole if whole is not None else mine[0]).shape[1]
    tile = 32 if count % 32 == 0 else count
    half = length // 2
    per = features // kept
    args = ([] if held is None else [held]) + [gains] + ([] if whole is None else [whole])
    args += list(mine) + list(theirs)

    def kernel(h_ref, *refs):
        at_place = Here(h_ref)
        core, own, into = at_place.core, at_place.own, at_place.slot(slot)
        out_ref = refs[-1]
        refs = list(refs[0 if held is None else 1 : -1])
        gain_ref = refs.pop(0)
        whole_ref = None if whole is None else refs.pop(0)
        shard_of = [lax.rem(own - step + shards, shards) for step in range(shards)]

        def step(i, carry):
            for group, first in ((refs[: len(mine)], core), (refs[len(mine) :], 1 - core)):
                row = pl.multiple_of(first * half + start + i * tile, tile)
                at = pl.ds(pl.multiple_of(i * tile, tile), tile)
                found = [(ref, at) for ref in group]
                if whole_ref is not None:
                    found = [(whole_ref, pl.ds(row, tile))] + found
                total = jnp.zeros((tile, 1), F32)
                for ref, rows in found:
                    wide = ref[rows, :].astype(F32)
                    total = total + jnp.sum(wide * wide, axis=-1, keepdims=True)
                inverse = lax.rsqrt(total / (shards * features) + 1e-05)
                for shard, (ref, rows) in zip(shard_of, found):
                    for j in range(per):
                        block = shard * per + j
                        wide = ref[rows, j * kept : (j + 1) * kept].astype(F32)
                        out_ref[into, block, pl.ds(row, tile), :] = (
                            wide * inverse * gain_ref[block]
                        ).astype(BF16)
            return carry

        lax.fori_loop(0, count // tile, step, 0)

    return call("normalize", kernel, here, args, shaped(shape), None if held is None else {1: 0})


def project(here, slot, normed, blocks, total=None, final=False, fresh=False):
    slots, _, length, kept = normed.shape
    kinds, _, width = blocks[0][1].shape
    count = len(blocks)
    args = [normed] + [b for _, near, far in blocks for b in (near, far)]
    args += [] if total is None else [total]

    def kernel(h_ref, *refs):
        at_place = Here(h_ref)
        into = at_place.slot(slot)
        normed_ref, out_ref = refs[0], refs[-1]
        for kind in range(kinds):
            columns = slice(kind * width, (kind + 1) * width)
            summed = None if fresh else refs[1 + 2 * count][into, :, columns]
            for i, (arrival, _, _) in enumerate(blocks):
                for j, y in enumerate((at_place.y, 1 - at_place.y)):
                    part = jnp.dot(
                        normed_ref[into, at_place.at[arrival] * 2 + y],
                        refs[1 + 2 * i + j][kind],
                        preferred_element_type=F32,
                    )
                    summed = part if summed is None else summed + part
            if final:
                out_ref[:, columns] = summed.astype(BF16)
            else:
                out_ref[into, :, columns] = summed

    if final:
        return call("project", kernel, here, args, shaped((length, kinds * width)))
    aliases = None if total is None else {2 + 2 * count: 0}
    return call("project", kernel, here, args, shaped((slots, length, kinds * width), F32), aliases)


def attend(here, own_kind, other_kind, own, got):
    length, width = own.shape[0], own.shape[1] // 3
    heads = width // HDIM
    scale = HDIM ** (-0.5)
    tile = 128 if length % 128 == 0 else length

    def kernel(h_ref, own_kind_ref, other_kind_ref, own_ref, got_ref, out_ref):
        at_place = Here(h_ref)
        kind = jnp.where(at_place.which == 0, own_kind_ref[...], other_kind_ref[...])
        keep = by_row(kind) == at_place.core

        def pick(j):
            columns = slice(j * HDIM, (j + 1) * HDIM)
            return jnp.where(
                keep, own_ref[:, columns].astype(F32), got_ref[:, columns].astype(F32)
            ).astype(BF16)

        for h in range(heads):
            query, key, value = pick(h), pick(heads + h), pick(2 * heads + h)
            for i in range(length // tile):
                low, high = i * tile, (i + 1) * tile
                scores = lax.dot_general(
                    query[low:high], key[:high], (((1,), (1,)), ((), ())), preferred_element_type=F32
                )
                rows = low + lax.broadcasted_iota(I32, (tile, high), 0)
                cols = lax.broadcasted_iota(I32, (tile, high), 1)
                scores = jnp.where(cols <= rows, scores * scale, -jnp.inf)
                top = jnp.max(scores, axis=-1, keepdims=True)
                raised = jnp.exp(scores - top)
                share = 1.0 / jnp.sum(raised, axis=-1, keepdims=True)
                probs = (raised * share).astype(BF16)
                out = jnp.dot(probs, value[:high], preferred_element_type=F32)
                out_ref[low:high, h * HDIM : (h + 1) * HDIM] = out.astype(BF16)

    return call("attend", kernel, here, [own_kind, other_kind, own, got], shaped((length, width)))


def combine(here, slots, groups, total=None, final=False, offset=0, cut=False):
    held_pieces, length, held = groups[0][0].shape
    shards = held_pieces // 2
    features = groups[0][3][0][1].shape[2]
    tile = min(features, 256)
    half = length // 2
    terms = [group[:3] + (pair,) for group in groups for pair in group[3]]
    count = len(terms)
    args = [pieces for term in terms for pieces in term[:2]]
    args += [b for term in terms for b in term[3][1:]] + ([] if total is None else [total])

    def kernel(h_ref, *refs):
        at_place = Here(h_ref)
        outs = refs[-2:] if cut else refs[-1:]
        found = []
        for z in at_place.at:
            shard = lax.rem(at_place.own - (z >> 1) + shards, shards)
            found.append(jnp.where((z & 1) == at_place.column, 0, shards) + shard)
        for s, name in enumerate(slots):
            first_slot = at_place.slot(name) == 0
            rows = [
                jnp.where(
                    first_slot, refs[2 * i][found[arrival]], refs[2 * i + 1][found[arrival]]
                )
                for i, (_, _, _, (arrival, _, _)) in enumerate(terms)
            ]
            for n in range(features // tile):
                columns = slice(n * tile, (n + 1) * tile)
                summed = None if total is None else refs[4 * count][offset + s, :, columns]
                for i, (_, _, parity, _) in enumerate(terms):
                    near = refs[2 * count + 2 * i][0, :, columns]
                    far = refs[2 * count + 2 * i + 1][0, :, columns]
                    block = jnp.where(at_place.y == parity, near, far)
                    part = jnp.dot(rows[i], block, preferred_element_type=F32)
                    summed = part if summed is None else summed + part
                if not final:
                    outs[0][s, :, columns] = summed
                elif cut:
                    result = summed.astype(BF16)
                    first = at_place.core == 0
                    outs[0][:, columns] = jnp.where(first, result[:half], result[half:])
                    outs[1][:, columns] = jnp.where(first, result[half:], result[:half])
                else:
                    outs[0][:, columns] = summed.astype(BF16)

    if not final:
        out_shape = shaped((len(slots), length, features), F32)
    elif cut:
        out_shape = [shaped((half, features))] * 2
    else:
        out_shape = shaped((length, features))
    return call("combine", kernel, here, args, out_shape)


def join(here, kind, kept, got):
    half = kept.shape[0]

    def kernel(h_ref, kind_ref, a_ref, b_ref, out_ref):
        core = h_ref[0]
        rows = by_row(kind_ref[...])[:, :1]
        rows = jnp.where(core == 0, rows[:half], rows[half:])
        out_ref[...] = jnp.where(
            rows == core, a_ref[...].astype(F32), b_ref[...].astype(F32)
        ).astype(BF16)

    return call("join", kernel, here, [kind, kept, got], shaped(kept.shape))


def assemble(here, kind, near, near_other, far, far_other):
    length, width = near.shape
    steps = 4
    tile = length // steps
    half = length // 2
    args = [kind, near, near_other, far, far_other]

    def kernel(h_ref, kind_ref, a_ref, b_ref, c_ref, d_ref, out_ref, held, sems):
        at_place = Here(h_ref)
        core, first = at_place.core, at_place.column == 0
        copies = []
        kind = by_row(kind_ref[...])[:, :1]
        for i in range(steps):
            rows = slice(i * tile, (i + 1) * tile)
            keep = kind[rows] == core
            own = jnp.where(keep, a_ref[rows].astype(F32), b_ref[rows].astype(F32)).astype(BF16)
            part = slice(i * tile % half, i * tile % half + tile)
            other = jnp.where(core == i * tile // half, c_ref[part], d_ref[part])
            held[i, :, :width] = jnp.where(first, own, other)
            held[i, :, width:] = jnp.where(first, other, own)
            copies.append(pltpu.make_async_copy(held.at[i], out_ref.at[rows], sems.at[i]))
            copies[-1].start()
        for copy in copies:
            copy.wait()

    return pl.pallas_call(
        kernel,
        in_specs=[pl.BlockSpec(memory_space=SMEM)] + [pl.BlockSpec(memory_space=VMEM)] * 5,
        out_specs=pl.BlockSpec(memory_space=pl.ANY),
        out_shape=shaped((length, 2 * width)),
        scratch_shapes=[VMEM((steps, tile, 2 * width), BF16), pltpu.SemaphoreType.DMA((steps,))],
        compiler_params=pltpu.CompilerParams(vmem_limit_bytes=8 * 2**20),
    )(here, *[pltpu.with_memory_space_constraint(a, VMEM) for a in args])


def from_partner(x, axis, bit):
    return lax.ppermute(x, axis, [(i, i ^ 1 << bit) for i in range(lax.axis_size(axis))])


def gathered_plan(tokens, modality, norm_gains, qkv_weight, out_weight):
    tower_id = lax.axis_index("mod")
    own_rows = modality == tower_id
    gathered = lax.all_gather(tokens, "tensor", axis=1, tiled=True)
    length = gathered.shape[0]
    local_width = qkv_weight.shape[3]
    local_heads = local_width // HDIM
    gain_row = norm_gains[0]
    scale = HDIM ** (-0.5)
    wide_rows = gathered.astype(jnp.float32)
    inverse = lax.rsqrt(jnp.mean(wide_rows * wide_rows, axis=-1, keepdims=True) + 1e-05)
    row_block = (wide_rows * inverse * gain_row).astype(jnp.bfloat16)
    weight_piece = lax.all_gather(qkv_weight, "dp", axis=1, tiled=True)
    count = weight_piece.shape[1]
    columns = row_block
    projected = (
        jnp.dot(
            columns,
            weight_piece[0].reshape(count, 3 * local_width),
            preferred_element_type=jnp.float32,
        )
        .astype(jnp.bfloat16)
        .reshape(length, 3, local_heads, HDIM)
    )
    queries = projected[:, 0]
    own_pair = projected[:, 1:]
    other_pair = from_partner(own_pair, "mod", 0)
    key_pairs = jnp.where(own_rows[:, None, None, None], own_pair, other_pair)
    key_pos = jnp.arange(length, dtype=jnp.int32)
    scores = (
        jnp.einsum("qhd,khd->hqk", queries, key_pairs[:, 0], preferred_element_type=jnp.float32)
        * scale
    )
    allowed = key_pos[None, :] <= key_pos[:, None]
    scores = jnp.where(allowed[None], scores, -jnp.inf)
    soft_weights = jax.nn.softmax(scores, axis=-1).astype(jnp.bfloat16)
    attended = jnp.einsum(
        "hqk,khd->qhd", soft_weights, key_pairs[:, 1], preferred_element_type=jnp.float32
    )
    attended = attended.astype(jnp.bfloat16).reshape(queries.shape[0], local_width)
    all_heads = lax.all_gather(attended, "tensor", axis=1, tiled=True)
    weight_piece = lax.all_gather(out_weight, "dp", axis=1, tiled=True)
    columns = all_heads
    projected_out = jnp.dot(columns, weight_piece[0], preferred_element_type=jnp.float32).astype(
        jnp.bfloat16
    )
    placed = jnp.where(own_rows[:, None], projected_out, jnp.zeros_like(projected_out))
    combined = lax.psum(placed.astype(jnp.float32).astype(jnp.bfloat16), "mod")
    return combined


def solution(mesh):
    places, shards = mesh.shape["dp"], mesh.shape["tensor"]
    mods = mesh.shape["mod"]

    def move(array, where, *earlier):
        pairs = []
        for m in range(mods):
            for d in range(places):
                for x in range(shards):
                    to = where(m, d, x)
                    if to is not None:
                        target = (to[0] * places + to[1]) * shards + to[2]
                        pairs.append(((m * places + d) * shards + x, target))
        return lax.ppermute(after(array, *earlier) if earlier else array, AXES, pairs)

    def to_core(array, *earlier):
        return move(array, lambda m, d, x: (1 - m, d, x), *earlier)

    def over_tensor(array, *earlier):
        return [array] + [
            move(array, lambda m, d, x: (m, d, (x + step) % shards), *earlier)
            for step in range(1, shards)
        ]

    def edge(m, d, x):
        return m, d ^ 2, x

    def outward(m, d, x):
        return (m, d ^ 2, x) if d // 2 in (1, 2) else None

    def inward(m, d, x):
        return (m, d ^ 2, x) if d // 2 in (0, 3) else None

    def across(m, d, x):
        return (m, (3 - d // 2) * 2 + d % 2, x) if d // 2 in (1, 2) else None

    def across_or_stay(m, d, x):
        return across(m, d, x) or (m, d, x)

    def pair(m, d, x):
        return m, d ^ 1, x

    def line_plan(tokens, modality, norm_gains, qkv_weight, out_weight):
        here = jnp.stack([lax.axis_index(name).astype(I32) for name in AXES])
        length = tokens.shape[0]
        kept = qkv_weight.shape[1]
        half = length // 2
        gains = norm_gains[0].reshape(places, 1, kept)
        own_kind = modality[None, :]

        weight = after(qkv_weight[0].transpose(1, 0, 2), here, gains, own_kind)
        low_a, high_a, mine_a, away_a = halves(here, weight, 0, 2)
        m1a = move(low_a, across_or_stay)
        e1a = move(away_a, edge)
        p1a = move(mine_a, pair)

        begun = (m1a,)
        m2a = move(high_a, across, e1a, p1a, *begun)
        e2a = move(m1a, edge, e1a, p1a)
        p2a = move(e1a, pair, p1a, *begun)
        rows, top, bottom = own_rows_of(here, after(tokens, *begun), own_kind)
        fetched = over_tensor(rows)
        low_b, high_b, mine_b, away_b = halves(here, after(weight, *begun), 1, 2)

        begun = (m2a, mine_b)
        m3a = move(e2a, across, p2a, *begun)
        passed_top = move(top, edge, e2a, p2a, *begun)
        low_o, high_o, mine_o, away_o = halves(here, after(out_weight, *begun), 0, 1)
        third_a = choose(here, after(e2a, *begun), m2a)
        p3a = move(third_a, pair, p2a)

        begun = (m3a, mine_o)
        swapped = [to_core(a, *begun) for a in fetched[1:]]
        shape = (2, places, length, kept)
        normed = normalize(
            here, "own", None, gains, after(tokens, *begun), fetched[1:], swapped, shape, 0, half
        )
        m4a = move(e1a, across, passed_top, p3a, *begun)
        m1b = move(low_b, across_or_stay, passed_top, p3a, *begun)
        passed_bottom = move(bottom, edge, passed_top, p3a, *begun)
        o1o = move(low_o, outward, passed_top, p3a, *begun)
        p1b = move(mine_b, pair, p3a, *begun)
        part_top = over_tensor(after(passed_top, *begun))

        begun = (passed_bottom, o1o, normed)
        e3a = move(m3a, outward, part_top[-1], *begun)
        i1o = move(low_o, inward, part_top[-1], *begun)
        p1o = move(mine_o, pair, p1b, *begun)
        other_kind = kinds_behind(here, after(passed_bottom, *begun), length)
        part_bottom = over_tensor(after(passed_bottom, *begun))
        top_swapped = [to_core(a, *begun) for a in part_top]
        first_a = [(0, mine_a, p1a), (1, e1a, p2a), (2, third_a, p3a)]
        total_a = project(here, "own", after(normed, *begun), first_a, fresh=True)
        normed = normalize(
            here, "partner", normed, gains, None, part_top, top_swapped, shape, 0, half // 2
        )

        begun = (m4a, m1b, normed, total_a, other_kind)
        m2b = move(high_b, across, *begun)
        e2b = move(m1b, edge, e3a, i1o, p1o, part_bottom[-1], *begun)
        fourth_a = choose(here, after(e3a, *begun), m4a)
        p4a = move(fourth_a, pair, p1o)
        bottom_swapped = [to_core(a, *begun) for a in part_bottom]
        normed = normalize(
            here, "partner", normed, gains, None, part_bottom, bottom_swapped, shape, half // 2, half // 2
        )
        total_a = project(here, "partner", normed, first_a, total_a, fresh=True)

        begun = (m2b, total_a)
        m3b = move(e2b, across, *begun)
        e1b = move(away_b, edge, e2b, p4a, *begun)
        third_b = choose(here, after(e2b, *begun), m2b)
        p3b = move(third_b, pair, p4a)
        last_a = [(3, fourth_a, p4a)]
        late_normed = after(normed, *begun)
        theirs_a = project(here, 1, late_normed, last_a, total_a, final=True)
        got_a = to_core(theirs_a)
        ours_a = project(here, 0, late_normed, last_a, total_a, final=True)

        begun = (m3b, theirs_a, ours_a)
        m4b = move(e1b, across, *begun)
        e3b = move(m3b, outward, e1b, p3b, *begun)
        i2o = move(high_o, inward, e1b, p3b, *begun)
        p2b = move(e1b, pair, p3b, *begun)
        attended_a = attend(here, own_kind, other_kind, after(ours_a, *begun), got_a)
        first_b = [(0, mine_b, p1b), (2, third_b, p3b)]
        late_normed = after(normed, *begun)
        total_b = project(here, "own", late_normed, first_b, fresh=True)
        total_b = project(here, "partner", late_normed, first_b, total_b, fresh=True)

        begun = (m4b, attended_a, total_b)
        m12o = move(out_weight, across, i2o, *begun)
        fourth_b = choose(here, after(e3b, *begun), m4b)
        p4b = move(fourth_b, pair, p2b)
        passed_a = move(attended_a, edge, e3b, p2b, *begun)
        held_a = over_tensor(after(attended_a, *begun))
        second_o = choose(here, after(o1o, *begun), i2o)
        second_b = [(1, e1b, p2b)]
        late_normed = after(normed, *begun)
        total_b = project(here, "own", late_normed, second_b, total_b)
        total_b = project(here, "partner", late_normed, second_b, total_b)

        begun = (m12o, total_b, passed_a, held_a[1], second_o)
        m3o = move(i1o, across, *begun)
        m1o, m2o = split(here, after(m12o, *begun))
        o2o = move(m1o, outward)
        p2o = move(second_o, pair, p4b, *begun)
        held_a += over_tensor(after(passed_a, *begun))
        last_b = [(3, fourth_b, p4b)]
        late_normed = after(normed, *begun)
        theirs_b = project(here, 1, late_normed, last_b, total_b, final=True)
        got_b = to_core(theirs_b)
        ours_b = project(here, 0, late_normed, last_b, total_b, final=True)
        attended_b = attend(here, own_kind, other_kind, ours_b, got_b)

        passed_b = move(attended_b, edge, o2o, m3o, p2o)
        begun = (passed_b, held_a[-1])
        m4o = move(i2o, across, *begun)
        o3o = move(m3o, outward, *begun)
        third_o = choose(here, after(o2o, *begun), m2o)
        p3o = move(third_o, pair, p2o)
        held_b = over_tensor(after(attended_b, *begun)) + over_tensor(after(passed_b, *begun))
        pieces_a = stack(here, [after(held_a[0], *begun)] + held_a[1:])
        pieces_a = (pieces_a, to_core(pieces_a))
        both = ("partner", "own")
        blocks = [(0, mine_o, p1o), (1, second_o, p2o), (2, third_o, p3o)]
        total = combine(here, both, [pieces_a + (0, blocks[:2])])

        begun = (o3o, m4o, p3o, total)
        fourth_o = choose(here, after(o3o, *begun), m4o)
        p4o = move(fourth_o, pair)
        pieces_b = stack(here, [after(held_b[0], fourth_o)] + held_b[1:])
        pieces_b = (pieces_b, to_core(pieces_b))
        total = combine(here, both, [pieces_b + (1, blocks)], total)
        last = [(3, fourth_o, p4o)]
        rest = [pieces_a + (0, blocks[2:] + last), pieces_b + (1, last)]

        kept_away, sent_away = combine(here, ("partner",), rest, total, True, 0, True)
        sent_away = to_core(sent_away)
        near = combine(here, ("own",), rest, total, True, 1)
        far = move(join(here, other_kind, kept_away, sent_away), edge)
        return assemble(here, own_kind, near, to_core(near), far, to_core(far))

    return jax.shard_map(
        line_plan if places == 8 else gathered_plan,
        mesh=mesh,
        in_specs=(
            P("dp", "tensor"),
            P("dp"),
            P("mod", None),
            P("mod", "dp", None, "tensor"),
            P("mod", "dp", "tensor"),
        ),
        out_specs=P("dp", "tensor"),
        check_vma=False,
    )
```

```python
import jax
import jax.numpy as jnp
from jax import lax
from jax.experimental import pallas as pl
from jax.experimental.pallas import tpu as pltpu
from jax.sharding import PartitionSpec as P

HDIM = 128
AXES = ("mod", "dp", "tensor")
F32, BF16, I32 = jnp.float32, jnp.bfloat16, jnp.int32
VMEM, SMEM = pltpu.VMEM, pltpu.SMEM


def after(array, *earlier):
    return lax.optimization_barrier((array,) + earlier)[0]


class Here:
    def __init__(self, ref):
        self.core, place, self.own = ref[0], ref[1], ref[2]
        self.z, self.y = place >> 1, place & 1
        self.column = (self.z ^ (self.z >> 1)) & 1
        self.outer = self.column == 0
        self.which = self.core ^ (self.z & 1)
        self.at = [self.z, self.z ^ 1, jnp.where(self.z < 2, 2, 1), 3 - 3 * (self.z >> 1)]

    def slot(self, name):
        return {"own": self.which, "partner": 1 - self.which}.get(name, name)


def call(name, kernel, here, args, out_shape, aliases=None, scratch=8):
    return pl.pallas_call(
        kernel,
        in_specs=[pl.BlockSpec(memory_space=SMEM)] + [pl.BlockSpec(memory_space=VMEM)] * len(args),
        out_specs=jax.tree.map(lambda _: pl.BlockSpec(memory_space=VMEM), out_shape),
        out_shape=jax.tree.map(lambda shape: VMEM(shape.shape, shape.dtype), out_shape),
        input_output_aliases=aliases or {},
        compiler_params=pltpu.CompilerParams(vmem_limit_bytes=scratch * 2**20),
        name=name,
    )(here, *[pltpu.with_memory_space_constraint(a, VMEM) for a in args])


def shaped(shape, dtype=BF16):
    return jax.ShapeDtypeStruct(shape, dtype)


def by_row(kind):
    return jnp.broadcast_to(kind.astype(F32), (128, kind.shape[1])).T.astype(I32)


def halves(here, weight, chunk, chunks):
    kinds, depth, width = weight.shape
    half = width // 2
    part = half // chunks

    def kernel(h_ref, in_ref, low_ref, high_ref, mine_ref, away_ref):
        outer = Here(h_ref).outer
        for kind in range(kinds):
            low = in_ref[kind, :, chunk * part : (chunk + 1) * part]
            high = in_ref[kind, :, half + chunk * part : half + (chunk + 1) * part]
            low_ref[kind] = low
            high_ref[kind] = high
            mine_ref[kind] = jnp.where(outer, low, high)
            away_ref[kind] = jnp.where(outer, high, low)

    return call("halves", kernel, here, [weight], [shaped((kinds, depth, part))] * 4)


def own_rows_of(here, tokens, kind):
    length, features = tokens.shape
    half = length // 2
    extra = 16

    def kernel(h_ref, in_ref, kind_ref, rows_ref, top_ref, bottom_ref):
        rows = jnp.where(h_ref[0] == 0, in_ref[:half], in_ref[half:])
        rows_ref[...] = rows
        top_ref[...] = rows[: half // 2]
        bottom_ref[: half // 2] = rows[half // 2 :]
        bottom_ref[half // 2 :, :length] = jnp.broadcast_to(
            kind_ref[...].astype(F32), (extra, length)
        ).astype(BF16)
        bottom_ref[half // 2 :, length:] = jnp.zeros((extra, features - length), BF16)

    outs = [shaped((rows, features)) for rows in (half, half // 2, half // 2 + extra)]
    return call("own_rows_of", kernel, here, [tokens, kind], outs)


def kinds_behind(here, part, length):
    def kernel(_, in_ref, out_ref):
        out_ref[...] = in_ref[length // 4 :, :length].astype(F32)[:1].astype(I32)

    return call("kinds_behind", kernel, here, [part], shaped((1, length), I32))


def split(here, block):
    kinds, depth, width = block.shape
    half = width // 2

    def kernel(_, in_ref, low_ref, high_ref):
        low_ref[...] = in_ref[:, :, :half]
        high_ref[...] = in_ref[:, :, half:]

    return call("split", kernel, here, [block], [shaped((kinds, depth, half))] * 2)


def choose(here, from_edge, from_middle):
    def kernel(h_ref, a_ref, b_ref, out_ref):
        outer = Here(h_ref).outer

        @pl.when(outer)
        def _():
            out_ref[...] = a_ref[...]

        @pl.when(jnp.logical_not(outer))
        def _():
            out_ref[...] = b_ref[...]

    return call("choose", kernel, here, [from_edge, from_middle], shaped(from_edge.shape))


def stack(here, arrays):
    def kernel(_, *refs):
        for i in range(len(arrays)):
            refs[-1][i] = refs[i][...]

    return call("stack", kernel, here, arrays, shaped((len(arrays),) + arrays[0].shape))


def normalize(here, slot, held, gains, whole, mine, theirs, shape, start, count):
    _, _, length, kept = shape
    shards = len(mine) + (whole is not None)
    features = (whole if whole is not None else mine[0]).shape[1]
    tile = 32 if count % 32 == 0 else count
    half = length // 2
    per = features // kept
    args = ([] if held is None else [held]) + [gains] + ([] if whole is None else [whole])
    args += list(mine) + list(theirs)

    def kernel(h_ref, *refs):
        at_place = Here(h_ref)
        core, own, into = at_place.core, at_place.own, at_place.slot(slot)
        out_ref = refs[-1]
        refs = list(refs[0 if held is None else 1 : -1])
        gain_ref = refs.pop(0)
        whole_ref = None if whole is None else refs.pop(0)
        shard_of = [lax.rem(own - step + shards, shards) for step in range(shards)]

        def step(i, carry):
            for group, first in ((refs[: len(mine)], core), (refs[len(mine) :], 1 - core)):
                row = pl.multiple_of(first * half + start + i * tile, tile)
                at = pl.ds(pl.multiple_of(i * tile, tile), tile)
                found = [(ref, at) for ref in group]
                if whole_ref is not None:
                    found = [(whole_ref, pl.ds(row, tile))] + found
                total = jnp.zeros((tile, 1), F32)
                for ref, rows in found:
                    wide = ref[rows, :].astype(F32)
                    total = total + jnp.sum(wide * wide, axis=-1, keepdims=True)
                inverse = lax.rsqrt(total / (shards * features) + 1e-05)
                for shard, (ref, rows) in zip(shard_of, found):
                    for j in range(per):
                        block = shard * per + j
                        wide = ref[rows, j * kept : (j + 1) * kept].astype(F32)
                        out_ref[into, block, pl.ds(row, tile), :] = (
                            wide * inverse * gain_ref[block]
                        ).astype(BF16)
            return carry

        lax.fori_loop(0, count // tile, step, 0)

    return call("normalize", kernel, here, args, shaped(shape), None if held is None else {1: 0})


def project(here, slot, normed, blocks, total=None, final=False, fresh=False):
    slots, _, length, kept = normed.shape
    kinds, _, width = blocks[0][1].shape
    count = len(blocks)
    args = [normed] + [b for _, near, far in blocks for b in (near, far)]
    args += [] if total is None else [total]

    def kernel(h_ref, *refs):
        at_place = Here(h_ref)
        into = at_place.slot(slot)
        normed_ref, out_ref = refs[0], refs[-1]
        for kind in range(kinds):
            columns = slice(kind * width, (kind + 1) * width)
            summed = None if fresh else refs[1 + 2 * count][into, :, columns]
            for i, (arrival, _, _) in enumerate(blocks):
                for j, y in enumerate((at_place.y, 1 - at_place.y)):
                    part = jnp.dot(
                        normed_ref[into, at_place.at[arrival] * 2 + y],
                        refs[1 + 2 * i + j][kind],
                        preferred_element_type=F32,
                    )
                    summed = part if summed is None else summed + part
            if final:
                out_ref[:, columns] = summed.astype(BF16)
            else:
                out_ref[into, :, columns] = summed

    if final:
        return call("project", kernel, here, args, shaped((length, kinds * width)))
    aliases = None if total is None else {2 + 2 * count: 0}
    return call("project", kernel, here, args, shaped((slots, length, kinds * width), F32), aliases)


def attend(here, own_kind, other_kind, own, got):
    length, width = own.shape[0], own.shape[1] // 3
    heads = width // HDIM
    scale = HDIM ** (-0.5)
    tile = 128 if length % 128 == 0 else length

    def kernel(h_ref, own_kind_ref, other_kind_ref, own_ref, got_ref, out_ref):
        at_place = Here(h_ref)
        kind = jnp.where(at_place.which == 0, own_kind_ref[...], other_kind_ref[...])
        keep = by_row(kind) == at_place.core

        def pick(j):
            columns = slice(j * HDIM, (j + 1) * HDIM)
            return jnp.where(
                keep, own_ref[:, columns].astype(F32), got_ref[:, columns].astype(F32)
            ).astype(BF16)

        for h in range(heads):
            query, key, value = pick(h), pick(heads + h), pick(2 * heads + h)
            for i in range(length // tile):
                low, high = i * tile, (i + 1) * tile
                scores = lax.dot_general(
                    query[low:high], key[:high], (((1,), (1,)), ((), ())), preferred_element_type=F32
                )
                rows = low + lax.broadcasted_iota(I32, (tile, high), 0)
                cols = lax.broadcasted_iota(I32, (tile, high), 1)
                scores = jnp.where(cols <= rows, scores * scale, -jnp.inf)
                top = jnp.max(scores, axis=-1, keepdims=True)
                raised = jnp.exp(scores - top)
                share = 1.0 / jnp.sum(raised, axis=-1, keepdims=True)
                probs = (raised * share).astype(BF16)
                out = jnp.dot(probs, value[:high], preferred_element_type=F32)
                out_ref[low:high, h * HDIM : (h + 1) * HDIM] = out.astype(BF16)

    return call("attend", kernel, here, [own_kind, other_kind, own, got], shaped((length, width)))


def combine(here, slots, groups, total=None, final=False, offset=0, cut=False):
    held_pieces, length, held = groups[0][0].shape
    shards = held_pieces // 2
    features = groups[0][3][0][1].shape[2]
    tile = min(features, 256)
    half = length // 2
    terms = [group[:3] + (pair,) for group in groups for pair in group[3]]
    count = len(terms)
    args = [pieces for term in terms for pieces in term[:2]]
    args += [b for term in terms for b in term[3][1:]] + ([] if total is None else [total])

    def kernel(h_ref, *refs):
        at_place = Here(h_ref)
        outs = refs[-2:] if cut else refs[-1:]
        found = []
        for z in at_place.at:
            shard = lax.rem(at_place.own - (z >> 1) + shards, shards)
            found.append(jnp.where((z & 1) == at_place.column, 0, shards) + shard)
        for s, name in enumerate(slots):
            first_slot = at_place.slot(name) == 0
            rows = [
                jnp.where(
                    first_slot, refs[2 * i][found[arrival]], refs[2 * i + 1][found[arrival]]
                )
                for i, (_, _, _, (arrival, _, _)) in enumerate(terms)
            ]
            for n in range(features // tile):
                columns = slice(n * tile, (n + 1) * tile)
                summed = None if total is None else refs[4 * count][offset + s, :, columns]
                for i, (_, _, parity, _) in enumerate(terms):
                    near = refs[2 * count + 2 * i][0, :, columns]
                    far = refs[2 * count + 2 * i + 1][0, :, columns]
                    block = jnp.where(at_place.y == parity, near, far)
                    part = jnp.dot(rows[i], block, preferred_element_type=F32)
                    summed = part if summed is None else summed + part
                if not final:
                    outs[0][s, :, columns] = summed
                elif cut:
                    result = summed.astype(BF16)
                    first = at_place.core == 0
                    outs[0][:, columns] = jnp.where(first, result[:half], result[half:])
                    outs[1][:, columns] = jnp.where(first, result[half:], result[:half])
                else:
                    outs[0][:, columns] = summed.astype(BF16)

    if not final:
        out_shape = shaped((len(slots), length, features), F32)
    elif cut:
        out_shape = [shaped((half, features))] * 2
    else:
        out_shape = shaped((length, features))
    return call("combine", kernel, here, args, out_shape)


def join(here, kind, kept, got):
    half = kept.shape[0]

    def kernel(h_ref, kind_ref, a_ref, b_ref, out_ref):
        core = h_ref[0]
        rows = by_row(kind_ref[...])[:, :1]
        rows = jnp.where(core == 0, rows[:half], rows[half:])
        out_ref[...] = jnp.where(
            rows == core, a_ref[...].astype(F32), b_ref[...].astype(F32)
        ).astype(BF16)

    return call("join", kernel, here, [kind, kept, got], shaped(kept.shape))


def assemble(here, kind, near, near_other, far, far_other):
    length, width = near.shape
    steps = 4
    tile = length // steps
    half = length // 2
    args = [kind, near, near_other, far, far_other]

    def kernel(h_ref, kind_ref, a_ref, b_ref, c_ref, d_ref, out_ref, held, sems):
        at_place = Here(h_ref)
        core, first = at_place.core, at_place.column == 0
        copies = []
        kind = by_row(kind_ref[...])[:, :1]
        for i in range(steps):
            rows = slice(i * tile, (i + 1) * tile)
            keep = kind[rows] == core
            own = jnp.where(keep, a_ref[rows].astype(F32), b_ref[rows].astype(F32)).astype(BF16)
            part = slice(i * tile % half, i * tile % half + tile)
            other = jnp.where(core == i * tile // half, c_ref[part], d_ref[part])
            held[i, :, :width] = jnp.where(first, own, other)
            held[i, :, width:] = jnp.where(first, other, own)
            copies.append(pltpu.make_async_copy(held.at[i], out_ref.at[rows], sems.at[i]))
            copies[-1].start()
        for copy in copies:
            copy.wait()

    return pl.pallas_call(
        kernel,
        in_specs=[pl.BlockSpec(memory_space=SMEM)] + [pl.BlockSpec(memory_space=VMEM)] * 5,
        out_specs=pl.BlockSpec(memory_space=pl.ANY),
        out_shape=shaped((length, 2 * width)),
        scratch_shapes=[VMEM((steps, tile, 2 * width), BF16), pltpu.SemaphoreType.DMA((steps,))],
        compiler_params=pltpu.CompilerParams(vmem_limit_bytes=8 * 2**20),
    )(here, *[pltpu.with_memory_space_constraint(a, VMEM) for a in args])


def from_partner(x, axis, bit):
    return lax.ppermute(x, axis, [(i, i ^ 1 << bit) for i in range(lax.axis_size(axis))])


def gathered_plan(tokens, modality, norm_gains, qkv_weight, out_weight):
    tower_id = lax.axis_index("mod")
    own_rows = modality == tower_id
    gathered = lax.all_gather(tokens, "tensor", axis=1, tiled=True)
    length = gathered.shape[0]
    local_width = qkv_weight.shape[3]
    local_heads = local_width // HDIM
    gain_row = norm_gains[0]
    scale = HDIM ** (-0.5)
    wide_rows = gathered.astype(jnp.float32)
    inverse = lax.rsqrt(jnp.mean(wide_rows * wide_rows, axis=-1, keepdims=True) + 1e-05)
    row_block = (wide_rows * inverse * gain_row).astype(jnp.bfloat16)
    weight_piece = lax.all_gather(qkv_weight, "dp", axis=1, tiled=True)
    count = weight_piece.shape[1]
    columns = row_block
    projected = (
        jnp.dot(
            columns,
            weight_piece[0].reshape(count, 3 * local_width),
            preferred_element_type=jnp.float32,
        )
        .astype(jnp.bfloat16)
        .reshape(length, 3, local_heads, HDIM)
    )
    queries = projected[:, 0]
    own_pair = projected[:, 1:]
    other_pair = from_partner(own_pair, "mod", 0)
    key_pairs = jnp.where(own_rows[:, None, None, None], own_pair, other_pair)
    key_pos = jnp.arange(length, dtype=jnp.int32)
    scores = (
        jnp.einsum("qhd,khd->hqk", queries, key_pairs[:, 0], preferred_element_type=jnp.float32)
        * scale
    )
    allowed = key_pos[None, :] <= key_pos[:, None]
    scores = jnp.where(allowed[None], scores, -jnp.inf)
    soft_weights = jax.nn.softmax(scores, axis=-1).astype(jnp.bfloat16)
    attended = jnp.einsum(
        "hqk,khd->qhd", soft_weights, key_pairs[:, 1], preferred_element_type=jnp.float32
    )
    attended = attended.astype(jnp.bfloat16).reshape(queries.shape[0], local_width)
    all_heads = lax.all_gather(attended, "tensor", axis=1, tiled=True)
    weight_piece = lax.all_gather(out_weight, "dp", axis=1, tiled=True)
    columns = all_heads
    projected_out = jnp.dot(columns, weight_piece[0], preferred_element_type=jnp.float32).astype(
        jnp.bfloat16
    )
    placed = jnp.where(own_rows[:, None], projected_out, jnp.zeros_like(projected_out))
    combined = lax.psum(placed.astype(jnp.float32).astype(jnp.bfloat16), "mod")
    return combined


def solution(mesh):
    places, shards = mesh.shape["dp"], mesh.shape["tensor"]
    mods = mesh.shape["mod"]

    def move(array, where, *earlier):
        pairs = []
        for m in range(mods):
            for d in range(places):
                for x in range(shards):
                    to = where(m, d, x)
                    if to is not None:
                        target = (to[0] * places + to[1]) * shards + to[2]
                        pairs.append(((m * places + d) * shards + x, target))
        return lax.ppermute(after(array, *earlier) if earlier else array, AXES, pairs)

    def to_core(array, *earlier):
        return move(array, lambda m, d, x: (1 - m, d, x), *earlier)

    def over_tensor(array, *earlier):
        return [array] + [
            move(array, lambda m, d, x: (m, d, (x + step) % shards), *earlier)
            for step in range(1, shards)
        ]

    def edge(m, d, x):
        return m, d ^ 2, x

    def outward(m, d, x):
        return (m, d ^ 2, x) if d // 2 in (1, 2) else None

    def inward(m, d, x):
        return (m, d ^ 2, x) if d // 2 in (0, 3) else None

    def across(m, d, x):
        return (m, (3 - d // 2) * 2 + d % 2, x) if d // 2 in (1, 2) else None

    def across_or_stay(m, d, x):
        return across(m, d, x) or (m, d, x)

    def pair(m, d, x):
        return m, d ^ 1, x

    def line_plan(tokens, modality, norm_gains, qkv_weight, out_weight):
        here = jnp.stack([lax.axis_index(name).astype(I32) for name in AXES])
        length = tokens.shape[0]
        kept = qkv_weight.shape[1]
        half = length // 2
        gains = norm_gains[0].reshape(places, 1, kept)
        own_kind = modality[None, :]

        weight = after(qkv_weight[0].transpose(1, 0, 2), here, gains, own_kind)
        low_a, high_a, mine_a, away_a = halves(here, weight, 0, 2)
        m1a = move(low_a, across_or_stay)
        e1a = move(away_a, edge)
        p1a = move(mine_a, pair)

        begun = (m1a,)
        m2a = move(high_a, across, e1a, p1a, *begun)
        e2a = move(m1a, edge, e1a, p1a)
        p2a = move(e1a, pair, p1a, *begun)
        rows, top, bottom = own_rows_of(here, after(tokens, *begun), own_kind)
        fetched = over_tensor(rows)
        low_b, high_b, mine_b, away_b = halves(here, after(weight, *begun), 1, 2)
        low_o, high_o, mine_o, away_o = halves(here, after(out_weight, *begun), 0, 1)

        begun = (m2a, mine_b, mine_o)
        m3a = move(e2a, across, p2a, *begun)
        passed_top = move(top, edge, e2a, p2a, *begun)
        o1o = move(low_o, outward, e2a, p2a, *begun)
        third_a = choose(here, after(e2a, *begun), m2a)
        p3a = move(third_a, pair, p2a)

        begun = (m3a,)
        swapped = [to_core(a, passed_top, p3a, *begun) for a in fetched[1:]]
        shape = (2, places, length, kept)
        normed = normalize(
            here, "own", None, gains, after(tokens, *begun), fetched[1:], swapped, shape, 0, half
        )
        m4a = move(e1a, across, passed_top, p3a, *begun)
        m1b = move(low_b, across_or_stay, passed_top, p3a, *begun)
        passed_bottom = move(bottom, edge, passed_top, p3a, *begun)
        p1b = move(mine_b, pair, p3a, *begun)
        part_top = over_tensor(after(passed_top, *begun))

        begun = (passed_bottom, normed)
        e3a = move(m3a, outward, part_top[-1], o1o, *begun)
        i1o = move(low_o, inward, part_top[-1], *begun)
        p1o = move(mine_o, pair, p1b, *begun)
        other_kind = kinds_behind(here, after(passed_bottom, *begun), length)
        part_bottom = over_tensor(after(passed_bottom, *begun))
        top_swapped = [to_core(a, *begun) for a in part_top]
        first_a = [(0, mine_a, p1a), (1, e1a, p2a), (2, third_a, p3a)]
        total_a = project(here, "own", after(normed, *begun), first_a, fresh=True)
        normed = normalize(
            here, "partner", normed, gains, None, part_top, top_swapped, shape, 0, half // 2
        )

        begun = (m4a, m1b, normed, total_a, other_kind)
        m2b = move(high_b, across, *begun)
        e2b = move(m1b, edge, e3a, i1o, p1o, part_bottom[-1], *begun)
        fourth_a = choose(here, after(e3a, *begun), m4a)
        p4a = move(fourth_a, pair, p1o)
        bottom_swapped = [to_core(a, *begun) for a in part_bottom]
        normed = normalize(
            here, "partner", normed, gains, None, part_bottom, bottom_swapped, shape, half // 2, half // 2
        )
        total_a = project(here, "partner", normed, first_a, total_a, fresh=True)

        begun = (m2b, total_a)
        m3b = move(e2b, across, *begun)
        e1b = move(away_b, edge, e2b, p4a, *begun)
        third_b = choose(here, after(e2b, *begun), m2b)
        p3b = move(third_b, pair, p4a)
        last_a = [(3, fourth_a, p4a)]
        late_normed = after(normed, *begun)
        theirs_a = project(here, 1, late_normed, last_a, total_a, final=True)
        got_a = to_core(theirs_a)
        ours_a = project(here, 0, late_normed, last_a, total_a, final=True)

        begun = (m3b, theirs_a, ours_a)
        m4b = move(e1b, across, *begun)
        e3b = move(m3b, outward, e1b, p3b, *begun)
        i2o = move(high_o, inward, e1b, p3b, *begun)
        p2b = move(e1b, pair, p3b, *begun)
        attended_a = attend(here, own_kind, other_kind, after(ours_a, *begun), got_a)
        first_b = [(0, mine_b, p1b), (2, third_b, p3b)]
        late_normed = after(normed, *begun)
        total_b = project(here, "own", late_normed, first_b, fresh=True)
        total_b = project(here, "partner", late_normed, first_b, total_b, fresh=True)

        begun = (m4b, attended_a, total_b)
        m12o = move(out_weight, across, i2o, *begun)
        fourth_b = choose(here, after(e3b, *begun), m4b)
        p4b = move(fourth_b, pair, p2b)
        passed_a = move(attended_a, edge, e3b, p2b, *begun)
        held_a = over_tensor(after(attended_a, *begun))
        second_o = choose(here, after(o1o, *begun), i2o)
        second_b = [(1, e1b, p2b)]
        late_normed = after(normed, *begun)
        total_b = project(here, "own", late_normed, second_b, total_b)
        total_b = project(here, "partner", late_normed, second_b, total_b)

        begun = (m12o, total_b, passed_a, held_a[1], second_o)
        m3o = move(i1o, across, *begun)
        m1o, m2o = split(here, after(m12o, *begun))
        o2o = move(m1o, outward)
        p2o = move(second_o, pair, p4b, *begun)
        held_a += over_tensor(after(passed_a, *begun))
        last_b = [(3, fourth_b, p4b)]
        late_normed = after(normed, *begun)
        theirs_b = project(here, 1, late_normed, last_b, total_b, final=True)
        got_b = to_core(theirs_b)
        ours_b = project(here, 0, late_normed, last_b, total_b, final=True)
        attended_b = attend(here, own_kind, other_kind, ours_b, got_b)

        begun = (m3o, o2o, p2o, attended_b, held_a[-1])
        passed_b = move(attended_b, edge, *begun)
        held_b = over_tensor(after(attended_b, *begun))
        m4o = move(i2o, across, held_b[1], *begun)
        o3o = move(m3o, outward, *begun)
        third_o = choose(here, after(o2o, *begun), m2o)
        p3o = move(third_o, pair, p2o)
        held_b += over_tensor(after(passed_b, *begun))
        pieces_a = stack(here, [after(held_a[0], *begun)] + held_a[1:])
        pieces_a = (pieces_a, to_core(pieces_a))
        both = ("partner", "own")
        blocks = [(0, mine_o, p1o), (1, second_o, p2o), (2, third_o, p3o)]
        total = combine(here, both, [pieces_a + (0, blocks[:2])])

        begun = (o3o, m4o, p3o, total)
        fourth_o = choose(here, after(o3o, *begun), m4o)
        p4o = move(fourth_o, pair)
        pieces_b = stack(here, [after(held_b[0], fourth_o)] + held_b[1:])
        pieces_b = (pieces_b, to_core(pieces_b))
        total = combine(here, both, [pieces_b + (1, blocks)], total)
        last = [(3, fourth_o, p4o)]
        rest = [pieces_a + (0, blocks[2:] + last), pieces_b + (1, last)]

        kept_away, sent_away = combine(here, ("partner",), rest, total, True, 0, True)
        sent_away = to_core(sent_away)
        near = combine(here, ("own",), rest, total, True, 1)
        far = move(join(here, other_kind, kept_away, sent_away), edge)
        return assemble(here, own_kind, near, to_core(near), far, to_core(far))

    return jax.shard_map(
        line_plan if places == 8 else gathered_plan,
        mesh=mesh,
        in_specs=(
            P("dp", "tensor"),
            P("dp"),
            P("mod", None),
            P("mod", "dp", None, "tensor"),
            P("mod", "dp", "tensor"),
        ),
        out_specs=P("dp", "tensor"),
        check_vma=False,
    )
```

```python
import jax
import jax.numpy as jnp
from jax import lax
from jax.experimental import pallas as pl
from jax.experimental.pallas import tpu as pltpu
from jax.sharding import PartitionSpec as P

HDIM = 128
AXES = ("mod", "dp", "tensor")
F32, BF16, I32 = jnp.float32, jnp.bfloat16, jnp.int32
VMEM, SMEM = pltpu.VMEM, pltpu.SMEM


def after(array, *earlier):
    return lax.optimization_barrier((array,) + earlier)[0]


class Here:
    def __init__(self, ref):
        self.core, place, self.own = ref[0], ref[1], ref[2]
        self.z, self.y = place >> 1, place & 1
        self.column = (self.z ^ (self.z >> 1)) & 1
        self.outer = self.column == 0
        self.which = self.core ^ (self.z & 1)
        self.at = [self.z, self.z ^ 1, jnp.where(self.z < 2, 2, 1), 3 - 3 * (self.z >> 1)]

    def slot(self, name):
        return {"own": self.which, "partner": 1 - self.which}.get(name, name)


def call(name, kernel, here, args, out_shape, aliases=None, scratch=8):
    return pl.pallas_call(
        kernel,
        in_specs=[pl.BlockSpec(memory_space=SMEM)] + [pl.BlockSpec(memory_space=VMEM)] * len(args),
        out_specs=jax.tree.map(lambda _: pl.BlockSpec(memory_space=VMEM), out_shape),
        out_shape=jax.tree.map(lambda shape: VMEM(shape.shape, shape.dtype), out_shape),
        input_output_aliases=aliases or {},
        compiler_params=pltpu.CompilerParams(vmem_limit_bytes=scratch * 2**20),
        name=name,
    )(here, *[pltpu.with_memory_space_constraint(a, VMEM) for a in args])


def shaped(shape, dtype=BF16):
    return jax.ShapeDtypeStruct(shape, dtype)


def by_row(kind):
    return jnp.broadcast_to(kind.astype(F32), (128, kind.shape[1])).T.astype(I32)


def halves(here, weight, chunk, chunks):
    kinds, depth, width = weight.shape
    half = width // 2
    part = half // chunks

    def kernel(h_ref, in_ref, low_ref, high_ref, mine_ref, away_ref):
        outer = Here(h_ref).outer
        for kind in range(kinds):
            low = in_ref[kind, :, chunk * part : (chunk + 1) * part]
            high = in_ref[kind, :, half + chunk * part : half + (chunk + 1) * part]
            low_ref[kind] = low
            high_ref[kind] = high
            mine_ref[kind] = jnp.where(outer, low, high)
            away_ref[kind] = jnp.where(outer, high, low)

    return call("halves", kernel, here, [weight], [shaped((kinds, depth, part))] * 4)


def own_rows_of(here, tokens, kind):
    length, features = tokens.shape
    half = length // 2
    extra = 16

    def kernel(h_ref, in_ref, kind_ref, rows_ref, top_ref, bottom_ref):
        rows = jnp.where(h_ref[0] == 0, in_ref[:half], in_ref[half:])
        rows_ref[...] = rows
        top_ref[...] = rows[: half // 2]
        bottom_ref[: half // 2] = rows[half // 2 :]
        bottom_ref[half // 2 :, :length] = jnp.broadcast_to(
            kind_ref[...].astype(F32), (extra, length)
        ).astype(BF16)
        bottom_ref[half // 2 :, length:] = jnp.zeros((extra, features - length), BF16)

    outs = [shaped((rows, features)) for rows in (half, half // 2, half // 2 + extra)]
    return call("own_rows_of", kernel, here, [tokens, kind], outs)


def kinds_behind(here, part, length):
    def kernel(_, in_ref, out_ref):
        out_ref[...] = in_ref[length // 4 :, :length].astype(F32)[:1].astype(I32)

    return call("kinds_behind", kernel, here, [part], shaped((1, length), I32))


def choose(here, from_edge, from_middle):
    def kernel(h_ref, a_ref, b_ref, out_ref):
        outer = Here(h_ref).outer

        @pl.when(outer)
        def _():
            out_ref[...] = a_ref[...]

        @pl.when(jnp.logical_not(outer))
        def _():
            out_ref[...] = b_ref[...]

    return call("choose", kernel, here, [from_edge, from_middle], shaped(from_edge.shape))


def stack(here, arrays):
    def kernel(_, *refs):
        for i in range(len(arrays)):
            refs[-1][i] = refs[i][...]

    return call("stack", kernel, here, arrays, shaped((len(arrays),) + arrays[0].shape))


def pack(here, block, piece):
    _, depth, features = block.shape
    length, width = piece.shape
    cuts = features // width

    def kernel(_, block_ref, piece_ref, out_ref):
        for i in range(cuts):
            out_ref[i * depth : (i + 1) * depth] = block_ref[0, :, i * width : (i + 1) * width]
        out_ref[cuts * depth :] = piece_ref[...]

    return call("pack", kernel, here, [block, piece], shaped((cuts * depth + length, width)))


def unpack(here, packed, block, piece):
    _, depth, features = block.shape
    _, width = piece.shape
    cuts = features // width

    def kernel(_, in_ref, block_ref, piece_ref):
        for i in range(cuts):
            block_ref[0, :, i * width : (i + 1) * width] = in_ref[i * depth : (i + 1) * depth]
        piece_ref[...] = in_ref[cuts * depth :]

    return call("unpack", kernel, here, [packed], [shaped(block.shape), shaped(piece.shape)])


def normalize(here, slot, held, gains, whole, mine, theirs, shape, start, count):
    _, _, length, kept = shape
    shards = len(mine) + (whole is not None)
    features = (whole if whole is not None else mine[0]).shape[1]
    tile = 32 if count % 32 == 0 else count
    half = length // 2
    per = features // kept
    args = ([] if held is None else [held]) + [gains] + ([] if whole is None else [whole])
    args += list(mine) + list(theirs)

    def kernel(h_ref, *refs):
        at_place = Here(h_ref)
        core, own, into = at_place.core, at_place.own, at_place.slot(slot)
        out_ref = refs[-1]
        refs = list(refs[0 if held is None else 1 : -1])
        gain_ref = refs.pop(0)
        whole_ref = None if whole is None else refs.pop(0)
        shard_of = [lax.rem(own - step + shards, shards) for step in range(shards)]

        def step(i, carry):
            for group, first in ((refs[: len(mine)], core), (refs[len(mine) :], 1 - core)):
                row = pl.multiple_of(first * half + start + i * tile, tile)
                at = pl.ds(pl.multiple_of(i * tile, tile), tile)
                found = [(ref, at) for ref in group]
                if whole_ref is not None:
                    found = [(whole_ref, pl.ds(row, tile))] + found
                total = jnp.zeros((tile, 1), F32)
                for ref, rows in found:
                    wide = ref[rows, :].astype(F32)
                    total = total + jnp.sum(wide * wide, axis=-1, keepdims=True)
                inverse = lax.rsqrt(total / (shards * features) + 1e-05)
                for shard, (ref, rows) in zip(shard_of, found):
                    for j in range(per):
                        block = shard * per + j
                        wide = ref[rows, j * kept : (j + 1) * kept].astype(F32)
                        out_ref[into, block, pl.ds(row, tile), :] = (
                            wide * inverse * gain_ref[block]
                        ).astype(BF16)
            return carry

        lax.fori_loop(0, count // tile, step, 0)

    return call("normalize", kernel, here, args, shaped(shape), None if held is None else {1: 0})


def project(here, slot, normed, blocks, total=None, final=False, fresh=False):
    slots, _, length, kept = normed.shape
    kinds, _, width = blocks[0][1].shape
    count = len(blocks)
    args = [normed] + [b for _, near, far in blocks for b in (near, far)]
    args += [] if total is None else [total]

    def kernel(h_ref, *refs):
        at_place = Here(h_ref)
        into = at_place.slot(slot)
        normed_ref, out_ref = refs[0], refs[-1]
        for kind in range(kinds):
            columns = slice(kind * width, (kind + 1) * width)
            summed = None if fresh else refs[1 + 2 * count][into, :, columns]
            for i, (arrival, _, _) in enumerate(blocks):
                for j, y in enumerate((at_place.y, 1 - at_place.y)):
                    part = jnp.dot(
                        normed_ref[into, at_place.at[arrival] * 2 + y],
                        refs[1 + 2 * i + j][kind],
                        preferred_element_type=F32,
                    )
                    summed = part if summed is None else summed + part
            if final:
                out_ref[:, columns] = summed.astype(BF16)
            else:
                out_ref[into, :, columns] = summed

    if final:
        return call("project", kernel, here, args, shaped((length, kinds * width)))
    aliases = None if total is None else {2 + 2 * count: 0}
    return call("project", kernel, here, args, shaped((slots, length, kinds * width), F32), aliases)


def attend(here, own_kind, other_kind, own, got):
    length, width = own.shape[0], own.shape[1] // 3
    heads = width // HDIM
    scale = HDIM ** (-0.5)
    tile = 128 if length % 128 == 0 else length

    def kernel(h_ref, own_kind_ref, other_kind_ref, own_ref, got_ref, out_ref):
        at_place = Here(h_ref)
        kind = jnp.where(at_place.which == 0, own_kind_ref[...], other_kind_ref[...])
        keep = by_row(kind) == at_place.core

        def pick(j):
            columns = slice(j * HDIM, (j + 1) * HDIM)
            return jnp.where(
                keep, own_ref[:, columns].astype(F32), got_ref[:, columns].astype(F32)
            ).astype(BF16)

        for h in range(heads):
            query, key, value = pick(h), pick(heads + h), pick(2 * heads + h)
            for i in range(length // tile):
                low, high = i * tile, (i + 1) * tile
                scores = lax.dot_general(
                    query[low:high], key[:high], (((1,), (1,)), ((), ())), preferred_element_type=F32
                )
                rows = low + lax.broadcasted_iota(I32, (tile, high), 0)
                cols = lax.broadcasted_iota(I32, (tile, high), 1)
                scores = jnp.where(cols <= rows, scores * scale, -jnp.inf)
                top = jnp.max(scores, axis=-1, keepdims=True)
                raised = jnp.exp(scores - top)
                share = 1.0 / jnp.sum(raised, axis=-1, keepdims=True)
                probs = (raised * share).astype(BF16)
                out = jnp.dot(probs, value[:high], preferred_element_type=F32)
                out_ref[low:high, h * HDIM : (h + 1) * HDIM] = out.astype(BF16)

    return call("attend", kernel, here, [own_kind, other_kind, own, got], shaped((length, width)))


def combine(here, slots, groups, total=None, final=False, offset=0, cut=False):
    held_pieces, length, held = groups[0][0].shape
    shards = held_pieces // 2
    features = groups[0][3][0][1].shape[-1]
    tile = min(features, 256)
    half = length // 2
    terms = [group[:3] + (pair,) for group in groups for pair in group[3]]
    count = len(terms)
    args = [pieces for term in terms for pieces in term[:2]]
    args += [b for term in terms for b in term[3][1:3]] + ([] if total is None else [total])

    def kernel(h_ref, *refs):
        at_place = Here(h_ref)
        outs = refs[-2:] if cut else refs[-1:]
        found = []
        for z in at_place.at:
            shard = lax.rem(at_place.own - (z >> 1) + shards, shards)
            found.append(jnp.where((z & 1) == at_place.column, 0, shards) + shard)
        for s, name in enumerate(slots):
            first_slot = at_place.slot(name) == 0
            rows = [
                jnp.where(
                    first_slot, refs[2 * i][found[arrival]], refs[2 * i + 1][found[arrival]]
                )
                for i, (_, _, _, (arrival, *_)) in enumerate(terms)
            ]
            for n in range(features // tile):
                columns = slice(n * tile, (n + 1) * tile)
                summed = None if total is None else refs[4 * count][offset + s, :, columns]
                for i, (_, _, parity, (_, _, _, *index)) in enumerate(terms):
                    near = refs[2 * count + 2 * i][(*index, 0, slice(None), columns)]
                    far = refs[2 * count + 2 * i + 1][(*index, 0, slice(None), columns)]
                    block = jnp.where(at_place.y == parity, near, far)
                    part = jnp.dot(rows[i], block, preferred_element_type=F32)
                    summed = part if summed is None else summed + part
                if not final:
                    outs[0][s, :, columns] = summed
                elif cut:
                    result = summed.astype(BF16)
                    first = at_place.core == 0
                    outs[0][:, columns] = jnp.where(first, result[:half], result[half:])
                    outs[1][:, columns] = jnp.where(first, result[half:], result[:half])
                else:
                    outs[0][:, columns] = summed.astype(BF16)

    if not final:
        out_shape = shaped((len(slots), length, features), F32)
    elif cut:
        out_shape = [shaped((half, features))] * 2
    else:
        out_shape = shaped((length, features))
    return call("combine", kernel, here, args, out_shape)


def join(here, kind, kept, got):
    half = kept.shape[0]

    def kernel(h_ref, kind_ref, a_ref, b_ref, out_ref):
        core = h_ref[0]
        rows = by_row(kind_ref[...])[:, :1]
        rows = jnp.where(core == 0, rows[:half], rows[half:])
        out_ref[...] = jnp.where(
            rows == core, a_ref[...].astype(F32), b_ref[...].astype(F32)
        ).astype(BF16)

    return call("join", kernel, here, [kind, kept, got], shaped(kept.shape))


def assemble(here, kind, near, near_other, far, far_other):
    length, width = near.shape
    steps = 4
    tile = length // steps
    half = length // 2
    args = [kind, near, near_other, far, far_other]

    def kernel(h_ref, kind_ref, a_ref, b_ref, c_ref, d_ref, out_ref, held, sems):
        at_place = Here(h_ref)
        core, first = at_place.core, at_place.column == 0
        copies = []
        kind = by_row(kind_ref[...])[:, :1]
        for i in range(steps):
            rows = slice(i * tile, (i + 1) * tile)
            keep = kind[rows] == core
            own = jnp.where(keep, a_ref[rows].astype(F32), b_ref[rows].astype(F32)).astype(BF16)
            part = slice(i * tile % half, i * tile % half + tile)
            other = jnp.where(core == i * tile // half, c_ref[part], d_ref[part])
            held[i, :, :width] = jnp.where(first, own, other)
            held[i, :, width:] = jnp.where(first, other, own)
            copies.append(pltpu.make_async_copy(held.at[i], out_ref.at[rows], sems.at[i]))
            copies[-1].start()
        for copy in copies:
            copy.wait()

    return pl.pallas_call(
        kernel,
        in_specs=[pl.BlockSpec(memory_space=SMEM)] + [pl.BlockSpec(memory_space=VMEM)] * 5,
        out_specs=pl.BlockSpec(memory_space=pl.ANY),
        out_shape=shaped((length, 2 * width)),
        scratch_shapes=[VMEM((steps, tile, 2 * width), BF16), pltpu.SemaphoreType.DMA((steps,))],
        compiler_params=pltpu.CompilerParams(vmem_limit_bytes=8 * 2**20),
    )(here, *[pltpu.with_memory_space_constraint(a, VMEM) for a in args])


def from_partner(x, axis, bit):
    return lax.ppermute(x, axis, [(i, i ^ 1 << bit) for i in range(lax.axis_size(axis))])


def gathered_plan(tokens, modality, norm_gains, qkv_weight, out_weight):
    tower_id = lax.axis_index("mod")
    own_rows = modality == tower_id
    gathered = lax.all_gather(tokens, "tensor", axis=1, tiled=True)
    length = gathered.shape[0]
    local_width = qkv_weight.shape[3]
    local_heads = local_width // HDIM
    gain_row = norm_gains[0]
    scale = HDIM ** (-0.5)
    wide_rows = gathered.astype(jnp.float32)
    inverse = lax.rsqrt(jnp.mean(wide_rows * wide_rows, axis=-1, keepdims=True) + 1e-05)
    row_block = (wide_rows * inverse * gain_row).astype(jnp.bfloat16)
    weight_piece = lax.all_gather(qkv_weight, "dp", axis=1, tiled=True)
    count = weight_piece.shape[1]
    columns = row_block
    projected = (
        jnp.dot(
            columns,
            weight_piece[0].reshape(count, 3 * local_width),
            preferred_element_type=jnp.float32,
        )
        .astype(jnp.bfloat16)
        .reshape(length, 3, local_heads, HDIM)
    )
    queries = projected[:, 0]
    own_pair = projected[:, 1:]
    other_pair = from_partner(own_pair, "mod", 0)
    key_pairs = jnp.where(own_rows[:, None, None, None], own_pair, other_pair)
    key_pos = jnp.arange(length, dtype=jnp.int32)
    scores = (
        jnp.einsum("qhd,khd->hqk", queries, key_pairs[:, 0], preferred_element_type=jnp.float32)
        * scale
    )
    allowed = key_pos[None, :] <= key_pos[:, None]
    scores = jnp.where(allowed[None], scores, -jnp.inf)
    soft_weights = jax.nn.softmax(scores, axis=-1).astype(jnp.bfloat16)
    attended = jnp.einsum(
        "hqk,khd->qhd", soft_weights, key_pairs[:, 1], preferred_element_type=jnp.float32
    )
    attended = attended.astype(jnp.bfloat16).reshape(queries.shape[0], local_width)
    all_heads = lax.all_gather(attended, "tensor", axis=1, tiled=True)
    weight_piece = lax.all_gather(out_weight, "dp", axis=1, tiled=True)
    columns = all_heads
    projected_out = jnp.dot(columns, weight_piece[0], preferred_element_type=jnp.float32).astype(
        jnp.bfloat16
    )
    placed = jnp.where(own_rows[:, None], projected_out, jnp.zeros_like(projected_out))
    combined = lax.psum(placed.astype(jnp.float32).astype(jnp.bfloat16), "mod")
    return combined


def solution(mesh):
    places, shards = mesh.shape["dp"], mesh.shape["tensor"]
    mods = mesh.shape["mod"]

    def move(array, where, *earlier):
        pairs = []
        for m in range(mods):
            for d in range(places):
                for x in range(shards):
                    to = where(m, d, x)
                    if to is not None:
                        target = (to[0] * places + to[1]) * shards + to[2]
                        pairs.append(((m * places + d) * shards + x, target))
        return lax.ppermute(after(array, *earlier) if earlier else array, AXES, pairs)

    def to_core(array, *earlier):
        return move(array, lambda m, d, x: (1 - m, d, x), *earlier)

    def over_tensor(array, *earlier):
        return [array] + [
            move(array, lambda m, d, x: (m, d, (x + step) % shards), *earlier)
            for step in range(1, shards)
        ]

    def edge(m, d, x):
        return m, d ^ 2, x

    def outward(m, d, x):
        return (m, d ^ 2, x) if d // 2 in (1, 2) else None

    def inward(m, d, x):
        return (m, d ^ 2, x) if d // 2 in (0, 3) else None

    def across(m, d, x):
        return (m, (3 - d // 2) * 2 + d % 2, x) if d // 2 in (1, 2) else None

    def across_or_stay(m, d, x):
        return across(m, d, x) or (m, d, x)

    def pair(m, d, x):
        return m, d ^ 1, x

    def line_plan(tokens, modality, norm_gains, qkv_weight, out_weight):
        here = jnp.stack([lax.axis_index(name).astype(I32) for name in AXES])
        length = tokens.shape[0]
        kept = qkv_weight.shape[1]
        half = length // 2
        gains = norm_gains[0].reshape(places, 1, kept)
        own_kind = modality[None, :]

        weight = after(qkv_weight[0].transpose(1, 0, 2), here, gains, own_kind)
        low_a, high_a, mine_a, away_a = halves(here, weight, 0, 2)
        m1a = move(low_a, across_or_stay)
        e1a = move(away_a, edge)
        p1a = move(mine_a, pair)

        begun = (m1a,)
        m2a = move(high_a, across, e1a, p1a, *begun)
        e2a = move(m1a, edge, e1a, p1a)
        p2a = move(e1a, pair, p1a, *begun)
        rows, top, bottom = own_rows_of(here, after(tokens, *begun), own_kind)
        fetched = over_tensor(rows)
        low_b, high_b, mine_b, away_b = halves(here, after(weight, *begun), 1, 2)

        begun = (m2a, mine_b)
        m3a = move(e2a, across, p2a, *begun)
        passed_top = move(top, edge, e2a, p2a, *begun)
        third_a = choose(here, after(e2a, *begun), m2a)
        p3a = move(third_a, pair, p2a)

        begun = (m3a,)
        swapped = [to_core(a, *begun) for a in fetched[1:]]
        shape = (2, places, length, kept)
        normed = normalize(
            here, "own", None, gains, after(tokens, *begun), fetched[1:], swapped, shape, 0, half
        )
        m4a = move(e1a, across, passed_top, p3a, *begun)
        m1b = move(low_b, across_or_stay, passed_top, p3a, *begun)
        passed_bottom = move(bottom, edge, passed_top, p3a, *begun)
        p1b = move(mine_b, pair, p3a, *begun)
        part_top = over_tensor(after(passed_top, *begun))
        low_o, high_o, mine_o, away_o = halves(here, after(out_weight, *begun), 0, 1)

        begun = (passed_bottom, normed, mine_o)
        e3a = move(m3a, outward, part_top[-1], *begun)
        i1o = move(low_o, inward, part_top[-1], *begun)
        p1o = move(mine_o, pair, p1b, *begun)
        other_kind = kinds_behind(here, after(passed_bottom, *begun), length)
        part_bottom = over_tensor(after(passed_bottom, *begun))
        top_swapped = [to_core(a, *begun) for a in part_top]
        first_a = [(0, mine_a, p1a), (1, e1a, p2a), (2, third_a, p3a)]
        total_a = project(here, "own", after(normed, *begun), first_a, fresh=True)
        normed = normalize(
            here, "partner", normed, gains, None, part_top, top_swapped, shape, 0, half // 2
        )

        begun = (m4a, m1b, normed, total_a, other_kind)
        m2b = move(high_b, across, *begun)
        e2b = move(m1b, edge, e3a, i1o, p1o, part_bottom[-1], *begun)
        fourth_a = choose(here, after(e3a, *begun), m4a)
        p4a = move(fourth_a, pair, p1o)
        bottom_swapped = [to_core(a, *begun) for a in part_bottom]
        normed = normalize(
            here, "partner", normed, gains, None, part_bottom, bottom_swapped, shape, half // 2, half // 2
        )
        total_a = project(here, "partner", normed, first_a, total_a, fresh=True)

        begun = (m2b, total_a)
        m3b = move(e2b, across, *begun)
        e1b = move(away_b, edge, e2b, p4a, *begun)
        third_b = choose(here, after(e2b, *begun), m2b)
        p3b = move(third_b, pair, p4a)
        last_a = [(3, fourth_a, p4a)]
        late_normed = after(normed, *begun)
        theirs_a = project(here, 1, late_normed, last_a, total_a, final=True)
        got_a = to_core(theirs_a)
        ours_a = project(here, 0, late_normed, last_a, total_a, final=True)

        begun = (m3b, theirs_a, ours_a)
        m4b = move(e1b, across, *begun)
        e3b = move(m3b, outward, e1b, p3b, *begun)
        i2o = move(high_o, inward, e1b, p3b, *begun)
        p2b = move(e1b, pair, p3b, *begun)
        attended_a = attend(here, own_kind, other_kind, after(ours_a, *begun), got_a)
        first_b = [(0, mine_b, p1b), (2, third_b, p3b)]
        late_normed = after(normed, *begun)
        total_b = project(here, "own", late_normed, first_b, fresh=True)
        total_b = project(here, "partner", late_normed, first_b, total_b, fresh=True)
        lows = stack(here, [after(low_o, *begun), i1o])

        begun = (m4b, attended_a, total_b, lows)
        m13o = move(lows, across, i2o, *begun)
        fourth_b = choose(here, after(e3b, *begun), m4b)
        p4b = move(fourth_b, pair, p2b)
        packed_a = move(pack(here, after(low_o, *begun), attended_a), edge, e3b, p2b)
        held_a = over_tensor(after(attended_a, *begun))
        highs = stack(here, [after(high_o, *begun), i2o])
        second_b = [(1, e1b, p2b)]
        late_normed = after(normed, *begun)
        total_b = project(here, "own", late_normed, second_b, total_b)
        total_b = project(here, "partner", late_normed, second_b, total_b)

        begun = (m13o, total_b, packed_a, held_a[1], highs)
        m24o = move(highs, across, *begun)
        o23o = move(m13o, outward, *begun)
        last_b = [(3, fourth_b, p4b)]
        late_normed = after(normed, *begun)
        theirs_b = project(here, 1, late_normed, last_b, total_b, final=True)
        got_b = to_core(theirs_b)
        ours_b = project(here, 0, late_normed, last_b, total_b, final=True)
        o1o, passed_a = unpack(here, after(packed_a, ours_b), low_o, attended_a)
        second_o = choose(here, o1o, i2o)
        p2o = move(second_o, pair, p4b)
        held_a += over_tensor(passed_a)
        attended_b = attend(here, own_kind, other_kind, ours_b, got_b)
        held_b = over_tensor(attended_b)

        begun = (m24o, o23o, held_b[1], held_a[-1], p2o)
        late_o = choose(here, after(o23o, *begun), m24o)
        p34o = move(late_o, pair)
        passed_b = move(attended_b, edge, o23o)
        held_b += over_tensor(after(passed_b, late_o))
        pieces_a = stack(here, [after(held_a[0], late_o)] + held_a[1:])
        pieces_a = (pieces_a, to_core(pieces_a))
        both = ("partner", "own")
        near = [(0, mine_o, p1o), (1, second_o, p2o)]
        last = [(2, late_o, p34o, 0), (3, late_o, p34o, 1)]
        total = combine(here, both, [pieces_a + (0, near)])
        pieces_b = stack(here, [after(held_b[0], total, p34o)] + held_b[1:])
        pieces_b = (pieces_b, to_core(pieces_b))
        rest = [pieces_a + (0, last), pieces_b + (1, near + last)]

        kept_away, sent_away = combine(here, ("partner",), rest, total, True, 0, True)
        sent_away = to_core(sent_away)
        near = combine(here, ("own",), rest, total, True, 1)
        far = move(join(here, other_kind, kept_away, sent_away), edge)
        return assemble(here, own_kind, near, to_core(near), far, to_core(far))

    return jax.shard_map(
        line_plan if places == 8 else gathered_plan,
        mesh=mesh,
        in_specs=(
            P("dp", "tensor"),
            P("dp"),
            P("mod", None),
            P("mod", "dp", None, "tensor"),
            P("mod", "dp", "tensor"),
        ),
        out_specs=P("dp", "tensor"),
        check_vma=False,
    )
```

```python
import jax
import jax.numpy as jnp
from jax import lax
from jax.experimental import pallas as pl
from jax.experimental.pallas import tpu as pltpu
from jax.sharding import PartitionSpec as P

HDIM = 128
AXES = ("mod", "dp", "tensor")
F32, BF16, I32 = jnp.float32, jnp.bfloat16, jnp.int32
VMEM, SMEM = pltpu.VMEM, pltpu.SMEM


def after(array, *earlier):
    return lax.optimization_barrier((array,) + earlier)[0]


class Here:
    def __init__(self, ref):
        self.core, place, self.own = ref[0], ref[1], ref[2]
        self.z, self.y = place >> 1, place & 1
        self.column = (self.z ^ (self.z >> 1)) & 1
        self.outer = self.column == 0
        self.which = self.core ^ (self.z & 1)
        self.at = [self.z, self.z ^ 1, jnp.where(self.z < 2, 2, 1), 3 - 3 * (self.z >> 1)]

    def slot(self, name):
        return {"own": self.which, "partner": 1 - self.which}.get(name, name)


def call(name, kernel, here, args, out_shape, aliases=None, scratch=8):
    return pl.pallas_call(
        kernel,
        in_specs=[pl.BlockSpec(memory_space=SMEM)] + [pl.BlockSpec(memory_space=VMEM)] * len(args),
        out_specs=jax.tree.map(lambda _: pl.BlockSpec(memory_space=VMEM), out_shape),
        out_shape=jax.tree.map(lambda shape: VMEM(shape.shape, shape.dtype), out_shape),
        input_output_aliases=aliases or {},
        compiler_params=pltpu.CompilerParams(vmem_limit_bytes=scratch * 2**20),
        name=name,
    )(here, *[pltpu.with_memory_space_constraint(a, VMEM) for a in args])


def shaped(shape, dtype=BF16):
    return jax.ShapeDtypeStruct(shape, dtype)


def by_row(kind):
    return jnp.broadcast_to(kind.astype(F32), (128, kind.shape[1])).T.astype(I32)


def halves(here, weight, chunk, chunks):
    kinds, depth, width = weight.shape
    half = width // 2
    part = half // chunks

    def kernel(h_ref, in_ref, low_ref, high_ref, mine_ref, away_ref):
        outer = Here(h_ref).outer
        for kind in range(kinds):
            low = in_ref[kind, :, chunk * part : (chunk + 1) * part]
            high = in_ref[kind, :, half + chunk * part : half + (chunk + 1) * part]
            low_ref[kind] = low
            high_ref[kind] = high
            mine_ref[kind] = jnp.where(outer, low, high)
            away_ref[kind] = jnp.where(outer, high, low)

    return call("halves", kernel, here, [weight], [shaped((kinds, depth, part))] * 4)


def own_rows_of(here, tokens, kind):
    length, features = tokens.shape
    half = length // 2
    extra = 16

    def kernel(h_ref, in_ref, kind_ref, rows_ref, top_ref, bottom_ref):
        rows = jnp.where(h_ref[0] == 0, in_ref[:half], in_ref[half:])
        rows_ref[...] = rows
        top_ref[...] = rows[: half // 2]
        bottom_ref[: half // 2] = rows[half // 2 :]
        bottom_ref[half // 2 :, :length] = jnp.broadcast_to(
            kind_ref[...].astype(F32), (extra, length)
        ).astype(BF16)
        bottom_ref[half // 2 :, length:] = jnp.zeros((extra, features - length), BF16)

    outs = [shaped((rows, features)) for rows in (half, half // 2, half // 2 + extra)]
    return call("own_rows_of", kernel, here, [tokens, kind], outs)


def kinds_behind(here, part, length):
    def kernel(_, in_ref, out_ref):
        out_ref[...] = in_ref[length // 4 :, :length].astype(F32)[:1].astype(I32)

    return call("kinds_behind", kernel, here, [part], shaped((1, length), I32))


def choose(here, from_edge, from_middle):
    def kernel(h_ref, a_ref, b_ref, out_ref):
        outer = Here(h_ref).outer

        @pl.when(outer)
        def _():
            out_ref[...] = a_ref[...]

        @pl.when(jnp.logical_not(outer))
        def _():
            out_ref[...] = b_ref[...]

    return call("choose", kernel, here, [from_edge, from_middle], shaped(from_edge.shape))


def choose_halves(here, from_edge, from_middle):
    shape = from_edge.shape
    half = shape[-1] // 2

    def kernel(h_ref, a_ref, b_ref, low_ref, high_ref):
        outer = Here(h_ref).outer
        for ref, wanted in ((a_ref, outer), (b_ref, jnp.logical_not(outer))):

            @pl.when(wanted)
            def _(ref=ref):
                for i in range(shape[0]):
                    low_ref[i] = ref[i, :, :, :half]
                    high_ref[i] = ref[i, :, :, half:]

    outs = [shaped(shape[:-1] + (half,))] * 2
    return call("choose_halves", kernel, here, [from_edge, from_middle], outs)


def stack(here, arrays):
    def kernel(_, *refs):
        for i in range(len(arrays)):
            refs[-1][i] = refs[i][...]

    return call("stack", kernel, here, arrays, shaped((len(arrays),) + arrays[0].shape))


def pack(here, block, piece):
    _, depth, features = block.shape
    length, width = piece.shape
    cuts = features // width

    def kernel(_, block_ref, piece_ref, out_ref):
        for i in range(cuts):
            out_ref[i * depth : (i + 1) * depth] = block_ref[0, :, i * width : (i + 1) * width]
        out_ref[cuts * depth :] = piece_ref[...]

    return call("pack", kernel, here, [block, piece], shaped((cuts * depth + length, width)))


def unpack(here, packed, block, piece):
    _, depth, features = block.shape
    _, width = piece.shape
    cuts = features // width

    def kernel(_, in_ref, block_ref, piece_ref):
        for i in range(cuts):
            block_ref[0, :, i * width : (i + 1) * width] = in_ref[i * depth : (i + 1) * depth]
        piece_ref[...] = in_ref[cuts * depth :]

    return call("unpack", kernel, here, [packed], [shaped(block.shape), shaped(piece.shape)])


def normalize(here, slot, held, gains, whole, mine, theirs, shape, start, count):
    _, _, length, kept = shape
    shards = len(mine) + (whole is not None)
    features = (whole if whole is not None else mine[0]).shape[1]
    tile = 32 if count % 32 == 0 else count
    half = length // 2
    per = features // kept
    args = ([] if held is None else [held]) + [gains] + ([] if whole is None else [whole])
    args += list(mine) + list(theirs)

    def kernel(h_ref, *refs):
        at_place = Here(h_ref)
        core, own, into = at_place.core, at_place.own, at_place.slot(slot)
        out_ref = refs[-1]
        refs = list(refs[0 if held is None else 1 : -1])
        gain_ref = refs.pop(0)
        whole_ref = None if whole is None else refs.pop(0)
        shard_of = [lax.rem(own - step + shards, shards) for step in range(shards)]

        def step(i, carry):
            for group, first in ((refs[: len(mine)], core), (refs[len(mine) :], 1 - core)):
                row = pl.multiple_of(first * half + start + i * tile, tile)
                at = pl.ds(pl.multiple_of(i * tile, tile), tile)
                found = [(ref, at) for ref in group]
                if whole_ref is not None:
                    found = [(whole_ref, pl.ds(row, tile))] + found
                total = jnp.zeros((tile, 1), F32)
                for ref, rows in found:
                    wide = ref[rows, :].astype(F32)
                    total = total + jnp.sum(wide * wide, axis=-1, keepdims=True)
                inverse = lax.rsqrt(total / (shards * features) + 1e-05)
                for shard, (ref, rows) in zip(shard_of, found):
                    for j in range(per):
                        block = shard * per + j
                        wide = ref[rows, j * kept : (j + 1) * kept].astype(F32)
                        out_ref[into, block, pl.ds(row, tile), :] = (
                            wide * inverse * gain_ref[block]
                        ).astype(BF16)
            return carry

        lax.fori_loop(0, count // tile, step, 0)

    return call("normalize", kernel, here, args, shaped(shape), None if held is None else {1: 0})


def project(here, slot, normed, blocks, total=None, final=False, fresh=False):
    slots, _, length, kept = normed.shape
    kinds, _, width = blocks[0][1].shape
    count = len(blocks)
    args = [normed] + [b for _, near, far in blocks for b in (near, far)]
    args += [] if total is None else [total]

    def kernel(h_ref, *refs):
        at_place = Here(h_ref)
        into = at_place.slot(slot)
        normed_ref, out_ref = refs[0], refs[-1]
        for kind in range(kinds):
            columns = slice(kind * width, (kind + 1) * width)
            summed = None if fresh else refs[1 + 2 * count][into, :, columns]
            for i, (arrival, _, _) in enumerate(blocks):
                for j, y in enumerate((at_place.y, 1 - at_place.y)):
                    part = jnp.dot(
                        normed_ref[into, at_place.at[arrival] * 2 + y],
                        refs[1 + 2 * i + j][kind],
                        preferred_element_type=F32,
                    )
                    summed = part if summed is None else summed + part
            if final:
                out_ref[:, columns] = summed.astype(BF16)
            else:
                out_ref[into, :, columns] = summed

    if final:
        return call("project", kernel, here, args, shaped((length, kinds * width)))
    aliases = None if total is None else {2 + 2 * count: 0}
    return call("project", kernel, here, args, shaped((slots, length, kinds * width), F32), aliases)


def attend(here, own_kind, other_kind, own, got):
    length, width = own.shape[0], own.shape[1] // 3
    heads = width // HDIM
    scale = HDIM ** (-0.5)
    tile = 128 if length % 128 == 0 else length

    def kernel(h_ref, own_kind_ref, other_kind_ref, own_ref, got_ref, out_ref):
        at_place = Here(h_ref)
        kind = jnp.where(at_place.which == 0, own_kind_ref[...], other_kind_ref[...])
        keep = by_row(kind) == at_place.core

        def pick(j):
            columns = slice(j * HDIM, (j + 1) * HDIM)
            return jnp.where(
                keep, own_ref[:, columns].astype(F32), got_ref[:, columns].astype(F32)
            ).astype(BF16)

        for h in range(heads):
            query, key, value = pick(h), pick(heads + h), pick(2 * heads + h)
            for i in range(length // tile):
                low, high = i * tile, (i + 1) * tile
                scores = lax.dot_general(
                    query[low:high], key[:high], (((1,), (1,)), ((), ())), preferred_element_type=F32
                )
                rows = low + lax.broadcasted_iota(I32, (tile, high), 0)
                cols = lax.broadcasted_iota(I32, (tile, high), 1)
                scores = jnp.where(cols <= rows, scores * scale, -jnp.inf)
                top = jnp.max(scores, axis=-1, keepdims=True)
                raised = jnp.exp(scores - top)
                share = 1.0 / jnp.sum(raised, axis=-1, keepdims=True)
                probs = (raised * share).astype(BF16)
                out = jnp.dot(probs, value[:high], preferred_element_type=F32)
                out_ref[low:high, h * HDIM : (h + 1) * HDIM] = out.astype(BF16)

    return call("attend", kernel, here, [own_kind, other_kind, own, got], shaped((length, width)))


def combine(here, slots, groups, total=None, part=None, cut=False):
    held_pieces, length, held = groups[0][0].shape
    shards = held_pieces // 2
    plain = [pair for group in groups for pair in group[3] if len(pair) == 3]
    features = plain[0][1].shape[-1]
    offset, side = (0, 0) if part is None else part
    wide = features if part is None else features // 2
    tile = min(wide, 256)
    half = length // 2
    terms = [group[:3] + (pair,) for group in groups for pair in group[3]]
    count = len(terms)
    args = [pieces for term in terms for pieces in term[:2]]
    args += [b for term in terms for b in term[3][1:3]] + ([] if total is None else [total])

    def kernel(h_ref, *refs):
        at_place = Here(h_ref)
        outs = refs[-2:] if cut else refs[-1:]
        found = []
        for z in at_place.at:
            shard = lax.rem(at_place.own - (z >> 1) + shards, shards)
            found.append(jnp.where((z & 1) == at_place.column, 0, shards) + shard)
        for s, name in enumerate(slots):
            first_slot = at_place.slot(name) == 0
            rows = [
                jnp.where(
                    first_slot, refs[2 * i][found[arrival]], refs[2 * i + 1][found[arrival]]
                )
                for i, (_, _, _, (arrival, *_)) in enumerate(terms)
            ]
            for n in range(wide // tile):
                columns = slice(n * tile, (n + 1) * tile)
                whole = slice(side * wide + n * tile, side * wide + (n + 1) * tile)
                summed = None if total is None else refs[4 * count][offset + s, :, whole]
                for i, (_, _, parity, (_, _, _, *index)) in enumerate(terms):
                    place = (*index, 0, slice(None), columns if index else whole)
                    near = refs[2 * count + 2 * i][place]
                    far = refs[2 * count + 2 * i + 1][place]
                    block = jnp.where(at_place.y == parity, near, far)
                    product = jnp.dot(rows[i], block, preferred_element_type=F32)
                    summed = product if summed is None else summed + product
                if part is None:
                    outs[0][s, :, columns] = summed
                elif cut:
                    result = summed.astype(BF16)
                    first = at_place.core == 0
                    outs[0][:, columns] = jnp.where(first, result[:half], result[half:])
                    outs[1][:, columns] = jnp.where(first, result[half:], result[:half])
                else:
                    outs[0][:, columns] = summed.astype(BF16)

    if part is None:
        out_shape = shaped((len(slots), length, wide), F32)
    elif cut:
        out_shape = [shaped((half, wide))] * 2
    else:
        out_shape = shaped((length, wide))
    return call("combine", kernel, here, args, out_shape)


def join(here, kind, kept, got):
    half = kept.shape[0]

    def kernel(h_ref, kind_ref, a_ref, b_ref, out_ref):
        core = h_ref[0]
        rows = by_row(kind_ref[...])[:, :1]
        rows = jnp.where(core == 0, rows[:half], rows[half:])
        out_ref[...] = jnp.where(
            rows == core, a_ref[...].astype(F32), b_ref[...].astype(F32)
        ).astype(BF16)

    return call("join", kernel, here, [kind, kept, got], shaped(kept.shape))


def assemble(here, kind, parts):
    length, wide = parts[0][0].shape
    width = wide * len(parts)
    steps = 4
    tile = length // steps
    half = length // 2
    args = [kind] + [array for part in parts for array in part]

    def kernel(h_ref, kind_ref, *refs):
        out_ref, held, sems = refs[-3:]
        at_place = Here(h_ref)
        core, first = at_place.core, at_place.column == 0
        copies = []
        kind = by_row(kind_ref[...])[:, :1]
        for i in range(steps):
            rows = slice(i * tile, (i + 1) * tile)
            keep = kind[rows] == core
            part = slice(i * tile % half, i * tile % half + tile)
            for j in range(len(parts)):
                a_ref, b_ref, c_ref, d_ref = refs[4 * j : 4 * j + 4]
                own = jnp.where(keep, a_ref[rows].astype(F32), b_ref[rows].astype(F32)).astype(BF16)
                other = jnp.where(core == i * tile // half, c_ref[part], d_ref[part])
                low = slice(j * wide, (j + 1) * wide)
                high = slice(width + j * wide, width + (j + 1) * wide)
                held[i, :, low] = jnp.where(first, own, other)
                held[i, :, high] = jnp.where(first, other, own)
            copies.append(pltpu.make_async_copy(held.at[i], out_ref.at[rows], sems.at[i]))
            copies[-1].start()
        for copy in copies:
            copy.wait()

    return pl.pallas_call(
        kernel,
        in_specs=[pl.BlockSpec(memory_space=SMEM)] + [pl.BlockSpec(memory_space=VMEM)] * len(args),
        out_specs=pl.BlockSpec(memory_space=pl.ANY),
        out_shape=shaped((length, 2 * width)),
        scratch_shapes=[VMEM((steps, tile, 2 * width), BF16), pltpu.SemaphoreType.DMA((steps,))],
        compiler_params=pltpu.CompilerParams(vmem_limit_bytes=8 * 2**20),
        name="assemble",
    )(here, *[pltpu.with_memory_space_constraint(a, VMEM) for a in args])


def from_partner(x, axis, bit):
    return lax.ppermute(x, axis, [(i, i ^ 1 << bit) for i in range(lax.axis_size(axis))])


def gathered_plan(tokens, modality, norm_gains, qkv_weight, out_weight):
    tower_id = lax.axis_index("mod")
    own_rows = modality == tower_id
    gathered = lax.all_gather(tokens, "tensor", axis=1, tiled=True)
    length = gathered.shape[0]
    local_width = qkv_weight.shape[3]
    local_heads = local_width // HDIM
    gain_row = norm_gains[0]
    scale = HDIM ** (-0.5)
    wide_rows = gathered.astype(jnp.float32)
    inverse = lax.rsqrt(jnp.mean(wide_rows * wide_rows, axis=-1, keepdims=True) + 1e-05)
    row_block = (wide_rows * inverse * gain_row).astype(jnp.bfloat16)
    weight_piece = lax.all_gather(qkv_weight, "dp", axis=1, tiled=True)
    count = weight_piece.shape[1]
    columns = row_block
    projected = (
        jnp.dot(
            columns,
            weight_piece[0].reshape(count, 3 * local_width),
            preferred_element_type=jnp.float32,
        )
        .astype(jnp.bfloat16)
        .reshape(length, 3, local_heads, HDIM)
    )
    queries = projected[:, 0]
    own_pair = projected[:, 1:]
    other_pair = from_partner(own_pair, "mod", 0)
    key_pairs = jnp.where(own_rows[:, None, None, None], own_pair, other_pair)
    key_pos = jnp.arange(length, dtype=jnp.int32)
    scores = (
        jnp.einsum("qhd,khd->hqk", queries, key_pairs[:, 0], preferred_element_type=jnp.float32)
        * scale
    )
    allowed = key_pos[None, :] <= key_pos[:, None]
    scores = jnp.where(allowed[None], scores, -jnp.inf)
    soft_weights = jax.nn.softmax(scores, axis=-1).astype(jnp.bfloat16)
    attended = jnp.einsum(
        "hqk,khd->qhd", soft_weights, key_pairs[:, 1], preferred_element_type=jnp.float32
    )
    attended = attended.astype(jnp.bfloat16).reshape(queries.shape[0], local_width)
    all_heads = lax.all_gather(attended, "tensor", axis=1, tiled=True)
    weight_piece = lax.all_gather(out_weight, "dp", axis=1, tiled=True)
    columns = all_heads
    projected_out = jnp.dot(columns, weight_piece[0], preferred_element_type=jnp.float32).astype(
        jnp.bfloat16
    )
    placed = jnp.where(own_rows[:, None], projected_out, jnp.zeros_like(projected_out))
    combined = lax.psum(placed.astype(jnp.float32).astype(jnp.bfloat16), "mod")
    return combined


def solution(mesh):
    places, shards = mesh.shape["dp"], mesh.shape["tensor"]
    mods = mesh.shape["mod"]

    def move(array, where, *earlier):
        pairs = []
        for m in range(mods):
            for d in range(places):
                for x in range(shards):
                    to = where(m, d, x)
                    if to is not None:
                        target = (to[0] * places + to[1]) * shards + to[2]
                        pairs.append(((m * places + d) * shards + x, target))
        return lax.ppermute(after(array, *earlier) if earlier else array, AXES, pairs)

    def to_core(array, *earlier):
        return move(array, lambda m, d, x: (1 - m, d, x), *earlier)

    def over_tensor(array, *earlier):
        return [array] + [
            move(array, lambda m, d, x: (m, d, (x + step) % shards), *earlier)
            for step in range(1, shards)
        ]

    def edge(m, d, x):
        return m, d ^ 2, x

    def outward(m, d, x):
        return (m, d ^ 2, x) if d // 2 in (1, 2) else None

    def inward(m, d, x):
        return (m, d ^ 2, x) if d // 2 in (0, 3) else None

    def across(m, d, x):
        return (m, (3 - d // 2) * 2 + d % 2, x) if d // 2 in (1, 2) else None

    def across_or_stay(m, d, x):
        return across(m, d, x) or (m, d, x)

    def pair(m, d, x):
        return m, d ^ 1, x

    def line_plan(tokens, modality, norm_gains, qkv_weight, out_weight):
        here = jnp.stack([lax.axis_index(name).astype(I32) for name in AXES])
        length = tokens.shape[0]
        kept = qkv_weight.shape[1]
        half = length // 2
        gains = norm_gains[0].reshape(places, 1, kept)
        own_kind = modality[None, :]

        weight = after(qkv_weight[0].transpose(1, 0, 2), here, gains, own_kind)
        low_a, high_a, mine_a, away_a = halves(here, weight, 0, 2)
        m1a = move(low_a, across_or_stay)
        e1a = move(away_a, edge)
        p1a = move(mine_a, pair)

        begun = (m1a,)
        m2a = move(high_a, across, e1a, p1a, *begun)
        e2a = move(m1a, edge, e1a, p1a)
        p2a = move(e1a, pair, p1a, *begun)
        rows, top, bottom = own_rows_of(here, after(tokens, *begun), own_kind)
        fetched = over_tensor(rows)
        low_b, high_b, mine_b, away_b = halves(here, after(weight, *begun), 1, 2)

        begun = (m2a, mine_b)
        m3a = move(e2a, across, p2a, *begun)
        passed_top = move(top, edge, e2a, p2a, *begun)
        third_a = choose(here, after(e2a, *begun), m2a)
        p3a = move(third_a, pair, p2a)

        begun = (m3a,)
        swapped = [to_core(a, *begun) for a in fetched[1:]]
        shape = (2, places, length, kept)
        normed = normalize(
            here, "own", None, gains, after(tokens, *begun), fetched[1:], swapped, shape, 0, half
        )
        m4a = move(e1a, across, passed_top, p3a, *begun)
        m1b = move(low_b, across_or_stay, passed_top, p3a, *begun)
        passed_bottom = move(bottom, edge, passed_top, p3a, *begun)
        p1b = move(mine_b, pair, p3a, *begun)
        part_top = over_tensor(after(passed_top, *begun))
        low_o, high_o, mine_o, away_o = halves(here, after(out_weight, *begun), 0, 1)

        begun = (passed_bottom, normed, mine_o)
        e3a = move(m3a, outward, part_top[-1], *begun)
        i1o = move(low_o, inward, part_top[-1], *begun)
        p1o = move(mine_o, pair, p1b, *begun)
        other_kind = kinds_behind(here, after(passed_bottom, *begun), length)
        part_bottom = over_tensor(after(passed_bottom, *begun))
        top_swapped = [to_core(a, *begun) for a in part_top]
        first_a = [(0, mine_a, p1a), (1, e1a, p2a), (2, third_a, p3a)]
        total_a = project(here, "own", after(normed, *begun), first_a, fresh=True)
        normed = normalize(
            here, "partner", normed, gains, None, part_top, top_swapped, shape, 0, half // 2
        )

        begun = (m4a, m1b, normed, total_a, other_kind)
        m2b = move(high_b, across, *begun)
        e2b = move(m1b, edge, e3a, i1o, p1o, part_bottom[-1], *begun)
        fourth_a = choose(here, after(e3a, *begun), m4a)
        p4a = move(fourth_a, pair, p1o)
        bottom_swapped = [to_core(a, *begun) for a in part_bottom]
        normed = normalize(
            here, "partner", normed, gains, None, part_bottom, bottom_swapped, shape, half // 2, half // 2
        )
        total_a = project(here, "partner", normed, first_a, total_a, fresh=True)

        begun = (m2b, total_a)
        m3b = move(e2b, across, *begun)
        e1b = move(away_b, edge, e2b, p4a, *begun)
        third_b = choose(here, after(e2b, *begun), m2b)
        p3b = move(third_b, pair, p4a)
        last_a = [(3, fourth_a, p4a)]
        late_normed = after(normed, *begun)
        theirs_a = project(here, 1, late_normed, last_a, total_a, final=True)
        got_a = to_core(theirs_a)
        ours_a = project(here, 0, late_normed, last_a, total_a, final=True)

        begun = (m3b, theirs_a, ours_a)
        m4b = move(e1b, across, *begun)
        e3b = move(m3b, outward, e1b, p3b, *begun)
        i2o = move(high_o, inward, e1b, p3b, *begun)
        p2b = move(e1b, pair, p3b, *begun)
        attended_a = attend(here, own_kind, other_kind, after(ours_a, *begun), got_a)
        first_b = [(0, mine_b, p1b), (2, third_b, p3b)]
        late_normed = after(normed, *begun)
        total_b = project(here, "own", late_normed, first_b, fresh=True)
        total_b = project(here, "partner", late_normed, first_b, total_b, fresh=True)
        lows = stack(here, [after(low_o, *begun), i1o])

        begun = (m4b, attended_a, total_b, lows)
        m13o = move(lows, across, i2o, *begun)
        fourth_b = choose(here, after(e3b, *begun), m4b)
        p4b = move(fourth_b, pair, p2b)
        packed_a = move(pack(here, after(low_o, *begun), attended_a), edge, e3b, p2b)
        held_a = over_tensor(after(attended_a, *begun))
        highs = stack(here, [after(high_o, *begun), i2o])
        second_b = [(1, e1b, p2b)]
        late_normed = after(normed, *begun)
        total_b = project(here, "own", late_normed, second_b, total_b)
        total_b = project(here, "partner", late_normed, second_b, total_b)

        begun = (m13o, total_b, packed_a, held_a[1], highs)
        m24o = move(highs, across, *begun)
        o23o = move(m13o, outward, *begun)
        last_b = [(3, fourth_b, p4b)]
        late_normed = after(normed, *begun)
        theirs_b = project(here, 1, late_normed, last_b, total_b, final=True)
        got_b = to_core(theirs_b)
        ours_b = project(here, 0, late_normed, last_b, total_b, final=True)
        o1o, passed_a = unpack(here, after(packed_a, ours_b), low_o, attended_a)
        second_o = choose(here, o1o, i2o)
        p2o = move(second_o, pair, p4b)
        held_a += over_tensor(passed_a)
        attended_b = attend(here, own_kind, other_kind, ours_b, got_b)
        held_b = over_tensor(attended_b)

        begun = (m24o, o23o, held_b[1], held_a[-1], p2o)
        late_o = choose_halves(here, after(o23o, *begun), m24o)
        passed_b = move(attended_b, edge, o23o)
        held_b += over_tensor(after(passed_b, late_o[0]))
        p34o = [move(late_o[0], pair)]
        p34o.append(move(late_o[1], pair, p34o[0]))
        pieces_a = stack(here, [after(held_a[0], late_o[0])] + held_a[1:])
        pieces_a = (pieces_a, to_core(pieces_a))
        near = [(0, mine_o, p1o), (1, second_o, p2o)]
        total = combine(here, ("partner", "own"), [pieces_a + (0, near)])
        pieces_b = stack(here, [after(held_b[0], total, p34o[0])] + held_b[1:])
        pieces_b = (pieces_b, to_core(pieces_b))

        fars, rests = [], []
        for side in range(2):
            last = [(2, late_o[side], p34o[side], 0), (3, late_o[side], p34o[side], 1)]
            rests.append([pieces_a + (0, last), pieces_b + (1, near + last)])
            ready = after(total, fars[-1]) if fars else total
            kept_away, sent_away = combine(here, ("partner",), rests[side], ready, (0, side), True)
            joined = join(here, other_kind, kept_away, to_core(sent_away))
            fars.append(move(joined, edge))
        parts = []
        for side in range(2):
            near_part = combine(here, ("own",), rests[side], after(total, joined), (1, side))
            parts.append((near_part, to_core(near_part), fars[side], to_core(fars[side])))
        return assemble(here, own_kind, parts)

    return jax.shard_map(
        line_plan if places == 8 else gathered_plan,
        mesh=mesh,
        in_specs=(
            P("dp", "tensor"),
            P("dp"),
            P("mod", None),
            P("mod", "dp", None, "tensor"),
            P("mod", "dp", "tensor"),
        ),
        out_specs=P("dp", "tensor"),
        check_vma=False,
    )
```

```python
import jax
import jax.numpy as jnp
from jax import lax
from jax.experimental import pallas as pl
from jax.experimental.pallas import tpu as pltpu
from jax.sharding import PartitionSpec as P

HDIM = 128
AXES = ("mod", "dp", "tensor")
F32, BF16, I32 = jnp.float32, jnp.bfloat16, jnp.int32
VMEM, SMEM = pltpu.VMEM, pltpu.SMEM


def after(array, *earlier):
    return lax.optimization_barrier((array,) + earlier)[0]


class Here:
    def __init__(self, ref):
        self.core, place, self.own = ref[0], ref[1], ref[2]
        self.z, self.y = place >> 1, place & 1
        self.column = (self.z ^ (self.z >> 1)) & 1
        self.outer = self.column == 0
        self.which = self.core ^ (self.z & 1)
        self.at = [self.z, self.z ^ 1, jnp.where(self.z < 2, 2, 1), 3 - 3 * (self.z >> 1)]

    def slot(self, name):
        return {"own": self.which, "partner": 1 - self.which}.get(name, name)


def call(name, kernel, here, args, out_shape, aliases=None, scratch=8):
    return pl.pallas_call(
        kernel,
        in_specs=[pl.BlockSpec(memory_space=SMEM)] + [pl.BlockSpec(memory_space=VMEM)] * len(args),
        out_specs=jax.tree.map(lambda _: pl.BlockSpec(memory_space=VMEM), out_shape),
        out_shape=jax.tree.map(lambda shape: VMEM(shape.shape, shape.dtype), out_shape),
        input_output_aliases=aliases or {},
        compiler_params=pltpu.CompilerParams(vmem_limit_bytes=scratch * 2**20),
        name=name,
    )(here, *[pltpu.with_memory_space_constraint(a, VMEM) for a in args])


def shaped(shape, dtype=BF16):
    return jax.ShapeDtypeStruct(shape, dtype)


def by_row(kind):
    return jnp.broadcast_to(kind.astype(F32), (128, kind.shape[1])).T.astype(I32)


def halves(here, weight, chunk, chunks):
    kinds, depth, width = weight.shape
    half = width // 2
    part = half // chunks

    def kernel(h_ref, in_ref, low_ref, high_ref, mine_ref, away_ref):
        outer = Here(h_ref).outer
        for kind in range(kinds):
            low = in_ref[kind, :, chunk * part : (chunk + 1) * part]
            high = in_ref[kind, :, half + chunk * part : half + (chunk + 1) * part]
            low_ref[kind] = low
            high_ref[kind] = high
            mine_ref[kind] = jnp.where(outer, low, high)
            away_ref[kind] = jnp.where(outer, high, low)

    return call("halves", kernel, here, [weight], [shaped((kinds, depth, part))] * 4)


def own_rows_of(here, tokens, kind):
    length, features = tokens.shape
    half = length // 2
    extra = 16

    def kernel(h_ref, in_ref, kind_ref, rows_ref, top_ref, bottom_ref):
        rows = jnp.where(h_ref[0] == 0, in_ref[:half], in_ref[half:])
        rows_ref[...] = rows
        top_ref[...] = rows[: half // 2]
        bottom_ref[: half // 2] = rows[half // 2 :]
        bottom_ref[half // 2 :, :length] = jnp.broadcast_to(
            kind_ref[...].astype(F32), (extra, length)
        ).astype(BF16)
        bottom_ref[half // 2 :, length:] = jnp.zeros((extra, features - length), BF16)

    outs = [shaped((rows, features)) for rows in (half, half // 2, half // 2 + extra)]
    return call("own_rows_of", kernel, here, [tokens, kind], outs)


def kinds_behind(here, part, length):
    def kernel(_, in_ref, out_ref):
        out_ref[...] = in_ref[length // 4 :, :length].astype(F32)[:1].astype(I32)

    return call("kinds_behind", kernel, here, [part], shaped((1, length), I32))


def choose(here, from_edge, from_middle):
    def kernel(h_ref, a_ref, b_ref, out_ref):
        outer = Here(h_ref).outer

        @pl.when(outer)
        def _():
            out_ref[...] = a_ref[...]

        @pl.when(jnp.logical_not(outer))
        def _():
            out_ref[...] = b_ref[...]

    return call("choose", kernel, here, [from_edge, from_middle], shaped(from_edge.shape))


def choose_halves(here, from_edge, from_middle):
    shape = from_edge.shape
    half = shape[-1] // 2

    def kernel(h_ref, a_ref, b_ref, low_ref, high_ref):
        outer = Here(h_ref).outer
        for ref, wanted in ((a_ref, outer), (b_ref, jnp.logical_not(outer))):

            @pl.when(wanted)
            def _(ref=ref):
                for i in range(shape[0]):
                    low_ref[i] = ref[i, :, :, :half]
                    high_ref[i] = ref[i, :, :, half:]

    outs = [shaped(shape[:-1] + (half,))] * 2
    return call("choose_halves", kernel, here, [from_edge, from_middle], outs)


def stack(here, arrays):
    def kernel(_, *refs):
        for i in range(len(arrays)):
            refs[-1][i] = refs[i][...]

    return call("stack", kernel, here, arrays, shaped((len(arrays),) + arrays[0].shape))


def pack(here, block, piece):
    _, depth, features = block.shape
    length, width = piece.shape
    cuts = features // width

    def kernel(_, block_ref, piece_ref, out_ref):
        for i in range(cuts):
            out_ref[i * depth : (i + 1) * depth] = block_ref[0, :, i * width : (i + 1) * width]
        out_ref[cuts * depth :] = piece_ref[...]

    return call("pack", kernel, here, [block, piece], shaped((cuts * depth + length, width)))


def unpack(here, packed, block, piece):
    _, depth, features = block.shape
    _, width = piece.shape
    cuts = features // width

    def kernel(_, in_ref, block_ref, piece_ref):
        for i in range(cuts):
            block_ref[0, :, i * width : (i + 1) * width] = in_ref[i * depth : (i + 1) * depth]
        piece_ref[...] = in_ref[cuts * depth :]

    return call("unpack", kernel, here, [packed], [shaped(block.shape), shaped(piece.shape)])


def normalize(here, slot, held, gains, whole, mine, theirs, shape, start, count):
    _, _, length, kept = shape
    shards = len(mine) + (whole is not None)
    features = (whole if whole is not None else mine[0]).shape[1]
    tile = 32 if count % 32 == 0 else count
    half = length // 2
    per = features // kept
    args = ([] if held is None else [held]) + [gains] + ([] if whole is None else [whole])
    args += list(mine) + list(theirs)

    def kernel(h_ref, *refs):
        at_place = Here(h_ref)
        core, own, into = at_place.core, at_place.own, at_place.slot(slot)
        out_ref = refs[-1]
        refs = list(refs[0 if held is None else 1 : -1])
        gain_ref = refs.pop(0)
        whole_ref = None if whole is None else refs.pop(0)
        shard_of = [lax.rem(own - step + shards, shards) for step in range(shards)]

        def step(i, carry):
            for group, first in ((refs[: len(mine)], core), (refs[len(mine) :], 1 - core)):
                row = pl.multiple_of(first * half + start + i * tile, tile)
                at = pl.ds(pl.multiple_of(i * tile, tile), tile)
                found = [(ref, at) for ref in group]
                if whole_ref is not None:
                    found = [(whole_ref, pl.ds(row, tile))] + found
                total = jnp.zeros((tile, 1), F32)
                for ref, rows in found:
                    wide = ref[rows, :].astype(F32)
                    total = total + jnp.sum(wide * wide, axis=-1, keepdims=True)
                inverse = lax.rsqrt(total / (shards * features) + 1e-05)
                for shard, (ref, rows) in zip(shard_of, found):
                    for j in range(per):
                        block = shard * per + j
                        wide = ref[rows, j * kept : (j + 1) * kept].astype(F32)
                        out_ref[into, block, pl.ds(row, tile), :] = (
                            wide * inverse * gain_ref[block]
                        ).astype(BF16)
            return carry

        lax.fori_loop(0, count // tile, step, 0)

    return call("normalize", kernel, here, args, shaped(shape), None if held is None else {1: 0})


def project(here, slot, normed, blocks, total=None, final=False, fresh=False):
    slots, _, length, kept = normed.shape
    kinds, _, width = blocks[0][1].shape
    count = len(blocks)
    args = [normed] + [b for _, near, far in blocks for b in (near, far)]
    args += [] if total is None else [total]

    def kernel(h_ref, *refs):
        at_place = Here(h_ref)
        into = at_place.slot(slot)
        normed_ref, out_ref = refs[0], refs[-1]
        for kind in range(kinds):
            columns = slice(kind * width, (kind + 1) * width)
            summed = None if fresh else refs[1 + 2 * count][into, :, columns]
            for i, (arrival, _, _) in enumerate(blocks):
                for j, y in enumerate((at_place.y, 1 - at_place.y)):
                    part = jnp.dot(
                        normed_ref[into, at_place.at[arrival] * 2 + y],
                        refs[1 + 2 * i + j][kind],
                        preferred_element_type=F32,
                    )
                    summed = part if summed is None else summed + part
            if final:
                out_ref[:, columns] = summed.astype(BF16)
            else:
                out_ref[into, :, columns] = summed

    if final:
        return call("project", kernel, here, args, shaped((length, kinds * width)))
    aliases = None if total is None else {2 + 2 * count: 0}
    return call("project", kernel, here, args, shaped((slots, length, kinds * width), F32), aliases)


def attend(here, own_kind, other_kind, own, got):
    length, width = own.shape[0], own.shape[1] // 3
    heads = width // HDIM
    scale = HDIM ** (-0.5)
    tile = 128 if length % 128 == 0 else length

    def kernel(h_ref, own_kind_ref, other_kind_ref, own_ref, got_ref, out_ref):
        at_place = Here(h_ref)
        kind = jnp.where(at_place.which == 0, own_kind_ref[...], other_kind_ref[...])
        keep = by_row(kind) == at_place.core

        def pick(j):
            columns = slice(j * HDIM, (j + 1) * HDIM)
            return jnp.where(
                keep, own_ref[:, columns].astype(F32), got_ref[:, columns].astype(F32)
            ).astype(BF16)

        for h in range(heads):
            query, key, value = pick(h), pick(heads + h), pick(2 * heads + h)
            for i in range(length // tile):
                low, high = i * tile, (i + 1) * tile
                scores = lax.dot_general(
                    query[low:high], key[:high], (((1,), (1,)), ((), ())), preferred_element_type=F32
                )
                rows = low + lax.broadcasted_iota(I32, (tile, high), 0)
                cols = lax.broadcasted_iota(I32, (tile, high), 1)
                scores = jnp.where(cols <= rows, scores * scale, -jnp.inf)
                top = jnp.max(scores, axis=-1, keepdims=True)
                raised = jnp.exp(scores - top)
                share = 1.0 / jnp.sum(raised, axis=-1, keepdims=True)
                probs = (raised * share).astype(BF16)
                out = jnp.dot(probs, value[:high], preferred_element_type=F32)
                out_ref[low:high, h * HDIM : (h + 1) * HDIM] = out.astype(BF16)

    return call("attend", kernel, here, [own_kind, other_kind, own, got], shaped((length, width)))


def combine(here, slots, groups, total=None, part=None, cut=False):
    held_pieces, length, held = groups[0][0].shape
    shards = held_pieces // 2
    plain = [pair for group in groups for pair in group[3] if len(pair) == 3]
    features = plain[0][1].shape[-1]
    offset, side = (0, 0) if part is None else part
    wide = features if part is None else features // 2
    tile = min(wide, 256)
    half = length // 2
    terms = [group[:3] + (pair,) for group in groups for pair in group[3]]
    count = len(terms)
    args = [pieces for term in terms for pieces in term[:2]]
    args += [b for term in terms for b in term[3][1:3]] + ([] if total is None else [total])

    def kernel(h_ref, *refs):
        at_place = Here(h_ref)
        outs = refs[-2:] if cut else refs[-1:]
        found = []
        for z in at_place.at:
            shard = lax.rem(at_place.own - (z >> 1) + shards, shards)
            found.append(jnp.where((z & 1) == at_place.column, 0, shards) + shard)
        for s, name in enumerate(slots):
            first_slot = at_place.slot(name) == 0
            rows = [
                jnp.where(
                    first_slot, refs[2 * i][found[arrival]], refs[2 * i + 1][found[arrival]]
                )
                for i, (_, _, _, (arrival, *_)) in enumerate(terms)
            ]
            for n in range(wide // tile):
                columns = slice(n * tile, (n + 1) * tile)
                whole = slice(side * wide + n * tile, side * wide + (n + 1) * tile)
                summed = None if total is None else refs[4 * count][offset + s, :, whole]
                for i, (_, _, parity, (_, _, _, *index)) in enumerate(terms):
                    place = (*index, 0, slice(None), columns if index else whole)
                    near = refs[2 * count + 2 * i][place]
                    far = refs[2 * count + 2 * i + 1][place]
                    block = jnp.where(at_place.y == parity, near, far)
                    product = jnp.dot(rows[i], block, preferred_element_type=F32)
                    summed = product if summed is None else summed + product
                if part is None:
                    outs[0][s, :, columns] = summed
                elif cut:
                    result = summed.astype(BF16)
                    first = at_place.core == 0
                    outs[0][:, columns] = jnp.where(first, result[:half], result[half:])
                    outs[1][:, columns] = jnp.where(first, result[half:], result[:half])
                else:
                    outs[0][:, columns] = summed.astype(BF16)

    if part is None:
        out_shape = shaped((len(slots), length, wide), F32)
    elif cut:
        out_shape = [shaped((half, wide))] * 2
    else:
        out_shape = shaped((length, wide))
    return call("combine", kernel, here, args, out_shape)


def join(here, kind, kept, got):
    half = kept.shape[0]

    def kernel(h_ref, kind_ref, a_ref, b_ref, out_ref):
        core = h_ref[0]
        rows = by_row(kind_ref[...])[:, :1]
        rows = jnp.where(core == 0, rows[:half], rows[half:])
        out_ref[...] = jnp.where(
            rows == core, a_ref[...].astype(F32), b_ref[...].astype(F32)
        ).astype(BF16)

    return call("join", kernel, here, [kind, kept, got], shaped(kept.shape))


def assemble(here, kind, parts):
    length, wide = parts[0][0].shape
    width = wide * len(parts)
    steps = 4
    tile = length // steps
    half = length // 2
    args = [kind] + [array for part in parts for array in part]

    def kernel(h_ref, kind_ref, *refs):
        out_ref, held, sems = refs[-3:]
        at_place = Here(h_ref)
        core, first = at_place.core, at_place.column == 0
        copies = []
        kind = by_row(kind_ref[...])[:, :1]
        for i in range(steps):
            rows = slice(i * tile, (i + 1) * tile)
            keep = kind[rows] == core
            part = slice(i * tile % half, i * tile % half + tile)
            for j in range(len(parts)):
                a_ref, b_ref, c_ref, d_ref = refs[4 * j : 4 * j + 4]
                own = jnp.where(keep, a_ref[rows].astype(F32), b_ref[rows].astype(F32)).astype(BF16)
                other = jnp.where(core == i * tile // half, c_ref[part], d_ref[part])
                low = slice(j * wide, (j + 1) * wide)
                high = slice(width + j * wide, width + (j + 1) * wide)
                held[i, :, low] = jnp.where(first, own, other)
                held[i, :, high] = jnp.where(first, other, own)
            copies.append(pltpu.make_async_copy(held.at[i], out_ref.at[rows], sems.at[i]))
            copies[-1].start()
        for copy in copies:
            copy.wait()

    return pl.pallas_call(
        kernel,
        in_specs=[pl.BlockSpec(memory_space=SMEM)] + [pl.BlockSpec(memory_space=VMEM)] * len(args),
        out_specs=pl.BlockSpec(memory_space=pl.ANY),
        out_shape=shaped((length, 2 * width)),
        scratch_shapes=[VMEM((steps, tile, 2 * width), BF16), pltpu.SemaphoreType.DMA((steps,))],
        compiler_params=pltpu.CompilerParams(vmem_limit_bytes=8 * 2**20),
        name="assemble",
    )(here, *[pltpu.with_memory_space_constraint(a, VMEM) for a in args])


def from_partner(x, axis, bit):
    return lax.ppermute(x, axis, [(i, i ^ 1 << bit) for i in range(lax.axis_size(axis))])


def gathered_plan(tokens, modality, norm_gains, qkv_weight, out_weight):
    tower_id = lax.axis_index("mod")
    own_rows = modality == tower_id
    gathered = lax.all_gather(tokens, "tensor", axis=1, tiled=True)
    length = gathered.shape[0]
    local_width = qkv_weight.shape[3]
    local_heads = local_width // HDIM
    gain_row = norm_gains[0]
    scale = HDIM ** (-0.5)
    wide_rows = gathered.astype(jnp.float32)
    inverse = lax.rsqrt(jnp.mean(wide_rows * wide_rows, axis=-1, keepdims=True) + 1e-05)
    row_block = (wide_rows * inverse * gain_row).astype(jnp.bfloat16)
    weight_piece = lax.all_gather(qkv_weight, "dp", axis=1, tiled=True)
    count = weight_piece.shape[1]
    columns = row_block
    projected = (
        jnp.dot(
            columns,
            weight_piece[0].reshape(count, 3 * local_width),
            preferred_element_type=jnp.float32,
        )
        .astype(jnp.bfloat16)
        .reshape(length, 3, local_heads, HDIM)
    )
    queries = projected[:, 0]
    own_pair = projected[:, 1:]
    other_pair = from_partner(own_pair, "mod", 0)
    key_pairs = jnp.where(own_rows[:, None, None, None], own_pair, other_pair)
    key_pos = jnp.arange(length, dtype=jnp.int32)
    scores = (
        jnp.einsum("qhd,khd->hqk", queries, key_pairs[:, 0], preferred_element_type=jnp.float32)
        * scale
    )
    allowed = key_pos[None, :] <= key_pos[:, None]
    scores = jnp.where(allowed[None], scores, -jnp.inf)
    soft_weights = jax.nn.softmax(scores, axis=-1).astype(jnp.bfloat16)
    attended = jnp.einsum(
        "hqk,khd->qhd", soft_weights, key_pairs[:, 1], preferred_element_type=jnp.float32
    )
    attended = attended.astype(jnp.bfloat16).reshape(queries.shape[0], local_width)
    all_heads = lax.all_gather(attended, "tensor", axis=1, tiled=True)
    weight_piece = lax.all_gather(out_weight, "dp", axis=1, tiled=True)
    columns = all_heads
    projected_out = jnp.dot(columns, weight_piece[0], preferred_element_type=jnp.float32).astype(
        jnp.bfloat16
    )
    placed = jnp.where(own_rows[:, None], projected_out, jnp.zeros_like(projected_out))
    combined = lax.psum(placed.astype(jnp.float32).astype(jnp.bfloat16), "mod")
    return combined


def solution(mesh):
    places, shards = mesh.shape["dp"], mesh.shape["tensor"]
    mods = mesh.shape["mod"]

    def move(array, where, *earlier):
        pairs = []
        for m in range(mods):
            for d in range(places):
                for x in range(shards):
                    to = where(m, d, x)
                    if to is not None:
                        target = (to[0] * places + to[1]) * shards + to[2]
                        pairs.append(((m * places + d) * shards + x, target))
        return lax.ppermute(after(array, *earlier) if earlier else array, AXES, pairs)

    def to_core(array, *earlier):
        return move(array, lambda m, d, x: (1 - m, d, x), *earlier)

    def over_tensor(array, *earlier):
        return [array] + [
            move(array, lambda m, d, x: (m, d, (x + step) % shards), *earlier)
            for step in range(1, shards)
        ]

    def edge(m, d, x):
        return m, d ^ 2, x

    def outward(m, d, x):
        return (m, d ^ 2, x) if d // 2 in (1, 2) else None

    def inward(m, d, x):
        return (m, d ^ 2, x) if d // 2 in (0, 3) else None

    def across(m, d, x):
        return (m, (3 - d // 2) * 2 + d % 2, x) if d // 2 in (1, 2) else None

    def across_or_stay(m, d, x):
        return across(m, d, x) or (m, d, x)

    def pair(m, d, x):
        return m, d ^ 1, x

    def line_plan(tokens, modality, norm_gains, qkv_weight, out_weight):
        here = jnp.stack([lax.axis_index(name).astype(I32) for name in AXES])
        length = tokens.shape[0]
        kept = qkv_weight.shape[1]
        half = length // 2
        gains = norm_gains[0].reshape(places, 1, kept)
        own_kind = modality[None, :]

        weight = after(qkv_weight[0].transpose(1, 0, 2), here, gains, own_kind)
        low_a, high_a, mine_a, away_a = halves(here, weight, 0, 2)
        m1a = move(low_a, across_or_stay)
        e1a = move(away_a, edge)
        p1a = move(mine_a, pair)

        begun = (m1a,)
        m2a = move(high_a, across, e1a, p1a, *begun)
        e2a = move(m1a, edge, e1a, p1a)
        p2a = move(e1a, pair, p1a, *begun)
        rows, top, bottom = own_rows_of(here, after(tokens, *begun), own_kind)
        fetched = over_tensor(rows)
        low_b, high_b, mine_b, away_b = halves(here, after(weight, *begun), 1, 2)

        begun = (m2a, mine_b)
        m3a = move(e2a, across, p2a, *begun)
        passed_top = move(top, edge, e2a, p2a, *begun)
        third_a = choose(here, after(e2a, *begun), m2a)
        p3a = move(third_a, pair, p2a)

        begun = (m3a,)
        swapped = [to_core(a, *begun) for a in fetched[1:]]
        shape = (2, places, length, kept)
        normed = normalize(
            here, "own", None, gains, after(tokens, *begun), fetched[1:], swapped, shape, 0, half
        )
        m4a = move(e1a, across, passed_top, p3a, *begun)
        m1b = move(low_b, across_or_stay, passed_top, p3a, *begun)
        passed_bottom = move(bottom, edge, passed_top, p3a, *begun)
        p1b = move(mine_b, pair, p3a, *begun)
        part_top = over_tensor(after(passed_top, *begun))
        low_o, high_o, mine_o, away_o = halves(here, after(out_weight, *begun), 0, 1)

        begun = (passed_bottom, normed, mine_o)
        e3a = move(m3a, outward, part_top[-1], *begun)
        i1o = move(low_o, inward, part_top[-1], *begun)
        p1o = move(mine_o, pair, p1b, *begun)
        other_kind = kinds_behind(here, after(passed_bottom, *begun), length)
        part_bottom = over_tensor(after(passed_bottom, *begun))
        top_swapped = [to_core(a, *begun) for a in part_top]
        first_a = [(0, mine_a, p1a), (1, e1a, p2a), (2, third_a, p3a)]
        total_a = project(here, "own", after(normed, *begun), first_a, fresh=True)
        normed = normalize(
            here, "partner", normed, gains, None, part_top, top_swapped, shape, 0, half // 2
        )

        begun = (m4a, m1b, normed, total_a, other_kind)
        m2b = move(high_b, across, *begun)
        e2b = move(m1b, edge, e3a, i1o, p1o, part_bottom[-1], *begun)
        fourth_a = choose(here, after(e3a, *begun), m4a)
        p4a = move(fourth_a, pair, p1o)
        bottom_swapped = [to_core(a, *begun) for a in part_bottom]
        normed = normalize(
            here, "partner", normed, gains, None, part_bottom, bottom_swapped, shape, half // 2, half // 2
        )
        total_a = project(here, "partner", normed, first_a, total_a, fresh=True)

        begun = (m2b, total_a)
        m3b = move(e2b, across, *begun)
        e1b = move(away_b, edge, e2b, p4a, *begun)
        third_b = choose(here, after(e2b, *begun), m2b)
        p3b = move(third_b, pair, p4a)
        last_a = [(3, fourth_a, p4a)]
        late_normed = after(normed, *begun)
        theirs_a = project(here, 1, late_normed, last_a, total_a, final=True)
        got_a = to_core(theirs_a)
        ours_a = project(here, 0, late_normed, last_a, total_a, final=True)

        begun = (m3b, theirs_a, ours_a)
        m4b = move(e1b, across, *begun)
        e3b = move(m3b, outward, e1b, p3b, *begun)
        i2o = move(high_o, inward, e1b, p3b, *begun)
        p2b = move(e1b, pair, p3b, *begun)
        attended_a = attend(here, own_kind, other_kind, after(ours_a, *begun), got_a)
        first_b = [(0, mine_b, p1b), (2, third_b, p3b)]
        late_normed = after(normed, *begun)
        total_b = project(here, "own", late_normed, first_b, fresh=True)
        total_b = project(here, "partner", late_normed, first_b, total_b, fresh=True)
        lows = stack(here, [after(low_o, *begun), i1o])

        begun = (m4b, attended_a, total_b, lows)
        m13o = move(lows, across, i2o, *begun)
        fourth_b = choose(here, after(e3b, *begun), m4b)
        p4b = move(fourth_b, pair, p2b)
        packed_a = move(pack(here, after(low_o, *begun), attended_a), edge, e3b, p2b)
        held_a = over_tensor(after(attended_a, *begun))
        highs = stack(here, [after(high_o, *begun), i2o])
        second_b = [(1, e1b, p2b)]
        late_normed = after(normed, *begun)
        total_b = project(here, "own", late_normed, second_b, total_b)
        total_b = project(here, "partner", late_normed, second_b, total_b)

        begun = (m13o, total_b, packed_a, held_a[1], highs)
        m24o = move(highs, across, *begun)
        o23o = move(m13o, outward, *begun)
        last_b = [(3, fourth_b, p4b)]
        late_normed = after(normed, *begun)
        theirs_b = project(here, 1, late_normed, last_b, total_b, final=True)
        got_b = to_core(theirs_b)
        ours_b = project(here, 0, late_normed, last_b, total_b, final=True)
        o1o, passed_a = unpack(here, after(packed_a, ours_b), low_o, attended_a)
        second_o = choose(here, o1o, i2o)
        p2o = move(second_o, pair, p4b)
        held_a += over_tensor(passed_a)
        attended_b = attend(here, own_kind, other_kind, ours_b, got_b)
        held_b = over_tensor(attended_b)

        passed_b = move(attended_b, edge)
        begun = (m24o, o23o, held_b[1], held_a[-1], p2o, passed_b)
        late_o = choose_halves(here, after(o23o, *begun), m24o)
        held_b += over_tensor(after(passed_b, late_o[0]))
        p34o = [move(late_o[0], pair)]
        p34o.append(move(late_o[1], pair, p34o[0]))
        pieces_a = stack(here, [after(held_a[0], late_o[0])] + held_a[1:])
        pieces_a = (pieces_a, to_core(pieces_a))
        near = [(0, mine_o, p1o), (1, second_o, p2o)]
        total = combine(here, ("partner", "own"), [pieces_a + (0, near)])
        pieces_b = stack(here, [after(held_b[0], total, p34o[0])] + held_b[1:])
        pieces_b = (pieces_b, to_core(pieces_b))

        fars, rests = [], []
        for side in range(2):
            last = [(2, late_o[side], p34o[side], 0), (3, late_o[side], p34o[side], 1)]
            rests.append([pieces_a + (0, last), pieces_b + (1, near + last)])
            ready = after(total, fars[-1]) if fars else total
            kept_away, sent_away = combine(here, ("partner",), rests[side], ready, (0, side), True)
            joined = join(here, other_kind, kept_away, to_core(sent_away))
            fars.append(move(joined, edge))
        parts = []
        for side in range(2):
            near_part = combine(here, ("own",), rests[side], after(total, joined), (1, side))
            parts.append((near_part, to_core(near_part), fars[side], to_core(fars[side])))
        return assemble(here, own_kind, parts)

    return jax.shard_map(
        line_plan if places == 8 else gathered_plan,
        mesh=mesh,
        in_specs=(
            P("dp", "tensor"),
            P("dp"),
            P("mod", None),
            P("mod", "dp", None, "tensor"),
            P("mod", "dp", "tensor"),
        ),
        out_specs=P("dp", "tensor"),
        check_vma=False,
    )
```

```python
import jax
import jax.numpy as jnp
from jax import lax
from jax.experimental import pallas as pl
from jax.experimental.pallas import tpu as pltpu
from jax.sharding import PartitionSpec as P

HDIM = 128
AXES = ("mod", "dp", "tensor")
F32, BF16, I32 = jnp.float32, jnp.bfloat16, jnp.int32
VMEM, SMEM = pltpu.VMEM, pltpu.SMEM


def after(array, *earlier):
    return lax.optimization_barrier((array,) + earlier)[0]


class Here:
    def __init__(self, ref):
        self.core, place, self.own = ref[0], ref[1], ref[2]
        self.z, self.y = place >> 1, place & 1
        self.column = (self.z ^ (self.z >> 1)) & 1
        self.outer = self.column == 0
        self.which = self.core ^ (self.z & 1)
        self.at = [self.z, self.z ^ 1, jnp.where(self.z < 2, 2, 1), 3 - 3 * (self.z >> 1)]

    def slot(self, name):
        return {"own": self.which, "partner": 1 - self.which}.get(name, name)


def call(name, kernel, here, args, out_shape, aliases=None, scratch=8):
    return pl.pallas_call(
        kernel,
        in_specs=[pl.BlockSpec(memory_space=SMEM)] + [pl.BlockSpec(memory_space=VMEM)] * len(args),
        out_specs=jax.tree.map(lambda _: pl.BlockSpec(memory_space=VMEM), out_shape),
        out_shape=jax.tree.map(lambda shape: VMEM(shape.shape, shape.dtype), out_shape),
        input_output_aliases=aliases or {},
        compiler_params=pltpu.CompilerParams(vmem_limit_bytes=scratch * 2**20),
        name=name,
    )(here, *[pltpu.with_memory_space_constraint(a, VMEM) for a in args])


def shaped(shape, dtype=BF16):
    return jax.ShapeDtypeStruct(shape, dtype)


def by_row(kind):
    return jnp.broadcast_to(kind.astype(F32), (128, kind.shape[1])).T.astype(I32)


def halves(here, weight, chunk, chunks):
    kinds, depth, width = weight.shape
    half = width // 2
    part = half // chunks

    def kernel(h_ref, in_ref, low_ref, high_ref, mine_ref, away_ref):
        outer = Here(h_ref).outer
        for kind in range(kinds):
            low = in_ref[kind, :, chunk * part : (chunk + 1) * part]
            high = in_ref[kind, :, half + chunk * part : half + (chunk + 1) * part]
            low_ref[kind] = low
            high_ref[kind] = high
            mine_ref[kind] = jnp.where(outer, low, high)
            away_ref[kind] = jnp.where(outer, high, low)

    return call("halves", kernel, here, [weight], [shaped((kinds, depth, part))] * 4)


def own_rows_of(here, tokens, kind):
    length, features = tokens.shape
    half = length // 2
    extra = 16

    def kernel(h_ref, in_ref, kind_ref, rows_ref, top_ref, bottom_ref):
        rows = jnp.where(h_ref[0] == 0, in_ref[:half], in_ref[half:])
        rows_ref[...] = rows
        top_ref[...] = rows[: half // 2]
        bottom_ref[: half // 2] = rows[half // 2 :]
        bottom_ref[half // 2 :, :length] = jnp.broadcast_to(
            kind_ref[...].astype(F32), (extra, length)
        ).astype(BF16)
        bottom_ref[half // 2 :, length:] = jnp.zeros((extra, features - length), BF16)

    outs = [shaped((rows, features)) for rows in (half, half // 2, half // 2 + extra)]
    return call("own_rows_of", kernel, here, [tokens, kind], outs)


def kinds_behind(here, part, length):
    def kernel(_, in_ref, out_ref):
        out_ref[...] = in_ref[length // 4 :, :length].astype(F32)[:1].astype(I32)

    return call("kinds_behind", kernel, here, [part], shaped((1, length), I32))


def choose(here, from_edge, from_middle):
    def kernel(h_ref, a_ref, b_ref, out_ref):
        outer = Here(h_ref).outer

        @pl.when(outer)
        def _():
            out_ref[...] = a_ref[...]

        @pl.when(jnp.logical_not(outer))
        def _():
            out_ref[...] = b_ref[...]

    return call("choose", kernel, here, [from_edge, from_middle], shaped(from_edge.shape))


def choose_halves(here, from_edge, from_middle):
    shape = from_edge.shape
    half = shape[-1] // 2

    def kernel(h_ref, a_ref, b_ref, low_ref, high_ref):
        outer = Here(h_ref).outer
        for ref, wanted in ((a_ref, outer), (b_ref, jnp.logical_not(outer))):

            @pl.when(wanted)
            def _(ref=ref):
                for i in range(shape[0]):
                    low_ref[i] = ref[i, :, :, :half]
                    high_ref[i] = ref[i, :, :, half:]

    outs = [shaped(shape[:-1] + (half,))] * 2
    return call("choose_halves", kernel, here, [from_edge, from_middle], outs)


def stack(here, arrays):
    def kernel(_, *refs):
        for i in range(len(arrays)):
            refs[-1][i] = refs[i][...]

    return call("stack", kernel, here, arrays, shaped((len(arrays),) + arrays[0].shape))


def pack(here, block, piece):
    _, depth, features = block.shape
    length, width = piece.shape
    cuts = features // width

    def kernel(_, block_ref, piece_ref, out_ref):
        for i in range(cuts):
            out_ref[i * depth : (i + 1) * depth] = block_ref[0, :, i * width : (i + 1) * width]
        out_ref[cuts * depth :] = piece_ref[...]

    return call("pack", kernel, here, [block, piece], shaped((cuts * depth + length, width)))


def unpack(here, packed, block, piece):
    _, depth, features = block.shape
    _, width = piece.shape
    cuts = features // width

    def kernel(_, in_ref, block_ref, piece_ref):
        for i in range(cuts):
            block_ref[0, :, i * width : (i + 1) * width] = in_ref[i * depth : (i + 1) * depth]
        piece_ref[...] = in_ref[cuts * depth :]

    return call("unpack", kernel, here, [packed], [shaped(block.shape), shaped(piece.shape)])


def normalize(here, slot, held, gains, whole, mine, theirs, shape, start, count):
    _, _, length, kept = shape
    shards = len(mine) + (whole is not None)
    features = (whole if whole is not None else mine[0]).shape[1]
    tile = 32 if count % 32 == 0 else count
    half = length // 2
    per = features // kept
    args = ([] if held is None else [held]) + [gains] + ([] if whole is None else [whole])
    args += list(mine) + list(theirs)

    def kernel(h_ref, *refs):
        at_place = Here(h_ref)
        core, own, into = at_place.core, at_place.own, at_place.slot(slot)
        out_ref = refs[-1]
        refs = list(refs[0 if held is None else 1 : -1])
        gain_ref = refs.pop(0)
        whole_ref = None if whole is None else refs.pop(0)
        shard_of = [lax.rem(own - step + shards, shards) for step in range(shards)]

        def step(i, carry):
            for group, first in ((refs[: len(mine)], core), (refs[len(mine) :], 1 - core)):
                row = pl.multiple_of(first * half + start + i * tile, tile)
                at = pl.ds(pl.multiple_of(i * tile, tile), tile)
                found = [(ref, at) for ref in group]
                if whole_ref is not None:
                    found = [(whole_ref, pl.ds(row, tile))] + found
                total = jnp.zeros((tile, 1), F32)
                for ref, rows in found:
                    wide = ref[rows, :].astype(F32)
                    total = total + jnp.sum(wide * wide, axis=-1, keepdims=True)
                inverse = lax.rsqrt(total / (shards * features) + 1e-05)
                for shard, (ref, rows) in zip(shard_of, found):
                    for j in range(per):
                        block = shard * per + j
                        wide = ref[rows, j * kept : (j + 1) * kept].astype(F32)
                        out_ref[into, block, pl.ds(row, tile), :] = (
                            wide * inverse * gain_ref[block]
                        ).astype(BF16)
            return carry

        lax.fori_loop(0, count // tile, step, 0)

    return call("normalize", kernel, here, args, shaped(shape), None if held is None else {1: 0})


def project(here, slot, normed, blocks, total=None, final=False, fresh=False):
    slots, _, length, kept = normed.shape
    kinds, _, width = blocks[0][1].shape
    count = len(blocks)
    args = [normed] + [b for _, near, far in blocks for b in (near, far)]
    args += [] if total is None else [total]

    def kernel(h_ref, *refs):
        at_place = Here(h_ref)
        into = at_place.slot(slot)
        normed_ref, out_ref = refs[0], refs[-1]
        for kind in range(kinds):
            columns = slice(kind * width, (kind + 1) * width)
            summed = None if fresh else refs[1 + 2 * count][into, :, columns]
            for i, (arrival, _, _) in enumerate(blocks):
                for j, y in enumerate((at_place.y, 1 - at_place.y)):
                    part = jnp.dot(
                        normed_ref[into, at_place.at[arrival] * 2 + y],
                        refs[1 + 2 * i + j][kind],
                        preferred_element_type=F32,
                    )
                    summed = part if summed is None else summed + part
            if final:
                out_ref[:, columns] = summed.astype(BF16)
            else:
                out_ref[into, :, columns] = summed

    if final:
        return call("project", kernel, here, args, shaped((length, kinds * width)))
    aliases = None if total is None else {2 + 2 * count: 0}
    return call("project", kernel, here, args, shaped((slots, length, kinds * width), F32), aliases)


def attend(here, own_kind, other_kind, own, got):
    length, width = own.shape[0], own.shape[1] // 3
    heads = width // HDIM
    scale = HDIM ** (-0.5)
    tile = 128 if length % 128 == 0 else length

    def kernel(h_ref, own_kind_ref, other_kind_ref, own_ref, got_ref, out_ref):
        at_place = Here(h_ref)
        kind = jnp.where(at_place.which == 0, own_kind_ref[...], other_kind_ref[...])
        keep = by_row(kind) == at_place.core

        def pick(j):
            columns = slice(j * HDIM, (j + 1) * HDIM)
            return jnp.where(
                keep, own_ref[:, columns].astype(F32), got_ref[:, columns].astype(F32)
            ).astype(BF16)

        for h in range(heads):
            query, key, value = pick(h), pick(heads + h), pick(2 * heads + h)
            for i in range(length // tile):
                low, high = i * tile, (i + 1) * tile
                scores = lax.dot_general(
                    query[low:high], key[:high], (((1,), (1,)), ((), ())), preferred_element_type=F32
                )
                rows = low + lax.broadcasted_iota(I32, (tile, high), 0)
                cols = lax.broadcasted_iota(I32, (tile, high), 1)
                scores = jnp.where(cols <= rows, scores * scale, -jnp.inf)
                top = jnp.max(scores, axis=-1, keepdims=True)
                raised = jnp.exp(scores - top)
                share = 1.0 / jnp.sum(raised, axis=-1, keepdims=True)
                probs = (raised * share).astype(BF16)
                out = jnp.dot(probs, value[:high], preferred_element_type=F32)
                out_ref[low:high, h * HDIM : (h + 1) * HDIM] = out.astype(BF16)

    return call("attend", kernel, here, [own_kind, other_kind, own, got], shaped((length, width)))


def combine(here, slots, groups, total=None, part=None, cut=False):
    held_pieces, length, held = groups[0][0].shape
    shards = held_pieces // 2
    plain = [pair for group in groups for pair in group[3] if len(pair) == 3]
    features = plain[0][1].shape[-1]
    offset, side = (0, 0) if part is None else part
    wide = features if part is None else features // 2
    tile = min(wide, 256)
    half = length // 2
    terms = [group[:3] + (pair,) for group in groups for pair in group[3]]
    count = len(terms)
    args = [pieces for term in terms for pieces in term[:2]]
    args += [b for term in terms for b in term[3][1:3]] + ([] if total is None else [total])

    def kernel(h_ref, *refs):
        at_place = Here(h_ref)
        outs = refs[-2:] if cut else refs[-1:]
        found = []
        for z in at_place.at:
            shard = lax.rem(at_place.own - (z >> 1) + shards, shards)
            found.append(jnp.where((z & 1) == at_place.column, 0, shards) + shard)
        for s, name in enumerate(slots):
            first_slot = at_place.slot(name) == 0
            rows = [
                jnp.where(
                    first_slot, refs[2 * i][found[arrival]], refs[2 * i + 1][found[arrival]]
                )
                for i, (_, _, _, (arrival, *_)) in enumerate(terms)
            ]
            for n in range(wide // tile):
                columns = slice(n * tile, (n + 1) * tile)
                whole = slice(side * wide + n * tile, side * wide + (n + 1) * tile)
                summed = None if total is None else refs[4 * count][offset + s, :, whole]
                for i, (_, _, parity, (_, _, _, *index)) in enumerate(terms):
                    place = (*index, 0, slice(None), columns if index else whole)
                    near = refs[2 * count + 2 * i][place]
                    far = refs[2 * count + 2 * i + 1][place]
                    block = jnp.where(at_place.y == parity, near, far)
                    product = jnp.dot(rows[i], block, preferred_element_type=F32)
                    summed = product if summed is None else summed + product
                if part is None:
                    outs[0][s, :, columns] = summed
                elif cut:
                    result = summed.astype(BF16)
                    first = at_place.core == 0
                    outs[0][:, columns] = jnp.where(first, result[:half], result[half:])
                    outs[1][:, columns] = jnp.where(first, result[half:], result[:half])
                else:
                    outs[0][:, columns] = summed.astype(BF16)

    if part is None:
        out_shape = shaped((len(slots), length, wide), F32)
    elif cut:
        out_shape = [shaped((half, wide))] * 2
    else:
        out_shape = shaped((length, wide))
    return call("combine", kernel, here, args, out_shape)


def join(here, kind, kept, got):
    half = kept.shape[0]

    def kernel(h_ref, kind_ref, a_ref, b_ref, out_ref):
        core = h_ref[0]
        rows = by_row(kind_ref[...])[:, :1]
        rows = jnp.where(core == 0, rows[:half], rows[half:])
        out_ref[...] = jnp.where(
            rows == core, a_ref[...].astype(F32), b_ref[...].astype(F32)
        ).astype(BF16)

    return call("join", kernel, here, [kind, kept, got], shaped(kept.shape))


def assemble(here, kind, parts):
    length, wide = parts[0][0].shape
    width = wide * len(parts)
    steps = 4
    tile = length // steps
    half = length // 2
    args = [kind] + [array for part in parts for array in part]

    def kernel(h_ref, kind_ref, *refs):
        out_ref, held, sems = refs[-3:]
        at_place = Here(h_ref)
        core, first = at_place.core, at_place.column == 0
        copies = []
        kind = by_row(kind_ref[...])[:, :1]
        for i in range(steps):
            rows = slice(i * tile, (i + 1) * tile)
            keep = kind[rows] == core
            part = slice(i * tile % half, i * tile % half + tile)
            for j in range(len(parts)):
                a_ref, b_ref, c_ref, d_ref = refs[4 * j : 4 * j + 4]
                own = jnp.where(keep, a_ref[rows].astype(F32), b_ref[rows].astype(F32)).astype(BF16)
                other = jnp.where(core == i * tile // half, c_ref[part], d_ref[part])
                low = slice(j * wide, (j + 1) * wide)
                high = slice(width + j * wide, width + (j + 1) * wide)
                held[i, :, low] = jnp.where(first, own, other)
                held[i, :, high] = jnp.where(first, other, own)
            copies.append(pltpu.make_async_copy(held.at[i], out_ref.at[rows], sems.at[i]))
            copies[-1].start()
        for copy in copies:
            copy.wait()

    return pl.pallas_call(
        kernel,
        in_specs=[pl.BlockSpec(memory_space=SMEM)] + [pl.BlockSpec(memory_space=VMEM)] * len(args),
        out_specs=pl.BlockSpec(memory_space=pl.ANY),
        out_shape=shaped((length, 2 * width)),
        scratch_shapes=[VMEM((steps, tile, 2 * width), BF16), pltpu.SemaphoreType.DMA((steps,))],
        compiler_params=pltpu.CompilerParams(vmem_limit_bytes=8 * 2**20),
        name="assemble",
    )(here, *[pltpu.with_memory_space_constraint(a, VMEM) for a in args])


def from_partner(x, axis, bit):
    return lax.ppermute(x, axis, [(i, i ^ 1 << bit) for i in range(lax.axis_size(axis))])


def gathered_plan(tokens, modality, norm_gains, qkv_weight, out_weight):
    tower_id = lax.axis_index("mod")
    own_rows = modality == tower_id
    gathered = lax.all_gather(tokens, "tensor", axis=1, tiled=True)
    length = gathered.shape[0]
    local_width = qkv_weight.shape[3]
    local_heads = local_width // HDIM
    gain_row = norm_gains[0]
    scale = HDIM ** (-0.5)
    wide_rows = gathered.astype(jnp.float32)
    inverse = lax.rsqrt(jnp.mean(wide_rows * wide_rows, axis=-1, keepdims=True) + 1e-05)
    row_block = (wide_rows * inverse * gain_row).astype(jnp.bfloat16)
    weight_piece = lax.all_gather(qkv_weight, "dp", axis=1, tiled=True)
    count = weight_piece.shape[1]
    columns = row_block
    projected = (
        jnp.dot(
            columns,
            weight_piece[0].reshape(count, 3 * local_width),
            preferred_element_type=jnp.float32,
        )
        .astype(jnp.bfloat16)
        .reshape(length, 3, local_heads, HDIM)
    )
    queries = projected[:, 0]
    own_pair = projected[:, 1:]
    other_pair = from_partner(own_pair, "mod", 0)
    key_pairs = jnp.where(own_rows[:, None, None, None], own_pair, other_pair)
    key_pos = jnp.arange(length, dtype=jnp.int32)
    scores = (
        jnp.einsum("qhd,khd->hqk", queries, key_pairs[:, 0], preferred_element_type=jnp.float32)
        * scale
    )
    allowed = key_pos[None, :] <= key_pos[:, None]
    scores = jnp.where(allowed[None], scores, -jnp.inf)
    soft_weights = jax.nn.softmax(scores, axis=-1).astype(jnp.bfloat16)
    attended = jnp.einsum(
        "hqk,khd->qhd", soft_weights, key_pairs[:, 1], preferred_element_type=jnp.float32
    )
    attended = attended.astype(jnp.bfloat16).reshape(queries.shape[0], local_width)
    all_heads = lax.all_gather(attended, "tensor", axis=1, tiled=True)
    weight_piece = lax.all_gather(out_weight, "dp", axis=1, tiled=True)
    columns = all_heads
    projected_out = jnp.dot(columns, weight_piece[0], preferred_element_type=jnp.float32).astype(
        jnp.bfloat16
    )
    placed = jnp.where(own_rows[:, None], projected_out, jnp.zeros_like(projected_out))
    combined = lax.psum(placed.astype(jnp.float32).astype(jnp.bfloat16), "mod")
    return combined


def solution(mesh):
    places, shards = mesh.shape["dp"], mesh.shape["tensor"]
    mods = mesh.shape["mod"]

    def move(array, where, *earlier):
        pairs = []
        for m in range(mods):
            for d in range(places):
                for x in range(shards):
                    to = where(m, d, x)
                    if to is not None:
                        target = (to[0] * places + to[1]) * shards + to[2]
                        pairs.append(((m * places + d) * shards + x, target))
        return lax.ppermute(after(array, *earlier) if earlier else array, AXES, pairs)

    def to_core(array, *earlier):
        return move(array, lambda m, d, x: (1 - m, d, x), *earlier)

    def over_tensor(array, *earlier):
        return [array] + [
            move(array, lambda m, d, x: (m, d, (x + step) % shards), *earlier)
            for step in range(1, shards)
        ]

    def edge(m, d, x):
        return m, d ^ 2, x

    def outward(m, d, x):
        return (m, d ^ 2, x) if d // 2 in (1, 2) else None

    def inward(m, d, x):
        return (m, d ^ 2, x) if d // 2 in (0, 3) else None

    def across(m, d, x):
        return (m, (3 - d // 2) * 2 + d % 2, x) if d // 2 in (1, 2) else None

    def across_or_stay(m, d, x):
        return across(m, d, x) or (m, d, x)

    def pair(m, d, x):
        return m, d ^ 1, x

    def line_plan(tokens, modality, norm_gains, qkv_weight, out_weight):
        here = jnp.stack([lax.axis_index(name).astype(I32) for name in AXES])
        length = tokens.shape[0]
        kept = qkv_weight.shape[1]
        half = length // 2
        gains = norm_gains[0].reshape(places, 1, kept)
        own_kind = modality[None, :]

        weight = after(qkv_weight[0].transpose(1, 0, 2), here, gains, own_kind)
        low_a, high_a, mine_a, away_a = halves(here, weight, 0, 2)
        m1a = move(low_a, across_or_stay)
        e1a = move(away_a, edge)
        p1a = move(mine_a, pair)

        begun = (m1a,)
        m2a = move(high_a, across, e1a, p1a, *begun)
        e2a = move(m1a, edge, e1a, p1a)
        p2a = move(e1a, pair, p1a, *begun)
        rows, top, bottom = own_rows_of(here, after(tokens, *begun), own_kind)
        fetched = over_tensor(rows)
        low_b, high_b, mine_b, away_b = halves(here, after(weight, *begun), 1, 2)

        begun = (m2a, mine_b)
        m3a = move(e2a, across, p2a, *begun)
        passed_top = move(top, edge, e2a, p2a, *begun)
        third_a = choose(here, after(e2a, *begun), m2a)
        p3a = move(third_a, pair, p2a)

        begun = (m3a,)
        swapped = [to_core(a, *begun) for a in fetched[1:]]
        shape = (2, places, length, kept)
        normed = normalize(
            here, "own", None, gains, after(tokens, *begun), fetched[1:], swapped, shape, 0, half
        )
        m4a = move(e1a, across, passed_top, p3a, *begun)
        m1b = move(low_b, across_or_stay, passed_top, p3a, *begun)
        passed_bottom = move(bottom, edge, passed_top, p3a, *begun)
        p1b = move(mine_b, pair, p3a, *begun)
        part_top = over_tensor(after(passed_top, *begun))
        low_o, high_o, mine_o, away_o = halves(here, after(out_weight, *begun), 0, 1)

        begun = (passed_bottom, normed, mine_o)
        e3a = move(m3a, outward, part_top[-1], *begun)
        i1o = move(low_o, inward, part_top[-1], *begun)
        p1o = move(mine_o, pair, p1b, *begun)
        other_kind = kinds_behind(here, after(passed_bottom, *begun), length)
        part_bottom = over_tensor(after(passed_bottom, *begun))
        top_swapped = [to_core(a, *begun) for a in part_top]
        first_a = [(0, mine_a, p1a), (1, e1a, p2a), (2, third_a, p3a)]
        total_a = project(here, "own", after(normed, *begun), first_a, fresh=True)
        normed = normalize(
            here, "partner", normed, gains, None, part_top, top_swapped, shape, 0, half // 2
        )

        begun = (m4a, m1b, normed, total_a, other_kind)
        m2b = move(high_b, across, *begun)
        e2b = move(m1b, edge, e3a, i1o, p1o, part_bottom[-1], *begun)
        fourth_a = choose(here, after(e3a, *begun), m4a)
        p4a = move(fourth_a, pair, p1o)
        bottom_swapped = [to_core(a, *begun) for a in part_bottom]
        normed = normalize(
            here, "partner", normed, gains, None, part_bottom, bottom_swapped, shape, half // 2, half // 2
        )
        total_a = project(here, "partner", normed, first_a, total_a, fresh=True)

        begun = (m2b, total_a)
        m3b = move(e2b, across, *begun)
        e1b = move(away_b, edge, e2b, p4a, *begun)
        third_b = choose(here, after(e2b, *begun), m2b)
        p3b = move(third_b, pair, p4a)
        last_a = [(3, fourth_a, p4a)]
        late_normed = after(normed, *begun)
        theirs_a = project(here, 1, late_normed, last_a, total_a, final=True)
        got_a = to_core(theirs_a)
        ours_a = project(here, 0, late_normed, last_a, total_a, final=True)

        begun = (m3b, theirs_a, ours_a)
        m4b = move(e1b, across, *begun)
        e3b = move(m3b, outward, e1b, p3b, *begun)
        i2o = move(high_o, inward, e1b, p3b, *begun)
        p2b = move(e1b, pair, p3b, *begun)
        attended_a = attend(here, own_kind, other_kind, after(ours_a, *begun), got_a)
        first_b = [(0, mine_b, p1b), (2, third_b, p3b)]
        late_normed = after(normed, *begun)
        total_b = project(here, "own", late_normed, first_b, fresh=True)
        total_b = project(here, "partner", late_normed, first_b, total_b, fresh=True)
        lows = stack(here, [after(low_o, *begun), i1o])

        begun = (m4b, attended_a, total_b, lows)
        m13o = move(lows, across, i2o, *begun)
        fourth_b = choose(here, after(e3b, *begun), m4b)
        p4b = move(fourth_b, pair, p2b)
        packed_a = move(pack(here, after(low_o, *begun), attended_a), edge, e3b, p2b)
        held_a = over_tensor(after(attended_a, *begun))
        highs = stack(here, [after(high_o, *begun), i2o])
        second_b = [(1, e1b, p2b)]
        late_normed = after(normed, *begun)
        total_b = project(here, "own", late_normed, second_b, total_b)
        total_b = project(here, "partner", late_normed, second_b, total_b)

        begun = (m13o, total_b, packed_a, held_a[1], highs)
        m24o = move(highs, across, *begun)
        o23o = move(m13o, outward, *begun)
        last_b = [(3, fourth_b, p4b)]
        late_normed = after(normed, *begun)
        theirs_b = project(here, 1, late_normed, last_b, total_b, final=True)
        got_b = to_core(theirs_b)
        ours_b = project(here, 0, late_normed, last_b, total_b, final=True)
        o1o, passed_a = unpack(here, after(packed_a, ours_b), low_o, attended_a)
        second_o = choose(here, o1o, i2o)
        p2o = move(second_o, pair, p4b)
        held_a += over_tensor(passed_a)
        attended_b = attend(here, own_kind, other_kind, ours_b, got_b)
        held_b = over_tensor(attended_b)

        passed_b = move(attended_b, edge, o23o)
        begun = (m24o, o23o, held_b[1], held_a[-1], p2o, passed_b)
        late_o = choose_halves(here, after(o23o, *begun), m24o)
        held_b += over_tensor(after(passed_b, late_o[0]))
        p34o = [move(late_o[0], pair)]
        p34o.append(move(late_o[1], pair, p34o[0]))
        pieces_a = stack(here, [after(held_a[0], late_o[0])] + held_a[1:])
        pieces_a = (pieces_a, to_core(pieces_a))
        near = [(0, mine_o, p1o), (1, second_o, p2o)]
        total = combine(here, ("partner", "own"), [pieces_a + (0, near)])
        pieces_b = stack(here, [after(held_b[0], total, p34o[0])] + held_b[1:])
        pieces_b = (pieces_b, to_core(pieces_b))

        fars, rests = [], []
        for side in range(2):
            last = [(2, late_o[side], p34o[side], 0), (3, late_o[side], p34o[side], 1)]
            rests.append([pieces_a + (0, last), pieces_b + (1, near + last)])
            ready = after(total, fars[-1]) if fars else total
            kept_away, sent_away = combine(here, ("partner",), rests[side], ready, (0, side), True)
            joined = join(here, other_kind, kept_away, to_core(sent_away))
            fars.append(move(joined, edge))
        parts = []
        for side in range(2):
            near_part = combine(here, ("own",), rests[side], after(total, joined), (1, side))
            parts.append((near_part, to_core(near_part), fars[side], to_core(fars[side])))
        return assemble(here, own_kind, parts)

    return jax.shard_map(
        line_plan if places == 8 else gathered_plan,
        mesh=mesh,
        in_specs=(
            P("dp", "tensor"),
            P("dp"),
            P("mod", None),
            P("mod", "dp", None, "tensor"),
            P("mod", "dp", "tensor"),
        ),
        out_specs=P("dp", "tensor"),
        check_vma=False,
    )
```

```python
import jax
import jax.numpy as jnp
from jax import lax
from jax.experimental import pallas as pl
from jax.experimental.pallas import tpu as pltpu
from jax.sharding import PartitionSpec as P

HDIM = 128
AXES = ("mod", "dp", "tensor")
F32, BF16, I32 = jnp.float32, jnp.bfloat16, jnp.int32
VMEM, SMEM = pltpu.VMEM, pltpu.SMEM


def after(array, *earlier):
    return lax.optimization_barrier((array,) + earlier)[0]


class Here:
    def __init__(self, ref):
        self.core, place, self.own = ref[0], ref[1], ref[2]
        self.z, self.y = place >> 1, place & 1
        self.column = (self.z ^ (self.z >> 1)) & 1
        self.outer = self.column == 0
        self.which = self.core ^ (self.z & 1)
        self.at = [self.z, self.z ^ 1, jnp.where(self.z < 2, 2, 1), 3 - 3 * (self.z >> 1)]

    def slot(self, name):
        return {"own": self.which, "partner": 1 - self.which}.get(name, name)


def call(name, kernel, here, args, out_shape, aliases=None, scratch=8):
    return pl.pallas_call(
        kernel,
        in_specs=[pl.BlockSpec(memory_space=SMEM)] + [pl.BlockSpec(memory_space=VMEM)] * len(args),
        out_specs=jax.tree.map(lambda _: pl.BlockSpec(memory_space=VMEM), out_shape),
        out_shape=jax.tree.map(lambda shape: VMEM(shape.shape, shape.dtype), out_shape),
        input_output_aliases=aliases or {},
        compiler_params=pltpu.CompilerParams(vmem_limit_bytes=scratch * 2**20),
        name=name,
    )(here, *[pltpu.with_memory_space_constraint(a, VMEM) for a in args])


def shaped(shape, dtype=BF16):
    return jax.ShapeDtypeStruct(shape, dtype)


def by_row(kind):
    return jnp.broadcast_to(kind.astype(F32), (128, kind.shape[1])).T.astype(I32)


def halves(here, weight, chunk, chunks):
    kinds, depth, width = weight.shape
    half = width // 2
    part = half // chunks

    def kernel(h_ref, in_ref, low_ref, high_ref, mine_ref, away_ref):
        outer = Here(h_ref).outer
        for kind in range(kinds):
            low = in_ref[kind, :, chunk * part : (chunk + 1) * part]
            high = in_ref[kind, :, half + chunk * part : half + (chunk + 1) * part]
            low_ref[kind] = low
            high_ref[kind] = high
            mine_ref[kind] = jnp.where(outer, low, high)
            away_ref[kind] = jnp.where(outer, high, low)

    return call("halves", kernel, here, [weight], [shaped((kinds, depth, part))] * 4)


def own_rows_of(here, tokens, kind):
    length, features = tokens.shape
    half = length // 2
    extra = 16

    def kernel(h_ref, in_ref, kind_ref, rows_ref, top_ref, bottom_ref):
        rows = jnp.where(h_ref[0] == 0, in_ref[:half], in_ref[half:])
        rows_ref[...] = rows
        top_ref[...] = rows[: half // 2]
        bottom_ref[: half // 2] = rows[half // 2 :]
        bottom_ref[half // 2 :, :length] = jnp.broadcast_to(
            kind_ref[...].astype(F32), (extra, length)
        ).astype(BF16)
        bottom_ref[half // 2 :, length:] = jnp.zeros((extra, features - length), BF16)

    outs = [shaped((rows, features)) for rows in (half, half // 2, half // 2 + extra)]
    return call("own_rows_of", kernel, here, [tokens, kind], outs)


def kinds_behind(here, part, length):
    def kernel(_, in_ref, out_ref):
        out_ref[...] = in_ref[length // 4 :, :length].astype(F32)[:1].astype(I32)

    return call("kinds_behind", kernel, here, [part], shaped((1, length), I32))


def choose(here, from_edge, from_middle):
    def kernel(h_ref, a_ref, b_ref, out_ref):
        outer = Here(h_ref).outer

        @pl.when(outer)
        def _():
            out_ref[...] = a_ref[...]

        @pl.when(jnp.logical_not(outer))
        def _():
            out_ref[...] = b_ref[...]

    return call("choose", kernel, here, [from_edge, from_middle], shaped(from_edge.shape))


def choose_halves(here, from_edge, from_middle):
    shape = from_edge.shape
    half = shape[-1] // 2

    def kernel(h_ref, a_ref, b_ref, low_ref, high_ref):
        outer = Here(h_ref).outer
        for ref, wanted in ((a_ref, outer), (b_ref, jnp.logical_not(outer))):

            @pl.when(wanted)
            def _(ref=ref):
                for i in range(shape[0]):
                    low_ref[i] = ref[i, :, :, :half]
                    high_ref[i] = ref[i, :, :, half:]

    outs = [shaped(shape[:-1] + (half,))] * 2
    return call("choose_halves", kernel, here, [from_edge, from_middle], outs)


def stack(here, arrays):
    def kernel(_, *refs):
        for i in range(len(arrays)):
            refs[-1][i] = refs[i][...]

    return call("stack", kernel, here, arrays, shaped((len(arrays),) + arrays[0].shape))


def pack(here, block, piece):
    _, depth, features = block.shape
    length, width = piece.shape
    cuts = features // width

    def kernel(_, block_ref, piece_ref, out_ref):
        for i in range(cuts):
            out_ref[i * depth : (i + 1) * depth] = block_ref[0, :, i * width : (i + 1) * width]
        out_ref[cuts * depth :] = piece_ref[...]

    return call("pack", kernel, here, [block, piece], shaped((cuts * depth + length, width)))


def unpack(here, packed, block, piece):
    _, depth, features = block.shape
    _, width = piece.shape
    cuts = features // width

    def kernel(_, in_ref, block_ref, piece_ref):
        for i in range(cuts):
            block_ref[0, :, i * width : (i + 1) * width] = in_ref[i * depth : (i + 1) * depth]
        piece_ref[...] = in_ref[cuts * depth :]

    return call("unpack", kernel, here, [packed], [shaped(block.shape), shaped(piece.shape)])


def normalize(here, slot, held, gains, whole, mine, theirs, shape, start, count):
    _, _, length, kept = shape
    shards = len(mine) + (whole is not None)
    features = (whole if whole is not None else mine[0]).shape[1]
    tile = 32 if count % 32 == 0 else count
    half = length // 2
    per = features // kept
    args = ([] if held is None else [held]) + [gains] + ([] if whole is None else [whole])
    args += list(mine) + list(theirs)

    def kernel(h_ref, *refs):
        at_place = Here(h_ref)
        core, own, into = at_place.core, at_place.own, at_place.slot(slot)
        out_ref = refs[-1]
        refs = list(refs[0 if held is None else 1 : -1])
        gain_ref = refs.pop(0)
        whole_ref = None if whole is None else refs.pop(0)
        shard_of = [lax.rem(own - step + shards, shards) for step in range(shards)]

        def step(i, carry):
            for group, first in ((refs[: len(mine)], core), (refs[len(mine) :], 1 - core)):
                row = pl.multiple_of(first * half + start + i * tile, tile)
                at = pl.ds(pl.multiple_of(i * tile, tile), tile)
                found = [(ref, at) for ref in group]
                if whole_ref is not None:
                    found = [(whole_ref, pl.ds(row, tile))] + found
                total = jnp.zeros((tile, 1), F32)
                for ref, rows in found:
                    wide = ref[rows, :].astype(F32)
                    total = total + jnp.sum(wide * wide, axis=-1, keepdims=True)
                inverse = lax.rsqrt(total / (shards * features) + 1e-05)
                for shard, (ref, rows) in zip(shard_of, found):
                    for j in range(per):
                        block = shard * per + j
                        wide = ref[rows, j * kept : (j + 1) * kept].astype(F32)
                        out_ref[into, block, pl.ds(row, tile), :] = (
                            wide * inverse * gain_ref[block]
                        ).astype(BF16)
            return carry

        lax.fori_loop(0, count // tile, step, 0)

    return call("normalize", kernel, here, args, shaped(shape), None if held is None else {1: 0})


def project(here, slot, normed, blocks, total=None, final=False, fresh=False):
    slots, _, length, kept = normed.shape
    kinds, _, width = blocks[0][1].shape
    count = len(blocks)
    args = [normed] + [b for _, near, far in blocks for b in (near, far)]
    args += [] if total is None else [total]

    def kernel(h_ref, *refs):
        at_place = Here(h_ref)
        into = at_place.slot(slot)
        normed_ref, out_ref = refs[0], refs[-1]
        for kind in range(kinds):
            columns = slice(kind * width, (kind + 1) * width)
            summed = None if fresh else refs[1 + 2 * count][into, :, columns]
            for i, (arrival, _, _) in enumerate(blocks):
                for j, y in enumerate((at_place.y, 1 - at_place.y)):
                    part = jnp.dot(
                        normed_ref[into, at_place.at[arrival] * 2 + y],
                        refs[1 + 2 * i + j][kind],
                        preferred_element_type=F32,
                    )
                    summed = part if summed is None else summed + part
            if final:
                out_ref[:, columns] = summed.astype(BF16)
            else:
                out_ref[into, :, columns] = summed

    if final:
        return call("project", kernel, here, args, shaped((length, kinds * width)))
    aliases = None if total is None else {2 + 2 * count: 0}
    return call("project", kernel, here, args, shaped((slots, length, kinds * width), F32), aliases)


def attend(here, own_kind, other_kind, own, got):
    length, width = own.shape[0], own.shape[1] // 3
    heads = width // HDIM
    scale = HDIM ** (-0.5)
    tile = 128 if length % 128 == 0 else length

    def kernel(h_ref, own_kind_ref, other_kind_ref, own_ref, got_ref, out_ref):
        at_place = Here(h_ref)
        kind = jnp.where(at_place.which == 0, own_kind_ref[...], other_kind_ref[...])
        keep = by_row(kind) == at_place.core

        def pick(j):
            columns = slice(j * HDIM, (j + 1) * HDIM)
            return jnp.where(
                keep, own_ref[:, columns].astype(F32), got_ref[:, columns].astype(F32)
            ).astype(BF16)

        for h in range(heads):
            query, key, value = pick(h), pick(heads + h), pick(2 * heads + h)
            for i in range(length // tile):
                low, high = i * tile, (i + 1) * tile
                scores = lax.dot_general(
                    query[low:high], key[:high], (((1,), (1,)), ((), ())), preferred_element_type=F32
                )
                rows = low + lax.broadcasted_iota(I32, (tile, high), 0)
                cols = lax.broadcasted_iota(I32, (tile, high), 1)
                scores = jnp.where(cols <= rows, scores * scale, -jnp.inf)
                top = jnp.max(scores, axis=-1, keepdims=True)
                raised = jnp.exp(scores - top)
                share = 1.0 / jnp.sum(raised, axis=-1, keepdims=True)
                probs = (raised * share).astype(BF16)
                out = jnp.dot(probs, value[:high], preferred_element_type=F32)
                out_ref[low:high, h * HDIM : (h + 1) * HDIM] = out.astype(BF16)

    return call("attend", kernel, here, [own_kind, other_kind, own, got], shaped((length, width)))


def combine(here, slots, groups, total=None, part=None, cut=False):
    held_pieces, length, held = groups[0][0].shape
    shards = held_pieces // 2
    plain = [pair for group in groups for pair in group[3] if len(pair) == 3]
    features = plain[0][1].shape[-1]
    offset, side = (0, 0) if part is None else part
    wide = features if part is None else features // 2
    tile = min(wide, 256)
    half = length // 2
    terms = [group[:3] + (pair,) for group in groups for pair in group[3]]
    count = len(terms)
    args = [pieces for term in terms for pieces in term[:2]]
    args += [b for term in terms for b in term[3][1:3]] + ([] if total is None else [total])

    def kernel(h_ref, *refs):
        at_place = Here(h_ref)
        outs = refs[-2:] if cut else refs[-1:]
        found = []
        for z in at_place.at:
            shard = lax.rem(at_place.own - (z >> 1) + shards, shards)
            found.append(jnp.where((z & 1) == at_place.column, 0, shards) + shard)
        for s, name in enumerate(slots):
            first_slot = at_place.slot(name) == 0
            rows = [
                jnp.where(
                    first_slot, refs[2 * i][found[arrival]], refs[2 * i + 1][found[arrival]]
                )
                for i, (_, _, _, (arrival, *_)) in enumerate(terms)
            ]
            for n in range(wide // tile):
                columns = slice(n * tile, (n + 1) * tile)
                whole = slice(side * wide + n * tile, side * wide + (n + 1) * tile)
                summed = None if total is None else refs[4 * count][offset + s, :, whole]
                for i, (_, _, parity, (_, _, _, *index)) in enumerate(terms):
                    place = (*index, 0, slice(None), columns if index else whole)
                    near = refs[2 * count + 2 * i][place]
                    far = refs[2 * count + 2 * i + 1][place]
                    block = jnp.where(at_place.y == parity, near, far)
                    product = jnp.dot(rows[i], block, preferred_element_type=F32)
                    summed = product if summed is None else summed + product
                if part is None:
                    outs[0][s, :, columns] = summed
                elif cut:
                    result = summed.astype(BF16)
                    first = at_place.core == 0
                    outs[0][:, columns] = jnp.where(first, result[:half], result[half:])
                    outs[1][:, columns] = jnp.where(first, result[half:], result[:half])
                else:
                    outs[0][:, columns] = summed.astype(BF16)

    if part is None:
        out_shape = shaped((len(slots), length, wide), F32)
    elif cut:
        out_shape = [shaped((half, wide))] * 2
    else:
        out_shape = shaped((length, wide))
    return call("combine", kernel, here, args, out_shape)


def join(here, kind, kept, got):
    half = kept.shape[0]

    def kernel(h_ref, kind_ref, a_ref, b_ref, out_ref):
        core = h_ref[0]
        rows = by_row(kind_ref[...])[:, :1]
        rows = jnp.where(core == 0, rows[:half], rows[half:])
        out_ref[...] = jnp.where(
            rows == core, a_ref[...].astype(F32), b_ref[...].astype(F32)
        ).astype(BF16)

    return call("join", kernel, here, [kind, kept, got], shaped(kept.shape))


def assemble(here, kind, parts):
    length, wide = parts[0][0].shape
    width = wide * len(parts)
    steps = 4
    tile = length // steps
    half = length // 2
    args = [kind] + [array for part in parts for array in part]

    def kernel(h_ref, kind_ref, *refs):
        out_ref, held, sems = refs[-3:]
        at_place = Here(h_ref)
        core, first = at_place.core, at_place.column == 0
        copies = []
        kind = by_row(kind_ref[...])[:, :1]
        for i in range(steps):
            rows = slice(i * tile, (i + 1) * tile)
            keep = kind[rows] == core
            part = slice(i * tile % half, i * tile % half + tile)
            for j in range(len(parts)):
                a_ref, b_ref, c_ref, d_ref = refs[4 * j : 4 * j + 4]
                own = jnp.where(keep, a_ref[rows].astype(F32), b_ref[rows].astype(F32)).astype(BF16)
                other = jnp.where(core == i * tile // half, c_ref[part], d_ref[part])
                low = slice(j * wide, (j + 1) * wide)
                high = slice(width + j * wide, width + (j + 1) * wide)
                held[i, :, low] = jnp.where(first, own, other)
                held[i, :, high] = jnp.where(first, other, own)
            copies.append(pltpu.make_async_copy(held.at[i], out_ref.at[rows], sems.at[i]))
            copies[-1].start()
        for copy in copies:
            copy.wait()

    return pl.pallas_call(
        kernel,
        in_specs=[pl.BlockSpec(memory_space=SMEM)] + [pl.BlockSpec(memory_space=VMEM)] * len(args),
        out_specs=pl.BlockSpec(memory_space=pl.ANY),
        out_shape=shaped((length, 2 * width)),
        scratch_shapes=[VMEM((steps, tile, 2 * width), BF16), pltpu.SemaphoreType.DMA((steps,))],
        compiler_params=pltpu.CompilerParams(vmem_limit_bytes=8 * 2**20),
        name="assemble",
    )(here, *[pltpu.with_memory_space_constraint(a, VMEM) for a in args])


def from_partner(x, axis, bit):
    return lax.ppermute(x, axis, [(i, i ^ 1 << bit) for i in range(lax.axis_size(axis))])


def gathered_plan(tokens, modality, norm_gains, qkv_weight, out_weight):
    tower_id = lax.axis_index("mod")
    own_rows = modality == tower_id
    gathered = lax.all_gather(tokens, "tensor", axis=1, tiled=True)
    length = gathered.shape[0]
    local_width = qkv_weight.shape[3]
    local_heads = local_width // HDIM
    gain_row = norm_gains[0]
    scale = HDIM ** (-0.5)
    wide_rows = gathered.astype(jnp.float32)
    inverse = lax.rsqrt(jnp.mean(wide_rows * wide_rows, axis=-1, keepdims=True) + 1e-05)
    row_block = (wide_rows * inverse * gain_row).astype(jnp.bfloat16)
    weight_piece = lax.all_gather(qkv_weight, "dp", axis=1, tiled=True)
    count = weight_piece.shape[1]
    columns = row_block
    projected = (
        jnp.dot(
            columns,
            weight_piece[0].reshape(count, 3 * local_width),
            preferred_element_type=jnp.float32,
        )
        .astype(jnp.bfloat16)
        .reshape(length, 3, local_heads, HDIM)
    )
    queries = projected[:, 0]
    own_pair = projected[:, 1:]
    other_pair = from_partner(own_pair, "mod", 0)
    key_pairs = jnp.where(own_rows[:, None, None, None], own_pair, other_pair)
    key_pos = jnp.arange(length, dtype=jnp.int32)
    scores = (
        jnp.einsum("qhd,khd->hqk", queries, key_pairs[:, 0], preferred_element_type=jnp.float32)
        * scale
    )
    allowed = key_pos[None, :] <= key_pos[:, None]
    scores = jnp.where(allowed[None], scores, -jnp.inf)
    soft_weights = jax.nn.softmax(scores, axis=-1).astype(jnp.bfloat16)
    attended = jnp.einsum(
        "hqk,khd->qhd", soft_weights, key_pairs[:, 1], preferred_element_type=jnp.float32
    )
    attended = attended.astype(jnp.bfloat16).reshape(queries.shape[0], local_width)
    all_heads = lax.all_gather(attended, "tensor", axis=1, tiled=True)
    weight_piece = lax.all_gather(out_weight, "dp", axis=1, tiled=True)
    columns = all_heads
    projected_out = jnp.dot(columns, weight_piece[0], preferred_element_type=jnp.float32).astype(
        jnp.bfloat16
    )
    placed = jnp.where(own_rows[:, None], projected_out, jnp.zeros_like(projected_out))
    combined = lax.psum(placed.astype(jnp.float32).astype(jnp.bfloat16), "mod")
    return combined


def solution(mesh):
    places, shards = mesh.shape["dp"], mesh.shape["tensor"]
    mods = mesh.shape["mod"]

    def move(array, where, *earlier):
        pairs = []
        for m in range(mods):
            for d in range(places):
                for x in range(shards):
                    to = where(m, d, x)
                    if to is not None:
                        target = (to[0] * places + to[1]) * shards + to[2]
                        pairs.append(((m * places + d) * shards + x, target))
        return lax.ppermute(after(array, *earlier) if earlier else array, AXES, pairs)

    def to_core(array, *earlier):
        return move(array, lambda m, d, x: (1 - m, d, x), *earlier)

    def over_tensor(array, *earlier):
        return [array] + [
            move(array, lambda m, d, x: (m, d, (x + step) % shards), *earlier)
            for step in range(1, shards)
        ]

    def edge(m, d, x):
        return m, d ^ 2, x

    def outward(m, d, x):
        return (m, d ^ 2, x) if d // 2 in (1, 2) else None

    def inward(m, d, x):
        return (m, d ^ 2, x) if d // 2 in (0, 3) else None

    def across(m, d, x):
        return (m, (3 - d // 2) * 2 + d % 2, x) if d // 2 in (1, 2) else None

    def across_or_stay(m, d, x):
        return across(m, d, x) or (m, d, x)

    def pair(m, d, x):
        return m, d ^ 1, x

    def line_plan(tokens, modality, norm_gains, qkv_weight, out_weight):
        here = jnp.stack([lax.axis_index(name).astype(I32) for name in AXES])
        length = tokens.shape[0]
        kept = qkv_weight.shape[1]
        half = length // 2
        gains = norm_gains[0].reshape(places, 1, kept)
        own_kind = modality[None, :]

        weight = after(qkv_weight[0].transpose(1, 0, 2), here, gains, own_kind)
        low_a, high_a, mine_a, away_a = halves(here, weight, 0, 2)
        m1a = move(low_a, across_or_stay)
        e1a = move(away_a, edge)
        p1a = move(mine_a, pair)

        begun = (m1a,)
        m2a = move(high_a, across, e1a, p1a, *begun)
        e2a = move(m1a, edge, e1a, p1a)
        p2a = move(e1a, pair, p1a, *begun)
        rows, top, bottom = own_rows_of(here, after(tokens, *begun), own_kind)
        fetched = over_tensor(rows)
        low_b, high_b, mine_b, away_b = halves(here, after(weight, *begun), 1, 2)

        begun = (m2a, mine_b)
        m3a = move(e2a, across, p2a, *begun)
        passed_top = move(top, edge, e2a, p2a, *begun)
        third_a = choose(here, after(e2a, *begun), m2a)
        p3a = move(third_a, pair, p2a)

        begun = (m3a,)
        swapped = [to_core(a, *begun) for a in fetched[1:]]
        shape = (2, places, length, kept)
        normed = normalize(
            here, "own", None, gains, after(tokens, *begun), fetched[1:], swapped, shape, 0, half
        )
        m4a = move(e1a, across, passed_top, p3a, *begun)
        m1b = move(low_b, across_or_stay, passed_top, p3a, *begun)
        passed_bottom = move(bottom, edge, passed_top, p3a, *begun)
        p1b = move(mine_b, pair, p3a, *begun)
        part_top = over_tensor(after(passed_top, *begun))
        low_o, high_o, mine_o, away_o = halves(here, after(out_weight, *begun), 0, 1)

        begun = (passed_bottom, normed, mine_o)
        e3a = move(m3a, outward, part_top[-1], *begun)
        i1o = move(low_o, inward, part_top[-1], *begun)
        p1o = move(mine_o, pair, p1b, *begun)
        other_kind = kinds_behind(here, after(passed_bottom, *begun), length)
        part_bottom = over_tensor(after(passed_bottom, *begun))
        top_swapped = [to_core(a, *begun) for a in part_top]
        first_a = [(0, mine_a, p1a), (1, e1a, p2a), (2, third_a, p3a)]
        total_a = project(here, "own", after(normed, *begun), first_a, fresh=True)
        normed = normalize(
            here, "partner", normed, gains, None, part_top, top_swapped, shape, 0, half // 2
        )

        begun = (m4a, m1b, normed, total_a, other_kind)
        m2b = move(high_b, across, *begun)
        e2b = move(m1b, edge, e3a, i1o, p1o, part_bottom[-1], *begun)
        fourth_a = choose(here, after(e3a, *begun), m4a)
        p4a = move(fourth_a, pair, p1o)
        bottom_swapped = [to_core(a, *begun) for a in part_bottom]
        normed = normalize(
            here, "partner", normed, gains, None, part_bottom, bottom_swapped, shape, half // 2, half // 2
        )
        total_a = project(here, "partner", normed, first_a, total_a, fresh=True)

        begun = (m2b, total_a)
        m3b = move(e2b, across, *begun)
        e1b = move(away_b, edge, e2b, p4a, *begun)
        third_b = choose(here, after(e2b, *begun), m2b)
        p3b = move(third_b, pair, p4a)
        last_a = [(3, fourth_a, p4a)]
        late_normed = after(normed, *begun)
        theirs_a = project(here, 1, late_normed, last_a, total_a, final=True)
        got_a = to_core(theirs_a)
        ours_a = project(here, 0, late_normed, last_a, total_a, final=True)

        begun = (m3b, theirs_a, ours_a)
        m4b = move(e1b, across, *begun)
        e3b = move(m3b, outward, e1b, p3b, *begun)
        i2o = move(high_o, inward, e1b, p3b, *begun)
        p2b = move(e1b, pair, p3b, *begun)
        attended_a = attend(here, own_kind, other_kind, after(ours_a, *begun), got_a)
        first_b = [(0, mine_b, p1b), (2, third_b, p3b)]
        late_normed = after(normed, *begun)
        total_b = project(here, "own", late_normed, first_b, fresh=True)
        total_b = project(here, "partner", late_normed, first_b, total_b, fresh=True)
        lows = stack(here, [after(low_o, *begun), i1o])

        begun = (m4b, attended_a, total_b, lows)
        m13o = move(lows, across, i2o, *begun)
        fourth_b = choose(here, after(e3b, *begun), m4b)
        p4b = move(fourth_b, pair, p2b)
        packed_a = move(pack(here, after(low_o, *begun), attended_a), edge, e3b, p2b)
        held_a = over_tensor(after(attended_a, *begun))
        highs = stack(here, [after(high_o, *begun), i2o])
        second_b = [(1, e1b, p2b)]
        late_normed = after(normed, *begun)
        total_b = project(here, "own", late_normed, second_b, total_b)
        total_b = project(here, "partner", late_normed, second_b, total_b)

        begun = (m13o, total_b, packed_a, held_a[1], highs)
        m24o = move(highs, across, *begun)
        o23o = move(m13o, outward, *begun)
        last_b = [(3, fourth_b, p4b)]
        late_normed = after(normed, *begun)
        theirs_b = project(here, 1, late_normed, last_b, total_b, final=True)
        got_b = to_core(theirs_b)
        ours_b = project(here, 0, late_normed, last_b, total_b, final=True)
        o1o, passed_a = unpack(here, after(packed_a, ours_b), low_o, attended_a)
        second_o = choose(here, o1o, i2o)
        p2o = move(second_o, pair, p4b)
        held_a += over_tensor(passed_a)
        attended_b = attend(here, own_kind, other_kind, ours_b, got_b)
        held_b = over_tensor(attended_b)

        passed_b = move(attended_b, edge, o23o)
        begun = (m24o, o23o, held_b[1], held_a[-1], p2o, passed_b)
        late_o = choose_halves(here, after(o23o, *begun), m24o)
        held_b += over_tensor(after(passed_b, late_o[0]))
        p34o = [move(late_o[0], pair)]
        p34o.append(move(late_o[1], pair, p34o[0]))
        pieces_a = stack(here, [after(held_a[0], late_o[0])] + held_a[1:])
        pieces_a = (pieces_a, to_core(pieces_a))
        near = [(0, mine_o, p1o), (1, second_o, p2o)]
        swapped = [to_core(a, late_o[0]) for a in held_b[:-1]]
        total = combine(here, ("partner", "own"), [(after(pieces_a[0], *swapped), pieces_a[1], 0, near)])
        swapped.append(to_core(held_b[-1], total, p34o[0]))
        pieces_b = stack(here, [after(held_b[0], total, p34o[0])] + held_b[1:])
        pieces_b = (pieces_b, stack(here, swapped))

        fars, rests = [], []
        for side in range(2):
            last = [(2, late_o[side], p34o[side], 0), (3, late_o[side], p34o[side], 1)]
            rests.append([pieces_a + (0, last), pieces_b + (1, near + last)])
            ready = after(total, fars[-1]) if fars else total
            kept_away, sent_away = combine(here, ("partner",), rests[side], ready, (0, side), True)
            joined = join(here, other_kind, kept_away, to_core(sent_away))
            fars.append(move(joined, edge))
        parts = []
        for side in range(2):
            near_part = combine(here, ("own",), rests[side], after(total, joined), (1, side))
            parts.append((near_part, to_core(near_part), fars[side], to_core(fars[side])))
        return assemble(here, own_kind, parts)

    return jax.shard_map(
        line_plan if places == 8 else gathered_plan,
        mesh=mesh,
        in_specs=(
            P("dp", "tensor"),
            P("dp"),
            P("mod", None),
            P("mod", "dp", None, "tensor"),
            P("mod", "dp", "tensor"),
        ),
        out_specs=P("dp", "tensor"),
        check_vma=False,
    )
```

```python
import jax
import jax.numpy as jnp
from jax import lax
from jax.experimental import pallas as pl
from jax.experimental.pallas import tpu as pltpu
from jax.sharding import PartitionSpec as P

HDIM = 128
AXES = ("mod", "dp", "tensor")
F32, BF16, I32 = jnp.float32, jnp.bfloat16, jnp.int32
VMEM, SMEM = pltpu.VMEM, pltpu.SMEM


def after(array, *earlier):
    return lax.optimization_barrier((array,) + earlier)[0]


class Here:
    def __init__(self, ref):
        self.core, place, self.own = ref[0], ref[1], ref[2]
        self.z, self.y = place >> 1, place & 1
        self.column = (self.z ^ (self.z >> 1)) & 1
        self.outer = self.column == 0
        self.which = self.core ^ (self.z & 1)
        self.at = [self.z, self.z ^ 1, jnp.where(self.z < 2, 2, 1), 3 - 3 * (self.z >> 1)]

    def slot(self, name):
        return {"own": self.which, "partner": 1 - self.which}.get(name, name)


def call(name, kernel, here, args, out_shape, aliases=None, scratch=8):
    return pl.pallas_call(
        kernel,
        in_specs=[pl.BlockSpec(memory_space=SMEM)] + [pl.BlockSpec(memory_space=VMEM)] * len(args),
        out_specs=jax.tree.map(lambda _: pl.BlockSpec(memory_space=VMEM), out_shape),
        out_shape=jax.tree.map(lambda shape: VMEM(shape.shape, shape.dtype), out_shape),
        input_output_aliases=aliases or {},
        compiler_params=pltpu.CompilerParams(vmem_limit_bytes=scratch * 2**20),
        name=name,
    )(here, *[pltpu.with_memory_space_constraint(a, VMEM) for a in args])


def shaped(shape, dtype=BF16):
    return jax.ShapeDtypeStruct(shape, dtype)


def by_row(kind):
    return jnp.broadcast_to(kind.astype(F32), (128, kind.shape[1])).T.astype(I32)


def halves(here, weight, chunk, chunks):
    kinds, depth, width = weight.shape
    half = width // 2
    part = half // chunks

    def kernel(h_ref, in_ref, low_ref, high_ref, mine_ref, away_ref):
        outer = Here(h_ref).outer
        for kind in range(kinds):
            low = in_ref[kind, :, chunk * part : (chunk + 1) * part]
            high = in_ref[kind, :, half + chunk * part : half + (chunk + 1) * part]
            low_ref[kind] = low
            high_ref[kind] = high
            mine_ref[kind] = jnp.where(outer, low, high)
            away_ref[kind] = jnp.where(outer, high, low)

    return call("halves", kernel, here, [weight], [shaped((kinds, depth, part))] * 4)


def fetched_halves(here, weight, chunk, chunks):
    kinds, depth, width = weight.shape
    half = width // 2
    part = half // chunks

    def kernel(h_ref, in_ref, low_ref, high_ref, mine_ref, away_ref, sems):
        copies = []
        for i, ref in enumerate((low_ref, high_ref)):
            columns = pl.ds(i * half + chunk * part, part)
            copies.append(pltpu.make_async_copy(in_ref.at[:, :, columns], ref, sems.at[i]))
            copies[-1].start()
        for copy in copies:
            copy.wait()
        outer = Here(h_ref).outer
        mine_ref[...] = jnp.where(outer, low_ref[...], high_ref[...])
        away_ref[...] = jnp.where(outer, high_ref[...], low_ref[...])

    return pl.pallas_call(
        kernel,
        in_specs=[pl.BlockSpec(memory_space=SMEM), pl.BlockSpec(memory_space=pl.ANY)],
        out_specs=[pl.BlockSpec(memory_space=VMEM)] * 4,
        out_shape=[VMEM((kinds, depth, part), weight.dtype)] * 4,
        scratch_shapes=[pltpu.SemaphoreType.DMA((2,))],
        compiler_params=pltpu.CompilerParams(vmem_limit_bytes=60 * 2**20),
        name="fetched_halves",
    )(here, weight)


def own_rows_of(here, tokens, kind):
    length, features = tokens.shape
    half = length // 2
    extra = 16

    def kernel(h_ref, in_ref, kind_ref, rows_ref, top_ref, bottom_ref):
        rows = jnp.where(h_ref[0] == 0, in_ref[:half], in_ref[half:])
        rows_ref[...] = rows
        top_ref[...] = rows[: half // 2]
        bottom_ref[: half // 2] = rows[half // 2 :]
        bottom_ref[half // 2 :, :length] = jnp.broadcast_to(
            kind_ref[...].astype(F32), (extra, length)
        ).astype(BF16)
        bottom_ref[half // 2 :, length:] = jnp.zeros((extra, features - length), BF16)

    outs = [shaped((rows, features)) for rows in (half, half // 2, half // 2 + extra)]
    return call("own_rows_of", kernel, here, [tokens, kind], outs)


def kinds_behind(here, part, length):
    def kernel(_, in_ref, out_ref):
        out_ref[...] = in_ref[length // 4 :, :length].astype(F32)[:1].astype(I32)

    return call("kinds_behind", kernel, here, [part], shaped((1, length), I32))


def choose(here, from_edge, from_middle):
    def kernel(h_ref, a_ref, b_ref, out_ref):
        outer = Here(h_ref).outer

        @pl.when(outer)
        def _():
            out_ref[...] = a_ref[...]

        @pl.when(jnp.logical_not(outer))
        def _():
            out_ref[...] = b_ref[...]

    return call("choose", kernel, here, [from_edge, from_middle], shaped(from_edge.shape))


def choose_halves(here, from_edge, from_middle):
    shape = from_edge.shape
    half = shape[-1] // 2

    def kernel(h_ref, a_ref, b_ref, low_ref, high_ref):
        outer = Here(h_ref).outer
        for ref, wanted in ((a_ref, outer), (b_ref, jnp.logical_not(outer))):

            @pl.when(wanted)
            def _(ref=ref):
                for i in range(shape[0]):
                    low_ref[i] = ref[i, :, :, :half]
                    high_ref[i] = ref[i, :, :, half:]

    outs = [shaped(shape[:-1] + (half,))] * 2
    return call("choose_halves", kernel, here, [from_edge, from_middle], outs)


def stack(here, arrays):
    def kernel(_, *refs):
        for i in range(len(arrays)):
            refs[-1][i] = refs[i][...]

    return call("stack", kernel, here, arrays, shaped((len(arrays),) + arrays[0].shape))


def pack(here, block, piece):
    _, depth, features = block.shape
    length, width = piece.shape
    cuts = features // width

    def kernel(_, block_ref, piece_ref, out_ref):
        for i in range(cuts):
            out_ref[i * depth : (i + 1) * depth] = block_ref[0, :, i * width : (i + 1) * width]
        out_ref[cuts * depth :] = piece_ref[...]

    return call("pack", kernel, here, [block, piece], shaped((cuts * depth + length, width)))


def unpack(here, packed, block, piece):
    _, depth, features = block.shape
    _, width = piece.shape
    cuts = features // width

    def kernel(_, in_ref, block_ref, piece_ref):
        for i in range(cuts):
            block_ref[0, :, i * width : (i + 1) * width] = in_ref[i * depth : (i + 1) * depth]
        piece_ref[...] = in_ref[cuts * depth :]

    return call("unpack", kernel, here, [packed], [shaped(block.shape), shaped(piece.shape)])


def normalize(here, slot, held, gains, whole, mine, theirs, shape, start, count):
    _, _, length, kept = shape
    shards = len(mine) + (whole is not None)
    features = (whole if whole is not None else mine[0]).shape[1]
    tile = 32 if count % 32 == 0 else count
    half = length // 2
    per = features // kept
    args = ([] if held is None else [held]) + [gains] + ([] if whole is None else [whole])
    args += list(mine) + list(theirs)

    def kernel(h_ref, *refs):
        at_place = Here(h_ref)
        core, own, into = at_place.core, at_place.own, at_place.slot(slot)
        out_ref = refs[-1]
        refs = list(refs[0 if held is None else 1 : -1])
        gain_ref = refs.pop(0)
        whole_ref = None if whole is None else refs.pop(0)
        shard_of = [lax.rem(own - step + shards, shards) for step in range(shards)]

        def step(i, carry):
            for group, first in ((refs[: len(mine)], core), (refs[len(mine) :], 1 - core)):
                row = pl.multiple_of(first * half + start + i * tile, tile)
                at = pl.ds(pl.multiple_of(i * tile, tile), tile)
                found = [(ref, at) for ref in group]
                if whole_ref is not None:
                    found = [(whole_ref, pl.ds(row, tile))] + found
                total = jnp.zeros((tile, 1), F32)
                for ref, rows in found:
                    wide = ref[rows, :].astype(F32)
                    total = total + jnp.sum(wide * wide, axis=-1, keepdims=True)
                inverse = lax.rsqrt(total / (shards * features) + 1e-05)
                for shard, (ref, rows) in zip(shard_of, found):
                    for j in range(per):
                        block = shard * per + j
                        wide = ref[rows, j * kept : (j + 1) * kept].astype(F32)
                        out_ref[into, block, pl.ds(row, tile), :] = (
                            wide * inverse * gain_ref[block]
                        ).astype(BF16)
            return carry

        lax.fori_loop(0, count // tile, step, 0)

    return call("normalize", kernel, here, args, shaped(shape), None if held is None else {1: 0})


def project(here, slot, normed, blocks, total=None, final=False, fresh=False):
    slots, _, length, kept = normed.shape
    kinds, _, width = blocks[0][1].shape
    count = len(blocks)
    args = [normed] + [b for _, near, far in blocks for b in (near, far)]
    args += [] if total is None else [total]

    def kernel(h_ref, *refs):
        at_place = Here(h_ref)
        into = at_place.slot(slot)
        normed_ref, out_ref = refs[0], refs[-1]
        for kind in range(kinds):
            columns = slice(kind * width, (kind + 1) * width)
            summed = None if fresh else refs[1 + 2 * count][into, :, columns]
            for i, (arrival, _, _) in enumerate(blocks):
                for j, y in enumerate((at_place.y, 1 - at_place.y)):
                    part = jnp.dot(
                        normed_ref[into, at_place.at[arrival] * 2 + y],
                        refs[1 + 2 * i + j][kind],
                        preferred_element_type=F32,
                    )
                    summed = part if summed is None else summed + part
            if final:
                out_ref[:, columns] = summed.astype(BF16)
            else:
                out_ref[into, :, columns] = summed

    if final:
        return call("project", kernel, here, args, shaped((length, kinds * width)))
    aliases = None if total is None else {2 + 2 * count: 0}
    return call("project", kernel, here, args, shaped((slots, length, kinds * width), F32), aliases)


def attend(here, own_kind, other_kind, own, got):
    length, width = own.shape[0], own.shape[1] // 3
    heads = width // HDIM
    scale = HDIM ** (-0.5)
    tile = 128 if length % 128 == 0 else length

    def kernel(h_ref, own_kind_ref, other_kind_ref, own_ref, got_ref, out_ref):
        at_place = Here(h_ref)
        kind = jnp.where(at_place.which == 0, own_kind_ref[...], other_kind_ref[...])
        keep = by_row(kind) == at_place.core

        def pick(j):
            columns = slice(j * HDIM, (j + 1) * HDIM)
            return jnp.where(
                keep, own_ref[:, columns].astype(F32), got_ref[:, columns].astype(F32)
            ).astype(BF16)

        for h in range(heads):
            query, key, value = pick(h), pick(heads + h), pick(2 * heads + h)
            for i in range(length // tile):
                low, high = i * tile, (i + 1) * tile
                scores = lax.dot_general(
                    query[low:high], key[:high], (((1,), (1,)), ((), ())), preferred_element_type=F32
                )
                rows = low + lax.broadcasted_iota(I32, (tile, high), 0)
                cols = lax.broadcasted_iota(I32, (tile, high), 1)
                scores = jnp.where(cols <= rows, scores * scale, -jnp.inf)
                top = jnp.max(scores, axis=-1, keepdims=True)
                raised = jnp.exp(scores - top)
                share = 1.0 / jnp.sum(raised, axis=-1, keepdims=True)
                probs = (raised * share).astype(BF16)
                out = jnp.dot(probs, value[:high], preferred_element_type=F32)
                out_ref[low:high, h * HDIM : (h + 1) * HDIM] = out.astype(BF16)

    return call("attend", kernel, here, [own_kind, other_kind, own, got], shaped((length, width)))


def combine(here, slots, groups, total=None, part=None, cut=False):
    held_pieces, length, held = groups[0][0].shape
    shards = held_pieces // 2
    plain = [pair for group in groups for pair in group[3] if len(pair) == 3]
    features = plain[0][1].shape[-1]
    offset, side = (0, 0) if part is None else part
    wide = features if part is None else features // 2
    tile = min(wide, 256)
    half = length // 2
    terms = [group[:3] + (pair,) for group in groups for pair in group[3]]
    count = len(terms)
    args = [pieces for term in terms for pieces in term[:2]]
    args += [b for term in terms for b in term[3][1:3]] + ([] if total is None else [total])

    def kernel(h_ref, *refs):
        at_place = Here(h_ref)
        outs = refs[-2:] if cut else refs[-1:]
        found = []
        for z in at_place.at:
            shard = lax.rem(at_place.own - (z >> 1) + shards, shards)
            found.append(jnp.where((z & 1) == at_place.column, 0, shards) + shard)
        for s, name in enumerate(slots):
            first_slot = at_place.slot(name) == 0
            rows = [
                jnp.where(
                    first_slot, refs[2 * i][found[arrival]], refs[2 * i + 1][found[arrival]]
                )
                for i, (_, _, _, (arrival, *_)) in enumerate(terms)
            ]
            for n in range(wide // tile):
                columns = slice(n * tile, (n + 1) * tile)
                whole = slice(side * wide + n * tile, side * wide + (n + 1) * tile)
                summed = None if total is None else refs[4 * count][offset + s, :, whole]
                for i, (_, _, parity, (_, _, _, *index)) in enumerate(terms):
                    place = (*index, 0, slice(None), columns if index else whole)
                    near = refs[2 * count + 2 * i][place]
                    far = refs[2 * count + 2 * i + 1][place]
                    block = jnp.where(at_place.y == parity, near, far)
                    product = jnp.dot(rows[i], block, preferred_element_type=F32)
                    summed = product if summed is None else summed + product
                if part is None:
                    outs[0][s, :, columns] = summed
                elif cut:
                    result = summed.astype(BF16)
                    first = at_place.core == 0
                    outs[0][:, columns] = jnp.where(first, result[:half], result[half:])
                    outs[1][:, columns] = jnp.where(first, result[half:], result[:half])
                else:
                    outs[0][:, columns] = summed.astype(BF16)

    if part is None:
        out_shape = shaped((len(slots), length, wide), F32)
    elif cut:
        out_shape = [shaped((half, wide))] * 2
    else:
        out_shape = shaped((length, wide))
    return call("combine", kernel, here, args, out_shape)


def join(here, kind, kept, got):
    half = kept.shape[0]

    def kernel(h_ref, kind_ref, a_ref, b_ref, out_ref):
        core = h_ref[0]
        rows = by_row(kind_ref[...])[:, :1]
        rows = jnp.where(core == 0, rows[:half], rows[half:])
        out_ref[...] = jnp.where(
            rows == core, a_ref[...].astype(F32), b_ref[...].astype(F32)
        ).astype(BF16)

    return call("join", kernel, here, [kind, kept, got], shaped(kept.shape))


def assemble(here, kind, parts):
    length, wide = parts[0][0].shape
    width = wide * len(parts)
    steps = 4
    tile = length // steps
    half = length // 2
    args = [kind] + [array for part in parts for array in part]

    def kernel(h_ref, kind_ref, *refs):
        out_ref, held, sems = refs[-3:]
        at_place = Here(h_ref)
        core, first = at_place.core, at_place.column == 0
        copies = []
        kind = by_row(kind_ref[...])[:, :1]
        for i in range(steps):
            rows = slice(i * tile, (i + 1) * tile)
            keep = kind[rows] == core
            part = slice(i * tile % half, i * tile % half + tile)
            for j in range(len(parts)):
                a_ref, b_ref, c_ref, d_ref = refs[4 * j : 4 * j + 4]
                own = jnp.where(keep, a_ref[rows].astype(F32), b_ref[rows].astype(F32)).astype(BF16)
                other = jnp.where(core == i * tile // half, c_ref[part], d_ref[part])
                low = slice(j * wide, (j + 1) * wide)
                high = slice(width + j * wide, width + (j + 1) * wide)
                held[i, :, low] = jnp.where(first, own, other)
                held[i, :, high] = jnp.where(first, other, own)
            copies.append(pltpu.make_async_copy(held.at[i], out_ref.at[rows], sems.at[i]))
            copies[-1].start()
        for copy in copies:
            copy.wait()

    return pl.pallas_call(
        kernel,
        in_specs=[pl.BlockSpec(memory_space=SMEM)] + [pl.BlockSpec(memory_space=VMEM)] * len(args),
        out_specs=pl.BlockSpec(memory_space=pl.ANY),
        out_shape=shaped((length, 2 * width)),
        scratch_shapes=[VMEM((steps, tile, 2 * width), BF16), pltpu.SemaphoreType.DMA((steps,))],
        compiler_params=pltpu.CompilerParams(vmem_limit_bytes=8 * 2**20),
        name="assemble",
    )(here, *[pltpu.with_memory_space_constraint(a, VMEM) for a in args])


def from_partner(x, axis, bit):
    return lax.ppermute(x, axis, [(i, i ^ 1 << bit) for i in range(lax.axis_size(axis))])


def gathered_plan(tokens, modality, norm_gains, qkv_weight, out_weight):
    tower_id = lax.axis_index("mod")
    own_rows = modality == tower_id
    gathered = lax.all_gather(tokens, "tensor", axis=1, tiled=True)
    length = gathered.shape[0]
    local_width = qkv_weight.shape[3]
    local_heads = local_width // HDIM
    gain_row = norm_gains[0]
    scale = HDIM ** (-0.5)
    wide_rows = gathered.astype(jnp.float32)
    inverse = lax.rsqrt(jnp.mean(wide_rows * wide_rows, axis=-1, keepdims=True) + 1e-05)
    row_block = (wide_rows * inverse * gain_row).astype(jnp.bfloat16)
    weight_piece = lax.all_gather(qkv_weight, "dp", axis=1, tiled=True)
    count = weight_piece.shape[1]
    columns = row_block
    projected = (
        jnp.dot(
            columns,
            weight_piece[0].reshape(count, 3 * local_width),
            preferred_element_type=jnp.float32,
        )
        .astype(jnp.bfloat16)
        .reshape(length, 3, local_heads, HDIM)
    )
    queries = projected[:, 0]
    own_pair = projected[:, 1:]
    other_pair = from_partner(own_pair, "mod", 0)
    key_pairs = jnp.where(own_rows[:, None, None, None], own_pair, other_pair)
    key_pos = jnp.arange(length, dtype=jnp.int32)
    scores = (
        jnp.einsum("qhd,khd->hqk", queries, key_pairs[:, 0], preferred_element_type=jnp.float32)
        * scale
    )
    allowed = key_pos[None, :] <= key_pos[:, None]
    scores = jnp.where(allowed[None], scores, -jnp.inf)
    soft_weights = jax.nn.softmax(scores, axis=-1).astype(jnp.bfloat16)
    attended = jnp.einsum(
        "hqk,khd->qhd", soft_weights, key_pairs[:, 1], preferred_element_type=jnp.float32
    )
    attended = attended.astype(jnp.bfloat16).reshape(queries.shape[0], local_width)
    all_heads = lax.all_gather(attended, "tensor", axis=1, tiled=True)
    weight_piece = lax.all_gather(out_weight, "dp", axis=1, tiled=True)
    columns = all_heads
    projected_out = jnp.dot(columns, weight_piece[0], preferred_element_type=jnp.float32).astype(
        jnp.bfloat16
    )
    placed = jnp.where(own_rows[:, None], projected_out, jnp.zeros_like(projected_out))
    combined = lax.psum(placed.astype(jnp.float32).astype(jnp.bfloat16), "mod")
    return combined


def solution(mesh):
    places, shards = mesh.shape["dp"], mesh.shape["tensor"]
    mods = mesh.shape["mod"]

    def move(array, where, *earlier):
        pairs = []
        for m in range(mods):
            for d in range(places):
                for x in range(shards):
                    to = where(m, d, x)
                    if to is not None:
                        target = (to[0] * places + to[1]) * shards + to[2]
                        pairs.append(((m * places + d) * shards + x, target))
        return lax.ppermute(after(array, *earlier) if earlier else array, AXES, pairs)

    def to_core(array, *earlier):
        return move(array, lambda m, d, x: (1 - m, d, x), *earlier)

    def over_tensor(array, *earlier):
        return [array] + [
            move(array, lambda m, d, x: (m, d, (x + step) % shards), *earlier)
            for step in range(1, shards)
        ]

    def edge(m, d, x):
        return m, d ^ 2, x

    def outward(m, d, x):
        return (m, d ^ 2, x) if d // 2 in (1, 2) else None

    def inward(m, d, x):
        return (m, d ^ 2, x) if d // 2 in (0, 3) else None

    def across(m, d, x):
        return (m, (3 - d // 2) * 2 + d % 2, x) if d // 2 in (1, 2) else None

    def across_or_stay(m, d, x):
        return across(m, d, x) or (m, d, x)

    def pair(m, d, x):
        return m, d ^ 1, x

    def line_plan(tokens, modality, norm_gains, qkv_weight, out_weight):
        here = jnp.stack([lax.axis_index(name).astype(I32) for name in AXES])
        length = tokens.shape[0]
        kept = qkv_weight.shape[1]
        half = length // 2
        gains = norm_gains[0].reshape(places, 1, kept)
        own_kind = modality[None, :]

        weight = after(qkv_weight[0].transpose(1, 0, 2), here, gains, own_kind)
        low_a, high_a, mine_a, away_a = fetched_halves(here, weight, 0, 2)
        m1a = move(low_a, across_or_stay)
        e1a = move(away_a, edge)
        p1a = move(mine_a, pair)

        begun = (m1a,)
        m2a = move(high_a, across, e1a, p1a, *begun)
        e2a = move(m1a, edge, e1a, p1a)
        p2a = move(e1a, pair, p1a, *begun)
        rows, top, bottom = own_rows_of(here, after(tokens, *begun), own_kind)
        fetched = over_tensor(rows)
        low_b, high_b, mine_b, away_b = halves(here, after(weight, *begun), 1, 2)

        begun = (m2a, mine_b)
        m3a = move(e2a, across, p2a, *begun)
        passed_top = move(top, edge, e2a, p2a, *begun)
        third_a = choose(here, after(e2a, *begun), m2a)
        p3a = move(third_a, pair, p2a)

        begun = (m3a,)
        swapped = [to_core(a, *begun) for a in fetched[1:]]
        shape = (2, places, length, kept)
        normed = normalize(
            here, "own", None, gains, after(tokens, *begun), fetched[1:], swapped, shape, 0, half
        )
        m4a = move(e1a, across, passed_top, p3a, *begun)
        m1b = move(low_b, across_or_stay, passed_top, p3a, *begun)
        passed_bottom = move(bottom, edge, passed_top, p3a, *begun)
        p1b = move(mine_b, pair, p3a, *begun)
        part_top = over_tensor(after(passed_top, *begun))
        low_o, high_o, mine_o, away_o = halves(here, after(out_weight, *begun), 0, 1)

        begun = (passed_bottom, normed, mine_o)
        e3a = move(m3a, outward, part_top[-1], *begun)
        i1o = move(low_o, inward, part_top[-1], *begun)
        p1o = move(mine_o, pair, p1b, *begun)
        other_kind = kinds_behind(here, after(passed_bottom, *begun), length)
        part_bottom = over_tensor(after(passed_bottom, *begun))
        top_swapped = [to_core(a, *begun) for a in part_top]
        first_a = [(0, mine_a, p1a), (1, e1a, p2a), (2, third_a, p3a)]
        total_a = project(here, "own", after(normed, *begun), first_a, fresh=True)
        normed = normalize(
            here, "partner", normed, gains, None, part_top, top_swapped, shape, 0, half // 2
        )

        begun = (m4a, m1b, normed, total_a, other_kind)
        m2b = move(high_b, across, *begun)
        e2b = move(m1b, edge, e3a, i1o, p1o, part_bottom[-1], *begun)
        fourth_a = choose(here, after(e3a, *begun), m4a)
        p4a = move(fourth_a, pair, p1o)
        bottom_swapped = [to_core(a, *begun) for a in part_bottom]
        normed = normalize(
            here, "partner", normed, gains, None, part_bottom, bottom_swapped, shape, half // 2, half // 2
        )
        total_a = project(here, "partner", normed, first_a, total_a, fresh=True)

        begun = (m2b, total_a)
        m3b = move(e2b, across, *begun)
        e1b = move(away_b, edge, e2b, p4a, *begun)
        third_b = choose(here, after(e2b, *begun), m2b)
        p3b = move(third_b, pair, p4a)
        last_a = [(3, fourth_a, p4a)]
        late_normed = after(normed, *begun)
        theirs_a = project(here, 1, late_normed, last_a, total_a, final=True)
        got_a = to_core(theirs_a)
        ours_a = project(here, 0, late_normed, last_a, total_a, final=True)

        begun = (m3b, theirs_a, ours_a)
        m4b = move(e1b, across, *begun)
        e3b = move(m3b, outward, e1b, p3b, *begun)
        i2o = move(high_o, inward, e1b, p3b, *begun)
        p2b = move(e1b, pair, p3b, *begun)
        attended_a = attend(here, own_kind, other_kind, after(ours_a, *begun), got_a)
        first_b = [(0, mine_b, p1b), (2, third_b, p3b)]
        late_normed = after(normed, *begun)
        total_b = project(here, "own", late_normed, first_b, fresh=True)
        total_b = project(here, "partner", late_normed, first_b, total_b, fresh=True)
        lows = stack(here, [after(low_o, *begun), i1o])

        begun = (m4b, attended_a, total_b, lows)
        m13o = move(lows, across, i2o, *begun)
        fourth_b = choose(here, after(e3b, *begun), m4b)
        p4b = move(fourth_b, pair, p2b)
        packed_a = move(pack(here, after(low_o, *begun), attended_a), edge, e3b, p2b)
        held_a = over_tensor(after(attended_a, *begun))
        highs = stack(here, [after(high_o, *begun), i2o])
        second_b = [(1, e1b, p2b)]
        late_normed = after(normed, *begun)
        total_b = project(here, "own", late_normed, second_b, total_b)
        total_b = project(here, "partner", late_normed, second_b, total_b)

        begun = (m13o, total_b, packed_a, held_a[1], highs)
        m24o = move(highs, across, *begun)
        o23o = move(m13o, outward, *begun)
        last_b = [(3, fourth_b, p4b)]
        late_normed = after(normed, *begun)
        theirs_b = project(here, 1, late_normed, last_b, total_b, final=True)
        got_b = to_core(theirs_b)
        ours_b = project(here, 0, late_normed, last_b, total_b, final=True)
        o1o, passed_a = unpack(here, after(packed_a, ours_b), low_o, attended_a)
        second_o = choose(here, o1o, i2o)
        p2o = move(second_o, pair, p4b)
        held_a += over_tensor(passed_a)
        attended_b = attend(here, own_kind, other_kind, ours_b, got_b)
        held_b = over_tensor(attended_b)

        passed_b = move(attended_b, edge, o23o)
        begun = (m24o, o23o, held_b[1], held_a[-1], p2o, passed_b)
        late_o = choose_halves(here, after(o23o, *begun), m24o)
        held_b += over_tensor(after(passed_b, late_o[0]))
        p34o = [move(late_o[0], pair)]
        p34o.append(move(late_o[1], pair, p34o[0]))
        pieces_a = stack(here, [after(held_a[0], late_o[0])] + held_a[1:])
        pieces_a = (pieces_a, to_core(pieces_a))
        near = [(0, mine_o, p1o), (1, second_o, p2o)]
        swapped = [to_core(a, late_o[0]) for a in held_b[:-1]]
        total = combine(here, ("partner", "own"), [(after(pieces_a[0], *swapped), pieces_a[1], 0, near)])
        swapped.append(to_core(held_b[-1], total, p34o[0]))
        pieces_b = stack(here, [after(held_b[0], total, p34o[0])] + held_b[1:])
        pieces_b = (pieces_b, stack(here, swapped))

        fars, rests = [], []
        for side in range(2):
            last = [(2, late_o[side], p34o[side], 0), (3, late_o[side], p34o[side], 1)]
            rests.append([pieces_a + (0, last), pieces_b + (1, near + last)])
            ready = after(total, fars[-1]) if fars else total
            kept_away, sent_away = combine(here, ("partner",), rests[side], ready, (0, side), True)
            joined = join(here, other_kind, kept_away, to_core(sent_away))
            fars.append(move(joined, edge))
        parts = []
        for side in range(2):
            near_part = combine(here, ("own",), rests[side], after(total, joined), (1, side))
            parts.append((near_part, to_core(near_part), fars[side], to_core(fars[side])))
        return assemble(here, own_kind, parts)

    return jax.shard_map(
        line_plan if places == 8 else gathered_plan,
        mesh=mesh,
        in_specs=(
            P("dp", "tensor"),
            P("dp"),
            P("mod", None),
            P("mod", "dp", None, "tensor"),
            P("mod", "dp", "tensor"),
        ),
        out_specs=P("dp", "tensor"),
        check_vma=False,
    )
```
